32 devices in a mesh: grp: 2 (over x), lat: 4 (over z), lon: 4 (over y, core).
Axes of the slice: x: 2, y: 2, z: 4, core: 2. Of those that a mesh axis runs over, the one named last changes fastest.
Arguments:
- coupled_state: bfloat16 [2, 80, 64, 512], P('grp', None, 'lat', 'lon'), may hold values from -6 to 6
- land_mask: int32 [64, 512], P('lat', 'lon'), may hold values 0 or 1
- regrid_offsets: int32 [2, 2, 4, 64, 512], P('grp', None, None, 'lat', 'lon'), may hold values from -8 to 8
- regrid_weights: float32 [2, 4, 64, 512], P('grp', None, 'lat', 'lon'), may hold values from 0.1 to 0.4
- surface_proj: float32 [2, 4, 80], replicated, may hold values from -0.625 to 0.625
- atm_in: bfloat16 [384, 84], replicated, may hold values from -0.625 to 0.625
- atm_bias: float32 [384], replicated, may hold values from -3 to 3
- atm_out: bfloat16 [80, 384], replicated, may hold values from -0.3125 to 0.3125
- ocn_in: bfloat16 [200, 9, 84], replicated, may hold values from -0.21875 to 0.21875
- ocn_bias: float32 [200], replicated, may hold values from -3 to 3
- ocn_out: bfloat16 [80, 9, 200], replicated, may hold values from -0.125 to 0.125
Outputs:
- next_state: bfloat16 [2, 80, 64, 512], P('grp', None, 'lat', 'lon')
The draws below stay inside these ranges and needn't reach their ends.
All inputs are finite; a program needn't handle non-finite values. No bound on the sum of `land_mask` on one device may be relied on, other than what follows from the above.
Results may differ from the reference program's by a relative error of at most 0.008.
Values may be sent and summed in bfloat16 or wider, within the bound.
No kernel may reach another device: no remote copies, remote signals or barrier semaphores. Data moves between devices by JAX's collectives and lax.ppermute only.
A program may use at most 64 MiB of HBM per device.

```python
import jax
import jax.numpy as jnp
from jax import lax

CH = 80
NS = 4
HA = 384
HO = 200
NK = 4
HW = 8
STEPS = 2
NR = 64
NQ = 512


def touch_ends(drawn, key, smallest, largest):
    index_at = [jax.random.randint(jax.random.fold_in(key, axis), (), 0, length) for axis, length in enumerate(drawn.shape)]
    widest = drawn.shape.index(max(drawn.shape))
    next_to = index_at[:widest] + [(index_at[widest] + 1) % drawn.shape[widest]] + index_at[widest + 1:]
    return drawn.at[tuple(index_at)].set(smallest).at[tuple(next_to)].set(largest)


def steps_of(key, dims, shards, low, high):
    def one(position, parts):
        draws = jax.random.uniform(jax.random.fold_in(jax.random.fold_in(key, 6), position), (parts,), jnp.float32, low / len(shards), high / len(shards))
        return jnp.repeat(jnp.exp(draws), dims[position] // parts).reshape((-1,) + (1,) * (len(dims) - position - 1))

    factor_of = one(*shards[0])
    for cut in shards[1:]:
        factor_of = factor_of * one(*cut)
    return factor_of


def scatter_about(key, extent, spread, most, cuts=(), kind=jnp.bfloat16):
    entries = jax.random.normal(key, extent, jnp.float32) * spread
    if len(cuts) > 0:
        entries = steps_of(key, extent, cuts, -0.22, 0.18) * entries
    return jnp.clip(entries, min=-most, max=most).astype(kind)


def setup_inputs(seed: int = 0) -> dict:
    seeds = jax.random.split(jax.random.key(seed), 12)
    coupled_state = scatter_about(seeds[0], (2, CH, NR, NQ), 1.0, 6.0, ((0, 2), (2, 4), (3, 4)))
    land_mask = touch_ends((jax.random.randint(seeds[1], (NR, NQ), 0, 10) < 7).astype(jnp.int32), jax.random.fold_in(seeds[1], 1), 0, 1)
    regrid_offsets = touch_ends(jax.random.randint(seeds[2], (2, 2, NK, NR, NQ), -HW, HW + 1), jax.random.fold_in(seeds[2], 1), -HW, HW).astype(jnp.int32)
    regrid_weights = jnp.clip(0.1 + 0.3 * jax.random.uniform(seeds[3], (2, NK, NR, NQ), jnp.float32) ** steps_of(seeds[3], (2, NK, NR, NQ), ((0, 2), (2, 4), (3, 4)), -0.2, 0.2), 0.1, 0.4)
    surface_proj = scatter_about(seeds[4], (2, NS, CH), CH ** -0.5, 0.625, (), jnp.float32)
    atm_in = scatter_about(seeds[5], (HA, CH + NS), (CH + NS) ** -0.5, 0.625)
    atm_bias = scatter_about(seeds[6], (HA,), 0.5, 3.0, (), jnp.float32)
    atm_out = scatter_about(seeds[7], (CH, HA), HA ** -0.5, 0.3125)
    ocn_in = scatter_about(seeds[8], (HO, 9, CH + NS), (9 * (CH + NS)) ** -0.5, 0.21875)
    ocn_bias = scatter_about(seeds[9], (HO,), 0.5, 3.0, (), jnp.float32)
    ocn_out = scatter_about(seeds[10], (CH, 9, HO), (9 * HO) ** -0.5, 0.125)
    return {"coupled_state": coupled_state, "land_mask": land_mask, "regrid_offsets": regrid_offsets, "regrid_weights": regrid_weights, "surface_proj": surface_proj, "atm_in": atm_in, "atm_bias": atm_bias, "atm_out": atm_out, "ocn_in": ocn_in, "ocn_bias": ocn_bias, "ocn_out": ocn_out}


def surface_fields(values, projector, keeping):
    flattened = jnp.dot(projector, values.reshape(values.shape[0], -1).astype(jnp.float32), precision=lax.Precision.HIGHEST)
    return flattened.reshape(-1, values.shape[1], values.shape[2]) * keeping


def regrid(fields, offsets, weights):
    row_total = fields.shape[1]
    col_total = fields.shape[2]
    padded = jnp.pad(fields, ((0, 0), (HW, HW), (0, 0)))
    row_ids = jnp.arange(row_total, dtype=jnp.int32)[None, :, None]
    col_ids = jnp.arange(col_total, dtype=jnp.int32)[None, None, :]
    source_rows = row_ids + HW + offsets[0]
    source_cols = (col_ids + offsets[1]) % col_total
    sources = (source_rows * col_total + source_cols).astype(jnp.int32).reshape(-1)
    picked = jnp.take(padded.reshape(fields.shape[0], -1), sources, axis=1)
    picked = picked.reshape(fields.shape[0], offsets.shape[1], row_total, col_total)
    return jnp.sum(picked * weights[None], axis=1).astype(jnp.bfloat16)


def stencil_global(values, kernel):
    channels, row_total, col_total = values.shape
    padded = jnp.pad(values, ((0, 0), (1, 1), (0, 0)))
    padded = jnp.concatenate([padded[:, :, -1:], padded, padded[:, :, :1]], axis=2)
    total = jnp.zeros((kernel.shape[0], row_total * col_total), jnp.float32)
    for shift_row in range(3):
        for shift_col in range(3):
            window = padded[:, shift_row:shift_row + row_total, shift_col:shift_col + col_total].reshape(channels, -1)
            total = total + jnp.dot(kernel[:, 3 * shift_row + shift_col, :], window, preferred_element_type=jnp.float32)
    return total.reshape(kernel.shape[0], row_total, col_total)


def air_step(previous, forcing, atm_in, atm_bias, atm_out):
    inputs = jnp.concatenate([previous, forcing], 0)
    flattened = inputs.reshape(inputs.shape[0], -1)
    hidden = jax.nn.gelu(jnp.dot(atm_in, flattened, preferred_element_type=jnp.float32) + atm_bias[:, None]).astype(jnp.bfloat16)
    update = jnp.dot(atm_out, hidden, preferred_element_type=jnp.float32)
    result = previous.reshape(previous.shape[0], -1).astype(jnp.float32) + update
    return result.astype(jnp.bfloat16).reshape(previous.shape)


def sea_step(previous, forcing, wet_cells, ocn_in, ocn_bias, ocn_out):
    inputs = jnp.concatenate([previous, forcing], 0)
    hidden = jax.nn.gelu(stencil_global(inputs, ocn_in) + ocn_bias[:, None, None]).astype(jnp.bfloat16)
    update = stencil_global(hidden, ocn_out)
    return (previous.astype(jnp.float32) + wet_cells * update).astype(jnp.bfloat16)


def reference(coupled_state, land_mask, regrid_offsets, regrid_weights, surface_proj, atm_in, atm_bias, atm_out, ocn_in, ocn_bias, ocn_out):
    wet_cells = land_mask.astype(jnp.float32)
    unmasked = jnp.ones_like(wet_cells)
    air_state = coupled_state[0]
    sea_state = coupled_state[1]
    for repeat in range(STEPS):
        air_fields = surface_fields(air_state, surface_proj[0], unmasked)
        sea_fields = surface_fields(sea_state, surface_proj[1], wet_cells)
        air_forcing = regrid(sea_fields, regrid_offsets[0], regrid_weights[0])
        sea_forcing = regrid(air_fields, regrid_offsets[1], regrid_weights[1])
        air_state = air_step(air_state, air_forcing, atm_in, atm_bias, atm_out)
        sea_state = sea_step(sea_state, sea_forcing, wet_cells, ocn_in, ocn_bias, ocn_out)
    return jnp.stack([air_state, sea_state], 0)
```

```python
import functools

import jax
import jax.numpy as jnp
from jax import lax
from jax.experimental import pallas as pl
from jax.experimental.pallas import tpu as pltpu
from jax.sharding import PartitionSpec as P

CH = 80
NS = 4
NK = 4
HW = 8
SPAN = 2 * HW + 1
HIDP = 208
F32 = jnp.float32
BF16 = jnp.bfloat16


def roll(x, shift, axis=1):
    size = x.shape[axis]
    if isinstance(shift, int):
        shift = shift % size
        if shift == 0:
            return x
    return pltpu.roll(x, shift, axis)


def lanes(shape):
    return lax.broadcasted_iota(jnp.int32, shape, len(shape) - 1)


def subs(shape):
    return lax.broadcasted_iota(jnp.int32, shape, len(shape) - 2)


class Dims:
    def __init__(self, rows):
        self.rows = rows
        self.block = 32 if rows + 4 <= 32 else 64
        self.edge = 4 * self.block
        self.pieces = self.edge // 128
        self.edge_rows = CH * self.pieces
        self.tiles = -(-(rows + 4) // 8)
        self.tall = 8 * self.tiles
        self.strip = 2 * CH + self.edge_rows


def put_edges(ref, at, edges, d):
    for piece in range(d.pieces):
        ref[at + piece * CH : at + (piece + 1) * CH, :] = edges[:, piece * 128 : (piece + 1) * 128]


def get_edges(ref, at, d):
    return jnp.concatenate(
        [ref[at + piece * CH : at + (piece + 1) * CH, :] for piece in range(d.pieces)], axis=1
    )


def edge_columns(state, d):
    lane = lanes((1, d.edge))
    block = lane // d.block
    row = lane % d.block - 2
    column = jnp.where(block == 0, 126, jnp.where(block == 1, 0, jnp.where(block == 2, 127, 1)))
    half = d.rows // 2
    own = (row >= 0) & (row < d.rows)
    target = jnp.where(own, column + 128 * (row // half), -1)
    turn = row % half

    def body(step, total):
        place = subs((256, d.edge)) == jnp.where(turn == step, target, -1)
        pair = jnp.concatenate([state[step], state[step + half]], axis=1)
        return total + jnp.dot(
            pair, place.astype(F32).astype(BF16), preferred_element_type=F32
        )

    total = lax.fori_loop(0, half, body, jnp.zeros((CH, d.edge), F32))
    return total.astype(BF16)


def emit(state, proj, keeping, fields, own_edges, top, bottom, raw, d):
    half = d.rows // 2

    def body(step, carry):
        pair = jnp.concatenate([state[step], state[step + half]], axis=1)
        parts = jnp.dot(proj[...], pair, preferred_element_type=F32)
        whole = parts[0:8] + parts[8:16] + parts[16:24]
        raw[pl.ds(pl.multiple_of(step * 8, 8), 8), :] = whole[:, :128]
        raw[pl.ds(pl.multiple_of((step + half) * 8, 8), 8), :] = whole[:, 128:]
        return carry

    lax.fori_loop(0, half, body, 0)
    for field in range(NS):
        fields[field] = (raw[pl.ds(field, d.rows, stride=8), :] * keeping[...]).astype(BF16)
    edges = edge_columns(state, d)
    put_edges(own_edges, 0, edges, d)
    for ref, first in ((top, 0), (bottom, d.rows - 2)):
        ref[0:CH, :] = state[first]
        ref[CH : 2 * CH, :] = state[first + 1]
        put_edges(ref, 2 * CH, edges, d)


def start_kernel(d, state, planes, proj, keeping, fields, own_edges, top, bottom, raw, tall):
    emit(state, proj, keeping, fields, own_edges, top, bottom, raw, d)
    for plane in range(2 * NK):
        tall[plane * d.rows : (plane + 1) * d.rows, :] = planes[plane].astype(F32)
    for ref, first in ((top, 0), (bottom, d.rows - 2)):
        strip = [tall[pl.ds(first + step, 2 * NK, stride=d.rows), :] for step in range(2)]
        ref[d.strip : d.strip + 16, :] = jnp.concatenate(strip, axis=0).astype(BF16)


def decode(code):
    shifted = code.astype(jnp.int32) + (HW * SPAN + HW)
    rows = lax.shift_right_logical(shifted * 241, 12)
    return rows - HW, shifted - rows * SPAN - HW


def select_rows(sources_x, sources_y, start, picks):
    chosen = [[jnp.zeros((8, 128), F32) for _ in range(NS)] for _ in picks]
    for shift in range(-HW, HW + 1):
        at = pl.ds(start + shift, 8)
        inside = [sources_x[field, at, :] for field in range(NS)]
        beside = [sources_y[field, at, :] for field in range(NS)]
        for slot, (rows, index, within) in enumerate(picks):
            here = rows == shift
            here_x = here & within
            here_y = here & jnp.logical_not(within)
            for field in range(NS):
                from_x = jnp.take_along_axis(inside[field], index, axis=1)
                from_y = jnp.take_along_axis(beside[field], index, axis=1)
                value = jnp.where(here_x, from_x, chosen[slot][field])
                chosen[slot][field] = jnp.where(here_y, from_y, value)
    return chosen


def regrid(fields_x, fields_y, plan_x, plan_y, forcing_x, forcing_y, first, tiles, tall, sides):
    def tile(step, carry):
        at = first + step * 8
        lane = lanes((8, 128))
        picks = []
        weights = []
        for k in range(NK):
            rows, cols = decode(plan_x[pl.ds(k * tall + at, 8), :])
            column = lane + cols
            picks.append((rows, column & 127, (column >= 0) & (column < 128)))
            weights.append(plan_x[pl.ds((NK + k) * tall + at, 8), :])
        if sides:
            part = ((lane + 16) & 127) // 32
            codes = plan_y[pl.ds(at, 8), :]
            weight = plan_y[pl.ds(NK * tall + at, 8), :]
            for k in range(1, NK):
                codes = jnp.where(part == k, roll(plan_y[pl.ds(k * tall + at, 8), :], 32 * k), codes)
                weight = jnp.where(
                    part == k, roll(plan_y[pl.ds((NK + k) * tall + at, 8), :], 32 * k), weight
                )
            rows, cols = decode(codes)
            place = (lane - 32 * part) & 127
            column = jnp.where(place >= 64, place - 128, place + 128) + cols
            picks.append((rows, column & 127, (column >= 0) & (column < 128)))
            weights.append(weight)
        chosen = select_rows(fields_x, fields_y, at + 14, picks)
        for field in range(NS):
            total = chosen[0][field] * weights[0]
            for k in range(1, NK):
                total = total + chosen[k][field] * weights[k]
            forcing_x[pl.ds(at * 8 + field, 8, stride=8), :] = total
            forcing_x[pl.ds(at * 8 + field + 4, 8, stride=8), :] = total
            if sides:
                part_sum = chosen[NK][field] * weights[NK]
                total = part_sum
                for k in range(1, NK):
                    total = total + roll(part_sum, -32 * k)
                forcing_y[pl.ds(at * 8 + field, 8, stride=8), :] = total
                forcing_y[pl.ds(at * 8 + field + 4, 8, stride=8), :] = total
        return carry

    lax.fori_loop(0, tiles, tile, 0)


def place_columns(middle, left, right):
    lane = lanes(middle.shape)
    return jnp.where(lane < 64, right, left)


def gelu(x):
    return jax.nn.gelu(x)


def air(state, out, forcing_x, atm_in, atm_bias, atm_out, d):
    half = d.rows // 2
    blank = jnp.zeros((8, 128), F32)

    def inputs(row):
        at = pl.multiple_of((row + 2) * 8, 8)
        forced = jnp.concatenate([forcing_x[pl.ds(at, 8), :], blank], axis=0)
        return jnp.concatenate([state[row], forced.astype(BF16)], axis=0)

    def body(step, carry):
        pair = jnp.concatenate([inputs(step), inputs(step + half)], axis=1)
        hidden = gelu(jnp.dot(atm_in[...], pair, preferred_element_type=F32) + atm_bias[...])
        update = jnp.dot(atm_out[...], hidden.astype(BF16), preferred_element_type=F32)
        out[step] = (state[step].astype(F32) + update[:, :128]).astype(BF16)
        out[step + half] = (state[step + half].astype(F32) + update[:, 128:]).astype(BF16)
        return carry

    lax.fori_loop(0, half, body, 0)


def edge_forcing(forcing_x, forcing_y, d):
    lane = lanes((8, d.edge))
    block = lane // d.block
    row = lane % d.block

    def body(step, carry):
        inner, outer = carry
        at = pl.ds(pl.multiple_of(step * 8, 8), 8)
        pad = [jnp.zeros((8, 128), F32)] * (d.pieces - 1)
        here = jnp.concatenate([forcing_x[at, :]] + pad, axis=1)
        there = jnp.concatenate([forcing_y[at, :]] + pad, axis=1)
        for index, column in enumerate((126, 0, 127, 1)):
            shift = (step + index * d.block - column) % d.edge
            match = (block == index) & (row == step)
            inner = jnp.where(match, roll(here, shift), inner)
            outer = jnp.where(match, roll(there, shift), outer)
        return inner, outer

    blank = jnp.zeros((8, d.edge), F32)
    return lax.fori_loop(0, d.rows + 4, body, (blank, blank))


def sea(
    state, upper, lower, edges, left, right, out, forcing_x, forcing_y, ocn_in, ocn_bias, ocn_out,
    wet, at_top, at_bottom, stack, hidden, side, d,
):
    rows, block = d.rows, d.block
    lane = lanes((CH, 128))
    spot = lanes((CH, d.edge))
    part = spot // block
    inner = edges
    outer = jnp.where((part == 0) | (part == 2), left, right)

    def sides_of(inner, outer, spot):
        first = spot < block
        return (
            jnp.where(first, outer, roll(inner, -block)),
            jnp.where(first, roll(outer, -2 * block), outer),
            jnp.where(first, roll(inner, -block), roll(outer, -2 * block)),
        )

    beside = sides_of(inner, outer, spot)
    middle = beside[1]
    force_in, force_out = edge_forcing(forcing_x, forcing_y, d)
    beside_forcing = sides_of(force_in, force_out, lanes((8, d.edge)))
    sub = subs((8, d.edge))
    blank = jnp.zeros((8, d.edge), F32)
    forced = jnp.concatenate(
        [
            jnp.where(sub < 4, beside_forcing[0], beside_forcing[1]),
            jnp.where(sub < 4, beside_forcing[2], blank),
        ],
        axis=0,
    ).astype(BF16)
    columns = jnp.concatenate(list(beside) + [forced], axis=0)
    for tap in range(3):
        side[tap * 256 : (tap + 1) * 256, :] = roll(columns, -tap)

    sub_row = subs((8, 128))
    lane_row = lanes((8, 128))

    def build(row, values):
        entry = roll(middle, (127 - row) % d.edge)[:, :128]
        stack[row, 0:CH, :] = roll(jnp.where(lane == 127, entry, values), 1)
        stack[row, CH : 2 * CH, :] = values
        entry = roll(middle, (2 * d.edge - block - row) % d.edge)[:, :128]
        stack[row, 2 * CH : 3 * CH, :] = roll(jnp.where(lane == 0, entry, values), -1)
        at = pl.ds(pl.multiple_of(row * 8, 8), 8)
        here, there = forcing_x[at, :], forcing_y[at, :]
        before = roll(jnp.where(lane_row == 127, there, here), 1)
        after = roll(jnp.where(lane_row == 0, there, here), -1)
        stack[row, 3 * CH : 256, :] = jnp.concatenate(
            [jnp.where(sub_row < 4, before, here), jnp.where(sub_row < 4, after, jnp.zeros_like(after))],
            axis=0,
        ).astype(BF16)

    for step in range(2):
        build(jnp.int32(step), upper[step * CH : (step + 1) * CH, :])
        build(jnp.int32(rows + 2 + step), lower[step * CH : (step + 1) * CH, :])

    def build_own(step, carry):
        build(step + 2, state[step])
        return carry

    lax.fori_loop(0, rows, build_own, 0)

    pairs = (rows + 2) // 2

    def first(step, carry):
        taps = jnp.concatenate(
            [
                stack[pl.ds(step, 3)].reshape(3 * 256, 128),
                stack[pl.ds(step + pairs, 3)].reshape(3 * 256, 128),
            ],
            axis=1,
        )
        product = jnp.dot(ocn_in[...], taps, preferred_element_type=F32) + ocn_bias[...]
        active = gelu(product)
        keep_low = jnp.where((step == 0) & (at_top != 0), 0.0, 1.0).astype(F32)
        keep_high = jnp.where((step == pairs - 1) & (at_bottom != 0), 0.0, 1.0).astype(F32)
        hidden[step] = (active[:, :128] * keep_low).astype(BF16)
        hidden[step + pairs] = (active[:, 128:] * keep_high).astype(BF16)
        return carry

    lax.fori_loop(0, pairs, first, 0)

    product = jnp.dot(ocn_in[...], side[...], preferred_element_type=F32) + ocn_bias[...]
    spot = lanes((1, d.edge)) % block
    gone = ((spot == 0) & (at_top != 0)) | ((spot == rows + 1) & (at_bottom != 0))
    active = jnp.where(gone, 0.0, gelu(product)).astype(BF16)
    taps = jnp.concatenate([roll(active, -tap) for tap in range(3)], axis=0)
    partial = jnp.dot(ocn_out[...], taps, preferred_element_type=F32)
    from_left, from_right = partial[0:CH], partial[2 * CH : 3 * CH]
    half = rows // 2

    def second(step, carry):
        taps = jnp.concatenate(
            [
                hidden[pl.ds(step, 3)].reshape(3 * HIDP, 128),
                hidden[pl.ds(step + half, 3)].reshape(3 * HIDP, 128),
            ],
            axis=1,
        )
        product = jnp.dot(ocn_out[...], taps, preferred_element_type=F32)
        for offset in range(2):
            row = step + offset * half
            sums = product[:, offset * 128 : (offset + 1) * 128]
            entry = roll(from_left, (127 - row) % d.edge)[:, :128]
            total = sums[CH : 2 * CH] + roll(jnp.where(lane == 127, entry, sums[0:CH]), 1)
            entry = roll(from_right, (2 * d.edge - block - row) % d.edge)[:, :128]
            total = total + roll(jnp.where(lane == 0, entry, sums[2 * CH : 3 * CH]), -1)
            update = total * wet[pl.ds(row, 1), :]
            out[row] = (state[row].astype(F32) + update).astype(BF16)
        return carry

    lax.fori_loop(0, half, second, 0)


def join_rows(edge_up, edge_own, edge_down, d):
    row = lanes(edge_own.shape) % d.block
    above = roll(edge_up, -d.rows)
    below = roll(edge_down, d.rows)
    return jnp.where(row < 2, above, jnp.where(row < d.rows + 2, edge_own, below))


def step_kernel(d, opening, closing, *refs):
    refs = list(refs)
    take = lambda count: [refs.pop(0) for _ in range(count)]
    (flags,) = take(1)
    state, wet, above, beside, below, from_up, from_down, own_edges, from_left, from_right = take(10)
    if opening:
        (planes,) = take(1)
    else:
        plan_x, plan_y = take(2)
    atm_in, atm_bias, atm_out, ocn_in, ocn_bias, ocn_out, proj, keeping = take(8)
    (out,) = take(1)
    if not closing:
        fields, new_edges, top, bottom = take(4)
    if opening:
        plan_x, plan_y = take(2)
    fields_x, fields_y, forcing_x, forcing_y, stack, hidden, side, raw = take(8)
    rows, tall = d.rows, d.tall
    is_ocean, at_top, at_bottom = flags[0], flags[1], flags[2]

    if opening:

        @pl.when(is_ocean != 0)
        def _():
            plan_x[...] = jnp.zeros_like(plan_x)
            plan_y[...] = jnp.zeros_like(plan_y)
            base = d.strip
            side_base = 4 * (rows + 32) + 3 * d.edge_rows
            for step, ref in ((0, from_up), (rows + 2, from_down)):
                strip = ref[base : base + 16, :].astype(F32)
                for index in range(2):
                    plan_x[pl.ds(step + index, 2 * NK, stride=tall), :] = strip[index * 8 : (index + 1) * 8]
            for step, at in ((0, side_base), (rows + 2, side_base + 16 + 2 * NK * rows)):
                strip = place_columns(
                    from_left[at : at + 16, :],
                    from_left[at : at + 16, :].astype(F32),
                    from_right[at : at + 16, :].astype(F32),
                )
                for index in range(2):
                    plan_y[pl.ds(step + index, 2 * NK, stride=tall), :] = strip[index * 8 : (index + 1) * 8]
            for plane in range(2 * NK):
                at = side_base + 16 + plane * rows
                plan_y[plane * tall + 2 : plane * tall + 2 + rows, :] = place_columns(
                    from_left[at : at + rows, :],
                    from_left[at : at + rows, :].astype(F32),
                    from_right[at : at + rows, :].astype(F32),
                )

        for plane in range(2 * NK):
            plan_x[plane * tall + 2 : plane * tall + 2 + rows, :] = planes[plane].astype(F32)

    for field in range(NS):
        fields_x[field, 0:16, :] = above[field, rows - 16 : rows, :].astype(F32)
        fields_x[field, 16 : 16 + rows, :] = beside[field].astype(F32)
        fields_x[field, 16 + rows : 32 + rows, :] = below[field, 0:16, :].astype(F32)
        for at, start, count in (
            (0, field * 16, 16),
            (16, 64 + field * rows, rows),
            (16 + rows, 64 + 4 * rows + field * 16, 16),
        ):
            fields_y[field, at : at + count, :] = place_columns(
                from_left[start : start + count, :],
                from_left[start : start + count, :].astype(F32),
                from_right[start : start + count, :].astype(F32),
            )

    @pl.when(is_ocean == 0)
    def _():
        regrid(fields_x, fields_y, plan_x, plan_y, forcing_x, forcing_y, 2, rows // 8, tall, False)
        air(state, out, forcing_x, atm_in, atm_bias, atm_out, d)

    @pl.when(is_ocean != 0)
    def _():
        regrid(fields_x, fields_y, plan_x, plan_y, forcing_x, forcing_y, 0, d.tiles, tall, True)
        at = 4 * (rows + 32)
        size = d.edge_rows
        edges = join_rows(
            get_edges(from_up, 2 * CH, d), get_edges(own_edges, 0, d), get_edges(from_down, 2 * CH, d), d
        )
        left, right = [
            join_rows(*[get_edges(ref, at + index * size, d) for index in range(3)], d)
            for ref in (from_left, from_right)
        ]
        sea(
            state, from_up, from_down, edges, left, right, out, forcing_x, forcing_y,
            ocn_in, ocn_bias, ocn_out, wet, at_top, at_bottom, stack, hidden, side, d,
        )

    if not closing:
        emit(out, proj, keeping, fields, new_edges, top, bottom, raw, d)


VMEM = pl.BlockSpec(memory_space=pltpu.VMEM)
SMEM = pl.BlockSpec(memory_space=pltpu.SMEM)
PARAMS = pltpu.CompilerParams(vmem_limit_bytes=48 * 1024 * 1024)


def shape(*dims, dtype=BF16):
    return jax.ShapeDtypeStruct(dims, dtype)


def send(x, move):
    names = ("grp", "lat", "lon")
    sizes = [lax.axis_size(name) for name in names]
    pairs = []
    for group in range(sizes[0]):
        for lat in range(sizes[1]):
            for lon in range(sizes[2]):
                to = move(group, lat, lon)
                if to is None or not 0 <= to[1] < sizes[1]:
                    continue
                target = (to[0] * sizes[1] + to[1]) * sizes[2] + to[2] % sizes[2]
                pairs.append(((group * sizes[1] + lat) * sizes[2] + lon, target))
    return lax.ppermute(x, names, pairs)


def exchange(fields, own_edges, top, bottom, planes, d):
    rows = d.rows
    beside = send(fields, lambda g, i, j: (1 - g, i, j))
    above = send(fields, lambda g, i, j: (1 - g, i + 1, j))
    below = send(fields, lambda g, i, j: (1 - g, i - 1, j))
    from_up = send(bottom, lambda g, i, j: (1, i + 1, j) if g == 1 else None)
    from_down = send(top, lambda g, i, j: (1, i - 1, j) if g == 1 else None)
    edge_at = slice(2 * CH, d.strip)
    packed = [
        above[:, rows - 16 :].reshape(64, 128),
        beside.reshape(4 * rows, 128),
        below[:, :16].reshape(64, 128),
        from_up[edge_at],
        own_edges,
        from_down[edge_at],
    ]
    if planes is not None:
        packed += [from_up[d.strip :], planes.reshape(2 * NK * rows, 128), from_down[d.strip :]]
    packed = jnp.concatenate(packed, axis=0)
    from_left = send(packed, lambda g, i, j: (g, i, j + 1))
    from_right = send(packed, lambda g, i, j: (g, i, j - 1))
    return above, beside, below, from_up, from_down, own_edges, from_left, from_right


def local(
    coupled_state, land_mask, regrid_offsets, regrid_weights, surface_proj,
    atm_in, atm_bias, atm_out, ocn_in, ocn_bias, ocn_out,
):
    rows = coupled_state.shape[2]
    assert coupled_state.shape[3] == 128
    d = Dims(rows)
    group = lax.axis_index("grp")
    lat = lax.axis_index("lat")
    is_ocean = group == 1
    flags = jnp.stack([group, lat == 0, lat == lax.axis_size("lat") - 1]).astype(jnp.int32)
    state = jnp.transpose(coupled_state[0], (1, 0, 2))
    wet = land_mask.astype(F32)
    keeping = jnp.where(is_ocean, wet, 1.0)
    projector = lax.dynamic_index_in_dim(surface_proj, group, 0, keepdims=False)
    high = projector.astype(BF16)
    rest = projector - high.astype(F32)
    mid = rest.astype(BF16)
    low = (rest - mid.astype(F32)).astype(BF16)
    gap = jnp.zeros((4, CH), BF16)
    proj = jnp.concatenate([high, gap, mid, gap, low, gap], axis=0)
    codes = regrid_offsets[0, 0] * SPAN + regrid_offsets[0, 1]
    planes = jnp.concatenate([codes.astype(BF16), regrid_weights[0].astype(BF16)], axis=0)

    hidden_count = ocn_in.shape[0]
    taps = ocn_in.reshape(hidden_count, 3, 3, CH + NS)
    first = jnp.concatenate(
        [
            taps[..., :CH].reshape(hidden_count, 3, 3 * CH),
            taps[..., CH:].reshape(hidden_count, 3, 3 * NS),
            jnp.zeros((hidden_count, 3, 256 - 3 * (CH + NS)), BF16),
        ],
        axis=2,
    ).reshape(hidden_count, 768)
    extra = HIDP - hidden_count
    first = jnp.pad(first, ((0, extra), (0, 0)))
    first_bias = jnp.pad(ocn_bias, (0, extra))[:, None]
    second = jnp.transpose(ocn_out.reshape(CH, 3, 3, hidden_count), (2, 0, 1, 3))
    second = jnp.pad(second, ((0, 0), (0, 0), (0, 0), (0, extra))).reshape(3 * CH, 3 * HIDP)
    air_in = jnp.pad(atm_in, ((0, 0), (0, 16 - NS)))
    constants = (air_in, atm_bias[:, None], atm_out, first, first_bias, second, proj, keeping)

    emitted = [
        shape(NS, rows, 128),
        shape(d.edge_rows, 128),
        shape(d.strip, 128),
        shape(d.strip, 128),
    ]
    raw = pltpu.VMEM((rows * 8, 128), F32)
    fields, edges, top, bottom = pl.pallas_call(
        functools.partial(start_kernel, d),
        out_shape=emitted[:2] + [shape(d.strip + 16, 128)] * 2,
        in_specs=[VMEM] * 4,
        out_specs=[VMEM] * 4,
        scratch_shapes=[raw, pltpu.VMEM((2 * NK * rows, 128), F32)],
        compiler_params=PARAMS,
        name="start",
    )(state, planes, proj, keeping)

    scratch = [
        pltpu.VMEM((NS, rows + 32, 128), F32),
        pltpu.VMEM((NS, rows + 32, 128), F32),
        pltpu.VMEM((d.tall * 8, 128), F32),
        pltpu.VMEM((d.tall * 8, 128), F32),
        pltpu.VMEM((rows + 4, 256, 128), BF16),
        pltpu.VMEM((rows + 2, HIDP, 128), BF16),
        pltpu.VMEM((768, d.edge), BF16),
        raw,
    ]
    plans = [shape(2 * NK * d.tall, 128, dtype=F32)] * 2
    state_shape = shape(rows, CH, 128)

    received = exchange(fields, edges, top, bottom, planes, d)
    outs = [state_shape] + emitted + plans
    state, fields, edges, top, bottom, plan_x, plan_y = pl.pallas_call(
        functools.partial(step_kernel, d, True, False),
        out_shape=outs,
        in_specs=[SMEM] + [VMEM] * 19,
        out_specs=[VMEM] * len(outs),
        scratch_shapes=scratch,
        compiler_params=PARAMS,
        name="first_step",
    )(flags, state, wet, *received, planes, *constants)

    received = exchange(fields, edges, top, bottom, None, d)
    state = pl.pallas_call(
        functools.partial(step_kernel, d, False, True),
        out_shape=state_shape,
        in_specs=[SMEM] + [VMEM] * 20,
        out_specs=VMEM,
        scratch_shapes=scratch,
        compiler_params=PARAMS,
        name="second_step",
    )(flags, state, wet, *received, plan_x, plan_y, *constants)
    return jnp.transpose(state, (1, 0, 2))[None]


def solution(mesh):
    return jax.shard_map(
        local,
        mesh=mesh,
        in_specs=(
            P("grp", None, "lat", "lon"),
            P("lat", "lon"),
            P("grp", None, None, "lat", "lon"),
            P("grp", None, "lat", "lon"),
            P(),
            P(),
            P(),
            P(),
            P(),
            P(),
            P(),
        ),
        out_specs=P("grp", None, "lat", "lon"),
        check_vma=False,
    )
```

```python
import functools

import jax
import jax.numpy as jnp
from jax import lax
from jax.experimental import pallas as pl
from jax.experimental.pallas import tpu as pltpu
from jax.sharding import PartitionSpec as P

CH = 80
NS = 4
NK = 4
HW = 8
SPAN = 2 * HW + 1
HIDP = 208
F32 = jnp.float32
BF16 = jnp.bfloat16


def roll(x, shift, axis=1):
    size = x.shape[axis]
    if isinstance(shift, int):
        shift = shift % size
        if shift == 0:
            return x
    return pltpu.roll(x, shift, axis)


def lanes(shape):
    return lax.broadcasted_iota(jnp.int32, shape, len(shape) - 1)


def subs(shape):
    return lax.broadcasted_iota(jnp.int32, shape, len(shape) - 2)


class Dims:
    def __init__(self, rows):
        self.rows = rows
        self.block = 32 if rows + 4 <= 32 else 64
        self.edge = 4 * self.block
        self.pieces = self.edge // 128
        self.edge_rows = CH * self.pieces
        self.tiles = -(-(rows + 4) // 8)
        self.tall = 8 * self.tiles
        self.strip = 2 * CH + self.edge_rows


def put_edges(ref, at, edges, d):
    for piece in range(d.pieces):
        ref[at + piece * CH : at + (piece + 1) * CH, :] = edges[:, piece * 128 : (piece + 1) * 128]


def get_edges(ref, at, d):
    return jnp.concatenate(
        [ref[at + piece * CH : at + (piece + 1) * CH, :] for piece in range(d.pieces)], axis=1
    )


def edge_columns(state, d):
    lane = lanes((1, d.edge))
    block = lane // d.block
    row = lane % d.block - 2
    column = jnp.where(block == 0, 126, jnp.where(block == 1, 0, jnp.where(block == 2, 127, 1)))
    half = d.rows // 2
    own = (row >= 0) & (row < d.rows)
    target = jnp.where(own, column + 128 * (row // half), -1)
    turn = row % half

    def body(step, total):
        place = subs((256, d.edge)) == jnp.where(turn == step, target, -1)
        pair = jnp.concatenate([state[step], state[step + half]], axis=1)
        return total + jnp.dot(
            pair, place.astype(F32).astype(BF16), preferred_element_type=F32
        )

    total = lax.fori_loop(0, half, body, jnp.zeros((CH, d.edge), F32))
    return total.astype(BF16)


def strips(one, two, even, d):
    last = d.rows - 2
    return (one, jnp.where(even, last, 0)), (two, jnp.where(even, 0, last))


def emit(state, proj, keeping, fields, own_edges, one, two, even, raw, d):
    half = d.rows // 2

    def body(step, carry):
        pair = jnp.concatenate([state[step], state[step + half]], axis=1)
        parts = jnp.dot(proj[...], pair, preferred_element_type=F32)
        whole = parts[0:8] + parts[8:16] + parts[16:24]
        raw[pl.ds(pl.multiple_of(step * 8, 8), 8), :] = whole[:, :128]
        raw[pl.ds(pl.multiple_of((step + half) * 8, 8), 8), :] = whole[:, 128:]
        return carry

    lax.fori_loop(0, half, body, 0)
    for field in range(NS):
        fields[field] = (raw[pl.ds(field, d.rows, stride=8), :] * keeping[...]).astype(BF16)
    edges = edge_columns(state, d)
    put_edges(own_edges, 0, edges, d)
    for ref, first in strips(one, two, even, d):
        ref[0:CH, :] = state[first]
        ref[CH : 2 * CH, :] = state[first + 1]
        put_edges(ref, 2 * CH, edges, d)


def start_kernel(d, flags, state, planes, proj, keeping, fields, own_edges, one, two, raw, tall):
    even = flags[3] == 0
    emit(state, proj, keeping, fields, own_edges, one, two, even, raw, d)
    for plane in range(2 * NK):
        tall[plane * d.rows : (plane + 1) * d.rows, :] = planes[plane].astype(F32)
    for ref, first in strips(one, two, even, d):
        strip = [tall[pl.ds(first + step, 2 * NK, stride=d.rows), :] for step in range(2)]
        ref[d.strip : d.strip + 16, :] = jnp.concatenate(strip, axis=0).astype(BF16)


def decode(code):
    shifted = code.astype(jnp.int32) + (HW * SPAN + HW)
    rows = lax.shift_right_logical(shifted * 241, 12)
    return rows - HW, shifted - rows * SPAN - HW


def along_lanes(values, index):
    numbers = lax.GatherDimensionNumbers(
        offset_dims=(),
        collapsed_slice_dims=(1,),
        start_index_map=(1,),
        operand_batching_dims=(0,),
        start_indices_batching_dims=(0,),
    )
    return lax.gather(
        values, index[..., None], numbers, (1, 1), mode=lax.GatherScatterMode.PROMISE_IN_BOUNDS
    )


def select_rows(sources, start, picks):
    chosen = [[jnp.zeros((8, 128), F32) for _ in range(NS)] for _ in picks]
    for shift in range(-HW, HW + 1):
        at = pl.ds(start + shift, 8)
        values = [[source[field, at, :] for field in range(NS)] for source in sources]
        for slot, (rows, index, allowed) in enumerate(picks):
            here = rows == shift
            for source, within in enumerate(allowed):
                if within is None:
                    continue
                mask = here & within
                for field in range(NS):
                    picked = along_lanes(values[source][field], index)
                    chosen[slot][field] = jnp.where(mask, picked, chosen[slot][field])
    return chosen


def regrid(fields_x, fields_y, plan_x, plan_y, forcing_x, forcing_y, first, tiles, tall, sides):
    def tile(step, carry):
        at = first + step * 8
        lane = lanes((8, 128))
        picks = []
        weights = []
        codes = []
        for k in range(NK):
            code = plan_x[pl.ds(k * tall + at, 8), :]
            weight = plan_x[pl.ds((NK + k) * tall + at, 8), :]
            codes.append(code)
            weights.append(weight)
            rows, cols = decode(code)
            column = lane + cols
            picks.append((rows, column & 127, ((column >= 0) & (column < 128), None)))
        part = ((lane + 8) & 127) // 32
        place = ((lane + 8) & 31) - 8
        outer = place >= 8
        code = jnp.zeros((8, 128), F32)
        weight = jnp.zeros((8, 128), F32)
        for k in range(NK):
            edge_code = roll(codes[k], 32 * k)
            edge_weight = roll(weights[k], 32 * k)
            if sides:
                edge_code = jnp.where(
                    outer, roll(plan_y[pl.ds(k * tall + at, 8), :], 32 * k + 16), edge_code
                )
                edge_weight = jnp.where(
                    outer, roll(plan_y[pl.ds((NK + k) * tall + at, 8), :], 32 * k + 16), edge_weight
                )
            code = jnp.where(part == k, edge_code, code)
            weight = jnp.where(part == k, edge_weight, weight)
        rows, cols = decode(code)
        inner_column = place & 127
        outer_column = jnp.where(place < 16, place - 16, place + 112)
        column = jnp.where(outer, outer_column, inner_column) + cols
        within = (column >= 0) & (column < 128)
        picks.append(
            (rows, column & 127, (within & outer if sides else None, jnp.logical_not(within)))
        )
        chosen = select_rows((fields_x, fields_y), at + 14, picks)
        edge = (lane < 8) | (lane >= 120)
        for field in range(NS):
            total = chosen[0][field] * weights[0]
            for k in range(1, NK):
                total = total + chosen[k][field] * weights[k]
            part_sum = chosen[NK][field] * weight
            extra = part_sum
            for k in range(1, NK):
                extra = extra + roll(part_sum, -32 * k)
            total = total + jnp.where(edge, extra, 0.0)
            forcing_x[pl.ds(at * 8 + field, 8, stride=8), :] = total
            forcing_x[pl.ds(at * 8 + field + 4, 8, stride=8), :] = total
            if sides:
                extra = roll(extra, -16)
                forcing_y[pl.ds(at * 8 + field, 8, stride=8), :] = extra
                forcing_y[pl.ds(at * 8 + field + 4, 8, stride=8), :] = extra
        return carry

    lax.fori_loop(0, tiles, tile, 0)


def place_columns(left, right):
    return jnp.where(lanes(left.shape) < 64, right.astype(F32), left.astype(F32))


def gelu(x):
    return jax.nn.gelu(x)


def air(state, out, forcing_x, atm_in, atm_bias, atm_out, d):
    half = d.rows // 2
    blank = jnp.zeros((8, 128), F32)

    def inputs(row):
        at = pl.multiple_of((row + 2) * 8, 8)
        forced = jnp.concatenate([forcing_x[pl.ds(at, 8), :], blank], axis=0)
        return jnp.concatenate([state[row], forced.astype(BF16)], axis=0)

    def body(step, carry):
        pair = jnp.concatenate([inputs(step), inputs(step + half)], axis=1)
        hidden = gelu(jnp.dot(atm_in[...], pair, preferred_element_type=F32) + atm_bias[...])
        update = jnp.dot(atm_out[...], hidden.astype(BF16), preferred_element_type=F32)
        out[step] = (state[step].astype(F32) + update[:, :128]).astype(BF16)
        out[step + half] = (state[step + half].astype(F32) + update[:, 128:]).astype(BF16)
        return carry

    lax.fori_loop(0, half, body, 0)


def edge_forcing(forcing_x, forcing_y, d):
    lane = lanes((8, d.edge))
    block = lane // d.block
    row = lane % d.block

    def body(step, carry):
        inner, outer = carry
        at = pl.ds(pl.multiple_of(step * 8, 8), 8)
        pad = [jnp.zeros((8, 128), F32)] * (d.pieces - 1)
        here = jnp.concatenate([forcing_x[at, :]] + pad, axis=1)
        there = jnp.concatenate([forcing_y[at, :]] + pad, axis=1)
        for index, column in enumerate((126, 0, 127, 1)):
            shift = (step + index * d.block - column) % d.edge
            match = (block == index) & (row == step)
            inner = jnp.where(match, roll(here, shift), inner)
            outer = jnp.where(match, roll(there, shift), outer)
        return inner, outer

    blank = jnp.zeros((8, d.edge), F32)
    return lax.fori_loop(0, d.rows + 4, body, (blank, blank))


def sea(
    state, upper, lower, edges, left, right, out, forcing_x, forcing_y, ocn_in, ocn_bias, ocn_out,
    wet, at_top, at_bottom, stack, hidden, side, d,
):
    rows, block = d.rows, d.block
    lane = lanes((CH, 128))
    spot = lanes((CH, d.edge))
    part = spot // block
    inner = edges
    outer = jnp.where((part == 0) | (part == 2), left, right)

    def sides_of(inner, outer, spot):
        first = spot < block
        return (
            jnp.where(first, outer, roll(inner, -block)),
            jnp.where(first, roll(outer, -2 * block), outer),
            jnp.where(first, roll(inner, -block), roll(outer, -2 * block)),
        )

    beside = sides_of(inner, outer, spot)
    middle = beside[1]
    force_in, force_out = edge_forcing(forcing_x, forcing_y, d)
    beside_forcing = sides_of(force_in, force_out, lanes((8, d.edge)))
    sub = subs((8, d.edge))
    blank = jnp.zeros((8, d.edge), F32)
    forced = jnp.concatenate(
        [
            jnp.where(sub < 4, beside_forcing[0], beside_forcing[1]),
            jnp.where(sub < 4, beside_forcing[2], blank),
        ],
        axis=0,
    ).astype(BF16)
    columns = jnp.concatenate(list(beside) + [forced], axis=0)
    for tap in range(3):
        side[tap * 256 : (tap + 1) * 256, :] = roll(columns, -tap)

    sub_row = subs((8, 128))
    lane_row = lanes((8, 128))

    def build(row, values):
        entry = roll(middle, (127 - row) % d.edge)[:, :128]
        stack[row, 0:CH, :] = roll(jnp.where(lane == 127, entry, values), 1)
        stack[row, CH : 2 * CH, :] = values
        entry = roll(middle, (2 * d.edge - block - row) % d.edge)[:, :128]
        stack[row, 2 * CH : 3 * CH, :] = roll(jnp.where(lane == 0, entry, values), -1)
        at = pl.ds(pl.multiple_of(row * 8, 8), 8)
        here, there = forcing_x[at, :], forcing_y[at, :]
        before = roll(jnp.where(lane_row == 127, there, here), 1)
        after = roll(jnp.where(lane_row == 0, there, here), -1)
        stack[row, 3 * CH : 256, :] = jnp.concatenate(
            [jnp.where(sub_row < 4, before, here), jnp.where(sub_row < 4, after, jnp.zeros_like(after))],
            axis=0,
        ).astype(BF16)

    for step in range(2):
        build(jnp.int32(step), upper[step * CH : (step + 1) * CH, :])
        build(jnp.int32(rows + 2 + step), lower[step * CH : (step + 1) * CH, :])

    def build_own(step, carry):
        build(step + 2, state[step])
        return carry

    lax.fori_loop(0, rows, build_own, 0)

    pairs = (rows + 2) // 2

    def first(step, carry):
        taps = jnp.concatenate(
            [
                stack[pl.ds(step, 3)].reshape(3 * 256, 128),
                stack[pl.ds(step + pairs, 3)].reshape(3 * 256, 128),
            ],
            axis=1,
        )
        product = jnp.dot(ocn_in[...], taps, preferred_element_type=F32) + ocn_bias[...]
        active = gelu(product)
        keep_low = jnp.where((step == 0) & (at_top != 0), 0.0, 1.0).astype(F32)
        keep_high = jnp.where((step == pairs - 1) & (at_bottom != 0), 0.0, 1.0).astype(F32)
        hidden[step] = (active[:, :128] * keep_low).astype(BF16)
        hidden[step + pairs] = (active[:, 128:] * keep_high).astype(BF16)
        return carry

    lax.fori_loop(0, pairs, first, 0)

    product = jnp.dot(ocn_in[...], side[...], preferred_element_type=F32) + ocn_bias[...]
    spot = lanes((1, d.edge)) % block
    gone = ((spot == 0) & (at_top != 0)) | ((spot == rows + 1) & (at_bottom != 0))
    active = jnp.where(gone, 0.0, gelu(product)).astype(BF16)
    taps = jnp.concatenate([roll(active, -tap) for tap in range(3)], axis=0)
    partial = jnp.dot(ocn_out[...], taps, preferred_element_type=F32)
    from_left, from_right = partial[0:CH], partial[2 * CH : 3 * CH]
    half = rows // 2

    def second(step, carry):
        taps = jnp.concatenate(
            [
                hidden[pl.ds(step, 3)].reshape(3 * HIDP, 128),
                hidden[pl.ds(step + half, 3)].reshape(3 * HIDP, 128),
            ],
            axis=1,
        )
        product = jnp.dot(ocn_out[...], taps, preferred_element_type=F32)
        for offset in range(2):
            row = step + offset * half
            sums = product[:, offset * 128 : (offset + 1) * 128]
            entry = roll(from_left, (127 - row) % d.edge)[:, :128]
            total = sums[CH : 2 * CH] + roll(jnp.where(lane == 127, entry, sums[0:CH]), 1)
            entry = roll(from_right, (2 * d.edge - block - row) % d.edge)[:, :128]
            total = total + roll(jnp.where(lane == 0, entry, sums[2 * CH : 3 * CH]), -1)
            update = total * wet[pl.ds(row, 1), :]
            out[row] = (state[row].astype(F32) + update).astype(BF16)
        return carry

    lax.fori_loop(0, half, second, 0)


def join_rows(edge_up, edge_own, edge_down, d):
    row = lanes(edge_own.shape) % d.block
    above = roll(edge_up, -d.rows)
    below = roll(edge_down, d.rows)
    return jnp.where(row < 2, above, jnp.where(row < d.rows + 2, edge_own, below))


def step_kernel(d, opening, closing, *refs):
    refs = list(refs)
    take = lambda count: [refs.pop(0) for _ in range(count)]
    (flags,) = take(1)
    state, wet, field_one, beside, field_two, from_one, from_two, own_edges, from_left, from_right = take(10)
    if opening:
        (planes,) = take(1)
    else:
        plan_x, plan_y = take(2)
    atm_in, atm_bias, atm_out, ocn_in, ocn_bias, ocn_out, proj, keeping = take(8)
    (out,) = take(1)
    if not closing:
        fields, new_edges, one, two = take(4)
    if opening:
        plan_x, plan_y = take(2)
    fields_x, fields_y, forcing_x, forcing_y, stack, hidden, side, raw = take(8)
    rows, tall = d.rows, d.tall
    is_ocean, at_top, at_bottom = flags[0], flags[1], flags[2]
    even = flags[3] == 0

    def up(one, two):
        values = jnp.where(even, two, one).astype(F32)
        return jnp.where(at_top != 0, 0.0, values)

    def down(one, two):
        values = jnp.where(even, one, two).astype(F32)
        return jnp.where(at_bottom != 0, 0.0, values)

    def up_and_down(one, two):
        return up(one, two), down(one, two)

    if opening:

        @pl.when(is_ocean != 0)
        def _():
            plan_x[...] = jnp.zeros_like(plan_x)
            plan_y[...] = jnp.zeros_like(plan_y)
            base = d.strip
            side_base = 4 * (rows + 32) + 3 * d.edge_rows
            pair = up_and_down(from_one[base : base + 16, :], from_two[base : base + 16, :])
            for step, strip in zip((0, rows + 2), pair):
                for index in range(2):
                    plan_x[pl.ds(step + index, 2 * NK, stride=tall), :] = strip[index * 8 : (index + 1) * 8]
            ends = [
                place_columns(from_left[at : at + 16, :], from_right[at : at + 16, :])
                for at in (side_base, side_base + 16 + 2 * NK * rows)
            ]
            for step, strip in zip((0, rows + 2), up_and_down(*ends)):
                for index in range(2):
                    plan_y[pl.ds(step + index, 2 * NK, stride=tall), :] = strip[index * 8 : (index + 1) * 8]
            for plane in range(2 * NK):
                at = side_base + 16 + plane * rows
                plan_y[plane * tall + 2 : plane * tall + 2 + rows, :] = place_columns(
                    from_left[at : at + rows, :], from_right[at : at + rows, :]
                )

        for plane in range(2 * NK):
            plan_x[plane * tall + 2 : plane * tall + 2 + rows, :] = planes[plane].astype(F32)

    lower_at = 64 + 4 * rows
    for field in range(NS):
        ends = up_and_down(field_one[field], field_two[field])
        fields_x[field, 0:16, :] = ends[0][rows - 16 : rows]
        fields_x[field, 16 : 16 + rows, :] = beside[field].astype(F32)
        fields_x[field, 16 + rows : 32 + rows, :] = ends[1][0:16]
        start = 64 + field * rows
        fields_y[field, 16 : 16 + rows, :] = place_columns(
            from_left[start : start + rows, :], from_right[start : start + rows, :]
        )
        ends = [
            place_columns(from_left[at : at + 16, :], from_right[at : at + 16, :])
            for at in (field * 16, lower_at + field * 16)
        ]
        ends = up_and_down(*ends)
        fields_y[field, 0:16, :] = ends[0]
        fields_y[field, 16 + rows : 32 + rows, :] = ends[1]

    @pl.when(is_ocean == 0)
    def _():
        regrid(fields_x, fields_y, plan_x, plan_y, forcing_x, forcing_y, 2, rows // 8, tall, False)
        air(state, out, forcing_x, atm_in, atm_bias, atm_out, d)

    @pl.when(is_ocean != 0)
    def _():
        regrid(fields_x, fields_y, plan_x, plan_y, forcing_x, forcing_y, 0, d.tiles, tall, True)
        at = 4 * (rows + 32)
        size = d.edge_rows
        def joined(one, own, two):
            above, below = up_and_down(one, two)
            return join_rows(above.astype(BF16), own, below.astype(BF16), d)

        edges = joined(
            get_edges(from_one, 2 * CH, d), get_edges(own_edges, 0, d), get_edges(from_two, 2 * CH, d)
        )
        left, right = [
            joined(*[get_edges(ref, at + index * size, d) for index in range(3)])
            for ref in (from_left, from_right)
        ]
        upper, lower = up_and_down(from_one[0 : 2 * CH, :], from_two[0 : 2 * CH, :])
        sea(
            state, upper.astype(BF16), lower.astype(BF16), edges, left, right, out, forcing_x, forcing_y,
            ocn_in, ocn_bias, ocn_out, wet, at_top, at_bottom, stack, hidden, side, d,
        )

    if not closing:
        emit(out, proj, keeping, fields, new_edges, one, two, even, raw, d)


VMEM = pl.BlockSpec(memory_space=pltpu.VMEM)
SMEM = pl.BlockSpec(memory_space=pltpu.SMEM)
PARAMS = pltpu.CompilerParams(vmem_limit_bytes=48 * 1024 * 1024)


def shape(*dims, dtype=BF16):
    return jax.ShapeDtypeStruct(dims, dtype)


def send(x, move):
    names = ("grp", "lat", "lon")
    sizes = [lax.axis_size(name) for name in names]
    pairs = []
    for group in range(sizes[0]):
        for lat in range(sizes[1]):
            for lon in range(sizes[2]):
                to = move(group, lat, lon)
                if to is None or not 0 <= to[1] < sizes[1]:
                    continue
                target = (to[0] * sizes[1] + to[1]) * sizes[2] + to[2] % sizes[2]
                pairs.append(((group * sizes[1] + lat) * sizes[2] + lon, target))
    return lax.ppermute(x, names, pairs)


def swap_rows(x, turn, across):
    count = lax.axis_size("lat")

    def move(group, lat, lon):
        other = ((lat + turn) ^ 1) - turn
        to = 1 - group if across else group
        return to, other if 0 <= other < count else lat, lon

    return send(x, move)


def exchange(fields, own_edges, one, two, planes, d, hold):
    rows = d.rows
    beside = send(fields, lambda g, i, j: (1 - g, i, j))
    field_one = swap_rows(fields, 0, True)
    field_two = swap_rows(fields, 1, True)
    from_one = swap_rows(one, 0, False)
    from_two = swap_rows(two, 1, False)
    (beside, field_one, field_two, from_one, from_two), hold = lax.optimization_barrier(
        ((beside, field_one, field_two, from_one, from_two), hold)
    )
    edge_at = slice(2 * CH, d.strip)
    odd = lax.axis_index("lat") % 2
    if rows == 16:
        ends = [field_one, field_two]
    else:
        last = [field[:, rows - 16 :] for field in (field_one, field_two)]
        first = [field[:, :16] for field in (field_one, field_two)]
        ends = [jnp.where(odd == 1, last[0], first[0]), jnp.where(odd == 1, first[1], last[1])]
    packed = [
        ends[0].reshape(64, 128),
        beside.reshape(4 * rows, 128),
        ends[1].reshape(64, 128),
        from_one[edge_at],
        own_edges,
        from_two[edge_at],
    ]
    if planes is not None:
        packed += [from_one[d.strip :], planes.reshape(2 * NK * rows, 128), from_two[d.strip :]]
    packed = jnp.concatenate(packed, axis=0)
    from_left = send(packed, lambda g, i, j: (g, i, j + 1))
    from_right = send(packed, lambda g, i, j: (g, i, j - 1))
    return (field_one, beside, field_two, from_one, from_two, own_edges, from_left, from_right), hold


def local(
    coupled_state, land_mask, regrid_offsets, regrid_weights, surface_proj,
    atm_in, atm_bias, atm_out, ocn_in, ocn_bias, ocn_out,
):
    rows = coupled_state.shape[2]
    assert coupled_state.shape[3] == 128
    d = Dims(rows)
    group = lax.axis_index("grp")
    lat = lax.axis_index("lat")
    is_ocean = group == 1
    flags = jnp.stack(
        [group, lat == 0, lat == lax.axis_size("lat") - 1, lat % 2]
    ).astype(jnp.int32)
    state = jnp.transpose(coupled_state[0], (1, 0, 2))
    wet = land_mask.astype(F32)
    keeping = jnp.where(is_ocean, wet, 1.0)
    projector = lax.dynamic_index_in_dim(surface_proj, group, 0, keepdims=False)
    high = projector.astype(BF16)
    rest = projector - high.astype(F32)
    mid = rest.astype(BF16)
    low = (rest - mid.astype(F32)).astype(BF16)
    gap = jnp.zeros((4, CH), BF16)
    proj = jnp.concatenate([high, gap, mid, gap, low, gap], axis=0)
    codes = regrid_offsets[0, 0] * SPAN + regrid_offsets[0, 1]
    planes = jnp.concatenate([codes.astype(BF16), regrid_weights[0].astype(BF16)], axis=0)

    hidden_count = ocn_in.shape[0]
    taps = ocn_in.reshape(hidden_count, 3, 3, CH + NS)
    first = jnp.concatenate(
        [
            taps[..., :CH].reshape(hidden_count, 3, 3 * CH),
            taps[..., CH:].reshape(hidden_count, 3, 3 * NS),
            jnp.zeros((hidden_count, 3, 256 - 3 * (CH + NS)), BF16),
        ],
        axis=2,
    ).reshape(hidden_count, 768)
    extra = HIDP - hidden_count
    first = jnp.pad(first, ((0, extra), (0, 0)))
    first_bias = jnp.pad(ocn_bias, (0, extra))[:, None]
    second = jnp.transpose(ocn_out.reshape(CH, 3, 3, hidden_count), (2, 0, 1, 3))
    second = jnp.pad(second, ((0, 0), (0, 0), (0, 0), (0, extra))).reshape(3 * CH, 3 * HIDP)
    air_in = jnp.pad(atm_in, ((0, 0), (0, 16 - NS)))
    constants = (air_in, atm_bias[:, None], atm_out, first, first_bias, second, proj, keeping)

    emitted = [
        shape(NS, rows, 128),
        shape(d.edge_rows, 128),
        shape(d.strip, 128),
        shape(d.strip, 128),
    ]
    raw = pltpu.VMEM((rows * 8, 128), F32)
    fields, edges, one, two = pl.pallas_call(
        functools.partial(start_kernel, d),
        out_shape=emitted[:2] + [shape(d.strip + 16, 128)] * 2,
        in_specs=[SMEM] + [VMEM] * 4,
        out_specs=[VMEM] * 4,
        scratch_shapes=[raw, pltpu.VMEM((2 * NK * rows, 128), F32)],
        compiler_params=PARAMS,
        name="start",
    )(flags, state, planes, proj, keeping)

    scratch = [
        pltpu.VMEM((NS, rows + 32, 128), F32),
        pltpu.VMEM((NS, rows + 32, 128), F32),
        pltpu.VMEM((d.tall * 8, 128), F32),
        pltpu.VMEM((d.tall * 8, 128), F32),
        pltpu.VMEM((rows + 4, 256, 128), BF16),
        pltpu.VMEM((rows + 2, HIDP, 128), BF16),
        pltpu.VMEM((768, d.edge), BF16),
        raw,
    ]
    plans = [shape(2 * NK * d.tall, 128, dtype=F32)] * 2
    state_shape = shape(rows, CH, 128)

    received, constants = exchange(fields, edges, one, two, planes, d, constants)
    outs = [state_shape] + emitted + plans
    state, fields, edges, one, two, plan_x, plan_y = pl.pallas_call(
        functools.partial(step_kernel, d, True, False),
        out_shape=outs,
        in_specs=[SMEM] + [VMEM] * 19,
        out_specs=[VMEM] * len(outs),
        scratch_shapes=scratch,
        compiler_params=PARAMS,
        name="first_step",
    )(flags, state, wet, *received, planes, *constants)

    received, _ = exchange(fields, edges, one, two, None, d, ())
    state = pl.pallas_call(
        functools.partial(step_kernel, d, False, True),
        out_shape=state_shape,
        in_specs=[SMEM] + [VMEM] * 20,
        out_specs=VMEM,
        scratch_shapes=scratch,
        compiler_params=PARAMS,
        name="second_step",
    )(flags, state, wet, *received, plan_x, plan_y, *constants)
    return jnp.transpose(state, (1, 0, 2))[None]


def solution(mesh):
    return jax.shard_map(
        local,
        mesh=mesh,
        in_specs=(
            P("grp", None, "lat", "lon"),
            P("lat", "lon"),
            P("grp", None, None, "lat", "lon"),
            P("grp", None, "lat", "lon"),
            P(),
            P(),
            P(),
            P(),
            P(),
            P(),
            P(),
        ),
        out_specs=P("grp", None, "lat", "lon"),
        check_vma=False,
    )
```

```python
import functools

import jax
import jax.numpy as jnp
from jax import lax
from jax.experimental import pallas as pl
from jax.experimental.pallas import tpu as pltpu
from jax.sharding import PartitionSpec as P

CH = 80
NS = 4
NK = 4
HW = 8
SPAN = 2 * HW + 1
HIDP = 208
F32 = jnp.float32
BF16 = jnp.bfloat16


def roll(x, shift, axis=1):
    size = x.shape[axis]
    if isinstance(shift, int):
        shift = shift % size
        if shift == 0:
            return x
    return pltpu.roll(x, shift, axis)


def lanes(shape):
    return lax.broadcasted_iota(jnp.int32, shape, len(shape) - 1)


def subs(shape):
    return lax.broadcasted_iota(jnp.int32, shape, len(shape) - 2)


class Dims:
    def __init__(self, rows):
        self.rows = rows
        self.block = 32 if rows + 4 <= 32 else 64
        self.edge = 4 * self.block
        self.pieces = self.edge // 128
        self.edge_rows = CH * self.pieces
        self.tiles = -(-(rows + 4) // 8)
        self.tall = 8 * self.tiles
        self.strip = 2 * CH + self.edge_rows


def put_edges(ref, at, edges, d):
    for piece in range(d.pieces):
        ref[at + piece * CH : at + (piece + 1) * CH, :] = edges[:, piece * 128 : (piece + 1) * 128]


def get_edges(ref, at, d):
    return jnp.concatenate(
        [ref[at + piece * CH : at + (piece + 1) * CH, :] for piece in range(d.pieces)], axis=1
    )


def edge_columns(state, d):
    lane = lanes((1, d.edge))
    block = lane // d.block
    row = lane % d.block - 2
    column = jnp.where(block == 0, 126, jnp.where(block == 1, 0, jnp.where(block == 2, 127, 1)))
    own = (row >= 0) & (row < d.rows)
    target = jnp.where(own, column, -1)
    position = subs((128, d.edge))
    places = [
        (position == jnp.where(row == step, target, -1)).astype(F32).astype(BF16)
        for step in range(d.rows)
    ]
    whole = jnp.concatenate([state[step] for step in range(d.rows)], axis=1)
    total = jnp.dot(whole, jnp.concatenate(places, axis=0), preferred_element_type=F32)
    return total.astype(BF16)


def loop(count, unroll, body):
    while count % unroll:
        unroll -= 1

    def several(step, carry):
        for offset in range(unroll):
            body(step * unroll + offset)
        return carry

    lax.fori_loop(0, count // unroll, several, 0)


def strips(one, two, even, d):
    last = d.rows - 2
    return (one, jnp.where(even, last, 0)), (two, jnp.where(even, 0, last))


def emit(state, proj, keeping, fields, own_edges, one, two, even, raw, d):
    half = d.rows // 2

    def body(step):
        pair = jnp.concatenate([state[step], state[step + half]], axis=1)
        parts = jnp.dot(proj[...], pair, preferred_element_type=F32)
        whole = parts[0:8] + parts[8:16] + parts[16:24]
        raw[pl.ds(pl.multiple_of(step * 8, 8), 8), :] = whole[:, :128]
        raw[pl.ds(pl.multiple_of((step + half) * 8, 8), 8), :] = whole[:, 128:]

    loop(half, 8, body)
    for field in range(NS):
        fields[field] = (raw[pl.ds(field, d.rows, stride=8), :] * keeping[...]).astype(BF16)
    edges = edge_columns(state, d)
    put_edges(own_edges, 0, edges, d)
    for ref, first in strips(one, two, even, d):
        ref[0:CH, :] = state[first]
        ref[CH : 2 * CH, :] = state[first + 1]
        put_edges(ref, 2 * CH, edges, d)


def start_kernel(d, flags, state, planes, proj, keeping, fields, own_edges, one, two, raw, tall):
    even = flags[3] == 0
    emit(state, proj, keeping, fields, own_edges, one, two, even, raw, d)
    for plane in range(2 * NK):
        tall[plane * d.rows : (plane + 1) * d.rows, :] = planes[plane].astype(F32)
    for ref, first in strips(one, two, even, d):
        strip = [tall[pl.ds(first + step, 2 * NK, stride=d.rows), :] for step in range(2)]
        ref[d.strip : d.strip + 16, :] = jnp.concatenate(strip, axis=0).astype(BF16)


def decode(code):
    shifted = code.astype(jnp.int32) + (HW * SPAN + HW)
    rows = lax.shift_right_logical(shifted * 241, 12)
    return rows - HW, shifted - rows * SPAN - HW


def along_lanes(values, index):
    numbers = lax.GatherDimensionNumbers(
        offset_dims=(),
        collapsed_slice_dims=(1,),
        start_index_map=(1,),
        operand_batching_dims=(0,),
        start_indices_batching_dims=(0,),
    )
    return lax.gather(
        values, index[..., None], numbers, (1, 1), mode=lax.GatherScatterMode.PROMISE_IN_BOUNDS
    )


def select_rows(sources, start, picks):
    chosen = [[jnp.zeros((8, 128), F32) for _ in range(NS)] for _ in picks]
    for shift in range(-HW, HW + 1):
        at = pl.ds(start + shift, 8)
        values = [[source[field, at, :] for field in range(NS)] for source in sources]
        for slot, (rows, index, allowed) in enumerate(picks):
            here = rows == shift
            for source, within in enumerate(allowed):
                if within is None:
                    continue
                mask = here & within
                for field in range(NS):
                    picked = along_lanes(values[source][field], index)
                    chosen[slot][field] = jnp.where(mask, picked, chosen[slot][field])
    return chosen


def regrid(fields_x, fields_y, plan_x, plan_y, forcing_x, forcing_y, first, tiles, tall, sides):
    def tile(step, carry):
        at = first + step * 8
        lane = lanes((8, 128))
        picks = []
        weights = []
        codes = []
        for k in range(NK):
            code = plan_x[pl.ds(k * tall + at, 8), :]
            weight = plan_x[pl.ds((NK + k) * tall + at, 8), :]
            codes.append(code)
            weights.append(weight)
            rows, cols = decode(code)
            column = lane + cols
            picks.append((rows, column & 127, ((column >= 0) & (column < 128), None)))
        part = ((lane + 8) & 127) // 32
        place = ((lane + 8) & 31) - 8
        outer = place >= 8
        code = jnp.zeros((8, 128), F32)
        weight = jnp.zeros((8, 128), F32)
        for k in range(NK):
            edge_code = roll(codes[k], 32 * k)
            edge_weight = roll(weights[k], 32 * k)
            if sides:
                edge_code = jnp.where(
                    outer, roll(plan_y[pl.ds(k * tall + at, 8), :], 32 * k + 16), edge_code
                )
                edge_weight = jnp.where(
                    outer, roll(plan_y[pl.ds((NK + k) * tall + at, 8), :], 32 * k + 16), edge_weight
                )
            code = jnp.where(part == k, edge_code, code)
            weight = jnp.where(part == k, edge_weight, weight)
        rows, cols = decode(code)
        inner_column = place & 127
        outer_column = jnp.where(place < 16, place - 16, place + 112)
        column = jnp.where(outer, outer_column, inner_column) + cols
        within = (column >= 0) & (column < 128)
        picks.append(
            (rows, column & 127, (within & outer if sides else None, jnp.logical_not(within)))
        )
        chosen = select_rows((fields_x, fields_y), at + 14, picks)
        edge = (lane < 8) | (lane >= 120)
        for field in range(NS):
            total = chosen[0][field] * weights[0]
            for k in range(1, NK):
                total = total + chosen[k][field] * weights[k]
            part_sum = chosen[NK][field] * weight
            extra = part_sum
            for k in range(1, NK):
                extra = extra + roll(part_sum, -32 * k)
            total = total + jnp.where(edge, extra, 0.0)
            forcing_x[pl.ds(at * 8 + field, 8, stride=8), :] = total
            forcing_x[pl.ds(at * 8 + field + 4, 8, stride=8), :] = total
            if sides:
                extra = roll(extra, -16)
                forcing_y[pl.ds(at * 8 + field, 8, stride=8), :] = extra
                forcing_y[pl.ds(at * 8 + field + 4, 8, stride=8), :] = extra
        return carry

    lax.fori_loop(0, tiles, tile, 0)


def place_columns(left, right):
    return jnp.where(lanes(left.shape) < 64, right.astype(F32), left.astype(F32))


def gelu(x):
    return jax.nn.gelu(x)


def air(state, out, forcing_x, atm_in, atm_bias, atm_out, d):
    half = d.rows // 2
    blank = jnp.zeros((8, 128), F32)

    def inputs(row):
        at = pl.multiple_of((row + 2) * 8, 8)
        forced = jnp.concatenate([forcing_x[pl.ds(at, 8), :], blank], axis=0)
        return jnp.concatenate([state[row], forced.astype(BF16)], axis=0)

    def body(step):
        pair = jnp.concatenate([inputs(step), inputs(step + half)], axis=1)
        hidden = gelu(jnp.dot(atm_in[...], pair, preferred_element_type=F32) + atm_bias[...])
        update = jnp.dot(atm_out[...], hidden.astype(BF16), preferred_element_type=F32)
        out[step] = (state[step].astype(F32) + update[:, :128]).astype(BF16)
        out[step + half] = (state[step + half].astype(F32) + update[:, 128:]).astype(BF16)

    loop(half, 2, body)


def edge_forcing(forcing_x, forcing_y, d):
    lane = lanes((8, d.edge))
    block = lane // d.block
    row = lane % d.block

    inner = outer = jnp.zeros((8, d.edge), F32)
    for step in range(d.rows + 4):
        at = pl.ds(step * 8, 8)
        pad = [jnp.zeros((8, 128), F32)] * (d.pieces - 1)
        here = jnp.concatenate([forcing_x[at, :]] + pad, axis=1)
        there = jnp.concatenate([forcing_y[at, :]] + pad, axis=1)
        for index, column in enumerate((126, 0, 127, 1)):
            shift = step + index * d.block - column
            match = (block == index) & (row == step)
            if column in (0, 127):
                inner = jnp.where(match, roll(here, shift), inner)
            outer = jnp.where(match, roll(there, shift), outer)
    return inner, outer


def sea(
    state, upper, lower, edges, left, right, out, forcing_x, forcing_y, ocn_in, ocn_bias, ocn_out,
    wet, at_top, at_bottom, stack, hidden, side, d,
):
    rows, block = d.rows, d.block
    lane = lanes((CH, 128))
    spot = lanes((CH, d.edge))
    part = spot // block
    inner = edges
    outer = jnp.where((part == 0) | (part == 2), left, right)

    def sides_of(inner, outer, spot):
        first = spot < block
        return (
            jnp.where(first, outer, roll(inner, -block)),
            jnp.where(first, roll(outer, -2 * block), outer),
            jnp.where(first, roll(inner, -block), roll(outer, -2 * block)),
        )

    beside = sides_of(inner, outer, spot)
    middle = beside[1]
    force_in, force_out = edge_forcing(forcing_x, forcing_y, d)
    beside_forcing = sides_of(force_in, force_out, lanes((8, d.edge)))
    sub = subs((8, d.edge))
    blank = jnp.zeros((8, d.edge), F32)
    forced = jnp.concatenate(
        [
            jnp.where(sub < 4, beside_forcing[0], beside_forcing[1]),
            jnp.where(sub < 4, beside_forcing[2], blank),
        ],
        axis=0,
    ).astype(BF16)
    columns = jnp.concatenate(list(beside) + [forced], axis=0)
    for tap in range(3):
        side[tap * 256 : (tap + 1) * 256, :] = roll(columns, -tap)

    sub_row = subs((8, 128))
    lane_row = lanes((8, 128))

    def build(row, values):
        entry = roll(middle, (d.edge - row) % d.edge)[:, :128]
        stack[row, 0:CH, :] = jnp.where(lane == 0, entry, roll(values, 1))
        stack[row, CH : 2 * CH, :] = values
        entry = roll(middle, (2 * d.edge + 127 - block - row) % d.edge)[:, :128]
        stack[row, 2 * CH : 3 * CH, :] = jnp.where(lane == 127, entry, roll(values, -1))
        at = pl.ds(pl.multiple_of(row * 8, 8), 8)
        here, there = forcing_x[at, :], forcing_y[at, :]
        before = roll(jnp.where(lane_row == 127, there, here), 1)
        after = roll(jnp.where(lane_row == 0, there, here), -1)
        stack[row, 3 * CH : 256, :] = jnp.concatenate(
            [jnp.where(sub_row < 4, before, here), jnp.where(sub_row < 4, after, jnp.zeros_like(after))],
            axis=0,
        ).astype(BF16)

    for step in range(2):
        build(jnp.int32(step), upper[step * CH : (step + 1) * CH, :])
        build(jnp.int32(rows + 2 + step), lower[step * CH : (step + 1) * CH, :])

    loop(rows, 4, lambda step: build(step + 2, state[step]))

    pairs = (rows + 2) // 2

    def first(step):
        taps = jnp.concatenate(
            [
                stack[pl.ds(step, 3)].reshape(3 * 256, 128),
                stack[pl.ds(step + pairs, 3)].reshape(3 * 256, 128),
            ],
            axis=1,
        )
        product = jnp.dot(ocn_in[...], taps, preferred_element_type=F32) + ocn_bias[...]
        active = gelu(product)
        keep_low = jnp.where((step == 0) & (at_top != 0), 0.0, 1.0).astype(F32)
        keep_high = jnp.where((step == pairs - 1) & (at_bottom != 0), 0.0, 1.0).astype(F32)
        hidden[step] = (active[:, :128] * keep_low).astype(BF16)
        hidden[step + pairs] = (active[:, 128:] * keep_high).astype(BF16)

    loop(pairs, 3, first)

    product = jnp.dot(ocn_in[...], side[...], preferred_element_type=F32) + ocn_bias[...]
    spot = lanes((1, d.edge)) % block
    gone = ((spot == 0) & (at_top != 0)) | ((spot == rows + 1) & (at_bottom != 0))
    active = jnp.where(gone, 0.0, gelu(product)).astype(BF16)
    taps = jnp.concatenate([roll(active, -tap) for tap in range(3)], axis=0)
    partial = jnp.dot(ocn_out[...], taps, preferred_element_type=F32)
    from_left, from_right = partial[0:CH], partial[2 * CH : 3 * CH]
    half = rows // 2

    def second(step):
        taps = jnp.concatenate(
            [
                hidden[pl.ds(step, 3)].reshape(3 * HIDP, 128),
                hidden[pl.ds(step + half, 3)].reshape(3 * HIDP, 128),
            ],
            axis=1,
        )
        product = jnp.dot(ocn_out[...], taps, preferred_element_type=F32)
        for offset in range(2):
            row = step + offset * half
            sums = product[:, offset * 128 : (offset + 1) * 128]
            entry = roll(from_left, (d.edge - row) % d.edge)[:, :128]
            total = sums[CH : 2 * CH] + jnp.where(lane == 0, entry, roll(sums[0:CH], 1))
            entry = roll(from_right, (2 * d.edge + 127 - block - row) % d.edge)[:, :128]
            total = total + jnp.where(lane == 127, entry, roll(sums[2 * CH : 3 * CH], -1))
            update = total * wet[pl.ds(row, 1), :]
            out[row] = (state[row].astype(F32) + update).astype(BF16)

    loop(half, 2, second)


def join_rows(edge_up, edge_own, edge_down, d):
    row = lanes(edge_own.shape) % d.block
    above = roll(edge_up, -d.rows)
    below = roll(edge_down, d.rows)
    return jnp.where(row < 2, above, jnp.where(row < d.rows + 2, edge_own, below))


def step_kernel(d, opening, closing, *refs):
    refs = list(refs)
    take = lambda count: [refs.pop(0) for _ in range(count)]
    (flags,) = take(1)
    state, wet, field_one, beside, field_two, from_one, from_two, own_edges, from_left, from_right = take(10)
    if opening:
        (planes,) = take(1)
    else:
        plan_x, plan_y = take(2)
    atm_in, atm_bias, atm_out, ocn_in, ocn_bias, ocn_out, proj, keeping = take(8)
    (out,) = take(1)
    if not closing:
        fields, new_edges, one, two = take(4)
    if opening:
        plan_x, plan_y = take(2)
    fields_x, fields_y, forcing_x, forcing_y, stack, hidden, side, raw = take(8)
    rows, tall = d.rows, d.tall
    is_ocean, at_top, at_bottom = flags[0], flags[1], flags[2]
    even = flags[3] == 0

    def up(one, two):
        values = jnp.where(even, two, one).astype(F32)
        return jnp.where(at_top != 0, 0.0, values)

    def down(one, two):
        values = jnp.where(even, one, two).astype(F32)
        return jnp.where(at_bottom != 0, 0.0, values)

    def up_and_down(one, two):
        return up(one, two), down(one, two)

    if opening:

        @pl.when(is_ocean != 0)
        def _():
            plan_x[...] = jnp.zeros_like(plan_x)
            plan_y[...] = jnp.zeros_like(plan_y)
            base = d.strip
            side_base = 4 * (rows + 32) + 3 * d.edge_rows
            pair = up_and_down(from_one[base : base + 16, :], from_two[base : base + 16, :])
            for step, strip in zip((0, rows + 2), pair):
                for index in range(2):
                    plan_x[pl.ds(step + index, 2 * NK, stride=tall), :] = strip[index * 8 : (index + 1) * 8]
            ends = [
                place_columns(from_left[at : at + 16, :], from_right[at : at + 16, :])
                for at in (side_base, side_base + 16 + 2 * NK * rows)
            ]
            for step, strip in zip((0, rows + 2), up_and_down(*ends)):
                for index in range(2):
                    plan_y[pl.ds(step + index, 2 * NK, stride=tall), :] = strip[index * 8 : (index + 1) * 8]
            for plane in range(2 * NK):
                at = side_base + 16 + plane * rows
                plan_y[plane * tall + 2 : plane * tall + 2 + rows, :] = place_columns(
                    from_left[at : at + rows, :], from_right[at : at + rows, :]
                )

        for plane in range(2 * NK):
            plan_x[plane * tall + 2 : plane * tall + 2 + rows, :] = planes[plane].astype(F32)

    lower_at = 64 + 4 * rows
    for field in range(NS):
        ends = up_and_down(field_one[field], field_two[field])
        fields_x[field, 0:16, :] = ends[0][rows - 16 : rows]
        fields_x[field, 16 : 16 + rows, :] = beside[field].astype(F32)
        fields_x[field, 16 + rows : 32 + rows, :] = ends[1][0:16]
        start = 64 + field * rows
        fields_y[field, 16 : 16 + rows, :] = place_columns(
            from_left[start : start + rows, :], from_right[start : start + rows, :]
        )
        ends = [
            place_columns(from_left[at : at + 16, :], from_right[at : at + 16, :])
            for at in (field * 16, lower_at + field * 16)
        ]
        ends = up_and_down(*ends)
        fields_y[field, 0:16, :] = ends[0]
        fields_y[field, 16 + rows : 32 + rows, :] = ends[1]

    @pl.when(is_ocean == 0)
    def _():
        regrid(fields_x, fields_y, plan_x, plan_y, forcing_x, forcing_y, 2, rows // 8, tall, False)
        air(state, out, forcing_x, atm_in, atm_bias, atm_out, d)

    @pl.when(is_ocean != 0)
    def _():
        regrid(fields_x, fields_y, plan_x, plan_y, forcing_x, forcing_y, 0, d.tiles, tall, True)
        at = 4 * (rows + 32)
        size = d.edge_rows
        def joined(one, own, two):
            above, below = up_and_down(one, two)
            return join_rows(above.astype(BF16), own, below.astype(BF16), d)

        edges = joined(
            get_edges(from_one, 2 * CH, d), get_edges(own_edges, 0, d), get_edges(from_two, 2 * CH, d)
        )
        left, right = [
            joined(*[get_edges(ref, at + index * size, d) for index in range(3)])
            for ref in (from_left, from_right)
        ]
        upper, lower = up_and_down(from_one[0 : 2 * CH, :], from_two[0 : 2 * CH, :])
        sea(
            state, upper.astype(BF16), lower.astype(BF16), edges, left, right, out, forcing_x, forcing_y,
            ocn_in, ocn_bias, ocn_out, wet, at_top, at_bottom, stack, hidden, side, d,
        )

    if not closing:
        emit(out, proj, keeping, fields, new_edges, one, two, even, raw, d)


VMEM = pl.BlockSpec(memory_space=pltpu.VMEM)
SMEM = pl.BlockSpec(memory_space=pltpu.SMEM)
PARAMS = pltpu.CompilerParams(vmem_limit_bytes=48 * 1024 * 1024)


def shape(*dims, dtype=BF16):
    return jax.ShapeDtypeStruct(dims, dtype)


def send(x, move):
    names = ("grp", "lat", "lon")
    sizes = [lax.axis_size(name) for name in names]
    pairs = []
    for group in range(sizes[0]):
        for lat in range(sizes[1]):
            for lon in range(sizes[2]):
                to = move(group, lat, lon)
                if to is None or not 0 <= to[1] < sizes[1]:
                    continue
                target = (to[0] * sizes[1] + to[1]) * sizes[2] + to[2] % sizes[2]
                pairs.append(((group * sizes[1] + lat) * sizes[2] + lon, target))
    return lax.ppermute(x, names, pairs)


def swap_rows(x, turn, across):
    count = lax.axis_size("lat")

    def move(group, lat, lon):
        other = ((lat + turn) ^ 1) - turn
        to = 1 - group if across else group
        return to, other if 0 <= other < count else lat, lon

    return send(x, move)


def exchange(fields, own_edges, one, two, planes, d):
    rows = d.rows
    beside = send(fields, lambda g, i, j: (1 - g, i, j))
    field_one = swap_rows(fields, 0, True)
    field_two = swap_rows(fields, 1, True)
    from_one = swap_rows(one, 0, False)
    from_two = swap_rows(two, 1, False)
    edge_at = slice(2 * CH, d.strip)
    odd = lax.axis_index("lat") % 2
    if rows == 16:
        ends = [field_one, field_two]
    else:
        last = [field[:, rows - 16 :] for field in (field_one, field_two)]
        first = [field[:, :16] for field in (field_one, field_two)]
        ends = [jnp.where(odd == 1, last[0], first[0]), jnp.where(odd == 1, first[1], last[1])]
    packed = [
        ends[0].reshape(64, 128),
        beside.reshape(4 * rows, 128),
        ends[1].reshape(64, 128),
        from_one[edge_at],
        own_edges,
        from_two[edge_at],
    ]
    if planes is not None:
        packed += [from_one[d.strip :], planes.reshape(2 * NK * rows, 128), from_two[d.strip :]]
    packed = jnp.concatenate(packed, axis=0)
    from_left = send(packed, lambda g, i, j: (g, i, j + 1))
    from_right = send(packed, lambda g, i, j: (g, i, j - 1))
    return field_one, beside, field_two, from_one, from_two, own_edges, from_left, from_right


def local(
    coupled_state, land_mask, regrid_offsets, regrid_weights, surface_proj,
    atm_in, atm_bias, atm_out, ocn_in, ocn_bias, ocn_out,
):
    rows = coupled_state.shape[2]
    assert coupled_state.shape[3] == 128
    d = Dims(rows)
    group = lax.axis_index("grp")
    lat = lax.axis_index("lat")
    is_ocean = group == 1
    flags = jnp.stack(
        [group, lat == 0, lat == lax.axis_size("lat") - 1, lat % 2]
    ).astype(jnp.int32)
    state = jnp.transpose(coupled_state[0], (1, 0, 2))
    wet = land_mask.astype(F32)
    keeping = jnp.where(is_ocean, wet, 1.0)
    projector = lax.dynamic_index_in_dim(surface_proj, group, 0, keepdims=False)
    high = projector.astype(BF16)
    rest = projector - high.astype(F32)
    mid = rest.astype(BF16)
    low = (rest - mid.astype(F32)).astype(BF16)
    gap = jnp.zeros((4, CH), BF16)
    proj = jnp.concatenate([high, gap, mid, gap, low, gap], axis=0)
    codes = regrid_offsets[0, 0] * SPAN + regrid_offsets[0, 1]
    planes = jnp.concatenate([codes.astype(BF16), regrid_weights[0].astype(BF16)], axis=0)

    hidden_count = ocn_in.shape[0]
    taps = ocn_in.reshape(hidden_count, 3, 3, CH + NS)
    first = jnp.concatenate(
        [
            taps[..., :CH].reshape(hidden_count, 3, 3 * CH),
            taps[..., CH:].reshape(hidden_count, 3, 3 * NS),
            jnp.zeros((hidden_count, 3, 256 - 3 * (CH + NS)), BF16),
        ],
        axis=2,
    ).reshape(hidden_count, 768)
    extra = HIDP - hidden_count
    first = jnp.pad(first, ((0, extra), (0, 0)))
    first_bias = jnp.pad(ocn_bias, (0, extra))[:, None]
    second = jnp.transpose(ocn_out.reshape(CH, 3, 3, hidden_count), (2, 0, 1, 3))
    second = jnp.pad(second, ((0, 0), (0, 0), (0, 0), (0, extra))).reshape(3 * CH, 3 * HIDP)
    air_in = jnp.pad(atm_in, ((0, 0), (0, 16 - NS)))
    constants = (air_in, atm_bias[:, None], atm_out, first, first_bias, second, proj, keeping)

    emitted = [
        shape(NS, rows, 128),
        shape(d.edge_rows, 128),
        shape(d.strip, 128),
        shape(d.strip, 128),
    ]
    raw = pltpu.VMEM((rows * 8, 128), F32)
    fields, edges, one, two = pl.pallas_call(
        functools.partial(start_kernel, d),
        out_shape=emitted[:2] + [shape(d.strip + 16, 128)] * 2,
        in_specs=[SMEM] + [VMEM] * 4,
        out_specs=[VMEM] * 4,
        scratch_shapes=[raw, pltpu.VMEM((2 * NK * rows, 128), F32)],
        compiler_params=PARAMS,
        name="start",
    )(flags, state, planes, proj, keeping)

    scratch = [
        pltpu.VMEM((NS, rows + 32, 128), F32),
        pltpu.VMEM((NS, rows + 32, 128), F32),
        pltpu.VMEM((d.tall * 8, 128), F32),
        pltpu.VMEM((d.tall * 8, 128), F32),
        pltpu.VMEM((rows + 4, 256, 128), BF16),
        pltpu.VMEM((rows + 2, HIDP, 128), BF16),
        pltpu.VMEM((768, d.edge), BF16),
        raw,
    ]
    plans = [shape(2 * NK * d.tall, 128, dtype=F32)] * 2
    state_shape = shape(rows, CH, 128)

    received = exchange(fields, edges, one, two, planes, d)
    outs = [state_shape] + emitted + plans
    state, fields, edges, one, two, plan_x, plan_y = pl.pallas_call(
        functools.partial(step_kernel, d, True, False),
        out_shape=outs,
        in_specs=[SMEM] + [VMEM] * 19,
        out_specs=[VMEM] * len(outs),
        scratch_shapes=scratch,
        compiler_params=PARAMS,
        name="first_step",
    )(flags, state, wet, *received, planes, *constants)

    received = exchange(fields, edges, one, two, None, d)
    state = pl.pallas_call(
        functools.partial(step_kernel, d, False, True),
        out_shape=state_shape,
        in_specs=[SMEM] + [VMEM] * 20,
        out_specs=VMEM,
        scratch_shapes=scratch,
        compiler_params=PARAMS,
        name="second_step",
    )(flags, state, wet, *received, plan_x, plan_y, *constants)
    return jnp.transpose(state, (1, 0, 2))[None]


def solution(mesh):
    return jax.shard_map(
        local,
        mesh=mesh,
        in_specs=(
            P("grp", None, "lat", "lon"),
            P("lat", "lon"),
            P("grp", None, None, "lat", "lon"),
            P("grp", None, "lat", "lon"),
            P(),
            P(),
            P(),
            P(),
            P(),
            P(),
            P(),
        ),
        out_specs=P("grp", None, "lat", "lon"),
        check_vma=False,
    )
```

```python
import functools

import jax
import jax.numpy as jnp
from jax import lax
from jax.experimental import pallas as pl
from jax.experimental.pallas import tpu as pltpu
from jax.sharding import PartitionSpec as P

CH = 80
NS = 4
NK = 4
HA = 384
HW = 8
SPAN = 2 * HW + 1
HIDK = 208
HIDP = 256
F32 = jnp.float32
BF16 = jnp.bfloat16


def roll(x, shift, axis=1):
    size = x.shape[axis]
    if isinstance(shift, int):
        shift = shift % size
        if shift == 0:
            return x
    return pltpu.roll(x, shift, axis)


def lanes(shape):
    return lax.broadcasted_iota(jnp.int32, shape, len(shape) - 1)


def subs(shape):
    return lax.broadcasted_iota(jnp.int32, shape, len(shape) - 2)


class Dims:
    def __init__(self, rows):
        self.rows = rows
        self.block = 32 if rows + 4 <= 32 else 64
        self.edge = 4 * self.block
        self.pieces = self.edge // 128
        self.edge_rows = CH * self.pieces
        self.tiles = -(-(rows + 4) // 8)
        self.tall = 8 * self.tiles
        self.strip = 2 * CH + self.edge_rows


def put_edges(ref, at, edges, d):
    for piece in range(d.pieces):
        ref[at + piece * CH : at + (piece + 1) * CH, :] = edges[:, piece * 128 : (piece + 1) * 128]


def get_edges(ref, at, d):
    return jnp.concatenate(
        [ref[at + piece * CH : at + (piece + 1) * CH, :] for piece in range(d.pieces)], axis=1
    )


def edge_columns(state, d):
    lane = lanes((1, d.edge))
    block = lane // d.block
    row = lane % d.block - 2
    column = jnp.where(block == 0, 126, jnp.where(block == 1, 0, jnp.where(block == 2, 127, 1)))
    own = (row >= 0) & (row < d.rows)
    target = jnp.where(own, column, -1)
    position = subs((128, d.edge))
    places = [
        (position == jnp.where(row == step, target, -1)).astype(F32).astype(BF16)
        for step in range(d.rows)
    ]
    whole = jnp.concatenate([state[step] for step in range(d.rows)], axis=1)
    total = jnp.dot(whole, jnp.concatenate(places, axis=0), preferred_element_type=F32)
    return total.astype(BF16)


def loop(count, unroll, body):
    while count % unroll:
        unroll -= 1

    def several(step, carry):
        for offset in range(unroll):
            body(step * unroll + offset)
        return carry

    lax.fori_loop(0, count // unroll, several, 0)


def strips(one, two, even, d):
    last = d.rows - 2
    return (one, jnp.where(even, last, 0)), (two, jnp.where(even, 0, last))


def split_bf16(values):
    high = values.astype(BF16).astype(F32)
    mid = (values - high).astype(BF16).astype(F32)
    return high, mid, values - high - mid


def emit(state, surface, wet, flags, fields, own_edges, one, two, raw, d):
    half = d.rows // 2
    is_ocean, even = flags[0] != 0, flags[3] == 0
    gap = jnp.zeros((4, CH), F32)
    terms = []
    for term in split_bf16(surface[flags[0]]):
        terms += [term, gap]
    proj = jnp.concatenate(terms + [gap, gap], axis=0).astype(BF16)
    for step in range(half):
        pair = jnp.concatenate([state[step], state[step + half]], axis=1)
        parts = jnp.dot(proj, pair, preferred_element_type=F32)
        whole = parts[0:8] + parts[8:16] + parts[16:24]
        raw[step * 8 : step * 8 + 8, :] = whole[:, :128]
        raw[(step + half) * 8 : (step + half) * 8 + 8, :] = whole[:, 128:]
    keeping = jnp.where(is_ocean, wet[...].astype(F32), 1.0)
    for field in range(NS):
        fields[field] = (raw[pl.ds(field, d.rows, stride=8), :] * keeping).astype(BF16)
    edges = edge_columns(state, d)
    put_edges(own_edges, 0, edges, d)
    for ref, first in strips(one, two, even, d):
        ref[0:CH, :] = state[first]
        ref[CH : 2 * CH, :] = state[first + 1]
        put_edges(ref, 2 * CH, edges, d)


def start_kernel(
    d, flags, given, offsets, weights, surface, wet, state, planes, fields, own_edges, one, two,
    raw, tall, turned,
):
    rows = d.rows
    turned[...] = given[...].astype(F32).reshape(CH * rows, 128)
    for row in range(rows):
        state[row] = turned[pl.ds(row, CH, stride=rows), :].astype(BF16)
    emit(state, surface, wet, flags, fields, own_edges, one, two, raw, d)
    for k in range(NK):
        code = (offsets[0, k] * SPAN + offsets[1, k]).astype(F32)
        tall[k * rows : (k + 1) * rows, :] = code
        tall[(NK + k) * rows : (NK + k + 1) * rows, :] = weights[k]
        planes[k] = code.astype(BF16)
        planes[NK + k] = weights[k].astype(BF16)
    for ref, first in strips(one, two, flags[3] == 0, d):
        strip = [tall[pl.ds(first + step, 2 * NK, stride=rows), :] for step in range(2)]
        ref[d.strip : d.strip + 16, :] = jnp.concatenate(strip, axis=0).astype(BF16)


def decode(code):
    shifted = code.astype(jnp.int32) + (HW * SPAN + HW)
    rows = lax.shift_right_logical(shifted * 241, 12)
    return rows - HW, shifted - rows * SPAN - HW


def along_lanes(values, index):
    numbers = lax.GatherDimensionNumbers(
        offset_dims=(),
        collapsed_slice_dims=(1,),
        start_index_map=(1,),
        operand_batching_dims=(0,),
        start_indices_batching_dims=(0,),
    )
    return lax.gather(
        values, index[..., None], numbers, (1, 1), mode=lax.GatherScatterMode.PROMISE_IN_BOUNDS
    )


def select_rows(sources, start, picks):
    chosen = [[jnp.zeros((8, 128), F32) for _ in range(NS)] for _ in picks]
    for shift in range(-HW, HW + 1):
        at = pl.ds(start + shift, 8)
        used = [any(pick[2][index] is not None for pick in picks) for index in range(len(sources))]
        values = [
            [source[field, at, :] for field in range(NS)] if use else None
            for source, use in zip(sources, used)
        ]
        for slot, (rows, index, allowed) in enumerate(picks):
            here = rows == shift
            for source, within in enumerate(allowed):
                if within is None:
                    continue
                mask = here & within
                for field in range(NS):
                    picked = along_lanes(values[source][field], index)
                    chosen[slot][field] = jnp.where(mask, picked, chosen[slot][field])
    return chosen


def regrid_inside(fields_x, plan_x, part_x, first, tiles, tall):
    lane = lanes((8, 128))
    for step in range(tiles):
        at = first + step * 8
        picks = []
        weights = []
        for k in range(NK):
            rows, cols = decode(plan_x[pl.ds(k * tall + at, 8), :])
            weights.append(plan_x[pl.ds((NK + k) * tall + at, 8), :])
            column = lane + cols
            picks.append((rows, column & 127, ((column >= 0) & (column < 128),)))
        chosen = select_rows((fields_x,), at + 14, picks)
        for field in range(NS):
            total = chosen[0][field] * weights[0]
            for k in range(1, NK):
                total = total + chosen[k][field] * weights[k]
            part_x[pl.ds(field * tall + at, 8), :] = total


def regrid_beside(
    fields_x, fields_y, plan_x, plan_y, part_x, forcing_x, forcing_y, first, tiles, tall, sides
):
    lane = lanes((8, 128))
    part = ((lane + 8) & 127) // 32
    place = ((lane + 8) & 31) - 8
    outer = place >= 8
    inner_column = place & 127
    outer_column = jnp.where(place < 16, place - 16, place + 112)
    edge = (lane < 8) | (lane >= 120)
    for step in range(tiles):
        at = first + step * 8
        code = jnp.zeros((8, 128), F32)
        weight = jnp.zeros((8, 128), F32)
        for k in range(NK):
            edge_code = roll(plan_x[pl.ds(k * tall + at, 8), :], 32 * k)
            edge_weight = roll(plan_x[pl.ds((NK + k) * tall + at, 8), :], 32 * k)
            if sides:
                edge_code = jnp.where(
                    outer, roll(plan_y[pl.ds(k * tall + at, 8), :], 32 * k + 16), edge_code
                )
                edge_weight = jnp.where(
                    outer, roll(plan_y[pl.ds((NK + k) * tall + at, 8), :], 32 * k + 16), edge_weight
                )
            code = jnp.where(part == k, edge_code, code)
            weight = jnp.where(part == k, edge_weight, weight)
        rows, cols = decode(code)
        column = jnp.where(outer, outer_column, inner_column) + cols
        within = (column >= 0) & (column < 128)
        picks = [(rows, column & 127, (within & outer if sides else None, jnp.logical_not(within)))]
        (chosen,) = select_rows((fields_x, fields_y), at + 14, picks)
        for field in range(NS):
            part_sum = chosen[field] * weight
            extra = part_sum
            for k in range(1, NK):
                extra = extra + roll(part_sum, -32 * k)
            total = part_x[pl.ds(field * tall + at, 8), :] + jnp.where(edge, extra, 0.0)
            forcing_x[pl.ds(at * 8 + field, 8, stride=8), :] = total
            forcing_x[pl.ds(at * 8 + field + 4, 8, stride=8), :] = total
            if sides:
                extra = roll(extra, -16)
                forcing_y[pl.ds(at * 8 + field, 8, stride=8), :] = extra
                forcing_y[pl.ds(at * 8 + field + 4, 8, stride=8), :] = extra


def place_columns(left, right):
    return jnp.where(lanes(left.shape) < 64, right.astype(F32), left.astype(F32))


def gelu(x):
    scale = (2 / jnp.pi) ** 0.5
    half = 0.5 * x
    return half + half * jnp.tanh(x * (scale + (scale * 0.044715) * (x * x)))


def air(state, out, forcing_x, air_in, atm_out, d):
    half = d.rows // 2
    first = subs((8, 128)) < 4
    blank = jnp.zeros((32, 128), BF16)

    def inputs(row):
        at = (row + 2) * 8
        forced = jnp.where(first, forcing_x[at : at + 8, :], 1.0)
        forced = jnp.concatenate([forced, jnp.zeros_like(forced)], axis=0).astype(BF16)
        return jnp.concatenate([state[row], forced, blank], axis=0)

    for step in range(half):
        pair = jnp.concatenate([inputs(step), inputs(step + half)], axis=1)
        hidden = gelu(jnp.dot(air_in[...], pair, preferred_element_type=F32)).astype(BF16)
        update = jnp.dot(atm_out[...], hidden, preferred_element_type=F32)
        for offset in range(2):
            row = step + offset * half
            change = update[:, offset * 128 : (offset + 1) * 128]
            out(row, state[row].astype(F32) + change)


def edge_forcing(forcing_x, forcing_y, d):
    lane = lanes((8, d.edge))
    block = lane // d.block
    row = lane % d.block

    inner = outer = jnp.zeros((8, d.edge), F32)
    for step in range(d.rows + 4):
        at = pl.ds(step * 8, 8)
        pad = [jnp.zeros((8, 128), F32)] * (d.pieces - 1)
        here = jnp.concatenate([forcing_x[at, :]] + pad, axis=1)
        there = jnp.concatenate([forcing_y[at, :]] + pad, axis=1)
        for index, column in enumerate((126, 0, 127, 1)):
            shift = step + index * d.block - column
            match = (block == index) & (row == step)
            if column in (0, 127):
                inner = jnp.where(match, roll(here, shift), inner)
            outer = jnp.where(match, roll(there, shift), outer)
    return inner, outer


def roll_rows(state, upper, lower, rolled, d):
    def put(row, values):
        rolled[row, 0:CH, :] = roll(values, 1)
        rolled[row, CH : 2 * CH, :] = values
        rolled[row, 2 * CH : 3 * CH, :] = roll(values, -1)

    for step in range(2):
        put(step, upper[step * CH : (step + 1) * CH, :])
        put(d.rows + 2 + step, lower[step * CH : (step + 1) * CH, :])
    for row in range(d.rows):
        put(row + 2, state[row])


def sea(
    state, rolled, edges, left, right, out, forcing_x, forcing_y, ocn_in, ocn_out, wet,
    at_top, at_bottom, stack, hidden, side, d,
):
    rows, block = d.rows, d.block
    lane = lanes((CH, 128))
    spot = lanes((CH, d.edge))
    part = spot // block
    inner = edges
    outer = jnp.where((part == 0) | (part == 2), left, right)

    def sides_of(inner, outer, spot):
        first = spot < block
        return (
            jnp.where(first, outer, roll(inner, -block)),
            jnp.where(first, roll(outer, -2 * block), outer),
            jnp.where(first, roll(inner, -block), roll(outer, -2 * block)),
        )

    beside = sides_of(inner, outer, spot)
    middle = beside[1]
    force_in, force_out = edge_forcing(forcing_x, forcing_y, d)
    beside_forcing = sides_of(force_in, force_out, lanes((8, d.edge)))
    sub = subs((8, d.edge))
    ones = jnp.ones((8, d.edge), F32)
    forced = jnp.concatenate(
        [
            jnp.where(sub < 4, beside_forcing[0], beside_forcing[1]),
            jnp.where(sub < 4, beside_forcing[2], ones),
        ],
        axis=0,
    ).astype(BF16)
    columns = jnp.concatenate(list(beside) + [forced], axis=0)
    for tap in range(3):
        side[tap * 256 : (tap + 1) * 256, :] = roll(columns, -tap)

    sub_row = subs((8, 128))
    lane_row = lanes((8, 128))

    for row in range(rows + 4):
        entry = roll(middle, -row)[:, :128]
        stack[row, 0:CH, :] = jnp.where(lane == 0, entry, rolled[row, 0:CH, :])
        stack[row, CH : 2 * CH, :] = rolled[row, CH : 2 * CH, :]
        entry = roll(middle, 127 - block - row)[:, :128]
        stack[row, 2 * CH : 3 * CH, :] = jnp.where(lane == 127, entry, rolled[row, 2 * CH : 3 * CH, :])
        here, there = forcing_x[row * 8 : row * 8 + 8, :], forcing_y[row * 8 : row * 8 + 8, :]
        before = roll(jnp.where(lane_row == 127, there, here), 1)
        after = roll(jnp.where(lane_row == 0, there, here), -1)
        stack[row, 3 * CH : 256, :] = jnp.concatenate(
            [jnp.where(sub_row < 4, before, here), jnp.where(sub_row < 4, after, 1.0)], axis=0
        ).astype(BF16)

    pairs = (rows + 2) // 2

    for step in range(pairs):
        taps = jnp.concatenate(
            [
                stack[step : step + 3].reshape(3 * 256, 128),
                stack[step + pairs : step + pairs + 3].reshape(3 * 256, 128),
            ],
            axis=1,
        )
        active = gelu(jnp.dot(ocn_in[...], taps, preferred_element_type=F32))
        low, high = active[:, :128], active[:, 128:]
        if step == 0:
            low = jnp.where(at_top != 0, 0.0, low)
        if step == pairs - 1:
            high = jnp.where(at_bottom != 0, 0.0, high)
        hidden[step, 0:HIDK, :] = low.astype(BF16)
        hidden[step + pairs, 0:HIDK, :] = high.astype(BF16)
        blank = jnp.zeros((HIDP - HIDK, 128), BF16)
        hidden[step, HIDK:HIDP, :] = blank
        hidden[step + pairs, HIDK:HIDP, :] = blank

    product = jnp.dot(ocn_in[...], side[...], preferred_element_type=F32)
    spot = lanes((1, d.edge)) % block
    gone = ((spot == 0) & (at_top != 0)) | ((spot == rows + 1) & (at_bottom != 0))
    active = jnp.where(gone, 0.0, gelu(product)).astype(BF16)
    active = jnp.concatenate([active, jnp.zeros((HIDP - HIDK, d.edge), BF16)], axis=0)

    def taps_of(slices):
        total = None
        for tap, values in enumerate(slices):
            weights = ocn_out[tap * 3 * CH : (tap + 1) * 3 * CH, :]
            product = jnp.dot(weights, values, preferred_element_type=F32)
            total = product if total is None else total + product
        return total

    partial = taps_of([roll(active, -tap) for tap in range(3)])
    from_left, from_right = partial[0:CH], partial[2 * CH : 3 * CH]
    half = rows // 2
    for step in range(half):
        product = taps_of(
            [
                jnp.concatenate([hidden[step + tap], hidden[step + half + tap]], axis=1)
                for tap in range(3)
            ]
        )
        for offset in range(2):
            row = step + offset * half
            sums = product[:, offset * 128 : (offset + 1) * 128]
            entry = roll(from_left, -row)[:, :128]
            total = sums[CH : 2 * CH] + jnp.where(lane == 0, entry, roll(sums[0:CH], 1))
            entry = roll(from_right, 127 - block - row)[:, :128]
            total = total + jnp.where(lane == 127, entry, roll(sums[2 * CH : 3 * CH], -1))
            update = total * wet[row : row + 1, :].astype(F32)
            out(row, state[row].astype(F32) + update)


def join_rows(edge_up, edge_own, edge_down, d):
    row = lanes(edge_own.shape) % d.block
    above = roll(edge_up, -d.rows)
    below = roll(edge_down, d.rows)
    return jnp.where(row < 2, above, jnp.where(row < d.rows + 2, edge_own, below))


def prepare(atm_in, atm_bias, ocn_in, ocn_bias, ocn_out, air_in, first, second, is_ocean):
    def bias_rows(ref, width):
        row = ref[0:1, :]
        terms = list(split_bf16(row)) + [jnp.zeros_like(row)]
        bias = jnp.concatenate(terms, axis=0)
        return jnp.pad(bias, ((0, 0), (0, width - bias.shape[1])))

    @pl.when(is_ocean == 0)
    def _():
        columns = jnp.concatenate(
            [atm_in[...].astype(F32), bias_rows(atm_bias, HA), jnp.zeros((40, HA), F32)], axis=0
        )
        air_in[...] = columns.T.astype(BF16)

    @pl.when(is_ocean != 0)
    def _():
        bias = bias_rows(ocn_bias, 256)
        count = ocn_in.shape[2]
        for tap in range(3):
            whole = [ocn_in[3 * tap + side].astype(F32) for side in range(3)]
            whole = [jnp.pad(values, ((0, 0), (0, 256 - count))) for values in whole]
            rows = [values[:CH] for values in whole] + [values[CH:] for values in whole]
            rows.append(bias if tap == 0 else jnp.zeros((4, 256), F32))
            columns = jnp.concatenate(rows, axis=0).T
            first[:, tap * 256 : (tap + 1) * 256] = columns[:HIDK].astype(BF16)
        for tap in range(9):
            values = ocn_out[tap].astype(F32)
            second[tap * CH : (tap + 1) * CH, :] = jnp.pad(
                values, ((0, 0), (0, HIDP - count))
            ).astype(BF16)


def ends(flags):
    at_top, at_bottom, even = flags[1] != 0, flags[2] != 0, flags[3] == 0

    def up_and_down(one, two):
        above = jnp.where(even, two, one).astype(F32)
        below = jnp.where(even, one, two).astype(F32)
        return jnp.where(at_top, 0.0, above), jnp.where(at_bottom, 0.0, below)

    return up_and_down


def middle_kernel(d, opening, *refs):
    refs = list(refs)
    take = lambda count: [refs.pop(0) for _ in range(count)]
    flags, state, field_one, beside, field_two, from_one, from_two, own_edges = take(8)
    if opening:
        planes, *raw_weights = take(6)
    else:
        (plan_x,) = take(1)
    part_x, fields_x, rolled, edges = take(4)
    if opening:
        plan_x, *made_weights = take(4)
    rows, tall = d.rows, d.tall
    is_ocean = flags[0]
    up_and_down = ends(flags)

    if opening:

        @pl.when(is_ocean != 0)
        def _():
            base = d.strip
            pair = up_and_down(from_one[base : base + 16, :], from_two[base : base + 16, :])
            plan_x[...] = jnp.zeros_like(plan_x)
            for step, strip in zip((0, rows + 2), pair):
                for index in range(2):
                    plan_x[pl.ds(step + index, 2 * NK, stride=tall), :] = strip[index * 8 : (index + 1) * 8]

        for plane in range(2 * NK):
            plan_x[plane * tall + 2 : plane * tall + 2 + rows, :] = planes[plane].astype(F32)

    for field in range(NS):
        pair = up_and_down(field_one[field], field_two[field])
        fields_x[field, 0:16, :] = pair[0][rows - 16 : rows]
        fields_x[field, 16 : 16 + rows, :] = beside[field].astype(F32)
        fields_x[field, 16 + rows : 32 + rows, :] = pair[1][0:16]

    @pl.when(is_ocean == 0)
    def _():
        regrid_inside(fields_x, plan_x, part_x, 2, rows // 8, tall)

    @pl.when(is_ocean != 0)
    def _():
        regrid_inside(fields_x, plan_x, part_x, 0, d.tiles, tall)
        upper, lower = up_and_down(from_one[0 : 2 * CH, :], from_two[0 : 2 * CH, :])
        roll_rows(state, upper.astype(BF16), lower.astype(BF16), rolled, d)
        above, below = up_and_down(get_edges(from_one, 2 * CH, d), get_edges(from_two, 2 * CH, d))
        joined = join_rows(above.astype(BF16), get_edges(own_edges, 0, d), below.astype(BF16), d)
        put_edges(edges, 0, joined, d)

    if opening:
        prepare(*raw_weights, *made_weights, is_ocean)


def step_kernel(d, opening, closing, *refs):
    refs = list(refs)
    take = lambda count: [refs.pop(0) for _ in range(count)]
    flags, state, wet, from_left, from_right = take(5)
    part_x, fields_x, rolled, edges, plan_x, air_in, first, second, atm_out = take(9)
    if not opening:
        (plan_y,) = take(1)
    if not closing:
        (surface,) = take(1)
    (out,) = take(1)
    if not closing:
        fields, new_edges, one, two = take(4)
    if opening:
        (plan_y,) = take(1)
    fields_y, forcing_x, forcing_y, stack, hidden, side, raw = take(7)
    rows, tall = d.rows, d.tall
    is_ocean, at_top, at_bottom = flags[0], flags[1], flags[2]
    up_and_down = ends(flags)

    if opening:

        @pl.when(is_ocean != 0)
        def _():
            plan_y[...] = jnp.zeros_like(plan_y)
            side_base = 4 * (rows + 32) + 3 * d.edge_rows
            pair = [
                place_columns(from_left[at : at + 16, :], from_right[at : at + 16, :])
                for at in (side_base, side_base + 16 + 2 * NK * rows)
            ]
            for step, strip in zip((0, rows + 2), up_and_down(*pair)):
                for index in range(2):
                    plan_y[pl.ds(step + index, 2 * NK, stride=tall), :] = strip[index * 8 : (index + 1) * 8]
            for plane in range(2 * NK):
                at = side_base + 16 + plane * rows
                plan_y[plane * tall + 2 : plane * tall + 2 + rows, :] = place_columns(
                    from_left[at : at + rows, :], from_right[at : at + rows, :]
                )

    lower_at = 64 + 4 * rows
    for field in range(NS):
        start = 64 + field * rows
        fields_y[field, 16 : 16 + rows, :] = place_columns(
            from_left[start : start + rows, :], from_right[start : start + rows, :]
        )
        pair = [
            place_columns(from_left[at : at + 16, :], from_right[at : at + 16, :])
            for at in (field * 16, lower_at + field * 16)
        ]
        pair = up_and_down(*pair)
        fields_y[field, 0:16, :] = pair[0]
        fields_y[field, 16 + rows : 32 + rows, :] = pair[1]

    def put(row, values):
        if closing:
            raw[pl.ds(row, CH, stride=rows), :] = values
        else:
            out[row] = values.astype(BF16)

    @pl.when(is_ocean == 0)
    def _():
        regrid_beside(
            fields_x, fields_y, plan_x, plan_y, part_x, forcing_x, forcing_y, 2, rows // 8, tall, False
        )
        air(state, put, forcing_x, air_in, atm_out, d)

    @pl.when(is_ocean != 0)
    def _():
        regrid_beside(
            fields_x, fields_y, plan_x, plan_y, part_x, forcing_x, forcing_y, 0, d.tiles, tall, True
        )
        at = 4 * (rows + 32)
        size = d.edge_rows
        joined = []
        for ref in (from_left, from_right):
            one_edges, middle, two_edges = [get_edges(ref, at + index * size, d) for index in range(3)]
            above, below = up_and_down(one_edges, two_edges)
            joined.append(join_rows(above.astype(BF16), middle, below.astype(BF16), d))
        sea(
            state, rolled, get_edges(edges, 0, d), *joined, put, forcing_x, forcing_y,
            first, second, wet, at_top, at_bottom, stack, hidden, side, d,
        )

    if closing:
        out[...] = raw[...].reshape(CH, rows, 128).astype(BF16)
    else:
        emit(out, surface, wet, flags, fields, new_edges, one, two, raw, d)


VMEM = pl.BlockSpec(memory_space=pltpu.VMEM)
SMEM = pl.BlockSpec(memory_space=pltpu.SMEM)
PARAMS = pltpu.CompilerParams(vmem_limit_bytes=48 * 1024 * 1024)


def shape(*dims, dtype=BF16):
    return jax.ShapeDtypeStruct(dims, dtype)


def send(x, move):
    names = ("grp", "lat", "lon")
    sizes = [lax.axis_size(name) for name in names]
    pairs = []
    for group in range(sizes[0]):
        for lat in range(sizes[1]):
            for lon in range(sizes[2]):
                to = move(group, lat, lon)
                if to is None or not 0 <= to[1] < sizes[1]:
                    continue
                target = (to[0] * sizes[1] + to[1]) * sizes[2] + to[2] % sizes[2]
                pairs.append(((group * sizes[1] + lat) * sizes[2] + lon, target))
    return lax.ppermute(x, names, pairs)


def swap_rows(x, turn, across):
    count = lax.axis_size("lat")

    def move(group, lat, lon):
        other = ((lat + turn) ^ 1) - turn
        to = 1 - group if across else group
        return to, other if 0 <= other < count else lat, lon

    return send(x, move)


def exchange(fields, own_edges, one, two, planes, d):
    rows = d.rows
    beside = send(fields, lambda g, i, j: (1 - g, i, j))
    field_one = swap_rows(fields, 0, True)
    field_two = swap_rows(fields, 1, True)
    from_one = swap_rows(one, 0, False)
    from_two = swap_rows(two, 1, False)
    edge_at = slice(2 * CH, d.strip)
    odd = lax.axis_index("lat") % 2
    if rows == 16:
        outer = [field_one, field_two]
    else:
        last = [field[:, rows - 16 :] for field in (field_one, field_two)]
        first = [field[:, :16] for field in (field_one, field_two)]
        outer = [jnp.where(odd == 1, last[0], first[0]), jnp.where(odd == 1, first[1], last[1])]
    packed = [
        outer[0].reshape(64, 128),
        beside.reshape(4 * rows, 128),
        outer[1].reshape(64, 128),
        from_one[edge_at],
        own_edges,
        from_two[edge_at],
    ]
    if planes is not None:
        packed += [from_one[d.strip :], planes.reshape(2 * NK * rows, 128), from_two[d.strip :]]
    packed = jnp.concatenate(packed, axis=0)
    from_left = send(packed, lambda g, i, j: (g, i, j + 1))
    from_right = send(packed, lambda g, i, j: (g, i, j - 1))
    return (field_one, beside, field_two, from_one, from_two), (from_left, from_right)


def local(
    coupled_state, land_mask, regrid_offsets, regrid_weights, surface_proj,
    atm_in, atm_bias, atm_out, ocn_in, ocn_bias, ocn_out,
):
    rows = coupled_state.shape[2]
    assert coupled_state.shape[3] == 128
    d = Dims(rows)
    group = lax.axis_index("grp")
    lat = lax.axis_index("lat")
    flags = jnp.stack(
        [group, lat == 0, lat == lax.axis_size("lat") - 1, lat % 2]
    ).astype(jnp.int32)
    raw_weights = (
        atm_in.T,
        atm_bias[None],
        jnp.transpose(ocn_in, (1, 2, 0)),
        ocn_bias[None],
        jnp.transpose(ocn_out, (1, 0, 2)),
    )
    state_shape = shape(rows, CH, 128)
    emitted = [
        shape(NS, rows, 128),
        shape(d.edge_rows, 128),
        shape(d.strip, 128),
        shape(d.strip, 128),
    ]
    raw = pltpu.VMEM((rows * 8, 128), F32)
    turned = pltpu.VMEM((CH * rows, 128), F32)

    def call(kernel, operands, outs, scratch, name):
        return pl.pallas_call(
            kernel,
            out_shape=outs,
            in_specs=[SMEM] + [VMEM] * len(operands),
            out_specs=[VMEM] * len(outs),
            scratch_shapes=scratch,
            compiler_params=PARAMS,
            name=name,
        )(flags, *operands)

    state, planes, fields, edges, one, two = call(
        functools.partial(start_kernel, d),
        (coupled_state[0], regrid_offsets[0], regrid_weights[0], surface_proj, land_mask),
        [state_shape, shape(2 * NK, rows, 128)] + emitted[:2] + [shape(d.strip + 16, 128)] * 2,
        [raw, pltpu.VMEM((2 * NK * rows, 128), F32), turned],
        "start",
    )

    plan = shape(2 * NK * d.tall, 128, dtype=F32)
    between = [
        shape(NS * d.tall, 128, dtype=F32),
        shape(NS, rows + 32, 128, dtype=F32),
        shape(rows + 4, 3 * CH, 128),
        shape(d.edge_rows, 128),
    ]
    made = [shape(HA, 128), shape(HIDK, 768), shape(9 * CH, HIDP)]
    scratch = [
        pltpu.VMEM((NS, rows + 32, 128), F32),
        pltpu.VMEM((d.tall * 8, 128), F32),
        pltpu.VMEM((d.tall * 8, 128), F32),
        pltpu.VMEM((rows + 4, 256, 128), BF16),
        pltpu.VMEM((rows + 2, HIDP, 128), BF16),
        pltpu.VMEM((768, d.edge), BF16),
    ]

    vertical, horizontal = exchange(fields, edges, one, two, planes, d)
    *shared, plan_x, air_in, first, second = call(
        functools.partial(middle_kernel, d, True),
        (state, *vertical, edges, planes, *raw_weights),
        between + [plan] + made,
        [],
        "first_middle",
    )
    weights = (air_in, first, second, atm_out)
    state, fields, edges, one, two, plan_y = call(
        functools.partial(step_kernel, d, True, False),
        (state, land_mask, *horizontal, *shared, plan_x, *weights, surface_proj),
        [state_shape] + emitted + [plan],
        scratch + [raw],
        "first_step",
    )

    vertical, horizontal = exchange(fields, edges, one, two, None, d)
    shared = call(
        functools.partial(middle_kernel, d, False),
        (state, *vertical, edges, plan_x),
        between,
        [],
        "second_middle",
    )
    (state,) = call(
        functools.partial(step_kernel, d, False, True),
        (state, land_mask, *horizontal, *shared, plan_x, *weights, plan_y),
        [shape(CH, rows, 128)],
        scratch + [turned],
        "second_step",
    )
    return state[None]


def solution(mesh):
    return jax.shard_map(
        local,
        mesh=mesh,
        in_specs=(
            P("grp", None, "lat", "lon"),
            P("lat", "lon"),
            P("grp", None, None, "lat", "lon"),
            P("grp", None, "lat", "lon"),
            P(),
            P(),
            P(),
            P(),
            P(),
            P(),
            P(),
        ),
        out_specs=P("grp", None, "lat", "lon"),
        check_vma=False,
    )
```

```python
import functools

import jax
import jax.numpy as jnp
from jax import lax
from jax.experimental import pallas as pl
from jax.experimental.pallas import tpu as pltpu
from jax.sharding import PartitionSpec as P

CH = 80
NS = 4
NK = 4
HA = 384
HW = 8
SPAN = 2 * HW + 1
HIDK = 208
HIDP = 256
F32 = jnp.float32
BF16 = jnp.bfloat16


def roll(x, shift, axis=1):
    size = x.shape[axis]
    if isinstance(shift, int):
        shift = shift % size
        if shift == 0:
            return x
    return pltpu.roll(x, shift, axis)


def lanes(shape):
    return lax.broadcasted_iota(jnp.int32, shape, len(shape) - 1)


def subs(shape):
    return lax.broadcasted_iota(jnp.int32, shape, len(shape) - 2)


class Dims:
    def __init__(self, rows):
        self.rows = rows
        self.block = 32 if rows + 4 <= 32 else 64
        self.edge = 4 * self.block
        self.pieces = self.edge // 128
        self.edge_rows = CH * self.pieces
        self.tiles = -(-(rows + 4) // 8)
        self.tall = 8 * self.tiles
        self.strip = 2 * CH + self.edge_rows


def put_edges(ref, at, edges, d):
    for piece in range(d.pieces):
        ref[at + piece * CH : at + (piece + 1) * CH, :] = edges[:, piece * 128 : (piece + 1) * 128]


def get_edges(ref, at, d):
    return jnp.concatenate(
        [ref[at + piece * CH : at + (piece + 1) * CH, :] for piece in range(d.pieces)], axis=1
    )


def edge_columns(state, d):
    lane = lanes((1, d.edge))
    block = lane // d.block
    row = lane % d.block - 2
    column = jnp.where(block == 0, 126, jnp.where(block == 1, 0, jnp.where(block == 2, 127, 1)))
    own = (row >= 0) & (row < d.rows)
    target = jnp.where(own, column, -1)
    position = subs((128, d.edge))
    places = [
        (position == jnp.where(row == step, target, -1)).astype(F32).astype(BF16)
        for step in range(d.rows)
    ]
    whole = jnp.concatenate([state[step] for step in range(d.rows)], axis=1)
    total = jnp.dot(whole, jnp.concatenate(places, axis=0), preferred_element_type=F32)
    return total.astype(BF16)


def loop(count, unroll, body):
    while count % unroll:
        unroll -= 1

    def several(step, carry):
        for offset in range(unroll):
            body(step * unroll + offset)
        return carry

    lax.fori_loop(0, count // unroll, several, 0)


def strips(one, two, even, d):
    last = d.rows - 2
    return (one, jnp.where(even, last, 0)), (two, jnp.where(even, 0, last))


def split_bf16(values):
    high = values.astype(BF16).astype(F32)
    mid = (values - high).astype(BF16).astype(F32)
    return high, mid, values - high - mid


def emit(state, surface, wet, flags, fields, own_edges, one, two, raw, d):
    half = d.rows // 2
    is_ocean, even = flags[0] != 0, flags[3] == 0
    gap = jnp.zeros((4, CH), F32)
    terms = []
    for term in split_bf16(surface[flags[0]]):
        terms += [term, gap]
    proj = jnp.concatenate(terms + [gap, gap], axis=0).astype(BF16)
    for step in range(half):
        pair = jnp.concatenate([state[step], state[step + half]], axis=1)
        parts = jnp.dot(proj, pair, preferred_element_type=F32)
        whole = parts[0:8] + parts[8:16] + parts[16:24]
        raw[step * 8 : step * 8 + 8, :] = whole[:, :128]
        raw[(step + half) * 8 : (step + half) * 8 + 8, :] = whole[:, 128:]
    keeping = jnp.where(is_ocean, wet[...].astype(F32), 1.0)
    for field in range(NS):
        fields[field] = (raw[pl.ds(field, d.rows, stride=8), :] * keeping).astype(BF16)
    edges = edge_columns(state, d)
    put_edges(own_edges, 0, edges, d)
    for ref, first in strips(one, two, even, d):
        ref[0:CH, :] = state[first]
        ref[CH : 2 * CH, :] = state[first + 1]
        put_edges(ref, 2 * CH, edges, d)


def fetch(sources, targets, sems):
    copies = [
        pltpu.make_async_copy(source, target, sems.at[index])
        for index, (source, target) in enumerate(zip(sources, targets))
    ]
    for copy in copies:
        copy.start()
    return copies


def start_kernel(
    d, flags, far_given, far_surface, far_wet, far_offsets, far_weights,
    state, planes, fields, own_edges, one, two,
    raw, tall, turned, given, surface, wet, offsets, weights, sems,
):
    rows = d.rows
    copies = fetch(
        (far_given, far_surface, far_wet, far_offsets, far_weights),
        (given, surface, wet, offsets, weights),
        sems,
    )
    copies[0].wait()
    turned[...] = given[...].astype(F32).reshape(CH * rows, 128)
    for row in range(rows):
        state[row] = turned[pl.ds(row, CH, stride=rows), :].astype(BF16)
    for copy in copies[1:]:
        copy.wait()
    emit(state, surface, wet, flags, fields, own_edges, one, two, raw, d)
    for k in range(NK):
        code = (offsets[0, k] * SPAN + offsets[1, k]).astype(F32)
        tall[k * rows : (k + 1) * rows, :] = code
        tall[(NK + k) * rows : (NK + k + 1) * rows, :] = weights[k]
        planes[k] = code.astype(BF16)
        planes[NK + k] = weights[k].astype(BF16)
    for ref, first in strips(one, two, flags[3] == 0, d):
        strip = [tall[pl.ds(first + step, 2 * NK, stride=rows), :] for step in range(2)]
        ref[d.strip : d.strip + 16, :] = jnp.concatenate(strip, axis=0).astype(BF16)


def decode(code):
    shifted = code.astype(jnp.int32) + (HW * SPAN + HW)
    rows = lax.shift_right_logical(shifted * 241, 12)
    return rows - HW, shifted - rows * SPAN - HW


def along_lanes(values, index):
    numbers = lax.GatherDimensionNumbers(
        offset_dims=(),
        collapsed_slice_dims=(1,),
        start_index_map=(1,),
        operand_batching_dims=(0,),
        start_indices_batching_dims=(0,),
    )
    return lax.gather(
        values, index[..., None], numbers, (1, 1), mode=lax.GatherScatterMode.PROMISE_IN_BOUNDS
    )


def select_rows(sources, start, picks):
    chosen = [[jnp.zeros((8, 128), F32) for _ in range(NS)] for _ in picks]
    for shift in range(-HW, HW + 1):
        at = pl.ds(start + shift, 8)
        used = [any(pick[2][index] is not None for pick in picks) for index in range(len(sources))]
        values = [
            [source[field, at, :] for field in range(NS)] if use else None
            for source, use in zip(sources, used)
        ]
        for slot, (rows, index, allowed) in enumerate(picks):
            here = rows == shift
            for source, within in enumerate(allowed):
                if within is None:
                    continue
                mask = here & within
                for field in range(NS):
                    picked = along_lanes(values[source][field], index)
                    chosen[slot][field] = jnp.where(mask, picked, chosen[slot][field])
    return chosen


def regrid_inside(fields_x, plan_x, part_x, first, tiles, tall):
    lane = lanes((8, 128))
    for step in range(tiles):
        at = first + step * 8
        picks = []
        weights = []
        for k in range(NK):
            rows, cols = decode(plan_x[pl.ds(k * tall + at, 8), :])
            weights.append(plan_x[pl.ds((NK + k) * tall + at, 8), :])
            column = lane + cols
            picks.append((rows, column & 127, ((column >= 0) & (column < 128),)))
        chosen = select_rows((fields_x,), at + 14, picks)
        for field in range(NS):
            total = chosen[0][field] * weights[0]
            for k in range(1, NK):
                total = total + chosen[k][field] * weights[k]
            part_x[pl.ds(field * tall + at, 8), :] = total


def regrid_beside(
    fields_x, fields_y, plan_x, plan_y, part_x, forcing_x, forcing_y, first, tiles, tall, sides
):
    lane = lanes((8, 128))
    part = ((lane + 8) & 127) // 32
    place = ((lane + 8) & 31) - 8
    outer = place >= 8
    inner_column = place & 127
    outer_column = jnp.where(place < 16, place - 16, place + 112)
    edge = (lane < 8) | (lane >= 120)
    for step in range(tiles):
        at = first + step * 8
        code = jnp.zeros((8, 128), F32)
        weight = jnp.zeros((8, 128), F32)
        for k in range(NK):
            edge_code = roll(plan_x[pl.ds(k * tall + at, 8), :], 32 * k)
            edge_weight = roll(plan_x[pl.ds((NK + k) * tall + at, 8), :], 32 * k)
            if sides:
                edge_code = jnp.where(
                    outer, roll(plan_y[pl.ds(k * tall + at, 8), :], 32 * k + 16), edge_code
                )
                edge_weight = jnp.where(
                    outer, roll(plan_y[pl.ds((NK + k) * tall + at, 8), :], 32 * k + 16), edge_weight
                )
            code = jnp.where(part == k, edge_code, code)
            weight = jnp.where(part == k, edge_weight, weight)
        rows, cols = decode(code)
        column = jnp.where(outer, outer_column, inner_column) + cols
        within = (column >= 0) & (column < 128)
        picks = [(rows, column & 127, (within & outer if sides else None, jnp.logical_not(within)))]
        (chosen,) = select_rows((fields_x, fields_y), at + 14, picks)
        for field in range(NS):
            part_sum = chosen[field] * weight
            extra = part_sum
            for k in range(1, NK):
                extra = extra + roll(part_sum, -32 * k)
            total = part_x[pl.ds(field * tall + at, 8), :] + jnp.where(edge, extra, 0.0)
            forcing_x[pl.ds(at * 8 + field, 8, stride=8), :] = total
            forcing_x[pl.ds(at * 8 + field + 4, 8, stride=8), :] = total
            if sides:
                extra = roll(extra, -16)
                forcing_y[pl.ds(at * 8 + field, 8, stride=8), :] = extra
                forcing_y[pl.ds(at * 8 + field + 4, 8, stride=8), :] = extra


def place_columns(left, right):
    return jnp.where(lanes(left.shape) < 64, right.astype(F32), left.astype(F32))


def gelu(x):
    scale = (2 / jnp.pi) ** 0.5
    half = 0.5 * x
    return half + half * jnp.tanh(x * (scale + (scale * 0.044715) * (x * x)))


def air(state, out, forcing_x, air_in, atm_out, d):
    half = d.rows // 2
    first = subs((8, 128)) < 4
    blank = jnp.zeros((32, 128), BF16)

    def inputs(row):
        at = (row + 2) * 8
        forced = jnp.where(first, forcing_x[at : at + 8, :], 1.0)
        forced = jnp.concatenate([forced, jnp.zeros_like(forced)], axis=0).astype(BF16)
        return jnp.concatenate([state[row], forced, blank], axis=0)

    for step in range(half):
        pair = jnp.concatenate([inputs(step), inputs(step + half)], axis=1)
        hidden = gelu(jnp.dot(air_in[...], pair, preferred_element_type=F32)).astype(BF16)
        update = jnp.dot(atm_out[...], hidden, preferred_element_type=F32)
        for offset in range(2):
            row = step + offset * half
            change = update[:, offset * 128 : (offset + 1) * 128]
            out(row, state[row].astype(F32) + change)


def edge_forcing(forcing_x, forcing_y, d):
    lane = lanes((8, d.edge))
    block = lane // d.block
    row = lane % d.block

    inner = outer = jnp.zeros((8, d.edge), F32)
    for step in range(d.rows + 4):
        at = pl.ds(step * 8, 8)
        pad = [jnp.zeros((8, 128), F32)] * (d.pieces - 1)
        here = jnp.concatenate([forcing_x[at, :]] + pad, axis=1)
        there = jnp.concatenate([forcing_y[at, :]] + pad, axis=1)
        for index, column in enumerate((126, 0, 127, 1)):
            shift = step + index * d.block - column
            match = (block == index) & (row == step)
            if column in (0, 127):
                inner = jnp.where(match, roll(here, shift), inner)
            outer = jnp.where(match, roll(there, shift), outer)
    return inner, outer


def roll_rows(state, upper, lower, rolled, d):
    def put(row, values):
        rolled[row, 0:CH, :] = roll(values, 1)
        rolled[row, CH : 2 * CH, :] = values
        rolled[row, 2 * CH : 3 * CH, :] = roll(values, -1)

    for step in range(2):
        put(step, upper[step * CH : (step + 1) * CH, :])
        put(d.rows + 2 + step, lower[step * CH : (step + 1) * CH, :])
    for row in range(d.rows):
        put(row + 2, state[row])


def sea(
    state, rolled, edges, left, right, out, forcing_x, forcing_y, ocn_in, ocn_out, wet,
    at_top, at_bottom, stack, hidden, side, d,
):
    rows, block = d.rows, d.block
    lane = lanes((CH, 128))
    spot = lanes((CH, d.edge))
    part = spot // block
    inner = edges
    outer = jnp.where((part == 0) | (part == 2), left, right)

    def sides_of(inner, outer, spot):
        first = spot < block
        return (
            jnp.where(first, outer, roll(inner, -block)),
            jnp.where(first, roll(outer, -2 * block), outer),
            jnp.where(first, roll(inner, -block), roll(outer, -2 * block)),
        )

    beside = sides_of(inner, outer, spot)
    middle = beside[1]
    force_in, force_out = edge_forcing(forcing_x, forcing_y, d)
    beside_forcing = sides_of(force_in, force_out, lanes((8, d.edge)))
    sub = subs((8, d.edge))
    ones = jnp.ones((8, d.edge), F32)
    forced = jnp.concatenate(
        [
            jnp.where(sub < 4, beside_forcing[0], beside_forcing[1]),
            jnp.where(sub < 4, beside_forcing[2], ones),
        ],
        axis=0,
    ).astype(BF16)
    columns = jnp.concatenate(list(beside) + [forced], axis=0)
    for tap in range(3):
        side[tap * 256 : (tap + 1) * 256, :] = roll(columns, -tap)

    sub_row = subs((8, 128))
    lane_row = lanes((8, 128))

    for row in range(rows + 4):
        entry = roll(middle, -row)[:, :128]
        stack[row, 0:CH, :] = jnp.where(lane == 0, entry, rolled[row, 0:CH, :])
        stack[row, CH : 2 * CH, :] = rolled[row, CH : 2 * CH, :]
        entry = roll(middle, 127 - block - row)[:, :128]
        stack[row, 2 * CH : 3 * CH, :] = jnp.where(lane == 127, entry, rolled[row, 2 * CH : 3 * CH, :])
        here, there = forcing_x[row * 8 : row * 8 + 8, :], forcing_y[row * 8 : row * 8 + 8, :]
        before = roll(jnp.where(lane_row == 127, there, here), 1)
        after = roll(jnp.where(lane_row == 0, there, here), -1)
        stack[row, 3 * CH : 256, :] = jnp.concatenate(
            [jnp.where(sub_row < 4, before, here), jnp.where(sub_row < 4, after, 1.0)], axis=0
        ).astype(BF16)

    pairs = (rows + 2) // 2

    for step in range(pairs):
        taps = jnp.concatenate(
            [
                stack[step : step + 3].reshape(3 * 256, 128),
                stack[step + pairs : step + pairs + 3].reshape(3 * 256, 128),
            ],
            axis=1,
        )
        active = gelu(jnp.dot(ocn_in[...], taps, preferred_element_type=F32))
        low, high = active[:, :128], active[:, 128:]
        if step == 0:
            low = jnp.where(at_top != 0, 0.0, low)
        if step == pairs - 1:
            high = jnp.where(at_bottom != 0, 0.0, high)
        hidden[step, 0:HIDK, :] = low.astype(BF16)
        hidden[step + pairs, 0:HIDK, :] = high.astype(BF16)
        blank = jnp.zeros((HIDP - HIDK, 128), BF16)
        hidden[step, HIDK:HIDP, :] = blank
        hidden[step + pairs, HIDK:HIDP, :] = blank

    product = jnp.dot(ocn_in[...], side[...], preferred_element_type=F32)
    spot = lanes((1, d.edge)) % block
    gone = ((spot == 0) & (at_top != 0)) | ((spot == rows + 1) & (at_bottom != 0))
    active = jnp.where(gone, 0.0, gelu(product)).astype(BF16)
    active = jnp.concatenate([active, jnp.zeros((HIDP - HIDK, d.edge), BF16)], axis=0)

    def taps_of(slices):
        total = None
        for tap, values in enumerate(slices):
            weights = ocn_out[tap * 3 * CH : (tap + 1) * 3 * CH, :]
            product = jnp.dot(weights, values, preferred_element_type=F32)
            total = product if total is None else total + product
        return total

    partial = taps_of([roll(active, -tap) for tap in range(3)])
    from_left, from_right = partial[0:CH], partial[2 * CH : 3 * CH]
    half = rows // 2
    for step in range(half):
        product = taps_of(
            [
                jnp.concatenate([hidden[step + tap], hidden[step + half + tap]], axis=1)
                for tap in range(3)
            ]
        )
        for offset in range(2):
            row = step + offset * half
            sums = product[:, offset * 128 : (offset + 1) * 128]
            entry = roll(from_left, -row)[:, :128]
            total = sums[CH : 2 * CH] + jnp.where(lane == 0, entry, roll(sums[0:CH], 1))
            entry = roll(from_right, 127 - block - row)[:, :128]
            total = total + jnp.where(lane == 127, entry, roll(sums[2 * CH : 3 * CH], -1))
            update = total * wet[row : row + 1, :].astype(F32)
            out(row, state[row].astype(F32) + update)


def join_rows(edge_up, edge_own, edge_down, d):
    row = lanes(edge_own.shape) % d.block
    above = roll(edge_up, -d.rows)
    below = roll(edge_down, d.rows)
    return jnp.where(row < 2, above, jnp.where(row < d.rows + 2, edge_own, below))


def prepare(atm_in, atm_bias, ocn_in, ocn_bias, ocn_out, air_in, first, second, is_ocean):
    def bias_rows(ref, width):
        row = jnp.concatenate([ref[index : index + 1, :] for index in range(ref.shape[0])], axis=1)
        terms = list(split_bf16(row)) + [jnp.zeros_like(row)]
        bias = jnp.concatenate(terms, axis=0)
        return jnp.pad(bias, ((0, 0), (0, width - bias.shape[1])))

    @pl.when(is_ocean == 0)
    def _():
        columns = jnp.concatenate(
            [atm_in[...].astype(F32), bias_rows(atm_bias, HA), jnp.zeros((40, HA), F32)], axis=0
        )
        air_in[...] = columns.T.astype(BF16)

    @pl.when(is_ocean != 0)
    def _():
        bias = bias_rows(ocn_bias, 256)
        count = ocn_in.shape[2]
        for tap in range(3):
            whole = [ocn_in[3 * tap + side].astype(F32) for side in range(3)]
            whole = [jnp.pad(values, ((0, 0), (0, 256 - count))) for values in whole]
            rows = [values[:CH] for values in whole] + [values[CH:] for values in whole]
            rows.append(bias if tap == 0 else jnp.zeros((4, 256), F32))
            columns = jnp.concatenate(rows, axis=0).T
            first[:, tap * 256 : (tap + 1) * 256] = columns[:HIDK].astype(BF16)
        for tap in range(9):
            values = ocn_out[tap].astype(F32)
            second[tap * CH : (tap + 1) * CH, :] = jnp.pad(
                values, ((0, 0), (0, HIDP - count))
            ).astype(BF16)


def ends(flags):
    at_top, at_bottom, even = flags[1] != 0, flags[2] != 0, flags[3] == 0

    def up_and_down(one, two):
        above = jnp.where(even, two, one).astype(F32)
        below = jnp.where(even, one, two).astype(F32)
        return jnp.where(at_top, 0.0, above), jnp.where(at_bottom, 0.0, below)

    return up_and_down


def middle_kernel(d, opening, *refs):
    refs = list(refs)
    take = lambda count: [refs.pop(0) for _ in range(count)]
    flags, state, field_one, beside, field_two, from_one, from_two, own_edges = take(8)
    if opening:
        planes, *far_weights = take(6)
    else:
        (plan_x,) = take(1)
    part_x, fields_x, rolled, edges = take(4)
    if opening:
        plan_x, *made_weights = take(4)
        *raw_weights, sems = take(6)
        copies = fetch(far_weights, raw_weights, sems)
    rows, tall = d.rows, d.tall
    is_ocean = flags[0]
    up_and_down = ends(flags)

    if opening:

        @pl.when(is_ocean != 0)
        def _():
            base = d.strip
            pair = up_and_down(from_one[base : base + 16, :], from_two[base : base + 16, :])
            plan_x[...] = jnp.zeros_like(plan_x)
            for step, strip in zip((0, rows + 2), pair):
                for index in range(2):
                    plan_x[pl.ds(step + index, 2 * NK, stride=tall), :] = strip[index * 8 : (index + 1) * 8]

        for plane in range(2 * NK):
            plan_x[plane * tall + 2 : plane * tall + 2 + rows, :] = planes[plane].astype(F32)

    for field in range(NS):
        pair = up_and_down(field_one[field], field_two[field])
        fields_x[field, 0:16, :] = pair[0][rows - 16 : rows]
        fields_x[field, 16 : 16 + rows, :] = beside[field].astype(F32)
        fields_x[field, 16 + rows : 32 + rows, :] = pair[1][0:16]

    @pl.when(is_ocean == 0)
    def _():
        regrid_inside(fields_x, plan_x, part_x, 2, rows // 8, tall)

    @pl.when(is_ocean != 0)
    def _():
        regrid_inside(fields_x, plan_x, part_x, 0, d.tiles, tall)
        upper, lower = up_and_down(from_one[0 : 2 * CH, :], from_two[0 : 2 * CH, :])
        roll_rows(state, upper.astype(BF16), lower.astype(BF16), rolled, d)
        above, below = up_and_down(get_edges(from_one, 2 * CH, d), get_edges(from_two, 2 * CH, d))
        joined = join_rows(above.astype(BF16), get_edges(own_edges, 0, d), below.astype(BF16), d)
        put_edges(edges, 0, joined, d)

    if opening:
        for copy in copies:
            copy.wait()
        prepare(*raw_weights, *made_weights, is_ocean)


def step_kernel(d, opening, closing, *refs):
    refs = list(refs)
    take = lambda count: [refs.pop(0) for _ in range(count)]
    flags, state, wet, from_left, from_right = take(5)
    part_x, fields_x, rolled, edges, plan_x, air_in, first, second, atm_out = take(9)
    if not opening:
        (plan_y,) = take(1)
    if not closing:
        (surface,) = take(1)
    (out,) = take(1)
    if not closing:
        fields, new_edges, one, two = take(4)
    if opening:
        (plan_y,) = take(1)
    fields_y, forcing_x, forcing_y, stack, hidden, side, raw = take(7)
    rows, tall = d.rows, d.tall
    is_ocean, at_top, at_bottom = flags[0], flags[1], flags[2]
    up_and_down = ends(flags)

    if opening:

        @pl.when(is_ocean != 0)
        def _():
            plan_y[...] = jnp.zeros_like(plan_y)
            side_base = 4 * (rows + 32) + 3 * d.edge_rows
            pair = [
                place_columns(from_left[at : at + 16, :], from_right[at : at + 16, :])
                for at in (side_base, side_base + 16 + 2 * NK * rows)
            ]
            for step, strip in zip((0, rows + 2), up_and_down(*pair)):
                for index in range(2):
                    plan_y[pl.ds(step + index, 2 * NK, stride=tall), :] = strip[index * 8 : (index + 1) * 8]
            for plane in range(2 * NK):
                at = side_base + 16 + plane * rows
                plan_y[plane * tall + 2 : plane * tall + 2 + rows, :] = place_columns(
                    from_left[at : at + rows, :], from_right[at : at + rows, :]
                )

    lower_at = 64 + 4 * rows
    for field in range(NS):
        start = 64 + field * rows
        fields_y[field, 16 : 16 + rows, :] = place_columns(
            from_left[start : start + rows, :], from_right[start : start + rows, :]
        )
        pair = [
            place_columns(from_left[at : at + 16, :], from_right[at : at + 16, :])
            for at in (field * 16, lower_at + field * 16)
        ]
        pair = up_and_down(*pair)
        fields_y[field, 0:16, :] = pair[0]
        fields_y[field, 16 + rows : 32 + rows, :] = pair[1]

    def put(row, values):
        if closing:
            raw[pl.ds(row, CH, stride=rows), :] = values
        else:
            out[row] = values.astype(BF16)

    @pl.when(is_ocean == 0)
    def _():
        regrid_beside(
            fields_x, fields_y, plan_x, plan_y, part_x, forcing_x, forcing_y, 2, rows // 8, tall, False
        )
        air(state, put, forcing_x, air_in, atm_out, d)

    @pl.when(is_ocean != 0)
    def _():
        regrid_beside(
            fields_x, fields_y, plan_x, plan_y, part_x, forcing_x, forcing_y, 0, d.tiles, tall, True
        )
        at = 4 * (rows + 32)
        size = d.edge_rows
        joined = []
        for ref in (from_left, from_right):
            one_edges, middle, two_edges = [get_edges(ref, at + index * size, d) for index in range(3)]
            above, below = up_and_down(one_edges, two_edges)
            joined.append(join_rows(above.astype(BF16), middle, below.astype(BF16), d))
        sea(
            state, rolled, get_edges(edges, 0, d), *joined, put, forcing_x, forcing_y,
            first, second, wet, at_top, at_bottom, stack, hidden, side, d,
        )

    if closing:
        out[...] = raw[...].reshape(CH, rows, 128).astype(BF16)
    else:
        emit(out, surface, wet, flags, fields, new_edges, one, two, raw, d)


VMEM = pl.BlockSpec(memory_space=pltpu.VMEM)
HBM = pl.BlockSpec(memory_space=pltpu.HBM)
SMEM = pl.BlockSpec(memory_space=pltpu.SMEM)
PARAMS = pltpu.CompilerParams(vmem_limit_bytes=48 * 1024 * 1024)


def shape(*dims, dtype=BF16):
    return jax.ShapeDtypeStruct(dims, dtype)


def send(x, move):
    names = ("grp", "lat", "lon")
    sizes = [lax.axis_size(name) for name in names]
    pairs = []
    for group in range(sizes[0]):
        for lat in range(sizes[1]):
            for lon in range(sizes[2]):
                to = move(group, lat, lon)
                if to is None or not 0 <= to[1] < sizes[1]:
                    continue
                target = (to[0] * sizes[1] + to[1]) * sizes[2] + to[2] % sizes[2]
                pairs.append(((group * sizes[1] + lat) * sizes[2] + lon, target))
    return lax.ppermute(x, names, pairs)


def swap_rows(x, turn, across):
    count = lax.axis_size("lat")

    def move(group, lat, lon):
        other = ((lat + turn) ^ 1) - turn
        to = 1 - group if across else group
        return to, other if 0 <= other < count else lat, lon

    return send(x, move)


def exchange(fields, own_edges, one, two, planes, d):
    rows = d.rows
    beside = send(fields, lambda g, i, j: (1 - g, i, j))
    field_one = swap_rows(fields, 0, True)
    field_two = swap_rows(fields, 1, True)
    from_one = swap_rows(one, 0, False)
    from_two = swap_rows(two, 1, False)
    edge_at = slice(2 * CH, d.strip)
    odd = lax.axis_index("lat") % 2
    if rows == 16:
        outer = [field_one, field_two]
    else:
        last = [field[:, rows - 16 :] for field in (field_one, field_two)]
        first = [field[:, :16] for field in (field_one, field_two)]
        outer = [jnp.where(odd == 1, last[0], first[0]), jnp.where(odd == 1, first[1], last[1])]
    packed = [
        outer[0].reshape(64, 128),
        beside.reshape(4 * rows, 128),
        outer[1].reshape(64, 128),
        from_one[edge_at],
        own_edges,
        from_two[edge_at],
    ]
    if planes is not None:
        packed += [from_one[d.strip :], planes.reshape(2 * NK * rows, 128), from_two[d.strip :]]
    packed = jnp.concatenate(packed, axis=0)
    from_left = send(packed, lambda g, i, j: (g, i, j + 1))
    from_right = send(packed, lambda g, i, j: (g, i, j - 1))
    return (field_one, beside, field_two, from_one, from_two), (from_left, from_right)


def local(
    coupled_state, land_mask, regrid_offsets, regrid_weights, surface_proj,
    atm_in, atm_bias, atm_out, ocn_in, ocn_bias, ocn_out,
):
    rows = coupled_state.shape[2]
    assert coupled_state.shape[3] == 128
    d = Dims(rows)
    group = lax.axis_index("grp")
    lat = lax.axis_index("lat")
    flags = jnp.stack(
        [group, lat == 0, lat == lax.axis_size("lat") - 1, lat % 2]
    ).astype(jnp.int32)
    raw_weights = (
        atm_in.T,
        atm_bias.reshape(HA // 128, 128),
        jnp.transpose(ocn_in, (1, 2, 0)),
        ocn_bias[None],
        jnp.transpose(ocn_out, (1, 0, 2)),
    )
    state_shape = shape(rows, CH, 128)
    emitted = [
        shape(NS, rows, 128),
        shape(d.edge_rows, 128),
        shape(d.strip, 128),
        shape(d.strip, 128),
    ]
    raw = pltpu.VMEM((rows * 8, 128), F32)
    turned = pltpu.VMEM((CH * rows, 128), F32)

    def call(kernel, operands, outs, scratch, name, far=()):
        scratch = scratch + [pltpu.VMEM(x.shape, x.dtype) for x in far]
        if far:
            scratch.append(pltpu.SemaphoreType.DMA((len(far),)))

        far = [pltpu.with_memory_space_constraint(x, pltpu.HBM) for x in far]
        return pl.pallas_call(
            kernel,
            out_shape=outs,
            in_specs=[SMEM] + [VMEM] * len(operands) + [HBM] * len(far),
            out_specs=[VMEM] * len(outs),
            scratch_shapes=scratch,
            compiler_params=PARAMS,
            name=name,
        )(flags, *operands, *far)

    state, planes, fields, edges, one, two = call(
        functools.partial(start_kernel, d),
        (),
        [state_shape, shape(2 * NK, rows, 128)] + emitted[:2] + [shape(d.strip + 16, 128)] * 2,
        [raw, pltpu.VMEM((2 * NK * rows, 128), F32), turned],
        "start",
        (coupled_state[0], surface_proj, land_mask, regrid_offsets[0], regrid_weights[0]),
    )

    plan = shape(2 * NK * d.tall, 128, dtype=F32)
    between = [
        shape(NS * d.tall, 128, dtype=F32),
        shape(NS, rows + 32, 128, dtype=F32),
        shape(rows + 4, 3 * CH, 128),
        shape(d.edge_rows, 128),
    ]
    made = [shape(HA, 128), shape(HIDK, 768), shape(9 * CH, HIDP)]
    scratch = [
        pltpu.VMEM((NS, rows + 32, 128), F32),
        pltpu.VMEM((d.tall * 8, 128), F32),
        pltpu.VMEM((d.tall * 8, 128), F32),
        pltpu.VMEM((rows + 4, 256, 128), BF16),
        pltpu.VMEM((rows + 2, HIDP, 128), BF16),
        pltpu.VMEM((768, d.edge), BF16),
    ]

    vertical, horizontal = exchange(fields, edges, one, two, planes, d)
    *shared, plan_x, air_in, first, second = call(
        functools.partial(middle_kernel, d, True),
        (state, *vertical, edges, planes),
        between + [plan] + made,
        [],
        "first_middle",
        raw_weights,
    )
    weights = (air_in, first, second, atm_out)
    state, fields, edges, one, two, plan_y = call(
        functools.partial(step_kernel, d, True, False),
        (state, land_mask, *horizontal, *shared, plan_x, *weights, surface_proj),
        [state_shape] + emitted + [plan],
        scratch + [raw],
        "first_step",
    )

    vertical, horizontal = exchange(fields, edges, one, two, None, d)
    shared = call(
        functools.partial(middle_kernel, d, False),
        (state, *vertical, edges, plan_x),
        between,
        [],
        "second_middle",
    )
    (state,) = call(
        functools.partial(step_kernel, d, False, True),
        (state, land_mask, *horizontal, *shared, plan_x, *weights, plan_y),
        [shape(CH, rows, 128)],
        scratch + [turned],
        "second_step",
    )
    return state[None]


def solution(mesh):
    return jax.shard_map(
        local,
        mesh=mesh,
        in_specs=(
            P("grp", None, "lat", "lon"),
            P("lat", "lon"),
            P("grp", None, None, "lat", "lon"),
            P("grp", None, "lat", "lon"),
            P(),
            P(),
            P(),
            P(),
            P(),
            P(),
            P(),
        ),
        out_specs=P("grp", None, "lat", "lon"),
        check_vma=False,
    )
```

```python
import functools

import jax
import jax.numpy as jnp
from jax import lax
from jax.experimental import pallas as pl
from jax.experimental.pallas import tpu as pltpu
from jax.sharding import PartitionSpec as P

CH = 80
NS = 4
NK = 4
HA = 384
HW = 8
SPAN = 2 * HW + 1
HIDK = 208
HIDP = 256
F32 = jnp.float32
BF16 = jnp.bfloat16


def roll(x, shift, axis=1):
    size = x.shape[axis]
    if isinstance(shift, int):
        shift = shift % size
        if shift == 0:
            return x
    return pltpu.roll(x, shift, axis)


def lanes(shape):
    return lax.broadcasted_iota(jnp.int32, shape, len(shape) - 1)


def subs(shape):
    return lax.broadcasted_iota(jnp.int32, shape, len(shape) - 2)


class Dims:
    def __init__(self, rows):
        self.rows = rows
        self.block = 32 if rows + 4 <= 32 else 64
        self.edge = 4 * self.block
        self.pieces = self.edge // 128
        self.edge_rows = CH * self.pieces
        self.tiles = -(-(rows + 4) // 8)
        self.tall = 8 * self.tiles
        self.strip = 2 * CH + self.edge_rows


def put_edges(ref, at, edges, d):
    for piece in range(d.pieces):
        ref[at + piece * CH : at + (piece + 1) * CH, :] = edges[:, piece * 128 : (piece + 1) * 128]


def get_edges(ref, at, d):
    return jnp.concatenate(
        [ref[at + piece * CH : at + (piece + 1) * CH, :] for piece in range(d.pieces)], axis=1
    )


def edge_columns(state, d):
    lane = lanes((1, d.edge))
    block = lane // d.block
    row = lane % d.block - 2
    column = jnp.where(block == 0, 126, jnp.where(block == 1, 0, jnp.where(block == 2, 127, 1)))
    own = (row >= 0) & (row < d.rows)
    target = jnp.where(own, column, -1)
    position = subs((128, d.edge))
    places = [
        (position == jnp.where(row == step, target, -1)).astype(F32).astype(BF16)
        for step in range(d.rows)
    ]
    whole = jnp.concatenate([state[step] for step in range(d.rows)], axis=1)
    total = jnp.dot(whole, jnp.concatenate(places, axis=0), preferred_element_type=F32)
    return total.astype(BF16)


def loop(count, unroll, body):
    while count % unroll:
        unroll -= 1

    def several(step, carry):
        for offset in range(unroll):
            body(step * unroll + offset)
        return carry

    lax.fori_loop(0, count // unroll, several, 0)


def strips(one, two, even, d):
    last = d.rows - 2
    return (one, jnp.where(even, last, 0)), (two, jnp.where(even, 0, last))


def split_bf16(values):
    high = values.astype(BF16).astype(F32)
    mid = (values - high).astype(BF16).astype(F32)
    return high, mid, values - high - mid


def emit(state, surface, wet, flags, fields, own_edges, one, two, raw, d):
    half = d.rows // 2
    is_ocean, even = flags[0] != 0, flags[3] == 0
    gap = jnp.zeros((4, CH), F32)
    terms = []
    for term in split_bf16(surface[flags[0]]):
        terms += [term, gap]
    proj = jnp.concatenate(terms + [gap, gap], axis=0).astype(BF16)
    for step in range(half):
        pair = jnp.concatenate([state[step], state[step + half]], axis=1)
        parts = jnp.dot(proj, pair, preferred_element_type=F32)
        whole = parts[0:8] + parts[8:16] + parts[16:24]
        raw[step * 8 : step * 8 + 8, :] = whole[:, :128]
        raw[(step + half) * 8 : (step + half) * 8 + 8, :] = whole[:, 128:]
    keeping = jnp.where(is_ocean, wet[...].astype(F32), 1.0)
    for field in range(NS):
        fields[field] = (raw[pl.ds(field, d.rows, stride=8), :] * keeping).astype(BF16)
    edges = edge_columns(state, d)
    put_edges(own_edges, 0, edges, d)
    for ref, first in strips(one, two, even, d):
        ref[0:CH, :] = state[first]
        ref[CH : 2 * CH, :] = state[first + 1]
        put_edges(ref, 2 * CH, edges, d)


def fetch(sources, targets, sems):
    copies = [
        pltpu.make_async_copy(source, target, sems.at[index])
        for index, (source, target) in enumerate(zip(sources, targets))
    ]
    for copy in copies:
        copy.start()
    return copies


def start_kernel(
    d, flags, far_given, far_surface, far_wet, far_offsets, far_weights,
    state, planes, fields, own_edges, one, two,
    raw, tall, turned, given, surface, wet, offsets, weights, sems,
):
    rows = d.rows
    copies = fetch(
        (far_given, far_surface, far_wet, far_offsets, far_weights),
        (given, surface, wet, offsets, weights),
        sems,
    )
    copies[0].wait()
    turned[...] = given[...].astype(F32).reshape(CH * rows, 128)
    for row in range(rows):
        state[row] = turned[pl.ds(row, CH, stride=rows), :].astype(BF16)
    for copy in copies[1:]:
        copy.wait()
    emit(state, surface, wet, flags, fields, own_edges, one, two, raw, d)
    for k in range(NK):
        code = (offsets[0, k] * SPAN + offsets[1, k]).astype(F32)
        tall[k * rows : (k + 1) * rows, :] = code
        tall[(NK + k) * rows : (NK + k + 1) * rows, :] = weights[k]
        planes[k] = code.astype(BF16)
        planes[NK + k] = weights[k].astype(BF16)
    for ref, first in strips(one, two, flags[3] == 0, d):
        strip = [tall[pl.ds(first + step, 2 * NK, stride=rows), :] for step in range(2)]
        ref[d.strip : d.strip + 16, :] = jnp.concatenate(strip, axis=0).astype(BF16)


def decode(code):
    shifted = code.astype(jnp.int32) + (HW * SPAN + HW)
    rows = lax.shift_right_logical(shifted * 241, 12)
    return rows - HW, shifted - rows * SPAN - HW


def along_lanes(values, index):
    numbers = lax.GatherDimensionNumbers(
        offset_dims=(),
        collapsed_slice_dims=(1,),
        start_index_map=(1,),
        operand_batching_dims=(0,),
        start_indices_batching_dims=(0,),
    )
    return lax.gather(
        values, index[..., None], numbers, (1, 1), mode=lax.GatherScatterMode.PROMISE_IN_BOUNDS
    )


def select_rows(sources, start, picks):
    chosen = [[jnp.zeros((8, 128), F32) for _ in range(NS)] for _ in picks]
    for shift in range(-HW, HW + 1):
        at = pl.ds(start + shift, 8)
        used = [any(pick[2][index] is not None for pick in picks) for index in range(len(sources))]
        values = [
            [source[field, at, :] for field in range(NS)] if use else None
            for source, use in zip(sources, used)
        ]
        for slot, (rows, index, allowed) in enumerate(picks):
            here = rows == shift
            for source, within in enumerate(allowed):
                if within is None:
                    continue
                mask = here & within
                for field in range(NS):
                    picked = along_lanes(values[source][field], index)
                    chosen[slot][field] = jnp.where(mask, picked, chosen[slot][field])
    return chosen


def regrid_inside(fields_x, plan_x, part_x, first, tiles, tall):
    lane = lanes((8, 128))
    for step in range(tiles):
        at = first + step * 8
        picks = []
        weights = []
        for k in range(NK):
            rows, cols = decode(plan_x[pl.ds(k * tall + at, 8), :])
            weights.append(plan_x[pl.ds((NK + k) * tall + at, 8), :])
            column = lane + cols
            picks.append((rows, column & 127, ((column >= 0) & (column < 128),)))
        chosen = select_rows((fields_x,), at + 14, picks)
        for field in range(NS):
            total = chosen[0][field] * weights[0]
            for k in range(1, NK):
                total = total + chosen[k][field] * weights[k]
            part_x[pl.ds(field * tall + at, 8), :] = total


def regrid_beside(
    fields_x, fields_y, plan_x, plan_y, part_x, forcing_x, forcing_y, first, tiles, tall, sides
):
    lane = lanes((8, 128))
    part = ((lane + 8) & 127) // 32
    place = ((lane + 8) & 31) - 8
    outer = place >= 8
    inner_column = place & 127
    outer_column = jnp.where(place < 16, place - 16, place + 112)
    edge = (lane < 8) | (lane >= 120)
    for step in range(tiles):
        at = first + step * 8
        code = jnp.zeros((8, 128), F32)
        weight = jnp.zeros((8, 128), F32)
        for k in range(NK):
            edge_code = roll(plan_x[pl.ds(k * tall + at, 8), :], 32 * k)
            edge_weight = roll(plan_x[pl.ds((NK + k) * tall + at, 8), :], 32 * k)
            if sides:
                edge_code = jnp.where(
                    outer, roll(plan_y[pl.ds(k * tall + at, 8), :], 32 * k + 16), edge_code
                )
                edge_weight = jnp.where(
                    outer, roll(plan_y[pl.ds((NK + k) * tall + at, 8), :], 32 * k + 16), edge_weight
                )
            code = jnp.where(part == k, edge_code, code)
            weight = jnp.where(part == k, edge_weight, weight)
        rows, cols = decode(code)
        column = jnp.where(outer, outer_column, inner_column) + cols
        within = (column >= 0) & (column < 128)
        picks = [(rows, column & 127, (within & outer if sides else None, jnp.logical_not(within)))]
        (chosen,) = select_rows((fields_x, fields_y), at + 14, picks)
        for field in range(NS):
            part_sum = chosen[field] * weight
            extra = part_sum
            for k in range(1, NK):
                extra = extra + roll(part_sum, -32 * k)
            total = part_x[pl.ds(field * tall + at, 8), :] + jnp.where(edge, extra, 0.0)
            forcing_x[pl.ds(at * 8 + field, 8, stride=8), :] = total
            forcing_x[pl.ds(at * 8 + field + 4, 8, stride=8), :] = total
            if sides:
                extra = roll(extra, -16)
                forcing_y[pl.ds(at * 8 + field, 8, stride=8), :] = extra
                forcing_y[pl.ds(at * 8 + field + 4, 8, stride=8), :] = extra


def place_columns(left, right):
    return jnp.where(lanes(left.shape) < 64, right.astype(F32), left.astype(F32))


def gelu(x):
    scale = (2 / jnp.pi) ** 0.5
    half = 0.5 * x
    return half + half * jnp.tanh(x * (scale + (scale * 0.044715) * (x * x)))


def air(state, out, forcing_x, air_in, atm_out, d):
    half = d.rows // 2
    first = subs((8, 128)) < 4
    blank = jnp.zeros((32, 128), BF16)

    def inputs(row):
        at = (row + 2) * 8
        forced = jnp.where(first, forcing_x[at : at + 8, :], 1.0)
        forced = jnp.concatenate([forced, jnp.zeros_like(forced)], axis=0).astype(BF16)
        return jnp.concatenate([state[row], forced, blank], axis=0)

    for step in range(half):
        pair = jnp.concatenate([inputs(step), inputs(step + half)], axis=1)
        hidden = gelu(jnp.dot(air_in[...], pair, preferred_element_type=F32)).astype(BF16)
        update = jnp.dot(atm_out[...], hidden, preferred_element_type=F32)
        for offset in range(2):
            row = step + offset * half
            change = update[:, offset * 128 : (offset + 1) * 128]
            out(row, state[row].astype(F32) + change)


def edge_forcing(forcing_x, forcing_y, d):
    lane = lanes((8, d.edge))
    block = lane // d.block
    row = lane % d.block

    inner = outer = jnp.zeros((8, d.edge), F32)
    for step in range(d.rows + 4):
        at = pl.ds(step * 8, 8)
        pad = [jnp.zeros((8, 128), F32)] * (d.pieces - 1)
        here = jnp.concatenate([forcing_x[at, :]] + pad, axis=1)
        there = jnp.concatenate([forcing_y[at, :]] + pad, axis=1)
        for index, column in enumerate((126, 0, 127, 1)):
            shift = step + index * d.block - column
            match = (block == index) & (row == step)
            if column in (0, 127):
                inner = jnp.where(match, roll(here, shift), inner)
            outer = jnp.where(match, roll(there, shift), outer)
    return inner, outer


def roll_rows(state, upper, lower, rolled, d):
    def put(row, values):
        rolled[row, 0:CH, :] = roll(values, 1)
        rolled[row, CH : 2 * CH, :] = values
        rolled[row, 2 * CH : 3 * CH, :] = roll(values, -1)

    for step in range(2):
        put(step, upper[step * CH : (step + 1) * CH, :])
        put(d.rows + 2 + step, lower[step * CH : (step + 1) * CH, :])
    for row in range(d.rows):
        put(row + 2, state[row])


def sea(
    state, rolled, edges, left, right, out, forcing_x, forcing_y, ocn_in, ocn_out, wet,
    at_top, at_bottom, stack, hidden, side, d,
):
    rows, block = d.rows, d.block
    lane = lanes((CH, 128))
    spot = lanes((CH, d.edge))
    part = spot // block
    inner = edges
    outer = jnp.where((part == 0) | (part == 2), left, right)

    def sides_of(inner, outer, spot):
        first = spot < block
        return (
            jnp.where(first, outer, roll(inner, -block)),
            jnp.where(first, roll(outer, -2 * block), outer),
            jnp.where(first, roll(inner, -block), roll(outer, -2 * block)),
        )

    beside = sides_of(inner, outer, spot)
    middle = beside[1]
    force_in, force_out = edge_forcing(forcing_x, forcing_y, d)
    beside_forcing = sides_of(force_in, force_out, lanes((8, d.edge)))
    sub = subs((8, d.edge))
    ones = jnp.ones((8, d.edge), F32)
    forced = jnp.concatenate(
        [
            jnp.where(sub < 4, beside_forcing[0], beside_forcing[1]),
            jnp.where(sub < 4, beside_forcing[2], ones),
        ],
        axis=0,
    ).astype(BF16)
    columns = jnp.concatenate(list(beside) + [forced], axis=0)
    for tap in range(3):
        side[tap * 256 : (tap + 1) * 256, :] = roll(columns, -tap)

    sub_row = subs((8, 128))
    lane_row = lanes((8, 128))

    for row in range(rows + 4):
        entry = roll(middle, -row)[:, :128]
        stack[row, 0:CH, :] = jnp.where(lane == 0, entry, rolled[row, 0:CH, :])
        stack[row, CH : 2 * CH, :] = rolled[row, CH : 2 * CH, :]
        entry = roll(middle, 127 - block - row)[:, :128]
        stack[row, 2 * CH : 3 * CH, :] = jnp.where(lane == 127, entry, rolled[row, 2 * CH : 3 * CH, :])
        here, there = forcing_x[row * 8 : row * 8 + 8, :], forcing_y[row * 8 : row * 8 + 8, :]
        before = roll(jnp.where(lane_row == 127, there, here), 1)
        after = roll(jnp.where(lane_row == 0, there, here), -1)
        stack[row, 3 * CH : 256, :] = jnp.concatenate(
            [jnp.where(sub_row < 4, before, here), jnp.where(sub_row < 4, after, 1.0)], axis=0
        ).astype(BF16)

    pairs = (rows + 2) // 2

    for step in range(pairs):
        taps = jnp.concatenate(
            [
                stack[step : step + 3].reshape(3 * 256, 128),
                stack[step + pairs : step + pairs + 3].reshape(3 * 256, 128),
            ],
            axis=1,
        )
        active = gelu(jnp.dot(ocn_in[...], taps, preferred_element_type=F32))
        low, high = active[:, :128], active[:, 128:]
        if step == 0:
            low = jnp.where(at_top != 0, 0.0, low)
        if step == pairs - 1:
            high = jnp.where(at_bottom != 0, 0.0, high)
        hidden[step, 0:HIDK, :] = low.astype(BF16)
        hidden[step + pairs, 0:HIDK, :] = high.astype(BF16)
        blank = jnp.zeros((HIDP - HIDK, 128), BF16)
        hidden[step, HIDK:HIDP, :] = blank
        hidden[step + pairs, HIDK:HIDP, :] = blank

    product = jnp.dot(ocn_in[...], side[...], preferred_element_type=F32)
    spot = lanes((1, d.edge)) % block
    gone = ((spot == 0) & (at_top != 0)) | ((spot == rows + 1) & (at_bottom != 0))
    active = jnp.where(gone, 0.0, gelu(product)).astype(BF16)
    active = jnp.concatenate([active, jnp.zeros((HIDP - HIDK, d.edge), BF16)], axis=0)

    def taps_of(slices):
        total = None
        for tap, values in enumerate(slices):
            weights = ocn_out[tap * 3 * CH : (tap + 1) * 3 * CH, :]
            product = jnp.dot(weights, values, preferred_element_type=F32)
            total = product if total is None else total + product
        return total

    partial = taps_of([roll(active, -tap) for tap in range(3)])
    from_left, from_right = partial[0:CH], partial[2 * CH : 3 * CH]
    half = rows // 2
    for step in range(half):
        product = taps_of(
            [
                jnp.concatenate([hidden[step + tap], hidden[step + half + tap]], axis=1)
                for tap in range(3)
            ]
        )
        for offset in range(2):
            row = step + offset * half
            sums = product[:, offset * 128 : (offset + 1) * 128]
            entry = roll(from_left, -row)[:, :128]
            total = sums[CH : 2 * CH] + jnp.where(lane == 0, entry, roll(sums[0:CH], 1))
            entry = roll(from_right, 127 - block - row)[:, :128]
            total = total + jnp.where(lane == 127, entry, roll(sums[2 * CH : 3 * CH], -1))
            update = total * wet[row : row + 1, :].astype(F32)
            out(row, state[row].astype(F32) + update)


def join_rows(edge_up, edge_own, edge_down, d):
    row = lanes(edge_own.shape) % d.block
    above = roll(edge_up, -d.rows)
    below = roll(edge_down, d.rows)
    return jnp.where(row < 2, above, jnp.where(row < d.rows + 2, edge_own, below))


def prepare(atm_in, atm_bias, ocn_in, ocn_bias, ocn_out, air_in, first, second, is_ocean):
    def bias_rows(ref, width):
        row = jnp.concatenate([ref[index : index + 1, :] for index in range(ref.shape[0])], axis=1)
        terms = list(split_bf16(row)) + [jnp.zeros_like(row)]
        bias = jnp.concatenate(terms, axis=0)
        return jnp.pad(bias, ((0, 0), (0, width - bias.shape[1])))

    @pl.when(is_ocean == 0)
    def _():
        columns = jnp.concatenate(
            [atm_in[...].astype(F32), bias_rows(atm_bias, HA), jnp.zeros((40, HA), F32)], axis=0
        )
        air_in[...] = columns.T.astype(BF16)

    @pl.when(is_ocean != 0)
    def _():
        bias = bias_rows(ocn_bias, 256)
        count = ocn_in.shape[2]
        for tap in range(3):
            whole = [ocn_in[3 * tap + side].astype(F32) for side in range(3)]
            whole = [jnp.pad(values, ((0, 0), (0, 256 - count))) for values in whole]
            rows = [values[:CH] for values in whole] + [values[CH:] for values in whole]
            rows.append(bias if tap == 0 else jnp.zeros((4, 256), F32))
            columns = jnp.concatenate(rows, axis=0).T
            first[:, tap * 256 : (tap + 1) * 256] = columns[:HIDK].astype(BF16)
        for tap in range(9):
            values = ocn_out[tap].astype(F32)
            second[tap * CH : (tap + 1) * CH, :] = jnp.pad(
                values, ((0, 0), (0, HIDP - count))
            ).astype(BF16)


def ends(flags):
    at_top, at_bottom, even = flags[1] != 0, flags[2] != 0, flags[3] == 0

    def up_and_down(one, two):
        above = jnp.where(even, two, one).astype(F32)
        below = jnp.where(even, one, two).astype(F32)
        return jnp.where(at_top, 0.0, above), jnp.where(at_bottom, 0.0, below)

    return up_and_down


def middle_kernel(d, opening, *refs):
    refs = list(refs)
    take = lambda count: [refs.pop(0) for _ in range(count)]
    flags, state, from_one, from_two, own_edges = take(5)
    if opening:
        (planes,) = take(1)
    else:
        (plan_x,) = take(1)
    (gathered,) = take(1)
    if opening:
        far_weights = take(5)
    part_x, fields_x, fields_y, rolled, edges = take(5)
    if opening:
        plan_x, *made_weights = take(4)
    tiles = take(1)[0]
    raw_weights = take(5) if opening else []
    (sems,) = take(1)
    copies = fetch(
        [gathered.at[flags[4 + index]] for index in range(9)] + (far_weights if opening else []),
        [tiles.at[index] for index in range(9)] + raw_weights,
        sems,
    )
    rows, tall = d.rows, d.tall
    is_ocean = flags[0]
    up_and_down = ends(flags)

    if opening:

        @pl.when(is_ocean != 0)
        def _():
            base = d.strip
            pair = up_and_down(from_one[base : base + 16, :], from_two[base : base + 16, :])
            plan_x[...] = jnp.zeros_like(plan_x)
            for step, strip in zip((0, rows + 2), pair):
                for index in range(2):
                    plan_x[pl.ds(step + index, 2 * NK, stride=tall), :] = strip[index * 8 : (index + 1) * 8]

        for plane in range(2 * NK):
            plan_x[plane * tall + 2 : plane * tall + 2 + rows, :] = planes[plane].astype(F32)

    for copy in copies[:9]:
        copy.wait()
    at_top, at_bottom = flags[1] != 0, flags[2] != 0
    for field in range(NS):
        for target, columns in ((fields_x, [tiles[3 * row + 1, field] for row in range(3)]),
                                (fields_y, [place_columns(tiles[3 * row, field], tiles[3 * row + 2, field])
                                            for row in range(3)])):
            above, own, below = [values.astype(F32) for values in columns]
            target[field, 0:16, :] = jnp.where(at_top, 0.0, above)[rows - 16 : rows]
            target[field, 16 : 16 + rows, :] = own
            target[field, 16 + rows : 32 + rows, :] = jnp.where(at_bottom, 0.0, below)[0:16]

    @pl.when(is_ocean == 0)
    def _():
        regrid_inside(fields_x, plan_x, part_x, 2, rows // 8, tall)

    @pl.when(is_ocean != 0)
    def _():
        regrid_inside(fields_x, plan_x, part_x, 0, d.tiles, tall)
        upper, lower = up_and_down(from_one[0 : 2 * CH, :], from_two[0 : 2 * CH, :])
        roll_rows(state, upper.astype(BF16), lower.astype(BF16), rolled, d)
        above, below = up_and_down(get_edges(from_one, 2 * CH, d), get_edges(from_two, 2 * CH, d))
        joined = join_rows(above.astype(BF16), get_edges(own_edges, 0, d), below.astype(BF16), d)
        put_edges(edges, 0, joined, d)

    if opening:
        for copy in copies[9:]:
            copy.wait()
        prepare(*raw_weights, *made_weights, is_ocean)


def step_kernel(d, opening, closing, *refs):
    refs = list(refs)
    take = lambda count: [refs.pop(0) for _ in range(count)]
    flags, state, wet, from_left, from_right = take(5)
    part_x, fields_x, fields_y, rolled, edges, plan_x, air_in, first, second, atm_out = take(10)
    if not opening:
        (plan_y,) = take(1)
    if not closing:
        (surface,) = take(1)
    (out,) = take(1)
    if not closing:
        fields, new_edges, one, two = take(4)
    if opening:
        (plan_y,) = take(1)
    forcing_x, forcing_y, stack, hidden, side, raw = take(6)
    rows, tall = d.rows, d.tall
    is_ocean, at_top, at_bottom = flags[0], flags[1], flags[2]
    up_and_down = ends(flags)

    if opening:

        @pl.when(is_ocean != 0)
        def _():
            plan_y[...] = jnp.zeros_like(plan_y)
            side_base = 3 * d.edge_rows
            pair = [
                place_columns(from_left[at : at + 16, :], from_right[at : at + 16, :])
                for at in (side_base, side_base + 16 + 2 * NK * rows)
            ]
            for step, strip in zip((0, rows + 2), up_and_down(*pair)):
                for index in range(2):
                    plan_y[pl.ds(step + index, 2 * NK, stride=tall), :] = strip[index * 8 : (index + 1) * 8]
            for plane in range(2 * NK):
                at = side_base + 16 + plane * rows
                plan_y[plane * tall + 2 : plane * tall + 2 + rows, :] = place_columns(
                    from_left[at : at + rows, :], from_right[at : at + rows, :]
                )

    def put(row, values):
        if closing:
            raw[pl.ds(row, CH, stride=rows), :] = values
        else:
            out[row] = values.astype(BF16)

    @pl.when(is_ocean == 0)
    def _():
        regrid_beside(
            fields_x, fields_y, plan_x, plan_y, part_x, forcing_x, forcing_y, 2, rows // 8, tall, False
        )
        air(state, put, forcing_x, air_in, atm_out, d)

    @pl.when(is_ocean != 0)
    def _():
        regrid_beside(
            fields_x, fields_y, plan_x, plan_y, part_x, forcing_x, forcing_y, 0, d.tiles, tall, True
        )
        at = 0
        size = d.edge_rows
        joined = []
        for ref in (from_left, from_right):
            one_edges, middle, two_edges = [get_edges(ref, at + index * size, d) for index in range(3)]
            above, below = up_and_down(one_edges, two_edges)
            joined.append(join_rows(above.astype(BF16), middle, below.astype(BF16), d))
        sea(
            state, rolled, get_edges(edges, 0, d), *joined, put, forcing_x, forcing_y,
            first, second, wet, at_top, at_bottom, stack, hidden, side, d,
        )

    if closing:
        out[...] = raw[...].reshape(CH, rows, 128).astype(BF16)
    else:
        emit(out, surface, wet, flags, fields, new_edges, one, two, raw, d)


VMEM = pl.BlockSpec(memory_space=pltpu.VMEM)
HBM = pl.BlockSpec(memory_space=pltpu.HBM)
SMEM = pl.BlockSpec(memory_space=pltpu.SMEM)
PARAMS = pltpu.CompilerParams(vmem_limit_bytes=48 * 1024 * 1024)


def shape(*dims, dtype=BF16):
    return jax.ShapeDtypeStruct(dims, dtype)


def send(x, move):
    names = ("grp", "lat", "lon")
    sizes = [lax.axis_size(name) for name in names]
    pairs = []
    for group in range(sizes[0]):
        for lat in range(sizes[1]):
            for lon in range(sizes[2]):
                to = move(group, lat, lon)
                if to is None or not 0 <= to[1] < sizes[1]:
                    continue
                target = (to[0] * sizes[1] + to[1]) * sizes[2] + to[2] % sizes[2]
                pairs.append(((group * sizes[1] + lat) * sizes[2] + lon, target))
    return lax.ppermute(x, names, pairs)


def swap_rows(x, turn):
    count = lax.axis_size("lat")

    def move(group, lat, lon):
        other = ((lat + turn) ^ 1) - turn
        return group, other if 0 <= other < count else lat, lon

    return send(x, move)


def exchange(fields, own_edges, one, two, planes, d):
    rows = d.rows
    gathered = lax.all_gather(fields, ("grp", "lat", "lon"))
    from_one = swap_rows(one, 0)
    from_two = swap_rows(two, 1)
    edge_at = slice(2 * CH, d.strip)
    packed = [from_one[edge_at], own_edges, from_two[edge_at]]
    if planes is not None:
        packed += [from_one[d.strip :], planes.reshape(2 * NK * rows, 128), from_two[d.strip :]]
    packed = jnp.concatenate(packed, axis=0)
    from_left = send(packed, lambda g, i, j: (g, i, j + 1))
    from_right = send(packed, lambda g, i, j: (g, i, j - 1))
    gathered, packed = lax.optimization_barrier((gathered, packed))
    return (from_one, from_two), (from_left, from_right), gathered


def local(
    coupled_state, land_mask, regrid_offsets, regrid_weights, surface_proj,
    atm_in, atm_bias, atm_out, ocn_in, ocn_bias, ocn_out,
):
    rows = coupled_state.shape[2]
    assert coupled_state.shape[3] == 128
    d = Dims(rows)
    group = lax.axis_index("grp")
    lat = lax.axis_index("lat")
    lon = lax.axis_index("lon")
    counts = lax.axis_size("lat"), lax.axis_size("lon")
    flags = [group, lat == 0, lat == counts[0] - 1, lat % 2]
    for row in range(-1, 2):
        for column in range(-1, 2):
            at = (1 - group) * counts[0] + jnp.clip(lat + row, 0, counts[0] - 1)
            flags.append(at * counts[1] + (lon + column) % counts[1])
    flags = jnp.stack([flag.astype(jnp.int32) for flag in flags])
    raw_weights = (
        atm_in.T,
        atm_bias.reshape(HA // 128, 128),
        jnp.transpose(ocn_in, (1, 2, 0)),
        ocn_bias[None],
        jnp.transpose(ocn_out, (1, 0, 2)),
    )
    state_shape = shape(rows, CH, 128)
    emitted = [
        shape(NS, rows, 128),
        shape(d.edge_rows, 128),
        shape(d.strip, 128),
        shape(d.strip, 128),
    ]
    raw = pltpu.VMEM((rows * 8, 128), F32)
    turned = pltpu.VMEM((CH * rows, 128), F32)

    def call(kernel, operands, outs, scratch, name, far=()):
        gathers = name.endswith("middle")
        scratch = scratch + [pltpu.VMEM(x.shape, x.dtype) for x in far[gathers:]]
        if far:
            scratch.append(pltpu.SemaphoreType.DMA((len(far) + 8 * gathers,)))

        far = [pltpu.with_memory_space_constraint(x, pltpu.HBM) for x in far]
        return pl.pallas_call(
            kernel,
            out_shape=outs,
            in_specs=[SMEM] + [VMEM] * len(operands) + [HBM] * len(far),
            out_specs=[VMEM] * len(outs),
            scratch_shapes=scratch,
            compiler_params=PARAMS,
            name=name,
        )(flags, *operands, *far)

    state, planes, fields, edges, one, two = call(
        functools.partial(start_kernel, d),
        (),
        [state_shape, shape(2 * NK, rows, 128)] + emitted[:2] + [shape(d.strip + 16, 128)] * 2,
        [raw, pltpu.VMEM((2 * NK * rows, 128), F32), turned],
        "start",
        (coupled_state[0], surface_proj, land_mask, regrid_offsets[0], regrid_weights[0]),
    )

    plan = shape(2 * NK * d.tall, 128, dtype=F32)
    between = [
        shape(NS * d.tall, 128, dtype=F32),
        shape(NS, rows + 32, 128, dtype=F32),
        shape(NS, rows + 32, 128, dtype=F32),
        shape(rows + 4, 3 * CH, 128),
        shape(d.edge_rows, 128),
    ]
    made = [shape(HA, 128), shape(HIDK, 768), shape(9 * CH, HIDP)]
    tiles = [pltpu.VMEM((9, NS, rows, 128), BF16)]
    scratch = [
        pltpu.VMEM((d.tall * 8, 128), F32),
        pltpu.VMEM((d.tall * 8, 128), F32),
        pltpu.VMEM((rows + 4, 256, 128), BF16),
        pltpu.VMEM((rows + 2, HIDP, 128), BF16),
        pltpu.VMEM((768, d.edge), BF16),
    ]

    vertical, horizontal, gathered = exchange(fields, edges, one, two, planes, d)
    *shared, plan_x, air_in, first, second = call(
        functools.partial(middle_kernel, d, True),
        (state, *vertical, edges, planes),
        between + [plan] + made,
        tiles,
        "first_middle",
        (gathered, *raw_weights),
    )
    weights = (air_in, first, second, atm_out)
    state, fields, edges, one, two, plan_y = call(
        functools.partial(step_kernel, d, True, False),
        (state, land_mask, *horizontal, *shared, plan_x, *weights, surface_proj),
        [state_shape] + emitted + [plan],
        scratch + [raw],
        "first_step",
    )

    vertical, horizontal, gathered = exchange(fields, edges, one, two, None, d)
    shared = call(
        functools.partial(middle_kernel, d, False),
        (state, *vertical, edges, plan_x),
        between,
        tiles,
        "second_middle",
        (gathered,),
    )
    (state,) = call(
        functools.partial(step_kernel, d, False, True),
        (state, land_mask, *horizontal, *shared, plan_x, *weights, plan_y),
        [shape(CH, rows, 128)],
        scratch + [turned],
        "second_step",
    )
    return state[None]


def solution(mesh):
    return jax.shard_map(
        local,
        mesh=mesh,
        in_specs=(
            P("grp", None, "lat", "lon"),
            P("lat", "lon"),
            P("grp", None, None, "lat", "lon"),
            P("grp", None, "lat", "lon"),
            P(),
            P(),
            P(),
            P(),
            P(),
            P(),
            P(),
        ),
        out_specs=P("grp", None, "lat", "lon"),
        check_vma=False,
    )
```

```python
import functools

import jax
import jax.numpy as jnp
from jax import lax
from jax.experimental import pallas as pl
from jax.experimental.pallas import tpu as pltpu
from jax.sharding import PartitionSpec as P

CH = 80
NS = 4
NK = 4
HA = 384
HW = 8
SPAN = 2 * HW + 1
HIDK = 208
HIDP = 256
F32 = jnp.float32
BF16 = jnp.bfloat16


def roll(x, shift, axis=1):
    size = x.shape[axis]
    if isinstance(shift, int):
        shift = shift % size
        if shift == 0:
            return x
    return pltpu.roll(x, shift, axis)


def lanes(shape):
    return lax.broadcasted_iota(jnp.int32, shape, len(shape) - 1)


def subs(shape):
    return lax.broadcasted_iota(jnp.int32, shape, len(shape) - 2)


class Dims:
    def __init__(self, rows):
        self.rows = rows
        self.block = 32 if rows + 4 <= 32 else 64
        self.edge = 4 * self.block
        self.pieces = self.edge // 128
        self.edge_rows = CH * self.pieces
        self.tiles = -(-(rows + 4) // 8)
        self.tall = 8 * self.tiles
        self.strip = 2 * CH + self.edge_rows


def put_edges(ref, at, edges, d):
    for piece in range(d.pieces):
        ref[at + piece * CH : at + (piece + 1) * CH, :] = edges[:, piece * 128 : (piece + 1) * 128]


def get_edges(ref, at, d):
    return jnp.concatenate(
        [ref[at + piece * CH : at + (piece + 1) * CH, :] for piece in range(d.pieces)], axis=1
    )


def edge_columns(state, d):
    lane = lanes((1, d.edge))
    block = lane // d.block
    row = lane % d.block - 2
    column = jnp.where(block == 0, 126, jnp.where(block == 1, 0, jnp.where(block == 2, 127, 1)))
    own = (row >= 0) & (row < d.rows)
    target = jnp.where(own, column, -1)
    position = subs((128, d.edge))
    places = [
        (position == jnp.where(row == step, target, -1)).astype(F32).astype(BF16)
        for step in range(d.rows)
    ]
    whole = jnp.concatenate([state[step] for step in range(d.rows)], axis=1)
    total = jnp.dot(whole, jnp.concatenate(places, axis=0), preferred_element_type=F32)
    return total.astype(BF16)


def loop(count, unroll, body):
    while count % unroll:
        unroll -= 1

    def several(step, carry):
        for offset in range(unroll):
            body(step * unroll + offset)
        return carry

    lax.fori_loop(0, count // unroll, several, 0)


def strips(one, two, even, d):
    last = d.rows - 2
    return (one, jnp.where(even, last, 0)), (two, jnp.where(even, 0, last))


def split_bf16(values):
    high = values.astype(BF16).astype(F32)
    mid = (values - high).astype(BF16).astype(F32)
    return high, mid, values - high - mid


def emit(state, surface, wet, flags, fields, own_edges, one, two, raw, d):
    half = d.rows // 2
    is_ocean, even = flags[0] != 0, flags[3] == 0
    gap = jnp.zeros((4, CH), F32)
    terms = []
    for term in split_bf16(surface[flags[0]]):
        terms += [term, gap]
    proj = jnp.concatenate(terms + [gap, gap], axis=0).astype(BF16)
    for step in range(half):
        pair = jnp.concatenate([state[step], state[step + half]], axis=1)
        parts = jnp.dot(proj, pair, preferred_element_type=F32)
        whole = parts[0:8] + parts[8:16] + parts[16:24]
        raw[step * 8 : step * 8 + 8, :] = whole[:, :128]
        raw[(step + half) * 8 : (step + half) * 8 + 8, :] = whole[:, 128:]
    keeping = jnp.where(is_ocean, wet[...].astype(F32), 1.0)
    for field in range(NS):
        fields[field] = (raw[pl.ds(field, d.rows, stride=8), :] * keeping).astype(BF16)
    edges = edge_columns(state, d)
    put_edges(own_edges, 0, edges, d)
    for ref, first in strips(one, two, even, d):
        ref[0:CH, :] = state[first]
        ref[CH : 2 * CH, :] = state[first + 1]
        put_edges(ref, 2 * CH, edges, d)


def fetch(sources, targets, sems):
    copies = [
        pltpu.make_async_copy(source, target, sems.at[index])
        for index, (source, target) in enumerate(zip(sources, targets))
    ]
    for copy in copies:
        copy.start()
    return copies


def start_kernel(
    d, flags, far_given, far_surface, far_wet, far_offsets, far_weights,
    state, planes, fields, own_edges, one, two,
    raw, tall, turned, given, surface, wet, offsets, weights, sems,
):
    rows = d.rows
    copies = fetch(
        (far_given, far_surface, far_wet, far_offsets, far_weights),
        (given, surface, wet, offsets, weights),
        sems,
    )
    copies[0].wait()
    turned[...] = given[...].astype(F32).reshape(CH * rows, 128)
    for row in range(rows):
        state[row] = turned[pl.ds(row, CH, stride=rows), :].astype(BF16)
    for copy in copies[1:]:
        copy.wait()
    emit(state, surface, wet, flags, fields, own_edges, one, two, raw, d)
    for k in range(NK):
        code = (offsets[0, k] * SPAN + offsets[1, k]).astype(F32)
        tall[k * rows : (k + 1) * rows, :] = code
        tall[(NK + k) * rows : (NK + k + 1) * rows, :] = weights[k]
        planes[k] = code.astype(BF16)
        planes[NK + k] = weights[k].astype(BF16)
    for ref, first in strips(one, two, flags[3] == 0, d):
        strip = [tall[pl.ds(first + step, 2 * NK, stride=rows), :] for step in range(2)]
        ref[d.strip : d.strip + 16, :] = jnp.concatenate(strip, axis=0).astype(BF16)


def decode(code):
    shifted = code.astype(jnp.int32) + (HW * SPAN + HW)
    rows = lax.shift_right_logical(shifted * 241, 12)
    return rows - HW, shifted - rows * SPAN - HW


def along_lanes(values, index):
    numbers = lax.GatherDimensionNumbers(
        offset_dims=(),
        collapsed_slice_dims=(1,),
        start_index_map=(1,),
        operand_batching_dims=(0,),
        start_indices_batching_dims=(0,),
    )
    return lax.gather(
        values, index[..., None], numbers, (1, 1), mode=lax.GatherScatterMode.PROMISE_IN_BOUNDS
    )


def select_rows(sources, start, picks):
    chosen = [[jnp.zeros((8, 128), F32) for _ in range(NS)] for _ in picks]
    for shift in range(-HW, HW + 1):
        at = pl.ds(start + shift, 8)
        used = [any(pick[2][index] is not None for pick in picks) for index in range(len(sources))]
        values = [
            [source[field, at, :] for field in range(NS)] if use else None
            for source, use in zip(sources, used)
        ]
        for slot, (rows, index, allowed) in enumerate(picks):
            here = rows == shift
            for source, within in enumerate(allowed):
                if within is None:
                    continue
                mask = here & within
                for field in range(NS):
                    picked = along_lanes(values[source][field], index)
                    chosen[slot][field] = jnp.where(mask, picked, chosen[slot][field])
    return chosen


def regrid_inside(fields_x, plan_x, part_x, first, tiles, tall):
    lane = lanes((8, 128))
    for step in range(tiles):
        at = first + step * 8
        picks = []
        weights = []
        for k in range(NK):
            rows, cols = decode(plan_x[pl.ds(k * tall + at, 8), :])
            weights.append(plan_x[pl.ds((NK + k) * tall + at, 8), :])
            column = lane + cols
            picks.append((rows, column & 127, ((column >= 0) & (column < 128),)))
        chosen = select_rows((fields_x,), at + 14, picks)
        for field in range(NS):
            total = chosen[0][field] * weights[0]
            for k in range(1, NK):
                total = total + chosen[k][field] * weights[k]
            part_x[pl.ds(field * tall + at, 8), :] = total


def regrid_beside(
    fields_x, fields_y, plan_x, plan_y, part_x, forcing_x, forcing_y, first, tiles, tall, sides
):
    lane = lanes((8, 128))
    part = ((lane + 8) & 127) // 32
    place = ((lane + 8) & 31) - 8
    outer = place >= 8
    inner_column = place & 127
    outer_column = jnp.where(place < 16, place - 16, place + 112)
    edge = (lane < 8) | (lane >= 120)
    for step in range(tiles):
        at = first + step * 8
        code = jnp.zeros((8, 128), F32)
        weight = jnp.zeros((8, 128), F32)
        for k in range(NK):
            edge_code = roll(plan_x[pl.ds(k * tall + at, 8), :], 32 * k)
            edge_weight = roll(plan_x[pl.ds((NK + k) * tall + at, 8), :], 32 * k)
            if sides:
                edge_code = jnp.where(
                    outer, roll(plan_y[pl.ds(k * tall + at, 8), :], 32 * k + 16), edge_code
                )
                edge_weight = jnp.where(
                    outer, roll(plan_y[pl.ds((NK + k) * tall + at, 8), :], 32 * k + 16), edge_weight
                )
            code = jnp.where(part == k, edge_code, code)
            weight = jnp.where(part == k, edge_weight, weight)
        rows, cols = decode(code)
        column = jnp.where(outer, outer_column, inner_column) + cols
        within = (column >= 0) & (column < 128)
        picks = [(rows, column & 127, (within & outer if sides else None, jnp.logical_not(within)))]
        (chosen,) = select_rows((fields_x, fields_y), at + 14, picks)
        for field in range(NS):
            part_sum = chosen[field] * weight
            extra = part_sum
            for k in range(1, NK):
                extra = extra + roll(part_sum, -32 * k)
            total = part_x[pl.ds(field * tall + at, 8), :] + jnp.where(edge, extra, 0.0)
            forcing_x[pl.ds(at * 8 + field, 8, stride=8), :] = total
            forcing_x[pl.ds(at * 8 + field + 4, 8, stride=8), :] = total
            if sides:
                extra = roll(extra, -16)
                forcing_y[pl.ds(at * 8 + field, 8, stride=8), :] = extra
                forcing_y[pl.ds(at * 8 + field + 4, 8, stride=8), :] = extra


def place_columns(left, right):
    return jnp.where(lanes(left.shape) < 64, right.astype(F32), left.astype(F32))


def gelu(x):
    scale = (2 / jnp.pi) ** 0.5
    half = 0.5 * x
    return half + half * jnp.tanh(x * (scale + (scale * 0.044715) * (x * x)))


def air(state, out, forcing_x, air_in, atm_out, d):
    half = d.rows // 2
    first = subs((8, 128)) < 4
    blank = jnp.zeros((32, 128), BF16)

    def inputs(row):
        at = (row + 2) * 8
        forced = jnp.where(first, forcing_x[at : at + 8, :], 1.0)
        forced = jnp.concatenate([forced, jnp.zeros_like(forced)], axis=0).astype(BF16)
        return jnp.concatenate([state[row], forced, blank], axis=0)

    for step in range(half):
        pair = jnp.concatenate([inputs(step), inputs(step + half)], axis=1)
        hidden = gelu(jnp.dot(air_in[...], pair, preferred_element_type=F32)).astype(BF16)
        update = jnp.dot(atm_out[...], hidden, preferred_element_type=F32)
        for offset in range(2):
            row = step + offset * half
            change = update[:, offset * 128 : (offset + 1) * 128]
            out(row, state[row].astype(F32) + change)


def edge_forcing(forcing_x, forcing_y, d):
    lane = lanes((8, d.edge))
    block = lane // d.block
    row = lane % d.block

    inner = outer = jnp.zeros((8, d.edge), F32)
    for step in range(d.rows + 4):
        at = pl.ds(step * 8, 8)
        pad = [jnp.zeros((8, 128), F32)] * (d.pieces - 1)
        here = jnp.concatenate([forcing_x[at, :]] + pad, axis=1)
        there = jnp.concatenate([forcing_y[at, :]] + pad, axis=1)
        for index, column in enumerate((126, 0, 127, 1)):
            shift = step + index * d.block - column
            match = (block == index) & (row == step)
            if column in (0, 127):
                inner = jnp.where(match, roll(here, shift), inner)
            outer = jnp.where(match, roll(there, shift), outer)
    return inner, outer


def roll_rows(state, upper, lower, rolled, d):
    def put(row, values):
        rolled[row, 0:CH, :] = roll(values, 1)
        rolled[row, CH : 2 * CH, :] = values
        rolled[row, 2 * CH : 3 * CH, :] = roll(values, -1)

    for step in range(2):
        put(step, upper[step * CH : (step + 1) * CH, :])
        put(d.rows + 2 + step, lower[step * CH : (step + 1) * CH, :])
    for row in range(d.rows):
        put(row + 2, state[row])


def sea(
    state, rolled, edges, left, right, out, forcing_x, forcing_y, ocn_in, ocn_out, wet,
    at_top, at_bottom, stack, hidden, side, d,
):
    rows, block = d.rows, d.block
    lane = lanes((CH, 128))
    spot = lanes((CH, d.edge))
    part = spot // block
    inner = edges
    outer = jnp.where((part == 0) | (part == 2), left, right)

    def sides_of(inner, outer, spot):
        first = spot < block
        return (
            jnp.where(first, outer, roll(inner, -block)),
            jnp.where(first, roll(outer, -2 * block), outer),
            jnp.where(first, roll(inner, -block), roll(outer, -2 * block)),
        )

    beside = sides_of(inner, outer, spot)
    middle = beside[1]
    force_in, force_out = edge_forcing(forcing_x, forcing_y, d)
    beside_forcing = sides_of(force_in, force_out, lanes((8, d.edge)))
    sub = subs((8, d.edge))
    ones = jnp.ones((8, d.edge), F32)
    forced = jnp.concatenate(
        [
            jnp.where(sub < 4, beside_forcing[0], beside_forcing[1]),
            jnp.where(sub < 4, beside_forcing[2], ones),
        ],
        axis=0,
    ).astype(BF16)
    columns = jnp.concatenate(list(beside) + [forced], axis=0)
    for tap in range(3):
        side[tap * 256 : (tap + 1) * 256, :] = roll(columns, -tap)

    sub_row = subs((8, 128))
    lane_row = lanes((8, 128))

    for row in range(rows + 4):
        entry = roll(middle, -row)[:, :128]
        stack[row, 0:CH, :] = jnp.where(lane == 0, entry, rolled[row, 0:CH, :])
        stack[row, CH : 2 * CH, :] = rolled[row, CH : 2 * CH, :]
        entry = roll(middle, 127 - block - row)[:, :128]
        stack[row, 2 * CH : 3 * CH, :] = jnp.where(lane == 127, entry, rolled[row, 2 * CH : 3 * CH, :])
        here, there = forcing_x[row * 8 : row * 8 + 8, :], forcing_y[row * 8 : row * 8 + 8, :]
        before = roll(jnp.where(lane_row == 127, there, here), 1)
        after = roll(jnp.where(lane_row == 0, there, here), -1)
        stack[row, 3 * CH : 256, :] = jnp.concatenate(
            [jnp.where(sub_row < 4, before, here), jnp.where(sub_row < 4, after, 1.0)], axis=0
        ).astype(BF16)

    pairs = (rows + 2) // 2

    for step in range(pairs):
        taps = jnp.concatenate(
            [
                stack[step : step + 3].reshape(3 * 256, 128),
                stack[step + pairs : step + pairs + 3].reshape(3 * 256, 128),
            ],
            axis=1,
        )
        active = gelu(jnp.dot(ocn_in[...], taps, preferred_element_type=F32))
        low, high = active[:, :128], active[:, 128:]
        if step == 0:
            low = jnp.where(at_top != 0, 0.0, low)
        if step == pairs - 1:
            high = jnp.where(at_bottom != 0, 0.0, high)
        hidden[step, 0:HIDK, :] = low.astype(BF16)
        hidden[step + pairs, 0:HIDK, :] = high.astype(BF16)
        blank = jnp.zeros((HIDP - HIDK, 128), BF16)
        hidden[step, HIDK:HIDP, :] = blank
        hidden[step + pairs, HIDK:HIDP, :] = blank

    product = jnp.dot(ocn_in[...], side[...], preferred_element_type=F32)
    spot = lanes((1, d.edge)) % block
    gone = ((spot == 0) & (at_top != 0)) | ((spot == rows + 1) & (at_bottom != 0))
    active = jnp.where(gone, 0.0, gelu(product)).astype(BF16)
    active = jnp.concatenate([active, jnp.zeros((HIDP - HIDK, d.edge), BF16)], axis=0)

    def taps_of(slices):
        total = None
        for tap, values in enumerate(slices):
            weights = ocn_out[tap * 3 * CH : (tap + 1) * 3 * CH, :]
            product = jnp.dot(weights, values, preferred_element_type=F32)
            total = product if total is None else total + product
        return total

    partial = taps_of([roll(active, -tap) for tap in range(3)])
    from_left, from_right = partial[0:CH], partial[2 * CH : 3 * CH]
    half = rows // 2
    for step in range(half):
        product = taps_of(
            [
                jnp.concatenate([hidden[step + tap], hidden[step + half + tap]], axis=1)
                for tap in range(3)
            ]
        )
        for offset in range(2):
            row = step + offset * half
            sums = product[:, offset * 128 : (offset + 1) * 128]
            entry = roll(from_left, -row)[:, :128]
            total = sums[CH : 2 * CH] + jnp.where(lane == 0, entry, roll(sums[0:CH], 1))
            entry = roll(from_right, 127 - block - row)[:, :128]
            total = total + jnp.where(lane == 127, entry, roll(sums[2 * CH : 3 * CH], -1))
            update = total * wet[row : row + 1, :].astype(F32)
            out(row, state[row].astype(F32) + update)


def join_rows(edge_up, edge_own, edge_down, d):
    row = lanes(edge_own.shape) % d.block
    above = roll(edge_up, -d.rows)
    below = roll(edge_down, d.rows)
    return jnp.where(row < 2, above, jnp.where(row < d.rows + 2, edge_own, below))


def prepare(atm_in, atm_bias, ocn_in, ocn_bias, ocn_out, air_in, first, second, is_ocean):
    def bias_rows(ref, width):
        row = jnp.concatenate([ref[index : index + 1, :] for index in range(ref.shape[0])], axis=1)
        terms = list(split_bf16(row)) + [jnp.zeros_like(row)]
        bias = jnp.concatenate(terms, axis=0)
        return jnp.pad(bias, ((0, 0), (0, width - bias.shape[1])))

    @pl.when(is_ocean == 0)
    def _():
        columns = jnp.concatenate(
            [atm_in[...].astype(F32), bias_rows(atm_bias, HA), jnp.zeros((40, HA), F32)], axis=0
        )
        air_in[...] = columns.T.astype(BF16)

    @pl.when(is_ocean != 0)
    def _():
        bias = bias_rows(ocn_bias, 256)
        count = ocn_in.shape[2]
        for tap in range(3):
            whole = [ocn_in[3 * tap + side].astype(F32) for side in range(3)]
            whole = [jnp.pad(values, ((0, 0), (0, 256 - count))) for values in whole]
            rows = [values[:CH] for values in whole] + [values[CH:] for values in whole]
            rows.append(bias if tap == 0 else jnp.zeros((4, 256), F32))
            columns = jnp.concatenate(rows, axis=0).T
            first[:, tap * 256 : (tap + 1) * 256] = columns[:HIDK].astype(BF16)
        for tap in range(9):
            values = ocn_out[tap].astype(F32)
            second[tap * CH : (tap + 1) * CH, :] = jnp.pad(
                values, ((0, 0), (0, HIDP - count))
            ).astype(BF16)


def ends(flags):
    at_top, at_bottom, even = flags[1] != 0, flags[2] != 0, flags[3] == 0

    def up_and_down(one, two):
        above = jnp.where(even, two, one).astype(F32)
        below = jnp.where(even, one, two).astype(F32)
        return jnp.where(at_top, 0.0, above), jnp.where(at_bottom, 0.0, below)

    return up_and_down


def middle_kernel(d, opening, *refs):
    refs = list(refs)
    take = lambda count: [refs.pop(0) for _ in range(count)]
    flags, state, field_one, beside, field_two, from_one, from_two, own_edges = take(8)
    if opening:
        planes, *far_weights = take(6)
    else:
        (plan_x,) = take(1)
    part_x, fields_x, rolled, edges = take(4)
    if opening:
        plan_x, *made_weights = take(4)
        *raw_weights, sems = take(6)
        copies = fetch(far_weights, raw_weights, sems)
    rows, tall = d.rows, d.tall
    is_ocean = flags[0]
    up_and_down = ends(flags)

    if opening:

        @pl.when(is_ocean != 0)
        def _():
            base = d.strip
            pair = up_and_down(from_one[base : base + 16, :], from_two[base : base + 16, :])
            plan_x[...] = jnp.zeros_like(plan_x)
            for step, strip in zip((0, rows + 2), pair):
                for index in range(2):
                    plan_x[pl.ds(step + index, 2 * NK, stride=tall), :] = strip[index * 8 : (index + 1) * 8]

        for plane in range(2 * NK):
            plan_x[plane * tall + 2 : plane * tall + 2 + rows, :] = planes[plane].astype(F32)

    for field in range(NS):
        pair = up_and_down(field_one[field], field_two[field])
        fields_x[field, 0:16, :] = pair[0][rows - 16 : rows]
        fields_x[field, 16 : 16 + rows, :] = beside[field].astype(F32)
        fields_x[field, 16 + rows : 32 + rows, :] = pair[1][0:16]

    @pl.when(is_ocean == 0)
    def _():
        regrid_inside(fields_x, plan_x, part_x, 2, rows // 8, tall)

    @pl.when(is_ocean != 0)
    def _():
        regrid_inside(fields_x, plan_x, part_x, 0, d.tiles, tall)
        upper, lower = up_and_down(from_one[0 : 2 * CH, :], from_two[0 : 2 * CH, :])
        roll_rows(state, upper.astype(BF16), lower.astype(BF16), rolled, d)
        above, below = up_and_down(get_edges(from_one, 2 * CH, d), get_edges(from_two, 2 * CH, d))
        joined = join_rows(above.astype(BF16), get_edges(own_edges, 0, d), below.astype(BF16), d)
        put_edges(edges, 0, joined, d)

    if opening:
        for copy in copies:
            copy.wait()
        prepare(*raw_weights, *made_weights, is_ocean)


def step_kernel(d, opening, closing, *refs):
    refs = list(refs)
    take = lambda count: [refs.pop(0) for _ in range(count)]
    flags, state, wet, from_left, from_right = take(5)
    part_x, fields_x, rolled, edges, plan_x, air_in, first, second, atm_out = take(9)
    if not opening:
        (plan_y,) = take(1)
    if not closing:
        (surface,) = take(1)
    (out,) = take(1)
    if not closing:
        fields, new_edges, one, two = take(4)
    if opening:
        (plan_y,) = take(1)
    fields_y, forcing_x, forcing_y, stack, hidden, side, raw = take(7)
    rows, tall = d.rows, d.tall
    is_ocean, at_top, at_bottom = flags[0], flags[1], flags[2]
    up_and_down = ends(flags)

    if opening:

        @pl.when(is_ocean != 0)
        def _():
            plan_y[...] = jnp.zeros_like(plan_y)
            side_base = 4 * (rows + 32) + 3 * d.edge_rows
            pair = [
                place_columns(from_left[at : at + 16, :], from_right[at : at + 16, :])
                for at in (side_base, side_base + 16 + 2 * NK * rows)
            ]
            for step, strip in zip((0, rows + 2), up_and_down(*pair)):
                for index in range(2):
                    plan_y[pl.ds(step + index, 2 * NK, stride=tall), :] = strip[index * 8 : (index + 1) * 8]
            for plane in range(2 * NK):
                at = side_base + 16 + plane * rows
                plan_y[plane * tall + 2 : plane * tall + 2 + rows, :] = place_columns(
                    from_left[at : at + rows, :], from_right[at : at + rows, :]
                )

    lower_at = 64 + 4 * rows
    for field in range(NS):
        start = 64 + field * rows
        fields_y[field, 16 : 16 + rows, :] = place_columns(
            from_left[start : start + rows, :], from_right[start : start + rows, :]
        )
        pair = [
            place_columns(from_left[at : at + 16, :], from_right[at : at + 16, :])
            for at in (field * 16, lower_at + field * 16)
        ]
        pair = up_and_down(*pair)
        fields_y[field, 0:16, :] = pair[0]
        fields_y[field, 16 + rows : 32 + rows, :] = pair[1]

    def put(row, values):
        if closing:
            raw[pl.ds(row, CH, stride=rows), :] = values
        else:
            out[row] = values.astype(BF16)

    @pl.when(is_ocean == 0)
    def _():
        regrid_beside(
            fields_x, fields_y, plan_x, plan_y, part_x, forcing_x, forcing_y, 2, rows // 8, tall, False
        )
        air(state, put, forcing_x, air_in, atm_out, d)

    @pl.when(is_ocean != 0)
    def _():
        regrid_beside(
            fields_x, fields_y, plan_x, plan_y, part_x, forcing_x, forcing_y, 0, d.tiles, tall, True
        )
        at = 4 * (rows + 32)
        size = d.edge_rows
        joined = []
        for ref in (from_left, from_right):
            one_edges, middle, two_edges = [get_edges(ref, at + index * size, d) for index in range(3)]
            above, below = up_and_down(one_edges, two_edges)
            joined.append(join_rows(above.astype(BF16), middle, below.astype(BF16), d))
        sea(
            state, rolled, get_edges(edges, 0, d), *joined, put, forcing_x, forcing_y,
            first, second, wet, at_top, at_bottom, stack, hidden, side, d,
        )

    if closing:
        out[...] = raw[...].reshape(CH, rows, 128).astype(BF16)
    else:
        emit(out, surface, wet, flags, fields, new_edges, one, two, raw, d)


VMEM = pl.BlockSpec(memory_space=pltpu.VMEM)
HBM = pl.BlockSpec(memory_space=pltpu.HBM)
SMEM = pl.BlockSpec(memory_space=pltpu.SMEM)
PARAMS = pltpu.CompilerParams(vmem_limit_bytes=48 * 1024 * 1024)


def shape(*dims, dtype=BF16):
    return jax.ShapeDtypeStruct(dims, dtype)


def send(x, move):
    names = ("grp", "lat", "lon")
    sizes = [lax.axis_size(name) for name in names]
    pairs = []
    for group in range(sizes[0]):
        for lat in range(sizes[1]):
            for lon in range(sizes[2]):
                to = move(group, lat, lon)
                if to is None or not 0 <= to[1] < sizes[1]:
                    continue
                target = (to[0] * sizes[1] + to[1]) * sizes[2] + to[2] % sizes[2]
                pairs.append(((group * sizes[1] + lat) * sizes[2] + lon, target))
    return lax.ppermute(x, names, pairs)


def swap_rows(x, turn, across):
    count = lax.axis_size("lat")

    def move(group, lat, lon):
        other = ((lat + turn) ^ 1) - turn
        if not 0 <= other < count:
            return 1 - group, lat, lon
        return (1 - group if across else group), other, lon

    return send(x, move)


def exchange(fields, own_edges, one, two, planes, d):
    rows = d.rows
    beside = send(fields, lambda g, i, j: (1 - g, i, j))
    field_one = swap_rows(fields, 0, True)
    field_two = swap_rows(fields, 1, True)
    from_one = swap_rows(one, 0, False)
    from_two = swap_rows(two, 1, False)
    edge_at = slice(2 * CH, d.strip)
    odd = lax.axis_index("lat") % 2
    if rows == 16:
        outer = [field_one, field_two]
    else:
        last = [field[:, rows - 16 :] for field in (field_one, field_two)]
        first = [field[:, :16] for field in (field_one, field_two)]
        outer = [jnp.where(odd == 1, last[0], first[0]), jnp.where(odd == 1, first[1], last[1])]
    packed = [
        outer[0].reshape(64, 128),
        beside.reshape(4 * rows, 128),
        outer[1].reshape(64, 128),
        from_one[edge_at],
        own_edges,
        from_two[edge_at],
    ]
    if planes is not None:
        packed += [from_one[d.strip :], planes.reshape(2 * NK * rows, 128), from_two[d.strip :]]
    packed = jnp.concatenate(packed, axis=0)
    from_left = send(packed, lambda g, i, j: (g, i, j + 1))
    from_right = send(packed, lambda g, i, j: (g, i, j - 1))
    return (field_one, beside, field_two, from_one, from_two), (from_left, from_right)


def local(
    coupled_state, land_mask, regrid_offsets, regrid_weights, surface_proj,
    atm_in, atm_bias, atm_out, ocn_in, ocn_bias, ocn_out,
):
    rows = coupled_state.shape[2]
    assert coupled_state.shape[3] == 128
    d = Dims(rows)
    group = lax.axis_index("grp")
    lat = lax.axis_index("lat")
    flags = jnp.stack(
        [group, lat == 0, lat == lax.axis_size("lat") - 1, lat % 2]
    ).astype(jnp.int32)
    raw_weights = (
        atm_in.T,
        atm_bias.reshape(HA // 128, 128),
        jnp.transpose(ocn_in, (1, 2, 0)),
        ocn_bias[None],
        jnp.transpose(ocn_out, (1, 0, 2)),
    )
    state_shape = shape(rows, CH, 128)
    emitted = [
        shape(NS, rows, 128),
        shape(d.edge_rows, 128),
        shape(d.strip, 128),
        shape(d.strip, 128),
    ]
    raw = pltpu.VMEM((rows * 8, 128), F32)
    turned = pltpu.VMEM((CH * rows, 128), F32)

    def call(kernel, operands, outs, scratch, name, far=()):
        scratch = scratch + [pltpu.VMEM(x.shape, x.dtype) for x in far]
        if far:
            scratch.append(pltpu.SemaphoreType.DMA((len(far),)))

        far = [pltpu.with_memory_space_constraint(x, pltpu.HBM) for x in far]
        return pl.pallas_call(
            kernel,
            out_shape=outs,
            in_specs=[SMEM] + [VMEM] * len(operands) + [HBM] * len(far),
            out_specs=[VMEM] * len(outs),
            scratch_shapes=scratch,
            compiler_params=PARAMS,
            name=name,
        )(flags, *operands, *far)

    state, planes, fields, edges, one, two = call(
        functools.partial(start_kernel, d),
        (),
        [state_shape, shape(2 * NK, rows, 128)] + emitted[:2] + [shape(d.strip + 16, 128)] * 2,
        [raw, pltpu.VMEM((2 * NK * rows, 128), F32), turned],
        "start",
        (coupled_state[0], surface_proj, land_mask, regrid_offsets[0], regrid_weights[0]),
    )

    plan = shape(2 * NK * d.tall, 128, dtype=F32)
    between = [
        shape(NS * d.tall, 128, dtype=F32),
        shape(NS, rows + 32, 128, dtype=F32),
        shape(rows + 4, 3 * CH, 128),
        shape(d.edge_rows, 128),
    ]
    made = [shape(HA, 128), shape(HIDK, 768), shape(9 * CH, HIDP)]
    scratch = [
        pltpu.VMEM((NS, rows + 32, 128), F32),
        pltpu.VMEM((d.tall * 8, 128), F32),
        pltpu.VMEM((d.tall * 8, 128), F32),
        pltpu.VMEM((rows + 4, 256, 128), BF16),
        pltpu.VMEM((rows + 2, HIDP, 128), BF16),
        pltpu.VMEM((768, d.edge), BF16),
    ]

    vertical, horizontal = exchange(fields, edges, one, two, planes, d)
    *shared, plan_x, air_in, first, second = call(
        functools.partial(middle_kernel, d, True),
        (state, *vertical, edges, planes),
        between + [plan] + made,
        [],
        "first_middle",
        raw_weights,
    )
    weights = (air_in, first, second, atm_out)
    state, fields, edges, one, two, plan_y = call(
        functools.partial(step_kernel, d, True, False),
        (state, land_mask, *horizontal, *shared, plan_x, *weights, surface_proj),
        [state_shape] + emitted + [plan],
        scratch + [raw],
        "first_step",
    )

    vertical, horizontal = exchange(fields, edges, one, two, None, d)
    shared = call(
        functools.partial(middle_kernel, d, False),
        (state, *vertical, edges, plan_x),
        between,
        [],
        "second_middle",
    )
    (state,) = call(
        functools.partial(step_kernel, d, False, True),
        (state, land_mask, *horizontal, *shared, plan_x, *weights, plan_y),
        [shape(CH, rows, 128)],
        scratch + [turned],
        "second_step",
    )
    return state[None]


def solution(mesh):
    return jax.shard_map(
        local,
        mesh=mesh,
        in_specs=(
            P("grp", None, "lat", "lon"),
            P("lat", "lon"),
            P("grp", None, None, "lat", "lon"),
            P("grp", None, "lat", "lon"),
            P(),
            P(),
            P(),
            P(),
            P(),
            P(),
            P(),
        ),
        out_specs=P("grp", None, "lat", "lon"),
        check_vma=False,
    )
```

```python
import functools

import jax
import jax.numpy as jnp
from jax import lax
from jax.experimental import pallas as pl
from jax.experimental.pallas import tpu as pltpu
from jax.sharding import PartitionSpec as P

CH = 80
NS = 4
NK = 4
HA = 384
HW = 8
SPAN = 2 * HW + 1
REACH = HW + 2
HIDK = 208
HIDP = 256
F32 = jnp.float32
BF16 = jnp.bfloat16


def roll(x, shift, axis=1):
    size = x.shape[axis]
    if isinstance(shift, int):
        shift = shift % size
        if shift == 0:
            return x
    return pltpu.roll(x, shift, axis)


def lanes(shape):
    return lax.broadcasted_iota(jnp.int32, shape, len(shape) - 1)


def subs(shape):
    return lax.broadcasted_iota(jnp.int32, shape, len(shape) - 2)


class Dims:
    def __init__(self, rows):
        self.rows = rows
        self.block = 32 if rows + 4 <= 32 else 64
        self.edge = 4 * self.block
        self.pieces = self.edge // 128
        self.edge_rows = CH * self.pieces
        self.tiles = -(-(rows + 4) // 8)
        self.tall = 8 * self.tiles
        self.strip = 2 * CH + self.edge_rows


def put_edges(ref, at, edges, d):
    for piece in range(d.pieces):
        ref[at + piece * CH : at + (piece + 1) * CH, :] = edges[:, piece * 128 : (piece + 1) * 128]


def get_edges(ref, at, d):
    return jnp.concatenate(
        [ref[at + piece * CH : at + (piece + 1) * CH, :] for piece in range(d.pieces)], axis=1
    )


def edge_columns(state, d):
    lane = lanes((1, d.edge))
    block = lane // d.block
    row = lane % d.block - 2
    column = jnp.where(block == 0, 126, jnp.where(block == 1, 0, jnp.where(block == 2, 127, 1)))
    own = (row >= 0) & (row < d.rows)
    target = jnp.where(own, column, -1)
    position = subs((128, d.edge))
    places = [
        (position == jnp.where(row == step, target, -1)).astype(F32).astype(BF16)
        for step in range(d.rows)
    ]
    whole = jnp.concatenate([state[step] for step in range(d.rows)], axis=1)
    total = jnp.dot(whole, jnp.concatenate(places, axis=0), preferred_element_type=F32)
    return total.astype(BF16)


def loop(count, unroll, body):
    while count % unroll:
        unroll -= 1

    def several(step, carry):
        for offset in range(unroll):
            body(step * unroll + offset)
        return carry

    lax.fori_loop(0, count // unroll, several, 0)


def pack_columns(values, reach):
    lane = lanes(values[0].shape)
    pitch = 128 // len(values)
    packed = jnp.zeros_like(values[0])
    for index, value in enumerate(values):
        at = index * pitch
        packed = jnp.where((lane >= at) & (lane < at + reach), roll(value, at), packed)
        at += reach
        packed = jnp.where((lane >= at) & (lane < at + reach), roll(value, at + reach - 128), packed)
    return packed


def unpack_columns(left, right, index, count, reach):
    at = index * (128 // count)
    left = roll(left.astype(F32), 128 - at - 2 * reach)
    return jnp.where(lanes(left.shape) < 64, roll(right.astype(F32), -at), left)


def strips(one, two, even, d):
    last = d.rows - 2
    return (one, jnp.where(even, last, 0)), (two, jnp.where(even, 0, last))


def split_bf16(values):
    high = values.astype(BF16).astype(F32)
    mid = (values - high).astype(BF16).astype(F32)
    return high, mid, values - high - mid


def emit(state, surface, wet, flags, fields, own_edges, one, two, raw, d):
    half = d.rows // 2
    is_ocean, even = flags[0] != 0, flags[3] == 0
    gap = jnp.zeros((4, CH), F32)
    terms = []
    for term in split_bf16(surface[flags[0]]):
        terms += [term, gap]
    proj = jnp.concatenate(terms + [gap, gap], axis=0).astype(BF16)
    for step in range(half):
        pair = jnp.concatenate([state[step], state[step + half]], axis=1)
        parts = jnp.dot(proj, pair, preferred_element_type=F32)
        whole = parts[0:8] + parts[8:16] + parts[16:24]
        raw[step * 8 : step * 8 + 8, :] = whole[:, :128]
        raw[(step + half) * 8 : (step + half) * 8 + 8, :] = whole[:, 128:]
    keeping = jnp.where(is_ocean, wet[...].astype(F32), 1.0)
    whole = [raw[pl.ds(field, d.rows, stride=8), :] * keeping for field in range(NS)]
    for field in range(NS):
        fields[field] = whole[field].astype(BF16)
    fields[NS] = pack_columns(whole, REACH).astype(BF16)
    edges = edge_columns(state, d)
    put_edges(own_edges, 0, edges, d)
    row = lanes(edges.shape) % d.block
    downward = jnp.where(row < 2, roll(edges, -d.rows), jnp.zeros_like(edges))
    upward = jnp.where(
        (row >= d.rows + 2) & (row < d.rows + 4), roll(edges, d.rows), jnp.zeros_like(edges)
    )
    for (ref, first), down in zip(strips(one, two, even, d), (even, jnp.logical_not(even))):
        ref[0:CH, :] = state[first]
        ref[CH : 2 * CH, :] = state[first + 1]
        put_edges(ref, 2 * CH, jnp.where(down, downward, upward), d)


def fetch(sources, targets, sems):
    copies = [
        pltpu.make_async_copy(source, target, sems.at[index])
        for index, (source, target) in enumerate(zip(sources, targets))
    ]
    for copy in copies:
        copy.start()
    return copies


def start_kernel(
    d, flags, far_given, far_surface, far_wet, far_offsets, far_weights,
    state, planes, sides, fields, own_edges, one, two,
    raw, tall, turned, given, surface, wet, offsets, weights, sems,
):
    rows = d.rows
    pieces = [pl.ds(at, 16) for at in range(0, CH, 16)]
    copies = fetch(
        [far_given.at[piece] for piece in pieces] + [far_surface, far_wet, far_offsets, far_weights],
        [given.at[piece] for piece in pieces] + [surface, wet, offsets, weights],
        sems,
    )
    for index, piece in enumerate(pieces):
        copies[index].wait()
        turned[index * 16 * rows : (index + 1) * 16 * rows, :] = (
            given[piece].astype(F32).reshape(16 * rows, 128)
        )
    for row in range(rows):
        state[row] = turned[pl.ds(row, CH, stride=rows), :].astype(BF16)
    for copy in copies[len(pieces) :]:
        copy.wait()
    emit(state, surface, wet, flags, fields, own_edges, one, two, raw, d)
    for k in range(NK):
        code = (offsets[0, k] * SPAN + offsets[1, k]).astype(F32)
        tall[k * rows : (k + 1) * rows, :] = code
        tall[(NK + k) * rows : (NK + k + 1) * rows, :] = weights[k]
        planes[k] = code.astype(BF16)
        planes[NK + k] = weights[k].astype(BF16)
    packed = pack_columns([tall[plane * rows : (plane + 1) * rows, :] for plane in range(2 * NK)], 2)
    sides[...] = packed.astype(BF16)
    even = flags[3] == 0
    for (ref, first), down in zip(strips(one, two, even, d), (even, jnp.logical_not(even))):
        strip = [tall[pl.ds(first + step, 2 * NK, stride=rows), :] for step in range(2)]
        ref[d.strip : d.strip + 16, :] = jnp.concatenate(strip, axis=0).astype(BF16)
        ref[d.strip + 16 : d.strip + 32, :] = jnp.where(
            down, packed[rows - 16 : rows], packed[0:16]
        ).astype(BF16)


def decode(code):
    shifted = code.astype(jnp.int32) + (HW * SPAN + HW)
    rows = lax.shift_right_logical(shifted * 241, 12)
    return rows - HW, shifted - rows * SPAN - HW


def along_lanes(values, index):
    numbers = lax.GatherDimensionNumbers(
        offset_dims=(),
        collapsed_slice_dims=(1,),
        start_index_map=(1,),
        operand_batching_dims=(0,),
        start_indices_batching_dims=(0,),
    )
    return lax.gather(
        values, index[..., None], numbers, (1, 1), mode=lax.GatherScatterMode.PROMISE_IN_BOUNDS
    )


def select_rows(sources, start, picks):
    chosen = [[jnp.zeros((8, 128), F32) for _ in range(NS)] for _ in picks]
    for shift in range(-HW, HW + 1):
        at = pl.ds(start + shift, 8)
        used = [any(pick[2][index] is not None for pick in picks) for index in range(len(sources))]
        values = [
            [source[field, at, :] for field in range(NS)] if use else None
            for source, use in zip(sources, used)
        ]
        for slot, (rows, index, allowed) in enumerate(picks):
            here = rows == shift
            for source, within in enumerate(allowed):
                if within is None:
                    continue
                mask = here & within
                for field in range(NS):
                    picked = along_lanes(values[source][field], index)
                    chosen[slot][field] = jnp.where(mask, picked, chosen[slot][field])
    return chosen


def regrid_inside(fields_x, plan_x, part_x, first, tiles, tall):
    lane = lanes((8, 128))
    for step in range(tiles):
        at = first + step * 8
        picks = []
        weights = []
        for k in range(NK):
            rows, cols = decode(plan_x[pl.ds(k * tall + at, 8), :])
            weights.append(plan_x[pl.ds((NK + k) * tall + at, 8), :])
            column = lane + cols
            picks.append((rows, column & 127, ((column >= 0) & (column < 128),)))
        chosen = select_rows((fields_x,), at + 14, picks)
        for field in range(NS):
            total = chosen[0][field] * weights[0]
            for k in range(1, NK):
                total = total + chosen[k][field] * weights[k]
            part_x[pl.ds(field * tall + at, 8), :] = total


def regrid_beside(
    fields_x, fields_y, plan_x, plan_y, part_x, forcing_x, forcing_y, first, tiles, tall, sides
):
    lane = lanes((8, 128))
    part = ((lane + 8) & 127) // 32
    place = ((lane + 8) & 31) - 8
    outer = place >= 8
    inner_column = place & 127
    outer_column = jnp.where(place < 16, place - 16, place + 112)
    edge = (lane < 8) | (lane >= 120)
    for step in range(tiles):
        at = first + step * 8
        code = jnp.zeros((8, 128), F32)
        weight = jnp.zeros((8, 128), F32)
        for k in range(NK):
            edge_code = roll(plan_x[pl.ds(k * tall + at, 8), :], 32 * k)
            edge_weight = roll(plan_x[pl.ds((NK + k) * tall + at, 8), :], 32 * k)
            if sides:
                edge_code = jnp.where(
                    outer, roll(plan_y[pl.ds(k * tall + at, 8), :], 32 * k + 16), edge_code
                )
                edge_weight = jnp.where(
                    outer, roll(plan_y[pl.ds((NK + k) * tall + at, 8), :], 32 * k + 16), edge_weight
                )
            code = jnp.where(part == k, edge_code, code)
            weight = jnp.where(part == k, edge_weight, weight)
        rows, cols = decode(code)
        column = jnp.where(outer, outer_column, inner_column) + cols
        within = (column >= 0) & (column < 128)
        picks = [(rows, column & 127, (within & outer if sides else None, jnp.logical_not(within)))]
        (chosen,) = select_rows((fields_x, fields_y), at + 14, picks)
        for field in range(NS):
            part_sum = chosen[field] * weight
            extra = part_sum
            for k in range(1, NK):
                extra = extra + roll(part_sum, -32 * k)
            total = part_x[pl.ds(field * tall + at, 8), :] + jnp.where(edge, extra, 0.0)
            forcing_x[pl.ds(at * 8 + field, 8, stride=8), :] = total
            forcing_x[pl.ds(at * 8 + field + 4, 8, stride=8), :] = total
            if sides:
                extra = roll(extra, -16)
                forcing_y[pl.ds(at * 8 + field, 8, stride=8), :] = extra
                forcing_y[pl.ds(at * 8 + field + 4, 8, stride=8), :] = extra


def gelu(x):
    scale = (2 / jnp.pi) ** 0.5
    half = 0.5 * x
    return half + half * jnp.tanh(x * (scale + (scale * 0.044715) * (x * x)))


def air(state, out, forcing_x, air_in, atm_out, d):
    half = d.rows // 2
    first = subs((8, 128)) < 4
    blank = jnp.zeros((32, 128), BF16)

    def inputs(row):
        at = (row + 2) * 8
        forced = jnp.where(first, forcing_x[at : at + 8, :], 1.0)
        forced = jnp.concatenate([forced, jnp.zeros_like(forced)], axis=0).astype(BF16)
        return jnp.concatenate([state[row], forced, blank], axis=0)

    for step in range(half):
        pair = jnp.concatenate([inputs(step), inputs(step + half)], axis=1)
        hidden = gelu(jnp.dot(air_in[...], pair, preferred_element_type=F32)).astype(BF16)
        update = jnp.dot(atm_out[...], hidden, preferred_element_type=F32)
        for offset in range(2):
            row = step + offset * half
            change = update[:, offset * 128 : (offset + 1) * 128]
            out(row, state[row].astype(F32) + change)


def edge_forcing(forcing_x, forcing_y, d):
    lane = lanes((8, d.edge))
    block = lane // d.block
    row = lane % d.block

    inner = outer = jnp.zeros((8, d.edge), F32)
    for step in range(d.rows + 4):
        at = pl.ds(step * 8, 8)
        pad = [jnp.zeros((8, 128), F32)] * (d.pieces - 1)
        here = jnp.concatenate([forcing_x[at, :]] + pad, axis=1)
        there = jnp.concatenate([forcing_y[at, :]] + pad, axis=1)
        for index, column in enumerate((126, 0, 127, 1)):
            shift = step + index * d.block - column
            match = (block == index) & (row == step)
            if column in (0, 127):
                inner = jnp.where(match, roll(here, shift), inner)
            outer = jnp.where(match, roll(there, shift), outer)
    return inner, outer


def roll_rows(state, upper, lower, rolled, d):
    def put(row, values):
        rolled[row, 0:CH, :] = roll(values, 1)
        rolled[row, CH : 2 * CH, :] = values
        rolled[row, 2 * CH : 3 * CH, :] = roll(values, -1)

    for step in range(2):
        put(step, upper[step * CH : (step + 1) * CH, :])
        put(d.rows + 2 + step, lower[step * CH : (step + 1) * CH, :])
    for row in range(d.rows):
        put(row + 2, state[row])


def sea(
    state, rolled, edges, left, right, out, forcing_x, forcing_y, ocn_in, ocn_out, wet,
    at_top, at_bottom, stack, hidden, side, d,
):
    rows, block = d.rows, d.block
    lane = lanes((CH, 128))
    spot = lanes((CH, d.edge))
    part = spot // block
    inner = edges
    outer = jnp.where((part == 0) | (part == 2), left, right)

    def sides_of(inner, outer, spot):
        first = spot < block
        return (
            jnp.where(first, outer, roll(inner, -block)),
            jnp.where(first, roll(outer, -2 * block), outer),
            jnp.where(first, roll(inner, -block), roll(outer, -2 * block)),
        )

    beside = sides_of(inner, outer, spot)
    middle = beside[1]
    force_in, force_out = edge_forcing(forcing_x, forcing_y, d)
    beside_forcing = sides_of(force_in, force_out, lanes((8, d.edge)))
    sub = subs((8, d.edge))
    ones = jnp.ones((8, d.edge), F32)
    forced = jnp.concatenate(
        [
            jnp.where(sub < 4, beside_forcing[0], beside_forcing[1]),
            jnp.where(sub < 4, beside_forcing[2], ones),
        ],
        axis=0,
    ).astype(BF16)
    columns = jnp.concatenate(list(beside) + [forced], axis=0)
    for tap in range(3):
        side[tap * 256 : (tap + 1) * 256, :] = roll(columns, -tap)

    sub_row = subs((8, 128))
    lane_row = lanes((8, 128))

    for row in range(rows + 4):
        entry = roll(middle, -row)[:, :128]
        stack[row, 0:CH, :] = jnp.where(lane == 0, entry, rolled[row, 0:CH, :])
        stack[row, CH : 2 * CH, :] = rolled[row, CH : 2 * CH, :]
        entry = roll(middle, 127 - block - row)[:, :128]
        stack[row, 2 * CH : 3 * CH, :] = jnp.where(lane == 127, entry, rolled[row, 2 * CH : 3 * CH, :])
        here, there = forcing_x[row * 8 : row * 8 + 8, :], forcing_y[row * 8 : row * 8 + 8, :]
        before = roll(jnp.where(lane_row == 127, there, here), 1)
        after = roll(jnp.where(lane_row == 0, there, here), -1)
        stack[row, 3 * CH : 256, :] = jnp.concatenate(
            [jnp.where(sub_row < 4, before, here), jnp.where(sub_row < 4, after, 1.0)], axis=0
        ).astype(BF16)

    pairs = (rows + 2) // 2

    for step in range(pairs):
        taps = jnp.concatenate(
            [
                stack[step : step + 3].reshape(3 * 256, 128),
                stack[step + pairs : step + pairs + 3].reshape(3 * 256, 128),
            ],
            axis=1,
        )
        active = gelu(jnp.dot(ocn_in[...], taps, preferred_element_type=F32))
        low, high = active[:, :128], active[:, 128:]
        if step == 0:
            low = jnp.where(at_top != 0, 0.0, low)
        if step == pairs - 1:
            high = jnp.where(at_bottom != 0, 0.0, high)
        hidden[step, 0:HIDK, :] = low.astype(BF16)
        hidden[step + pairs, 0:HIDK, :] = high.astype(BF16)
        blank = jnp.zeros((HIDP - HIDK, 128), BF16)
        hidden[step, HIDK:HIDP, :] = blank
        hidden[step + pairs, HIDK:HIDP, :] = blank

    product = jnp.dot(ocn_in[...], side[...], preferred_element_type=F32)
    spot = lanes((1, d.edge)) % block
    gone = ((spot == 0) & (at_top != 0)) | ((spot == rows + 1) & (at_bottom != 0))
    active = jnp.where(gone, 0.0, gelu(product)).astype(BF16)
    active = jnp.concatenate([active, jnp.zeros((HIDP - HIDK, d.edge), BF16)], axis=0)

    def taps_of(slices):
        total = None
        for tap, values in enumerate(slices):
            weights = ocn_out[tap * 3 * CH : (tap + 1) * 3 * CH, :]
            product = jnp.dot(weights, values, preferred_element_type=F32)
            total = product if total is None else total + product
        return total

    partial = taps_of([roll(active, -tap) for tap in range(3)])
    from_left, from_right = partial[0:CH], partial[2 * CH : 3 * CH]
    half = rows // 2
    for step in range(half):
        product = taps_of(
            [
                jnp.concatenate([hidden[step + tap], hidden[step + half + tap]], axis=1)
                for tap in range(3)
            ]
        )
        for offset in range(2):
            row = step + offset * half
            sums = product[:, offset * 128 : (offset + 1) * 128]
            entry = roll(from_left, -row)[:, :128]
            total = sums[CH : 2 * CH] + jnp.where(lane == 0, entry, roll(sums[0:CH], 1))
            entry = roll(from_right, 127 - block - row)[:, :128]
            total = total + jnp.where(lane == 127, entry, roll(sums[2 * CH : 3 * CH], -1))
            update = total * wet[row : row + 1, :].astype(F32)
            out(row, state[row].astype(F32) + update)


def prepare(atm_in, atm_bias, ocn_in, ocn_bias, ocn_out, air_in, first, second, is_ocean):
    def bias_rows(ref, width):
        row = jnp.concatenate([ref[index : index + 1, :] for index in range(ref.shape[0])], axis=1)
        terms = list(split_bf16(row)) + [jnp.zeros_like(row)]
        bias = jnp.concatenate(terms, axis=0)
        return jnp.pad(bias, ((0, 0), (0, width - bias.shape[1])))

    @pl.when(is_ocean == 0)
    def _():
        columns = jnp.concatenate(
            [atm_in[...].astype(F32), bias_rows(atm_bias, HA), jnp.zeros((40, HA), F32)], axis=0
        )
        air_in[...] = columns.T.astype(BF16)

    @pl.when(is_ocean != 0)
    def _():
        bias = bias_rows(ocn_bias, 256)
        count = ocn_in.shape[2]
        for tap in range(3):
            whole = [ocn_in[3 * tap + side].astype(F32) for side in range(3)]
            whole = [jnp.pad(values, ((0, 0), (0, 256 - count))) for values in whole]
            rows = [values[:CH] for values in whole] + [values[CH:] for values in whole]
            rows.append(bias if tap == 0 else jnp.zeros((4, 256), F32))
            columns = jnp.concatenate(rows, axis=0).T
            first[:, tap * 256 : (tap + 1) * 256] = columns[:HIDK].astype(BF16)
        for tap in range(9):
            values = ocn_out[tap].astype(F32)
            second[tap * CH : (tap + 1) * CH, :] = jnp.pad(
                values, ((0, 0), (0, HIDP - count))
            ).astype(BF16)


def ends(flags):
    at_top, at_bottom, even = flags[1] != 0, flags[2] != 0, flags[3] == 0

    def up_and_down(one, two):
        above = jnp.where(even, two, one).astype(F32)
        below = jnp.where(even, one, two).astype(F32)
        return jnp.where(at_top, 0.0, above), jnp.where(at_bottom, 0.0, below)

    return up_and_down


def middle_kernel(d, opening, *refs):
    refs = list(refs)
    take = lambda count: [refs.pop(0) for _ in range(count)]
    flags, state, field_one, beside, field_two, from_one, from_two = take(7)
    if opening:
        planes, *far_weights = take(6)
    else:
        (plan_x,) = take(1)
    part_x, fields_x, rolled = take(3)
    if opening:
        plan_x, *made_weights = take(4)
        *raw_weights, sems = take(6)
        copies = fetch(far_weights, raw_weights, sems)
    rows, tall = d.rows, d.tall
    is_ocean = flags[0]
    up_and_down = ends(flags)

    if opening:

        @pl.when(is_ocean != 0)
        def _():
            base = d.strip
            pair = up_and_down(from_one[base : base + 16, :], from_two[base : base + 16, :])
            plan_x[...] = jnp.zeros_like(plan_x)
            for step, strip in zip((0, rows + 2), pair):
                for index in range(2):
                    plan_x[pl.ds(step + index, 2 * NK, stride=tall), :] = strip[index * 8 : (index + 1) * 8]

        for plane in range(2 * NK):
            plan_x[plane * tall + 2 : plane * tall + 2 + rows, :] = planes[plane].astype(F32)

    for field in range(NS):
        pair = up_and_down(field_one[field], field_two[field])
        fields_x[field, 0:16, :] = pair[0][rows - 16 : rows]
        fields_x[field, 16 : 16 + rows, :] = beside[field].astype(F32)
        fields_x[field, 16 + rows : 32 + rows, :] = pair[1][0:16]

    @pl.when(is_ocean == 0)
    def _():
        regrid_inside(fields_x, plan_x, part_x, 2, rows // 8, tall)

    @pl.when(is_ocean != 0)
    def _():
        regrid_inside(fields_x, plan_x, part_x, 0, d.tiles, tall)
        upper, lower = up_and_down(from_one[0 : 2 * CH, :], from_two[0 : 2 * CH, :])
        roll_rows(state, upper.astype(BF16), lower.astype(BF16), rolled, d)

    if opening:
        for copy in copies:
            copy.wait()
        prepare(*raw_weights, *made_weights, is_ocean)


def step_kernel(d, opening, closing, *refs):
    refs = list(refs)
    take = lambda count: [refs.pop(0) for _ in range(count)]
    flags, state, wet, from_left, from_right = take(5)
    part_x, fields_x, rolled, edges, plan_x, air_in, first, second, atm_out = take(9)
    if not opening:
        (plan_y,) = take(1)
    if not closing:
        (surface,) = take(1)
    (out,) = take(1)
    if not closing:
        fields, new_edges, one, two = take(4)
    if opening:
        (plan_y,) = take(1)
    fields_y, forcing_x, forcing_y, stack, hidden, side, raw = take(7)
    rows, tall = d.rows, d.tall
    is_ocean, at_top, at_bottom = flags[0], flags[1], flags[2]
    up_and_down = ends(flags)

    if opening:

        @pl.when(is_ocean != 0)
        def _():
            plan_y[...] = jnp.zeros_like(plan_y)
            base = rows + 32 + d.edge_rows
            parts = [
                (ref[base : base + 16, :], ref[base + 16 + rows : base + 32 + rows, :],
                 ref[base + 16 : base + 16 + rows, :])
                for ref in (from_left, from_right)
            ]
            for plane in range(2 * NK):
                first_end, second_end, own = [
                    unpack_columns(left, right, plane, 2 * NK, 2) for left, right in zip(*parts)
                ]
                above, below = up_and_down(first_end, second_end)
                at = plane * tall
                plan_y[at : at + 2, :] = above[14:16]
                plan_y[at + 2 : at + 2 + rows, :] = own
                plan_y[at + 2 + rows : at + 4 + rows, :] = below[0:2]

    parts = [
        (ref[0:16, :], ref[16 + rows : 32 + rows, :], ref[16 : 16 + rows, :])
        for ref in (from_left, from_right)
    ]
    for field in range(NS):
        first_end, second_end, own = [
            unpack_columns(left, right, field, NS, REACH) for left, right in zip(*parts)
        ]
        above, below = up_and_down(first_end, second_end)
        fields_y[field, 0:16, :] = above
        fields_y[field, 16 : 16 + rows, :] = own
        fields_y[field, 16 + rows : 32 + rows, :] = below

    def put(row, values):
        if closing:
            raw[pl.ds(row, CH, stride=rows), :] = values
        else:
            out[row] = values.astype(BF16)

    @pl.when(is_ocean == 0)
    def _():
        regrid_beside(
            fields_x, fields_y, plan_x, plan_y, part_x, forcing_x, forcing_y, 2, rows // 8, tall, False
        )
        air(state, put, forcing_x, air_in, atm_out, d)

    @pl.when(is_ocean != 0)
    def _():
        regrid_beside(
            fields_x, fields_y, plan_x, plan_y, part_x, forcing_x, forcing_y, 0, d.tiles, tall, True
        )
        joined = [get_edges(ref, rows + 32, d) for ref in (from_left, from_right)]
        sea(
            state, rolled, get_edges(edges, 0, d), *joined, put, forcing_x, forcing_y,
            first, second, wet, at_top, at_bottom, stack, hidden, side, d,
        )

    if closing:
        out[...] = raw[...].reshape(CH, rows, 128).astype(BF16)
    else:
        emit(out, surface, wet, flags, fields, new_edges, one, two, raw, d)


VMEM = pl.BlockSpec(memory_space=pltpu.VMEM)
HBM = pl.BlockSpec(memory_space=pltpu.HBM)
SMEM = pl.BlockSpec(memory_space=pltpu.SMEM)
PARAMS = pltpu.CompilerParams(vmem_limit_bytes=48 * 1024 * 1024)


def shape(*dims, dtype=BF16):
    return jax.ShapeDtypeStruct(dims, dtype)


def send(x, move):
    names = ("grp", "lat", "lon")
    sizes = [lax.axis_size(name) for name in names]
    pairs = []
    for group in range(sizes[0]):
        for lat in range(sizes[1]):
            for lon in range(sizes[2]):
                to = move(group, lat, lon)
                if to is None or not 0 <= to[1] < sizes[1]:
                    continue
                target = (to[0] * sizes[1] + to[1]) * sizes[2] + to[2] % sizes[2]
                pairs.append(((group * sizes[1] + lat) * sizes[2] + lon, target))
    return lax.ppermute(x, names, pairs)


def swap_rows(x, turn, across):
    count = lax.axis_size("lat")

    def move(group, lat, lon):
        other = ((lat + turn) ^ 1) - turn
        if not 0 <= other < count:
            return 1 - group, lat, lon
        return (1 - group if across else group), other, lon

    return send(x, move)


def exchange(fields, own_edges, one, two, sides, d):
    rows = d.rows
    from_one = swap_rows(one, 0, False)
    from_two = swap_rows(two, 1, False)
    field_one = swap_rows(fields, 0, True)
    field_two = swap_rows(fields, 1, True)
    beside = send(fields, lambda g, i, j: (1 - g, i, j))
    lat, count = lax.axis_index("lat"), lax.axis_size("lat")
    odd = lat % 2 == 1
    edges = own_edges
    for turn, ref in ((0, from_one), (1, from_two)):
        other = ((lat + turn) ^ 1) - turn
        there = (other >= 0) & (other < count)
        edges = edges + jnp.where(there, ref[2 * CH : d.strip], 0)
    outer = [field_one[NS], field_two[NS]]
    if rows != 16:
        outer = [
            jnp.where(odd, outer[0][rows - 16 :], outer[0][:16]),
            jnp.where(odd, outer[1][:16], outer[1][rows - 16 :]),
        ]
    packed = [outer[0], beside[NS], outer[1], edges]
    if sides is not None:
        packed += [from_one[d.strip + 16 :], sides, from_two[d.strip + 16 :]]
    packed = jnp.concatenate(packed, axis=0)
    from_left = send(packed, lambda g, i, j: (g, i, j + 1))
    from_right = send(packed, lambda g, i, j: (g, i, j - 1))
    return (field_one, beside, field_two, from_one, from_two), (from_left, from_right), edges


def local(
    coupled_state, land_mask, regrid_offsets, regrid_weights, surface_proj,
    atm_in, atm_bias, atm_out, ocn_in, ocn_bias, ocn_out,
):
    rows = coupled_state.shape[2]
    assert coupled_state.shape[3] == 128
    d = Dims(rows)
    group = lax.axis_index("grp")
    lat = lax.axis_index("lat")
    flags = jnp.stack(
        [group, lat == 0, lat == lax.axis_size("lat") - 1, lat % 2]
    ).astype(jnp.int32)
    raw_weights = (
        atm_in.T,
        atm_bias.reshape(HA // 128, 128),
        jnp.transpose(ocn_in, (1, 2, 0)),
        ocn_bias[None],
        jnp.transpose(ocn_out, (1, 0, 2)),
    )
    state_shape = shape(rows, CH, 128)
    emitted = [
        shape(NS + 1, rows, 128),
        shape(d.edge_rows, 128),
        shape(d.strip, 128),
        shape(d.strip, 128),
    ]
    raw = pltpu.VMEM((rows * 8, 128), F32)
    turned = pltpu.VMEM((CH * rows, 128), F32)

    def call(kernel, operands, outs, scratch, name, far=()):
        scratch = scratch + [pltpu.VMEM(x.shape, x.dtype) for x in far]
        if far:
            scratch.append(pltpu.SemaphoreType.DMA((len(far) + CH // 16,)))

        far = [pltpu.with_memory_space_constraint(x, pltpu.HBM) for x in far]
        return pl.pallas_call(
            kernel,
            out_shape=outs,
            in_specs=[SMEM] + [VMEM] * len(operands) + [HBM] * len(far),
            out_specs=[VMEM] * len(outs),
            scratch_shapes=scratch,
            compiler_params=PARAMS,
            name=name,
        )(flags, *operands, *far)

    state, planes, sides, fields, edges, one, two = call(
        functools.partial(start_kernel, d),
        (),
        [state_shape, shape(2 * NK, rows, 128), shape(rows, 128)]
        + emitted[:2]
        + [shape(d.strip + 32, 128)] * 2,
        [raw, pltpu.VMEM((2 * NK * rows, 128), F32), turned],
        "start",
        (coupled_state[0], surface_proj, land_mask, regrid_offsets[0], regrid_weights[0]),
    )

    plan = shape(2 * NK * d.tall, 128, dtype=F32)
    between = [
        shape(NS * d.tall, 128, dtype=F32),
        shape(NS, rows + 32, 128, dtype=F32),
        shape(rows + 4, 3 * CH, 128),
    ]
    made = [shape(HA, 128), shape(HIDK, 768), shape(9 * CH, HIDP)]
    scratch = [
        pltpu.VMEM((NS, rows + 32, 128), F32),
        pltpu.VMEM((d.tall * 8, 128), F32),
        pltpu.VMEM((d.tall * 8, 128), F32),
        pltpu.VMEM((rows + 4, 256, 128), BF16),
        pltpu.VMEM((rows + 2, HIDP, 128), BF16),
        pltpu.VMEM((768, d.edge), BF16),
    ]

    vertical, horizontal, edges = exchange(fields, edges, one, two, sides, d)
    *shared, plan_x, air_in, first, second = call(
        functools.partial(middle_kernel, d, True),
        (state, *vertical, planes),
        between + [plan] + made,
        [],
        "first_middle",
        raw_weights,
    )
    weights = (air_in, first, second, atm_out)
    state, fields, edges, one, two, plan_y = call(
        functools.partial(step_kernel, d, True, False),
        (state, land_mask, *horizontal, *shared, edges, plan_x, *weights, surface_proj),
        [state_shape] + emitted + [plan],
        scratch + [raw],
        "first_step",
    )

    vertical, horizontal, edges = exchange(fields, edges, one, two, None, d)
    shared = call(
        functools.partial(middle_kernel, d, False),
        (state, *vertical, plan_x),
        between,
        [],
        "second_middle",
    )
    (state,) = call(
        functools.partial(step_kernel, d, False, True),
        (state, land_mask, *horizontal, *shared, edges, plan_x, *weights, plan_y),
        [shape(CH, rows, 128)],
        scratch + [turned],
        "second_step",
    )
    return state[None]


def solution(mesh):
    return jax.shard_map(
        local,
        mesh=mesh,
        in_specs=(
            P("grp", None, "lat", "lon"),
            P("lat", "lon"),
            P("grp", None, None, "lat", "lon"),
            P("grp", None, "lat", "lon"),
            P(),
            P(),
            P(),
            P(),
            P(),
            P(),
            P(),
        ),
        out_specs=P("grp", None, "lat", "lon"),
        check_vma=False,
    )
```

```python
import functools

import jax
import jax.numpy as jnp
from jax import lax
from jax.experimental import pallas as pl
from jax.experimental.pallas import tpu as pltpu
from jax.sharding import PartitionSpec as P

CH = 80
NS = 4
NK = 4
HA = 384
HW = 8
SPAN = 2 * HW + 1
REACH = HW + 2
HIDK = 208
HIDP = 256
F32 = jnp.float32
BF16 = jnp.bfloat16


def roll(x, shift, axis=1):
    size = x.shape[axis]
    if isinstance(shift, int):
        shift = shift % size
        if shift == 0:
            return x
    return pltpu.roll(x, shift, axis)


def lanes(shape):
    return lax.broadcasted_iota(jnp.int32, shape, len(shape) - 1)


def subs(shape):
    return lax.broadcasted_iota(jnp.int32, shape, len(shape) - 2)


class Dims:
    def __init__(self, rows):
        self.rows = rows
        self.block = 32 if rows + 4 <= 32 else 64
        self.edge = 4 * self.block
        self.pieces = self.edge // 128
        self.edge_rows = CH * self.pieces
        self.tiles = -(-(rows + 4) // 8)
        self.tall = 8 * self.tiles
        self.strip = 2 * CH + self.edge_rows


def put_edges(ref, at, edges, d):
    for piece in range(d.pieces):
        ref[at + piece * CH : at + (piece + 1) * CH, :] = edges[:, piece * 128 : (piece + 1) * 128]


def get_edges(ref, at, d):
    return jnp.concatenate(
        [ref[at + piece * CH : at + (piece + 1) * CH, :] for piece in range(d.pieces)], axis=1
    )


def edge_columns(state, d):
    lane = lanes((1, d.edge))
    block = lane // d.block
    row = lane % d.block - 2
    column = jnp.where(block == 0, 126, jnp.where(block == 1, 0, jnp.where(block == 2, 127, 1)))
    own = (row >= 0) & (row < d.rows)
    target = jnp.where(own, column, -1)
    position = subs((128, d.edge))
    places = [
        (position == jnp.where(row == step, target, -1)).astype(F32).astype(BF16)
        for step in range(d.rows)
    ]
    whole = jnp.concatenate([state[step] for step in range(d.rows)], axis=1)
    total = jnp.dot(whole, jnp.concatenate(places, axis=0), preferred_element_type=F32)
    return total.astype(BF16)


def loop(count, unroll, body):
    while count % unroll:
        unroll -= 1

    def several(step, carry):
        for offset in range(unroll):
            body(step * unroll + offset)
        return carry

    lax.fori_loop(0, count // unroll, several, 0)


def pack_columns(values, reach):
    lane = lanes(values[0].shape)
    pitch = 128 // len(values)
    packed = jnp.zeros_like(values[0])
    for index, value in enumerate(values):
        at = index * pitch
        packed = jnp.where((lane >= at) & (lane < at + reach), roll(value, at), packed)
        at += reach
        packed = jnp.where((lane >= at) & (lane < at + reach), roll(value, at + reach - 128), packed)
    return packed


def unpack_columns(left, right, index, count, reach):
    at = index * (128 // count)
    left = roll(left.astype(F32), 128 - at - 2 * reach)
    return jnp.where(lanes(left.shape) < 64, roll(right.astype(F32), -at), left)


def strips(one, two, even, d):
    last = d.rows - 2
    return (one, jnp.where(even, last, 0)), (two, jnp.where(even, 0, last))


def split_bf16(values):
    high = values.astype(BF16).astype(F32)
    mid = (values - high).astype(BF16).astype(F32)
    return high, mid, values - high - mid


def emit(state, surface, wet, flags, fields, own_edges, one, two, raw, d):
    half = d.rows // 2
    is_ocean, even = flags[0] != 0, flags[3] == 0
    gap = jnp.zeros((4, CH), F32)
    terms = []
    for term in split_bf16(surface[flags[0]]):
        terms += [term, gap]
    proj = jnp.concatenate(terms + [gap, gap], axis=0).astype(BF16)
    for step in range(half):
        pair = jnp.concatenate([state[step], state[step + half]], axis=1)
        parts = jnp.dot(proj, pair, preferred_element_type=F32)
        whole = parts[0:8] + parts[8:16] + parts[16:24]
        raw[step * 8 : step * 8 + 8, :] = whole[:, :128]
        raw[(step + half) * 8 : (step + half) * 8 + 8, :] = whole[:, 128:]
    keeping = jnp.where(is_ocean, wet[...].astype(F32), 1.0)
    whole = [raw[pl.ds(field, d.rows, stride=8), :] * keeping for field in range(NS)]
    for field in range(NS):
        fields[field] = whole[field].astype(BF16)
    fields[NS] = pack_columns(whole, REACH).astype(BF16)
    edges = edge_columns(state, d)
    put_edges(own_edges, 0, edges, d)
    row = lanes(edges.shape) % d.block
    downward = jnp.where(row < 2, roll(edges, -d.rows), jnp.zeros_like(edges))
    upward = jnp.where(
        (row >= d.rows + 2) & (row < d.rows + 4), roll(edges, d.rows), jnp.zeros_like(edges)
    )
    for (ref, first), down in zip(strips(one, two, even, d), (even, jnp.logical_not(even))):
        ref[0:CH, :] = state[first]
        ref[CH : 2 * CH, :] = state[first + 1]
        put_edges(ref, 2 * CH, jnp.where(down, downward, upward), d)


def fetch(sources, targets, sems):
    copies = [
        pltpu.make_async_copy(source, target, sems.at[index])
        for index, (source, target) in enumerate(zip(sources, targets))
    ]
    for copy in copies:
        copy.start()
    return copies


def start_kernel(
    d, flags, far_given, far_surface, far_wet, far_offsets, far_weights,
    state, planes, sides, fields, own_edges, one, two,
    raw, tall, turned, given, surface, wet, offsets, weights, sems,
):
    rows = d.rows
    pieces = [pl.ds(at, 16) for at in range(0, CH, 16)]
    copies = fetch(
        [far_given.at[piece] for piece in pieces] + [far_surface, far_wet, far_offsets, far_weights],
        [given.at[piece] for piece in pieces] + [surface, wet, offsets, weights],
        sems,
    )
    for index, piece in enumerate(pieces):
        copies[index].wait()
        turned[index * 16 * rows : (index + 1) * 16 * rows, :] = (
            given[piece].astype(F32).reshape(16 * rows, 128)
        )
    for row in range(rows):
        state[row] = turned[pl.ds(row, CH, stride=rows), :].astype(BF16)
    for copy in copies[len(pieces) :]:
        copy.wait()
    emit(state, surface, wet, flags, fields, own_edges, one, two, raw, d)
    for k in range(NK):
        code = (offsets[0, k] * SPAN + offsets[1, k]).astype(F32)
        tall[k * rows : (k + 1) * rows, :] = code
        tall[(NK + k) * rows : (NK + k + 1) * rows, :] = weights[k]
        planes[k] = code.astype(BF16)
        planes[NK + k] = weights[k].astype(BF16)
    packed = pack_columns([tall[plane * rows : (plane + 1) * rows, :] for plane in range(2 * NK)], 2)
    sides[...] = packed.astype(BF16)
    even = flags[3] == 0
    for (ref, first), down in zip(strips(one, two, even, d), (even, jnp.logical_not(even))):
        strip = [tall[pl.ds(first + step, 2 * NK, stride=rows), :] for step in range(2)]
        ref[d.strip : d.strip + 16, :] = jnp.concatenate(strip, axis=0).astype(BF16)
        ref[d.strip + 16 : d.strip + 32, :] = jnp.where(
            down, packed[rows - 16 : rows], packed[0:16]
        ).astype(BF16)


def decode(code):
    shifted = code.astype(jnp.int32) + (HW * SPAN + HW)
    rows = lax.shift_right_logical(shifted * 241, 12)
    return rows - HW, shifted - rows * SPAN - HW


def along_lanes(values, index):
    numbers = lax.GatherDimensionNumbers(
        offset_dims=(),
        collapsed_slice_dims=(1,),
        start_index_map=(1,),
        operand_batching_dims=(0,),
        start_indices_batching_dims=(0,),
    )
    return lax.gather(
        values, index[..., None], numbers, (1, 1), mode=lax.GatherScatterMode.PROMISE_IN_BOUNDS
    )


def select_rows(sources, start, picks):
    chosen = [[jnp.zeros((8, 128), F32) for _ in range(NS)] for _ in picks]
    for shift in range(-HW, HW + 1):
        at = pl.ds(start + shift, 8)
        used = [any(pick[2][index] is not None for pick in picks) for index in range(len(sources))]
        values = [
            [source[field, at, :] for field in range(NS)] if use else None
            for source, use in zip(sources, used)
        ]
        for slot, (rows, index, allowed) in enumerate(picks):
            here = rows == shift
            for source, within in enumerate(allowed):
                if within is None:
                    continue
                mask = here & within
                for field in range(NS):
                    picked = along_lanes(values[source][field], index)
                    chosen[slot][field] = jnp.where(mask, picked, chosen[slot][field])
    return chosen


def regrid_inside(fields_x, plan_x, part_x, first, tiles, tall):
    lane = lanes((8, 128))
    for step in range(tiles):
        at = first + step * 8
        picks = []
        weights = []
        for k in range(NK):
            rows, cols = decode(plan_x[pl.ds(k * tall + at, 8), :])
            weights.append(plan_x[pl.ds((NK + k) * tall + at, 8), :])
            column = lane + cols
            picks.append((rows, column & 127, ((column >= 0) & (column < 128),)))
        chosen = select_rows((fields_x,), at + 14, picks)
        for field in range(NS):
            total = chosen[0][field] * weights[0]
            for k in range(1, NK):
                total = total + chosen[k][field] * weights[k]
            part_x[pl.ds(field * tall + at, 8), :] = total


def regrid_beside(
    fields_x, fields_y, plan_x, plan_y, part_x, forcing_x, forcing_y, first, tiles, tall, sides
):
    lane = lanes((8, 128))
    part = ((lane + 8) & 127) // 32
    place = ((lane + 8) & 31) - 8
    outer = place >= 8
    inner_column = place & 127
    outer_column = jnp.where(place < 16, place - 16, place + 112)
    edge = (lane < 8) | (lane >= 120)
    for step in range(tiles):
        at = first + step * 8
        code = jnp.zeros((8, 128), F32)
        weight = jnp.zeros((8, 128), F32)
        for k in range(NK):
            edge_code = roll(plan_x[pl.ds(k * tall + at, 8), :], 32 * k)
            edge_weight = roll(plan_x[pl.ds((NK + k) * tall + at, 8), :], 32 * k)
            if sides:
                edge_code = jnp.where(
                    outer, roll(plan_y[pl.ds(k * tall + at, 8), :], 32 * k + 16), edge_code
                )
                edge_weight = jnp.where(
                    outer, roll(plan_y[pl.ds((NK + k) * tall + at, 8), :], 32 * k + 16), edge_weight
                )
            code = jnp.where(part == k, edge_code, code)
            weight = jnp.where(part == k, edge_weight, weight)
        rows, cols = decode(code)
        column = jnp.where(outer, outer_column, inner_column) + cols
        within = (column >= 0) & (column < 128)
        picks = [(rows, column & 127, (within & outer if sides else None, jnp.logical_not(within)))]
        (chosen,) = select_rows((fields_x, fields_y), at + 14, picks)
        for field in range(NS):
            part_sum = chosen[field] * weight
            extra = part_sum
            for k in range(1, NK):
                extra = extra + roll(part_sum, -32 * k)
            total = part_x[pl.ds(field * tall + at, 8), :] + jnp.where(edge, extra, 0.0)
            forcing_x[pl.ds(at * 8 + field, 8, stride=8), :] = total
            forcing_x[pl.ds(at * 8 + field + 4, 8, stride=8), :] = total
            if sides:
                extra = roll(extra, -16)
                forcing_y[pl.ds(at * 8 + field, 8, stride=8), :] = extra
                forcing_y[pl.ds(at * 8 + field + 4, 8, stride=8), :] = extra


def gelu(x):
    scale = (2 / jnp.pi) ** 0.5
    half = 0.5 * x
    return half + half * jnp.tanh(x * (scale + (scale * 0.044715) * (x * x)))


def air(state, out, forcing_x, air_in, atm_out, d):
    half = d.rows // 2
    first = subs((8, 128)) < 4
    blank = jnp.zeros((32, 128), BF16)

    def inputs(row):
        at = (row + 2) * 8
        forced = jnp.where(first, forcing_x[at : at + 8, :], 1.0)
        forced = jnp.concatenate([forced, jnp.zeros_like(forced)], axis=0).astype(BF16)
        return jnp.concatenate([state[row], forced, blank], axis=0)

    for step in range(half):
        pair = jnp.concatenate([inputs(step), inputs(step + half)], axis=1)
        hidden = gelu(jnp.dot(air_in[...], pair, preferred_element_type=F32)).astype(BF16)
        update = jnp.dot(atm_out[...], hidden, preferred_element_type=F32)
        for offset in range(2):
            row = step + offset * half
            change = update[:, offset * 128 : (offset + 1) * 128]
            out(row, state[row].astype(F32) + change)


def edge_forcing(forcing_x, forcing_y, d):
    lane = lanes((8, d.edge))
    block = lane // d.block
    row = lane % d.block

    inner = outer = jnp.zeros((8, d.edge), F32)
    for step in range(d.rows + 4):
        at = pl.ds(step * 8, 8)
        pad = [jnp.zeros((8, 128), F32)] * (d.pieces - 1)
        here = jnp.concatenate([forcing_x[at, :]] + pad, axis=1)
        there = jnp.concatenate([forcing_y[at, :]] + pad, axis=1)
        for index, column in enumerate((126, 0, 127, 1)):
            shift = step + index * d.block - column
            match = (block == index) & (row == step)
            if column in (0, 127):
                inner = jnp.where(match, roll(here, shift), inner)
            outer = jnp.where(match, roll(there, shift), outer)
    return inner, outer


def roll_rows(state, upper, lower, rolled, d):
    def put(row, values):
        rolled[row, 0:CH, :] = roll(values, 1)
        rolled[row, CH : 2 * CH, :] = values
        rolled[row, 2 * CH : 3 * CH, :] = roll(values, -1)

    for step in range(2):
        put(step, upper[step * CH : (step + 1) * CH, :])
        put(d.rows + 2 + step, lower[step * CH : (step + 1) * CH, :])
    for row in range(d.rows):
        put(row + 2, state[row])


def sea(
    state, rolled, edges, left, right, out, forcing_x, forcing_y, ocn_in, ocn_out, wet,
    at_top, at_bottom, stack, hidden, side, d,
):
    rows, block = d.rows, d.block
    lane = lanes((CH, 128))
    spot = lanes((CH, d.edge))
    part = spot // block
    inner = edges
    outer = jnp.where((part == 0) | (part == 2), left, right)

    def sides_of(inner, outer, spot):
        first = spot < block
        return (
            jnp.where(first, outer, roll(inner, -block)),
            jnp.where(first, roll(outer, -2 * block), outer),
            jnp.where(first, roll(inner, -block), roll(outer, -2 * block)),
        )

    beside = sides_of(inner, outer, spot)
    middle = beside[1]
    force_in, force_out = edge_forcing(forcing_x, forcing_y, d)
    beside_forcing = sides_of(force_in, force_out, lanes((8, d.edge)))
    sub = subs((8, d.edge))
    ones = jnp.ones((8, d.edge), F32)
    forced = jnp.concatenate(
        [
            jnp.where(sub < 4, beside_forcing[0], beside_forcing[1]),
            jnp.where(sub < 4, beside_forcing[2], ones),
        ],
        axis=0,
    ).astype(BF16)
    columns = jnp.concatenate(list(beside) + [forced], axis=0)
    for tap in range(3):
        side[tap * 256 : (tap + 1) * 256, :] = roll(columns, -tap)

    sub_row = subs((8, 128))
    lane_row = lanes((8, 128))

    for row in range(rows + 4):
        entry = roll(middle, -row)[:, :128]
        stack[row, 0:CH, :] = jnp.where(lane == 0, entry, rolled[row, 0:CH, :])
        stack[row, CH : 2 * CH, :] = rolled[row, CH : 2 * CH, :]
        entry = roll(middle, 127 - block - row)[:, :128]
        stack[row, 2 * CH : 3 * CH, :] = jnp.where(lane == 127, entry, rolled[row, 2 * CH : 3 * CH, :])
        here, there = forcing_x[row * 8 : row * 8 + 8, :], forcing_y[row * 8 : row * 8 + 8, :]
        before = roll(jnp.where(lane_row == 127, there, here), 1)
        after = roll(jnp.where(lane_row == 0, there, here), -1)
        stack[row, 3 * CH : 256, :] = jnp.concatenate(
            [jnp.where(sub_row < 4, before, here), jnp.where(sub_row < 4, after, 1.0)], axis=0
        ).astype(BF16)

    pairs = (rows + 2) // 2

    for step in range(pairs):
        taps = jnp.concatenate(
            [
                stack[step : step + 3].reshape(3 * 256, 128),
                stack[step + pairs : step + pairs + 3].reshape(3 * 256, 128),
            ],
            axis=1,
        )
        active = gelu(jnp.dot(ocn_in[...], taps, preferred_element_type=F32))
        low, high = active[:, :128], active[:, 128:]
        if step == 0:
            low = jnp.where(at_top != 0, 0.0, low)
        if step == pairs - 1:
            high = jnp.where(at_bottom != 0, 0.0, high)
        hidden[step, 0:HIDK, :] = low.astype(BF16)
        hidden[step + pairs, 0:HIDK, :] = high.astype(BF16)
        blank = jnp.zeros((HIDP - HIDK, 128), BF16)
        hidden[step, HIDK:HIDP, :] = blank
        hidden[step + pairs, HIDK:HIDP, :] = blank

    product = jnp.dot(ocn_in[...], side[...], preferred_element_type=F32)
    spot = lanes((1, d.edge)) % block
    gone = ((spot == 0) & (at_top != 0)) | ((spot == rows + 1) & (at_bottom != 0))
    active = jnp.where(gone, 0.0, gelu(product)).astype(BF16)
    active = jnp.concatenate([active, jnp.zeros((HIDP - HIDK, d.edge), BF16)], axis=0)

    def taps_of(slices):
        total = None
        for tap, values in enumerate(slices):
            weights = ocn_out[tap * 3 * CH : (tap + 1) * 3 * CH, :]
            product = jnp.dot(weights, values, preferred_element_type=F32)
            total = product if total is None else total + product
        return total

    partial = taps_of([roll(active, -tap) for tap in range(3)])
    from_left, from_right = partial[0:CH], partial[2 * CH : 3 * CH]
    half = rows // 2
    for step in range(half):
        product = taps_of(
            [
                jnp.concatenate([hidden[step + tap], hidden[step + half + tap]], axis=1)
                for tap in range(3)
            ]
        )
        for offset in range(2):
            row = step + offset * half
            sums = product[:, offset * 128 : (offset + 1) * 128]
            entry = roll(from_left, -row)[:, :128]
            total = sums[CH : 2 * CH] + jnp.where(lane == 0, entry, roll(sums[0:CH], 1))
            entry = roll(from_right, 127 - block - row)[:, :128]
            total = total + jnp.where(lane == 127, entry, roll(sums[2 * CH : 3 * CH], -1))
            update = total * wet[row : row + 1, :].astype(F32)
            out(row, state[row].astype(F32) + update)


def prepare(atm_in, atm_bias, ocn_in, ocn_bias, ocn_out, air_in, first, second, is_ocean):
    def bias_rows(ref, width):
        row = jnp.concatenate([ref[index : index + 1, :] for index in range(ref.shape[0])], axis=1)
        terms = list(split_bf16(row)) + [jnp.zeros_like(row)]
        bias = jnp.concatenate(terms, axis=0)
        return jnp.pad(bias, ((0, 0), (0, width - bias.shape[1])))

    @pl.when(is_ocean == 0)
    def _():
        columns = jnp.concatenate(
            [atm_in[...].astype(F32), bias_rows(atm_bias, HA), jnp.zeros((40, HA), F32)], axis=0
        )
        air_in[...] = columns.T.astype(BF16)

    @pl.when(is_ocean != 0)
    def _():
        bias = bias_rows(ocn_bias, 256)
        count = ocn_in.shape[2]
        for tap in range(3):
            whole = [ocn_in[3 * tap + side].astype(F32) for side in range(3)]
            whole = [jnp.pad(values, ((0, 0), (0, 256 - count))) for values in whole]
            rows = [values[:CH] for values in whole] + [values[CH:] for values in whole]
            rows.append(bias if tap == 0 else jnp.zeros((4, 256), F32))
            columns = jnp.concatenate(rows, axis=0).T
            first[:, tap * 256 : (tap + 1) * 256] = columns[:HIDK].astype(BF16)
        for tap in range(9):
            values = ocn_out[tap].astype(F32)
            second[tap * CH : (tap + 1) * CH, :] = jnp.pad(
                values, ((0, 0), (0, HIDP - count))
            ).astype(BF16)


def ends(flags):
    at_top, at_bottom, even = flags[1] != 0, flags[2] != 0, flags[3] == 0

    def up_and_down(one, two):
        above = jnp.where(even, two, one).astype(F32)
        below = jnp.where(even, one, two).astype(F32)
        return jnp.where(at_top, 0.0, above), jnp.where(at_bottom, 0.0, below)

    return up_and_down


def middle_kernel(d, opening, *refs):
    refs = list(refs)
    take = lambda count: [refs.pop(0) for _ in range(count)]
    flags, state, field_one, beside, field_two, from_one, from_two = take(7)
    if opening:
        planes, *far_weights = take(6)
    else:
        (plan_x,) = take(1)
    part_x, fields_x, rolled = take(3)
    if opening:
        plan_x, *made_weights = take(4)
        *raw_weights, sems = take(6)
        copies = fetch(far_weights, raw_weights, sems)
    rows, tall = d.rows, d.tall
    is_ocean = flags[0]
    up_and_down = ends(flags)

    if opening:

        @pl.when(is_ocean != 0)
        def _():
            base = d.strip
            pair = up_and_down(from_one[base : base + 16, :], from_two[base : base + 16, :])
            plan_x[...] = jnp.zeros_like(plan_x)
            for step, strip in zip((0, rows + 2), pair):
                for index in range(2):
                    plan_x[pl.ds(step + index, 2 * NK, stride=tall), :] = strip[index * 8 : (index + 1) * 8]

        for plane in range(2 * NK):
            plan_x[plane * tall + 2 : plane * tall + 2 + rows, :] = planes[plane].astype(F32)

    for field in range(NS):
        pair = up_and_down(field_one[field], field_two[field])
        fields_x[field, 0:16, :] = pair[0][rows - 16 : rows]
        fields_x[field, 16 : 16 + rows, :] = beside[field].astype(F32)
        fields_x[field, 16 + rows : 32 + rows, :] = pair[1][0:16]

    @pl.when(is_ocean == 0)
    def _():
        regrid_inside(fields_x, plan_x, part_x, 2, rows // 8, tall)

    @pl.when(is_ocean != 0)
    def _():
        regrid_inside(fields_x, plan_x, part_x, 0, d.tiles, tall)
        upper, lower = up_and_down(from_one[0 : 2 * CH, :], from_two[0 : 2 * CH, :])
        roll_rows(state, upper.astype(BF16), lower.astype(BF16), rolled, d)

    if opening:
        for copy in copies:
            copy.wait()
        prepare(*raw_weights, *made_weights, is_ocean)


def step_kernel(d, opening, closing, *refs):
    refs = list(refs)
    take = lambda count: [refs.pop(0) for _ in range(count)]
    flags, state, wet, from_left, from_right = take(5)
    part_x, fields_x, rolled, edges, plan_x, air_in, first, second, atm_out = take(9)
    if not opening:
        (plan_y,) = take(1)
    if not closing:
        (surface,) = take(1)
    (out,) = take(1)
    if not closing:
        fields, new_edges, one, two = take(4)
    if opening:
        (plan_y,) = take(1)
    fields_y, forcing_x, forcing_y, stack, hidden, side, raw = take(7)
    rows, tall = d.rows, d.tall
    is_ocean, at_top, at_bottom = flags[0], flags[1], flags[2]
    up_and_down = ends(flags)

    if opening:

        @pl.when(is_ocean != 0)
        def _():
            plan_y[...] = jnp.zeros_like(plan_y)
            base = d.edge_rows
            parts = [
                (ref[base : base + 16, :], ref[base + 16 + rows : base + 32 + rows, :],
                 ref[base + 16 : base + 16 + rows, :])
                for ref in (from_left, from_right)
            ]
            for plane in range(2 * NK):
                first_end, second_end, own = [
                    unpack_columns(left, right, plane, 2 * NK, 2) for left, right in zip(*parts)
                ]
                above, below = up_and_down(first_end, second_end)
                at = plane * tall
                plan_y[at : at + 2, :] = above[14:16]
                plan_y[at + 2 : at + 2 + rows, :] = own
                plan_y[at + 2 + rows : at + 4 + rows, :] = below[0:2]

    base = d.edge_rows + (rows + 32 if opening else 0)
    parts = [
        (ref[base : base + 16, :], ref[base + 16 + rows : base + 32 + rows, :],
         ref[base + 16 : base + 16 + rows, :])
        for ref in (from_left, from_right)
    ]
    for field in range(NS):
        first_end, second_end, own = [
            unpack_columns(left, right, field, NS, REACH) for left, right in zip(*parts)
        ]
        above, below = up_and_down(first_end, second_end)
        fields_y[field, 0:16, :] = above
        fields_y[field, 16 : 16 + rows, :] = own
        fields_y[field, 16 + rows : 32 + rows, :] = below

    def put(row, values):
        if closing:
            raw[pl.ds(row, CH, stride=rows), :] = values
        else:
            out[row] = values.astype(BF16)

    @pl.when(is_ocean == 0)
    def _():
        regrid_beside(
            fields_x, fields_y, plan_x, plan_y, part_x, forcing_x, forcing_y, 2, rows // 8, tall, False
        )
        air(state, put, forcing_x, air_in, atm_out, d)

    @pl.when(is_ocean != 0)
    def _():
        regrid_beside(
            fields_x, fields_y, plan_x, plan_y, part_x, forcing_x, forcing_y, 0, d.tiles, tall, True
        )
        joined = [get_edges(ref, 0, d) for ref in (from_left, from_right)]
        sea(
            state, rolled, get_edges(edges, 0, d), *joined, put, forcing_x, forcing_y,
            first, second, wet, at_top, at_bottom, stack, hidden, side, d,
        )

    if closing:
        out[...] = raw[...].reshape(CH, rows, 128).astype(BF16)
    else:
        emit(out, surface, wet, flags, fields, new_edges, one, two, raw, d)


VMEM = pl.BlockSpec(memory_space=pltpu.VMEM)
HBM = pl.BlockSpec(memory_space=pltpu.HBM)
SMEM = pl.BlockSpec(memory_space=pltpu.SMEM)
PARAMS = pltpu.CompilerParams(vmem_limit_bytes=48 * 1024 * 1024)


def shape(*dims, dtype=BF16):
    return jax.ShapeDtypeStruct(dims, dtype)


def send(x, move):
    names = ("grp", "lat", "lon")
    sizes = [lax.axis_size(name) for name in names]
    pairs = []
    for group in range(sizes[0]):
        for lat in range(sizes[1]):
            for lon in range(sizes[2]):
                to = move(group, lat, lon)
                if to is None or not 0 <= to[1] < sizes[1]:
                    continue
                target = (to[0] * sizes[1] + to[1]) * sizes[2] + to[2] % sizes[2]
                pairs.append(((group * sizes[1] + lat) * sizes[2] + lon, target))
    return lax.ppermute(x, names, pairs)


def swap_rows(x, turn, across):
    count = lax.axis_size("lat")

    def move(group, lat, lon):
        other = ((lat + turn) ^ 1) - turn
        if not 0 <= other < count:
            return 1 - group, lat, lon
        return (1 - group if across else group), other, lon

    return send(x, move)


def exchange(fields, own_edges, one, two, sides, d):
    rows = d.rows
    from_one = swap_rows(one, 0, False)
    from_two = swap_rows(two, 1, False)
    field_one = swap_rows(fields, 0, True)
    field_two = swap_rows(fields, 1, True)
    beside = send(fields, lambda g, i, j: (1 - g, i, j))
    lat, count = lax.axis_index("lat"), lax.axis_size("lat")
    odd = lat % 2 == 1
    edges = own_edges
    for turn, ref in ((0, from_one), (1, from_two)):
        other = ((lat + turn) ^ 1) - turn
        there = (other >= 0) & (other < count)
        edges = edges + jnp.where(there, ref[2 * CH : d.strip], 0)
    edges, beside, field_one, field_two = lax.optimization_barrier(
        (edges, beside, field_one, field_two)
    )
    outer = [field_one[NS], field_two[NS]]
    if rows != 16:
        outer = [
            jnp.where(odd, outer[0][rows - 16 :], outer[0][:16]),
            jnp.where(odd, outer[1][:16], outer[1][rows - 16 :]),
        ]
    packed = [edges]
    if sides is not None:
        packed += [from_one[d.strip + 16 :], sides, from_two[d.strip + 16 :]]
    packed += [outer[0], beside[NS], outer[1]]
    packed = jnp.concatenate(packed, axis=0)
    from_left = send(packed, lambda g, i, j: (g, i, j + 1))
    from_right = send(packed, lambda g, i, j: (g, i, j - 1))
    return (field_one, beside, field_two, from_one, from_two), (from_left, from_right), edges


def local(
    coupled_state, land_mask, regrid_offsets, regrid_weights, surface_proj,
    atm_in, atm_bias, atm_out, ocn_in, ocn_bias, ocn_out,
):
    rows = coupled_state.shape[2]
    assert coupled_state.shape[3] == 128
    d = Dims(rows)
    group = lax.axis_index("grp")
    lat = lax.axis_index("lat")
    flags = jnp.stack(
        [group, lat == 0, lat == lax.axis_size("lat") - 1, lat % 2]
    ).astype(jnp.int32)
    raw_weights = (
        atm_in.T,
        atm_bias.reshape(HA // 128, 128),
        jnp.transpose(ocn_in, (1, 2, 0)),
        ocn_bias[None],
        jnp.transpose(ocn_out, (1, 0, 2)),
    )
    state_shape = shape(rows, CH, 128)
    emitted = [
        shape(NS + 1, rows, 128),
        shape(d.edge_rows, 128),
        shape(d.strip, 128),
        shape(d.strip, 128),
    ]
    raw = pltpu.VMEM((rows * 8, 128), F32)
    turned = pltpu.VMEM((CH * rows, 128), F32)

    def call(kernel, operands, outs, scratch, name, far=()):
        scratch = scratch + [pltpu.VMEM(x.shape, x.dtype) for x in far]
        if far:
            scratch.append(pltpu.SemaphoreType.DMA((len(far) + CH // 16,)))

        far = [pltpu.with_memory_space_constraint(x, pltpu.HBM) for x in far]
        return pl.pallas_call(
            kernel,
            out_shape=outs,
            in_specs=[SMEM] + [VMEM] * len(operands) + [HBM] * len(far),
            out_specs=[VMEM] * len(outs),
            scratch_shapes=scratch,
            compiler_params=PARAMS,
            name=name,
        )(flags, *operands, *far)

    state, planes, sides, fields, edges, one, two = call(
        functools.partial(start_kernel, d),
        (),
        [state_shape, shape(2 * NK, rows, 128), shape(rows, 128)]
        + emitted[:2]
        + [shape(d.strip + 32, 128)] * 2,
        [raw, pltpu.VMEM((2 * NK * rows, 128), F32), turned],
        "start",
        (coupled_state[0], surface_proj, land_mask, regrid_offsets[0], regrid_weights[0]),
    )

    plan = shape(2 * NK * d.tall, 128, dtype=F32)
    between = [
        shape(NS * d.tall, 128, dtype=F32),
        shape(NS, rows + 32, 128, dtype=F32),
        shape(rows + 4, 3 * CH, 128),
    ]
    made = [shape(HA, 128), shape(HIDK, 768), shape(9 * CH, HIDP)]
    scratch = [
        pltpu.VMEM((NS, rows + 32, 128), F32),
        pltpu.VMEM((d.tall * 8, 128), F32),
        pltpu.VMEM((d.tall * 8, 128), F32),
        pltpu.VMEM((rows + 4, 256, 128), BF16),
        pltpu.VMEM((rows + 2, HIDP, 128), BF16),
        pltpu.VMEM((768, d.edge), BF16),
    ]

    vertical, horizontal, edges = exchange(fields, edges, one, two, sides, d)
    *shared, plan_x, air_in, first, second = call(
        functools.partial(middle_kernel, d, True),
        (state, *vertical, planes),
        between + [plan] + made,
        [],
        "first_middle",
        raw_weights,
    )
    weights = (air_in, first, second, atm_out)
    state, fields, edges, one, two, plan_y = call(
        functools.partial(step_kernel, d, True, False),
        (state, land_mask, *horizontal, *shared, edges, plan_x, *weights, surface_proj),
        [state_shape] + emitted + [plan],
        scratch + [raw],
        "first_step",
    )

    vertical, horizontal, edges = exchange(fields, edges, one, two, None, d)
    shared = call(
        functools.partial(middle_kernel, d, False),
        (state, *vertical, plan_x),
        between,
        [],
        "second_middle",
    )
    (state,) = call(
        functools.partial(step_kernel, d, False, True),
        (state, land_mask, *horizontal, *shared, edges, plan_x, *weights, plan_y),
        [shape(CH, rows, 128)],
        scratch + [turned],
        "second_step",
    )
    return state[None]


def solution(mesh):
    return jax.shard_map(
        local,
        mesh=mesh,
        in_specs=(
            P("grp", None, "lat", "lon"),
            P("lat", "lon"),
            P("grp", None, None, "lat", "lon"),
            P("grp", None, "lat", "lon"),
            P(),
            P(),
            P(),
            P(),
            P(),
            P(),
            P(),
        ),
        out_specs=P("grp", None, "lat", "lon"),
        check_vma=False,
    )
```

```python
import functools

import jax
import jax.numpy as jnp
from jax import lax
from jax.experimental import pallas as pl
from jax.experimental.pallas import tpu as pltpu
from jax.sharding import PartitionSpec as P

CH = 80
NS = 4
NK = 4
HA = 384
HW = 8
SPAN = 2 * HW + 1
REACH = HW + 2
HIDK = 208
HIDP = 256
F32 = jnp.float32
BF16 = jnp.bfloat16


def roll(x, shift, axis=1):
    size = x.shape[axis]
    if isinstance(shift, int):
        shift = shift % size
        if shift == 0:
            return x
    return pltpu.roll(x, shift, axis)


def lanes(shape):
    return lax.broadcasted_iota(jnp.int32, shape, len(shape) - 1)


def subs(shape):
    return lax.broadcasted_iota(jnp.int32, shape, len(shape) - 2)


class Dims:
    def __init__(self, rows):
        self.rows = rows
        self.block = 32 if rows + 4 <= 32 else 64
        self.edge = 4 * self.block
        self.pieces = self.edge // 128
        self.edge_rows = CH * self.pieces
        self.tiles = -(-(rows + 4) // 8)
        self.tall = 8 * self.tiles
        self.strip = 2 * CH + self.edge_rows
        self.sent = self.strip + 16 * (NS + 1)


def put_edges(ref, at, edges, d):
    for piece in range(d.pieces):
        ref[at + piece * CH : at + (piece + 1) * CH, :] = edges[:, piece * 128 : (piece + 1) * 128]


def get_edges(ref, at, d):
    return jnp.concatenate(
        [ref[at + piece * CH : at + (piece + 1) * CH, :] for piece in range(d.pieces)], axis=1
    )


def edge_columns(state, d):
    lane = lanes((1, d.edge))
    block = lane // d.block
    row = lane % d.block - 2
    column = jnp.where(block == 0, 126, jnp.where(block == 1, 0, jnp.where(block == 2, 127, 1)))
    own = (row >= 0) & (row < d.rows)
    target = jnp.where(own, column, -1)
    position = subs((128, d.edge))
    places = [
        (position == jnp.where(row == step, target, -1)).astype(F32).astype(BF16)
        for step in range(d.rows)
    ]
    whole = jnp.concatenate([state[step] for step in range(d.rows)], axis=1)
    total = jnp.dot(whole, jnp.concatenate(places, axis=0), preferred_element_type=F32)
    return total.astype(BF16)


def loop(count, unroll, body):
    while count % unroll:
        unroll -= 1

    def several(step, carry):
        for offset in range(unroll):
            body(step * unroll + offset)
        return carry

    lax.fori_loop(0, count // unroll, several, 0)


def pack_columns(values, reach):
    lane = lanes(values[0].shape)
    pitch = 128 // len(values)
    packed = jnp.zeros_like(values[0])
    for index, value in enumerate(values):
        at = index * pitch
        packed = jnp.where((lane >= at) & (lane < at + reach), roll(value, at), packed)
        at += reach
        packed = jnp.where((lane >= at) & (lane < at + reach), roll(value, at + reach - 128), packed)
    return packed


def unpack_columns(left, right, index, count, reach):
    at = index * (128 // count)
    left = roll(left.astype(F32), 128 - at - 2 * reach)
    return jnp.where(lanes(left.shape) < 64, roll(right.astype(F32), -at), left)


def strips(one, two, even, d):
    last = d.rows - 2
    return (one, jnp.where(even, last, 0)), (two, jnp.where(even, 0, last))


def split_bf16(values):
    high = values.astype(BF16).astype(F32)
    mid = (values - high).astype(BF16).astype(F32)
    return high, mid, values - high - mid


def emit(state, surface, wet, flags, fields, columns, own_edges, one, two, raw, d):
    half = d.rows // 2
    is_ocean, even = flags[0] != 0, flags[3] == 0
    gap = jnp.zeros((4, CH), F32)
    terms = []
    for term in split_bf16(surface[flags[0]]):
        terms += [term, gap]
    proj = jnp.concatenate(terms + [gap, gap], axis=0).astype(BF16)
    for step in range(half):
        pair = jnp.concatenate([state[step], state[step + half]], axis=1)
        parts = jnp.dot(proj, pair, preferred_element_type=F32)
        whole = parts[0:8] + parts[8:16] + parts[16:24]
        raw[step * 8 : step * 8 + 8, :] = whole[:, :128]
        raw[(step + half) * 8 : (step + half) * 8 + 8, :] = whole[:, 128:]
    keeping = jnp.where(is_ocean, wet[...].astype(F32), 1.0)
    whole = [raw[pl.ds(field, d.rows, stride=8), :] * keeping for field in range(NS)]
    for field in range(NS):
        fields[field * d.rows : (field + 1) * d.rows, :] = whole[field].astype(BF16)
    packed = pack_columns(whole, REACH)
    columns[...] = packed.astype(BF16)
    edges = edge_columns(state, d)
    put_edges(own_edges, 0, edges, d)
    row = lanes(edges.shape) % d.block
    downward = jnp.where(row < 2, roll(edges, -d.rows), jnp.zeros_like(edges))
    upward = jnp.where(
        (row >= d.rows + 2) & (row < d.rows + 4), roll(edges, d.rows), jnp.zeros_like(edges)
    )
    for (ref, first), down in zip(strips(one, two, even, d), (even, jnp.logical_not(even))):
        ref[0:CH, :] = state[first]
        ref[CH : 2 * CH, :] = state[first + 1]
        put_edges(ref, 2 * CH, jnp.where(down, downward, upward), d)
        for index, values in enumerate(whole + [packed]):
            part = jnp.where(down, values[d.rows - 16 :], values[:16])
            at = d.strip + 16 * index
            ref[at : at + 16, :] = part.astype(BF16)


def fetch(sources, targets, sems):
    copies = [
        pltpu.make_async_copy(source, target, sems.at[index])
        for index, (source, target) in enumerate(zip(sources, targets))
    ]
    for copy in copies:
        copy.start()
    return copies


def start_kernel(
    d, flags, far_given, far_surface, far_wet, far_offsets, far_weights,
    state, planes, sides, fields, columns, own_edges, one, two,
    raw, tall, turned, given, surface, wet, offsets, weights, sems,
):
    rows = d.rows
    pieces = [pl.ds(at, 16) for at in range(0, CH, 16)]
    copies = fetch(
        [far_given.at[piece] for piece in pieces] + [far_surface, far_wet, far_offsets, far_weights],
        [given.at[piece] for piece in pieces] + [surface, wet, offsets, weights],
        sems,
    )
    for index, piece in enumerate(pieces):
        copies[index].wait()
        turned[index * 16 * rows : (index + 1) * 16 * rows, :] = (
            given[piece].astype(F32).reshape(16 * rows, 128)
        )
    for row in range(rows):
        state[row] = turned[pl.ds(row, CH, stride=rows), :].astype(BF16)
    for copy in copies[len(pieces) :]:
        copy.wait()
    emit(state, surface, wet, flags, fields, columns, own_edges, one, two, raw, d)
    for k in range(NK):
        code = (offsets[0, k] * SPAN + offsets[1, k]).astype(F32)
        tall[k * rows : (k + 1) * rows, :] = code
        tall[(NK + k) * rows : (NK + k + 1) * rows, :] = weights[k]
        planes[k] = code.astype(BF16)
        planes[NK + k] = weights[k].astype(BF16)
    packed = pack_columns([tall[plane * rows : (plane + 1) * rows, :] for plane in range(2 * NK)], 2)
    sides[...] = packed.astype(BF16)
    even = flags[3] == 0
    for (ref, first), down in zip(strips(one, two, even, d), (even, jnp.logical_not(even))):
        strip = [tall[pl.ds(first + step, 2 * NK, stride=rows), :] for step in range(2)]
        ref[d.sent : d.sent + 16, :] = jnp.concatenate(strip, axis=0).astype(BF16)
        ref[d.sent + 16 : d.sent + 32, :] = jnp.where(
            down, packed[rows - 16 : rows], packed[0:16]
        ).astype(BF16)


def decode(code):
    shifted = code.astype(jnp.int32) + (HW * SPAN + HW)
    rows = lax.shift_right_logical(shifted * 241, 12)
    return rows - HW, shifted - rows * SPAN - HW


def along_lanes(values, index):
    numbers = lax.GatherDimensionNumbers(
        offset_dims=(),
        collapsed_slice_dims=(1,),
        start_index_map=(1,),
        operand_batching_dims=(0,),
        start_indices_batching_dims=(0,),
    )
    return lax.gather(
        values, index[..., None], numbers, (1, 1), mode=lax.GatherScatterMode.PROMISE_IN_BOUNDS
    )


def select_rows(sources, start, picks):
    chosen = [[jnp.zeros((8, 128), F32) for _ in range(NS)] for _ in picks]
    for shift in range(-HW, HW + 1):
        at = pl.ds(start + shift, 8)
        used = [any(pick[2][index] is not None for pick in picks) for index in range(len(sources))]
        values = [
            [source[field, at, :] for field in range(NS)] if use else None
            for source, use in zip(sources, used)
        ]
        for slot, (rows, index, allowed) in enumerate(picks):
            here = rows == shift
            for source, within in enumerate(allowed):
                if within is None:
                    continue
                mask = here & within
                for field in range(NS):
                    picked = along_lanes(values[source][field], index)
                    chosen[slot][field] = jnp.where(mask, picked, chosen[slot][field])
    return chosen


def regrid_inside(fields_x, plan_x, part_x, first, tiles, tall):
    lane = lanes((8, 128))
    for step in range(tiles):
        at = first + step * 8
        picks = []
        weights = []
        for k in range(NK):
            rows, cols = decode(plan_x[pl.ds(k * tall + at, 8), :])
            weights.append(plan_x[pl.ds((NK + k) * tall + at, 8), :])
            column = lane + cols
            picks.append((rows, column & 127, ((column >= 0) & (column < 128),)))
        chosen = select_rows((fields_x,), at + 14, picks)
        for field in range(NS):
            total = chosen[0][field] * weights[0]
            for k in range(1, NK):
                total = total + chosen[k][field] * weights[k]
            part_x[pl.ds(field * tall + at, 8), :] = total


def regrid_beside(
    fields_x, fields_y, plan_x, plan_y, part_x, forcing_x, forcing_y, first, tiles, tall, sides
):
    lane = lanes((8, 128))
    part = ((lane + 8) & 127) // 32
    place = ((lane + 8) & 31) - 8
    outer = place >= 8
    inner_column = place & 127
    outer_column = jnp.where(place < 16, place - 16, place + 112)
    edge = (lane < 8) | (lane >= 120)
    for step in range(tiles):
        at = first + step * 8
        code = jnp.zeros((8, 128), F32)
        weight = jnp.zeros((8, 128), F32)
        for k in range(NK):
            edge_code = roll(plan_x[pl.ds(k * tall + at, 8), :], 32 * k)
            edge_weight = roll(plan_x[pl.ds((NK + k) * tall + at, 8), :], 32 * k)
            if sides:
                edge_code = jnp.where(
                    outer, roll(plan_y[pl.ds(k * tall + at, 8), :], 32 * k + 16), edge_code
                )
                edge_weight = jnp.where(
                    outer, roll(plan_y[pl.ds((NK + k) * tall + at, 8), :], 32 * k + 16), edge_weight
                )
            code = jnp.where(part == k, edge_code, code)
            weight = jnp.where(part == k, edge_weight, weight)
        rows, cols = decode(code)
        column = jnp.where(outer, outer_column, inner_column) + cols
        within = (column >= 0) & (column < 128)
        picks = [(rows, column & 127, (within & outer if sides else None, jnp.logical_not(within)))]
        (chosen,) = select_rows((fields_x, fields_y), at + 14, picks)
        for field in range(NS):
            part_sum = chosen[field] * weight
            extra = part_sum
            for k in range(1, NK):
                extra = extra + roll(part_sum, -32 * k)
            total = part_x[pl.ds(field * tall + at, 8), :] + jnp.where(edge, extra, 0.0)
            forcing_x[pl.ds(at * 8 + field, 8, stride=8), :] = total
            forcing_x[pl.ds(at * 8 + field + 4, 8, stride=8), :] = total
            if sides:
                extra = roll(extra, -16)
                forcing_y[pl.ds(at * 8 + field, 8, stride=8), :] = extra
                forcing_y[pl.ds(at * 8 + field + 4, 8, stride=8), :] = extra


def gelu(x):
    scale = (2 / jnp.pi) ** 0.5
    half = 0.5 * x
    return half + half * jnp.tanh(x * (scale + (scale * 0.044715) * (x * x)))


def air(state, out, forcing_x, air_in, atm_out, d):
    half = d.rows // 2
    first = subs((8, 128)) < 4
    blank = jnp.zeros((32, 128), BF16)

    def inputs(row):
        at = (row + 2) * 8
        forced = jnp.where(first, forcing_x[at : at + 8, :], 1.0)
        forced = jnp.concatenate([forced, jnp.zeros_like(forced)], axis=0).astype(BF16)
        return jnp.concatenate([state[row], forced, blank], axis=0)

    for step in range(half):
        pair = jnp.concatenate([inputs(step), inputs(step + half)], axis=1)
        hidden = gelu(jnp.dot(air_in[...], pair, preferred_element_type=F32)).astype(BF16)
        update = jnp.dot(atm_out[...], hidden, preferred_element_type=F32)
        for offset in range(2):
            row = step + offset * half
            change = update[:, offset * 128 : (offset + 1) * 128]
            out(row, state[row].astype(F32) + change)


def edge_forcing(forcing_x, forcing_y, d):
    lane = lanes((8, d.edge))
    block = lane // d.block
    row = lane % d.block

    inner = outer = jnp.zeros((8, d.edge), F32)
    for step in range(d.rows + 4):
        at = pl.ds(step * 8, 8)
        pad = [jnp.zeros((8, 128), F32)] * (d.pieces - 1)
        here = jnp.concatenate([forcing_x[at, :]] + pad, axis=1)
        there = jnp.concatenate([forcing_y[at, :]] + pad, axis=1)
        for index, column in enumerate((126, 0, 127, 1)):
            shift = step + index * d.block - column
            match = (block == index) & (row == step)
            if column in (0, 127):
                inner = jnp.where(match, roll(here, shift), inner)
            outer = jnp.where(match, roll(there, shift), outer)
    return inner, outer


def roll_rows(state, upper, lower, rolled, d):
    def put(row, values):
        rolled[row, 0:CH, :] = roll(values, 1)
        rolled[row, CH : 2 * CH, :] = values
        rolled[row, 2 * CH : 3 * CH, :] = roll(values, -1)

    for step in range(2):
        put(step, upper[step * CH : (step + 1) * CH, :])
        put(d.rows + 2 + step, lower[step * CH : (step + 1) * CH, :])
    for row in range(d.rows):
        put(row + 2, state[row])


def sea(
    state, rolled, edges, left, right, out, forcing_x, forcing_y, ocn_in, ocn_out, wet,
    at_top, at_bottom, stack, hidden, side, d,
):
    rows, block = d.rows, d.block
    lane = lanes((CH, 128))
    spot = lanes((CH, d.edge))
    part = spot // block
    inner = edges
    outer = jnp.where((part == 0) | (part == 2), left, right)

    def sides_of(inner, outer, spot):
        first = spot < block
        return (
            jnp.where(first, outer, roll(inner, -block)),
            jnp.where(first, roll(outer, -2 * block), outer),
            jnp.where(first, roll(inner, -block), roll(outer, -2 * block)),
        )

    beside = sides_of(inner, outer, spot)
    middle = beside[1]
    force_in, force_out = edge_forcing(forcing_x, forcing_y, d)
    beside_forcing = sides_of(force_in, force_out, lanes((8, d.edge)))
    sub = subs((8, d.edge))
    ones = jnp.ones((8, d.edge), F32)
    forced = jnp.concatenate(
        [
            jnp.where(sub < 4, beside_forcing[0], beside_forcing[1]),
            jnp.where(sub < 4, beside_forcing[2], ones),
        ],
        axis=0,
    ).astype(BF16)
    columns = jnp.concatenate(list(beside) + [forced], axis=0)
    for tap in range(3):
        side[tap * 256 : (tap + 1) * 256, :] = roll(columns, -tap)

    sub_row = subs((8, 128))
    lane_row = lanes((8, 128))

    for row in range(rows + 4):
        entry = roll(middle, -row)[:, :128]
        stack[row, 0:CH, :] = jnp.where(lane == 0, entry, rolled[row, 0:CH, :])
        stack[row, CH : 2 * CH, :] = rolled[row, CH : 2 * CH, :]
        entry = roll(middle, 127 - block - row)[:, :128]
        stack[row, 2 * CH : 3 * CH, :] = jnp.where(lane == 127, entry, rolled[row, 2 * CH : 3 * CH, :])
        here, there = forcing_x[row * 8 : row * 8 + 8, :], forcing_y[row * 8 : row * 8 + 8, :]
        before = roll(jnp.where(lane_row == 127, there, here), 1)
        after = roll(jnp.where(lane_row == 0, there, here), -1)
        stack[row, 3 * CH : 256, :] = jnp.concatenate(
            [jnp.where(sub_row < 4, before, here), jnp.where(sub_row < 4, after, 1.0)], axis=0
        ).astype(BF16)

    pairs = (rows + 2) // 2

    for step in range(pairs):
        taps = jnp.concatenate(
            [
                stack[step : step + 3].reshape(3 * 256, 128),
                stack[step + pairs : step + pairs + 3].reshape(3 * 256, 128),
            ],
            axis=1,
        )
        active = gelu(jnp.dot(ocn_in[...], taps, preferred_element_type=F32))
        low, high = active[:, :128], active[:, 128:]
        if step == 0:
            low = jnp.where(at_top != 0, 0.0, low)
        if step == pairs - 1:
            high = jnp.where(at_bottom != 0, 0.0, high)
        hidden[step, 0:HIDK, :] = low.astype(BF16)
        hidden[step + pairs, 0:HIDK, :] = high.astype(BF16)
        blank = jnp.zeros((HIDP - HIDK, 128), BF16)
        hidden[step, HIDK:HIDP, :] = blank
        hidden[step + pairs, HIDK:HIDP, :] = blank

    product = jnp.dot(ocn_in[...], side[...], preferred_element_type=F32)
    spot = lanes((1, d.edge)) % block
    gone = ((spot == 0) & (at_top != 0)) | ((spot == rows + 1) & (at_bottom != 0))
    active = jnp.where(gone, 0.0, gelu(product)).astype(BF16)
    active = jnp.concatenate([active, jnp.zeros((HIDP - HIDK, d.edge), BF16)], axis=0)

    def taps_of(slices):
        total = None
        for tap, values in enumerate(slices):
            weights = ocn_out[tap * 3 * CH : (tap + 1) * 3 * CH, :]
            product = jnp.dot(weights, values, preferred_element_type=F32)
            total = product if total is None else total + product
        return total

    partial = taps_of([roll(active, -tap) for tap in range(3)])
    from_left, from_right = partial[0:CH], partial[2 * CH : 3 * CH]
    half = rows // 2
    for step in range(half):
        product = taps_of(
            [
                jnp.concatenate([hidden[step + tap], hidden[step + half + tap]], axis=1)
                for tap in range(3)
            ]
        )
        for offset in range(2):
            row = step + offset * half
            sums = product[:, offset * 128 : (offset + 1) * 128]
            entry = roll(from_left, -row)[:, :128]
            total = sums[CH : 2 * CH] + jnp.where(lane == 0, entry, roll(sums[0:CH], 1))
            entry = roll(from_right, 127 - block - row)[:, :128]
            total = total + jnp.where(lane == 127, entry, roll(sums[2 * CH : 3 * CH], -1))
            update = total * wet[row : row + 1, :].astype(F32)
            out(row, state[row].astype(F32) + update)


def prepare(atm_in, atm_bias, ocn_in, ocn_bias, ocn_out, air_in, first, second, is_ocean):
    def bias_rows(ref, width):
        row = jnp.concatenate([ref[index : index + 1, :] for index in range(ref.shape[0])], axis=1)
        terms = list(split_bf16(row)) + [jnp.zeros_like(row)]
        bias = jnp.concatenate(terms, axis=0)
        return jnp.pad(bias, ((0, 0), (0, width - bias.shape[1])))

    @pl.when(is_ocean == 0)
    def _():
        columns = jnp.concatenate(
            [atm_in[...].astype(F32), bias_rows(atm_bias, HA), jnp.zeros((40, HA), F32)], axis=0
        )
        air_in[...] = columns.T.astype(BF16)

    @pl.when(is_ocean != 0)
    def _():
        bias = bias_rows(ocn_bias, 256)
        count = ocn_in.shape[2]
        for tap in range(3):
            whole = [ocn_in[3 * tap + side].astype(F32) for side in range(3)]
            whole = [jnp.pad(values, ((0, 0), (0, 256 - count))) for values in whole]
            rows = [values[:CH] for values in whole] + [values[CH:] for values in whole]
            rows.append(bias if tap == 0 else jnp.zeros((4, 256), F32))
            columns = jnp.concatenate(rows, axis=0).T
            first[:, tap * 256 : (tap + 1) * 256] = columns[:HIDK].astype(BF16)
        for tap in range(9):
            values = ocn_out[tap].astype(F32)
            second[tap * CH : (tap + 1) * CH, :] = jnp.pad(
                values, ((0, 0), (0, HIDP - count))
            ).astype(BF16)


def ends(flags):
    at_top, at_bottom, even = flags[1] != 0, flags[2] != 0, flags[3] == 0

    def up_and_down(one, two):
        above = jnp.where(even, two, one).astype(F32)
        below = jnp.where(even, one, two).astype(F32)
        return jnp.where(at_top, 0.0, above), jnp.where(at_bottom, 0.0, below)

    return up_and_down


def middle_kernel(d, opening, *refs):
    refs = list(refs)
    take = lambda count: [refs.pop(0) for _ in range(count)]
    flags, state, beside, from_one, from_two = take(5)
    if opening:
        planes, *far_weights = take(6)
    else:
        (plan_x,) = take(1)
    part_x, fields_x, rolled = take(3)
    if opening:
        plan_x, *made_weights = take(4)
        *raw_weights, sems = take(6)
        copies = fetch(far_weights, raw_weights, sems)
    rows, tall = d.rows, d.tall
    is_ocean = flags[0]
    up_and_down = ends(flags)

    if opening:

        @pl.when(is_ocean != 0)
        def _():
            base = d.sent
            pair = up_and_down(from_one[base : base + 16, :], from_two[base : base + 16, :])
            plan_x[...] = jnp.zeros_like(plan_x)
            for step, strip in zip((0, rows + 2), pair):
                for index in range(2):
                    plan_x[pl.ds(step + index, 2 * NK, stride=tall), :] = strip[index * 8 : (index + 1) * 8]

        for plane in range(2 * NK):
            plan_x[plane * tall + 2 : plane * tall + 2 + rows, :] = planes[plane].astype(F32)

    last = 64 + NS * rows
    for field in range(NS):
        start = field * 16
        pair = up_and_down(beside[start : start + 16, :], beside[last + start : last + start + 16, :])
        fields_x[field, 0:16, :] = pair[0]
        start = 64 + field * rows
        fields_x[field, 16 : 16 + rows, :] = beside[start : start + rows, :].astype(F32)
        fields_x[field, 16 + rows : 32 + rows, :] = pair[1]

    @pl.when(is_ocean == 0)
    def _():
        regrid_inside(fields_x, plan_x, part_x, 2, rows // 8, tall)

    @pl.when(is_ocean != 0)
    def _():
        regrid_inside(fields_x, plan_x, part_x, 0, d.tiles, tall)
        upper, lower = up_and_down(from_one[0 : 2 * CH, :], from_two[0 : 2 * CH, :])
        roll_rows(state, upper.astype(BF16), lower.astype(BF16), rolled, d)

    if opening:
        for copy in copies:
            copy.wait()
        prepare(*raw_weights, *made_weights, is_ocean)


def step_kernel(d, opening, closing, *refs):
    refs = list(refs)
    take = lambda count: [refs.pop(0) for _ in range(count)]
    flags, state, wet, columns_left, columns_right, from_left, from_right = take(7)
    part_x, fields_x, rolled, edges, plan_x, air_in, first, second, atm_out = take(9)
    if not opening:
        (plan_y,) = take(1)
    if not closing:
        (surface,) = take(1)
    (out,) = take(1)
    if not closing:
        fields, columns, new_edges, one, two = take(5)
    if opening:
        (plan_y,) = take(1)
    fields_y, forcing_x, forcing_y, stack, hidden, side, raw = take(7)
    rows, tall = d.rows, d.tall
    is_ocean, at_top, at_bottom = flags[0], flags[1], flags[2]
    up_and_down = ends(flags)

    if opening:

        @pl.when(is_ocean != 0)
        def _():
            plan_y[...] = jnp.zeros_like(plan_y)
            base = d.edge_rows
            parts = [
                (ref[base : base + 16, :], ref[base + 16 + rows : base + 32 + rows, :],
                 ref[base + 16 : base + 16 + rows, :])
                for ref in (from_left, from_right)
            ]
            for plane in range(2 * NK):
                first_end, second_end, own = [
                    unpack_columns(left, right, plane, 2 * NK, 2) for left, right in zip(*parts)
                ]
                above, below = up_and_down(first_end, second_end)
                at = plane * tall
                plan_y[at : at + 2, :] = above[14:16]
                plan_y[at + 2 : at + 2 + rows, :] = own
                plan_y[at + 2 + rows : at + 4 + rows, :] = below[0:2]

    parts = [
        (ref[0:16, :], ref[16 + rows : 32 + rows, :], ref[16 : 16 + rows, :])
        for ref in (columns_left, columns_right)
    ]
    for field in range(NS):
        first_end, second_end, own = [
            unpack_columns(left, right, field, NS, REACH) for left, right in zip(*parts)
        ]
        above, below = up_and_down(first_end, second_end)
        fields_y[field, 0:16, :] = above
        fields_y[field, 16 : 16 + rows, :] = own
        fields_y[field, 16 + rows : 32 + rows, :] = below

    def put(row, values):
        if closing:
            raw[pl.ds(row, CH, stride=rows), :] = values
        else:
            out[row] = values.astype(BF16)

    @pl.when(is_ocean == 0)
    def _():
        regrid_beside(
            fields_x, fields_y, plan_x, plan_y, part_x, forcing_x, forcing_y, 2, rows // 8, tall, False
        )
        air(state, put, forcing_x, air_in, atm_out, d)

    @pl.when(is_ocean != 0)
    def _():
        regrid_beside(
            fields_x, fields_y, plan_x, plan_y, part_x, forcing_x, forcing_y, 0, d.tiles, tall, True
        )
        joined = [get_edges(ref, 0, d) for ref in (from_left, from_right)]
        sea(
            state, rolled, get_edges(edges, 0, d), *joined, put, forcing_x, forcing_y,
            first, second, wet, at_top, at_bottom, stack, hidden, side, d,
        )

    if closing:
        out[...] = raw[...].reshape(CH, rows, 128).astype(BF16)
    else:
        emit(out, surface, wet, flags, fields, columns, new_edges, one, two, raw, d)


VMEM = pl.BlockSpec(memory_space=pltpu.VMEM)
HBM = pl.BlockSpec(memory_space=pltpu.HBM)
SMEM = pl.BlockSpec(memory_space=pltpu.SMEM)
PARAMS = pltpu.CompilerParams(vmem_limit_bytes=48 * 1024 * 1024)


def shape(*dims, dtype=BF16):
    return jax.ShapeDtypeStruct(dims, dtype)


def send(x, move):
    names = ("grp", "lat", "lon")
    sizes = [lax.axis_size(name) for name in names]
    pairs = []
    for group in range(sizes[0]):
        for lat in range(sizes[1]):
            for lon in range(sizes[2]):
                to = move(group, lat, lon)
                if to is None or not 0 <= to[1] < sizes[1]:
                    continue
                target = (to[0] * sizes[1] + to[1]) * sizes[2] + to[2] % sizes[2]
                pairs.append(((group * sizes[1] + lat) * sizes[2] + lon, target))
    return lax.ppermute(x, names, pairs)


def swap_rows(x, turn):
    count = lax.axis_size("lat")

    def move(group, lat, lon):
        other = ((lat + turn) ^ 1) - turn
        if not 0 <= other < count:
            return 1 - group, lat, lon
        return group, other, lon

    return send(x, move)


def exchange(fields, columns, own_edges, one, two, sides, d):
    from_one = swap_rows(one, 0)
    from_two = swap_rows(two, 1)
    lat, count = lax.axis_index("lat"), lax.axis_size("lat")
    edges = own_edges
    for turn, ref in ((0, from_one), (1, from_two)):
        other = ((lat + turn) ^ 1) - turn
        there = (other >= 0) & (other < count)
        edges = edges + jnp.where(there, ref[2 * CH : d.strip], 0)
    across = d.strip + 16 * NS
    whole = [from_one[d.strip : across], fields, from_two[d.strip : across]]
    whole = jnp.concatenate(whole, axis=0)
    narrow = [from_one[across : d.sent], columns, from_two[across : d.sent]]
    narrow = jnp.concatenate(narrow, axis=0)
    packed = edges
    if sides is not None:
        packed = [edges, from_one[d.sent + 16 :], sides, from_two[d.sent + 16 :]]
        packed = jnp.concatenate(packed, axis=0)
    whole, narrow, packed = lax.optimization_barrier((whole, narrow, packed))
    beside = send(whole, lambda g, i, j: (1 - g, i, j))
    horizontal = (
        send(narrow, lambda g, i, j: (1 - g, i, j + 1)),
        send(narrow, lambda g, i, j: (1 - g, i, j - 1)),
        send(packed, lambda g, i, j: (g, i, j + 1)),
        send(packed, lambda g, i, j: (g, i, j - 1)),
    )
    return (beside, from_one, from_two), horizontal, edges


def local(
    coupled_state, land_mask, regrid_offsets, regrid_weights, surface_proj,
    atm_in, atm_bias, atm_out, ocn_in, ocn_bias, ocn_out,
):
    rows = coupled_state.shape[2]
    assert coupled_state.shape[3] == 128
    d = Dims(rows)
    group = lax.axis_index("grp")
    lat = lax.axis_index("lat")
    flags = jnp.stack(
        [group, lat == 0, lat == lax.axis_size("lat") - 1, lat % 2]
    ).astype(jnp.int32)
    raw_weights = (
        atm_in.T,
        atm_bias.reshape(HA // 128, 128),
        jnp.transpose(ocn_in, (1, 2, 0)),
        ocn_bias[None],
        jnp.transpose(ocn_out, (1, 0, 2)),
    )
    state_shape = shape(rows, CH, 128)
    emitted = [
        shape(NS * rows, 128),
        shape(rows, 128),
        shape(d.edge_rows, 128),
        shape(d.sent, 128),
        shape(d.sent, 128),
    ]
    raw = pltpu.VMEM((rows * 8, 128), F32)
    turned = pltpu.VMEM((CH * rows, 128), F32)

    def call(kernel, operands, outs, scratch, name, far=()):
        scratch = scratch + [pltpu.VMEM(x.shape, x.dtype) for x in far]
        if far:
            scratch.append(pltpu.SemaphoreType.DMA((len(far) + CH // 16,)))

        far = [pltpu.with_memory_space_constraint(x, pltpu.HBM) for x in far]
        return pl.pallas_call(
            kernel,
            out_shape=outs,
            in_specs=[SMEM] + [VMEM] * len(operands) + [HBM] * len(far),
            out_specs=[VMEM] * len(outs),
            scratch_shapes=scratch,
            compiler_params=PARAMS,
            name=name,
        )(flags, *operands, *far)

    state, planes, sides, *sending = call(
        functools.partial(start_kernel, d),
        (),
        [state_shape, shape(2 * NK, rows, 128), shape(rows, 128)]
        + emitted[:3]
        + [shape(d.sent + 32, 128)] * 2,
        [raw, pltpu.VMEM((2 * NK * rows, 128), F32), turned],
        "start",
        (coupled_state[0], surface_proj, land_mask, regrid_offsets[0], regrid_weights[0]),
    )

    plan = shape(2 * NK * d.tall, 128, dtype=F32)
    between = [
        shape(NS * d.tall, 128, dtype=F32),
        shape(NS, rows + 32, 128, dtype=F32),
        shape(rows + 4, 3 * CH, 128),
    ]
    made = [shape(HA, 128), shape(HIDK, 768), shape(9 * CH, HIDP)]
    scratch = [
        pltpu.VMEM((NS, rows + 32, 128), F32),
        pltpu.VMEM((d.tall * 8, 128), F32),
        pltpu.VMEM((d.tall * 8, 128), F32),
        pltpu.VMEM((rows + 4, 256, 128), BF16),
        pltpu.VMEM((rows + 2, HIDP, 128), BF16),
        pltpu.VMEM((768, d.edge), BF16),
    ]

    vertical, horizontal, edges = exchange(*sending, sides, d)
    *shared, plan_x, air_in, first, second = call(
        functools.partial(middle_kernel, d, True),
        (state, *vertical, planes),
        between + [plan] + made,
        [],
        "first_middle",
        raw_weights,
    )
    weights = (air_in, first, second, atm_out)
    state, *sending, plan_y = call(
        functools.partial(step_kernel, d, True, False),
        (state, land_mask, *horizontal, *shared, edges, plan_x, *weights, surface_proj),
        [state_shape] + emitted + [plan],
        scratch + [raw],
        "first_step",
    )

    vertical, horizontal, edges = exchange(*sending, None, d)
    shared = call(
        functools.partial(middle_kernel, d, False),
        (state, *vertical, plan_x),
        between,
        [],
        "second_middle",
    )
    (state,) = call(
        functools.partial(step_kernel, d, False, True),
        (state, land_mask, *horizontal, *shared, edges, plan_x, *weights, plan_y),
        [shape(CH, rows, 128)],
        scratch + [turned],
        "second_step",
    )
    return state[None]


def solution(mesh):
    return jax.shard_map(
        local,
        mesh=mesh,
        in_specs=(
            P("grp", None, "lat", "lon"),
            P("lat", "lon"),
            P("grp", None, None, "lat", "lon"),
            P("grp", None, "lat", "lon"),
            P(),
            P(),
            P(),
            P(),
            P(),
            P(),
            P(),
        ),
        out_specs=P("grp", None, "lat", "lon"),
        check_vma=False,
    )
```

```python
import functools

import jax
import jax.numpy as jnp
from jax import lax
from jax.experimental import pallas as pl
from jax.experimental.pallas import tpu as pltpu
from jax.sharding import PartitionSpec as P

CH = 80
NS = 4
NK = 4
HA = 384
HW = 8
SPAN = 2 * HW + 1
REACH = HW + 2
FIXED = 32767.0
HIDK = 208
HIDP = 256
F32 = jnp.float32
BF16 = jnp.bfloat16


def roll(x, shift, axis=1):
    size = x.shape[axis]
    if isinstance(shift, int):
        shift = shift % size
        if shift == 0:
            return x
    return pltpu.roll(x, shift, axis)


def lanes(shape):
    return lax.broadcasted_iota(jnp.int32, shape, len(shape) - 1)


def subs(shape):
    return lax.broadcasted_iota(jnp.int32, shape, len(shape) - 2)


class Dims:
    def __init__(self, rows):
        self.rows = rows
        self.block = 32 if rows + 4 <= 32 else 64
        self.edge = 4 * self.block
        self.pieces = self.edge // 128
        self.edge_rows = CH * self.pieces
        self.tiles = -(-(rows + 4) // 8)
        self.tall = 8 * self.tiles
        self.strip = 2 * CH + self.edge_rows


def put_edges(ref, at, edges, d):
    for piece in range(d.pieces):
        ref[at + piece * CH : at + (piece + 1) * CH, :] = edges[:, piece * 128 : (piece + 1) * 128]


def get_edges(ref, at, d):
    return jnp.concatenate(
        [ref[at + piece * CH : at + (piece + 1) * CH, :] for piece in range(d.pieces)], axis=1
    )


def edge_places(places, d):
    lane = lanes((1, d.edge))
    block = lane // d.block
    row = lane % d.block - 2
    column = jnp.where(block == 0, 126, jnp.where(block == 1, 0, jnp.where(block == 2, 127, 1)))
    own = (row >= 0) & (row < d.rows)
    target = jnp.where(own, column, -1)
    position = subs((128, d.edge))
    for step in range(d.rows):
        place = (position == jnp.where(row == step, target, -1)).astype(F32).astype(BF16)
        places[step * 128 : (step + 1) * 128, :] = place


def edge_columns(state, places, d):
    whole = jnp.concatenate([state[step] for step in range(d.rows)], axis=1)
    return jnp.dot(whole, places[...], preferred_element_type=F32).astype(BF16)


def pack_columns(values, reach):
    lane = lanes(values[0].shape)
    pitch = 128 // len(values)
    packed = jnp.zeros_like(values[0])
    for index, value in enumerate(values):
        at = index * pitch
        packed = jnp.where((lane >= at) & (lane < at + reach), roll(value, at), packed)
        at += reach
        packed = jnp.where((lane >= at) & (lane < at + reach), roll(value, at + reach - 128), packed)
    return packed


def unpack_columns(left, right, index, count, reach):
    at = index * (128 // count)
    left = roll(left.astype(F32), 128 - at - 2 * reach)
    return jnp.where(lanes(left.shape) < 64, roll(right.astype(F32), -at), left)


def strips(one, two, even, d):
    last = d.rows - 2
    return (one, jnp.where(even, last, 0)), (two, jnp.where(even, 0, last))


def split_bf16(values):
    high = values.astype(BF16).astype(F32)
    mid = (values - high).astype(BF16).astype(F32)
    return high, mid, values - high - mid


def emit(state, surface, wet, flags, places, fields, own_edges, one, two, raw, d):
    half = d.rows // 2
    is_ocean, even = flags[0] != 0, flags[3] == 0
    gap = jnp.zeros((4, CH), F32)
    terms = []
    for term in split_bf16(surface[flags[0]]):
        terms += [term, gap]
    proj = jnp.concatenate(terms + [gap, gap], axis=0).astype(BF16)
    for step in range(half):
        pair = jnp.concatenate([state[step], state[step + half]], axis=1)
        parts = jnp.dot(proj, pair, preferred_element_type=F32)
        whole = parts[0:8] + parts[8:16] + parts[16:24]
        raw[step * 8 : step * 8 + 8, :] = whole[:, :128]
        raw[(step + half) * 8 : (step + half) * 8 + 8, :] = whole[:, 128:]
    keeping = jnp.where(is_ocean, wet[...].astype(F32), 1.0)
    whole = [raw[pl.ds(field, d.rows, stride=8), :] * keeping for field in range(NS)]
    for field in range(NS):
        fields[field] = whole[field].astype(BF16)
    fields[NS] = pack_columns(whole, REACH).astype(BF16)
    edges = edge_columns(state, places, d)
    put_edges(own_edges, 0, edges, d)
    row = lanes(edges.shape) % d.block
    downward = jnp.where(row < 2, roll(edges, -d.rows), jnp.zeros_like(edges))
    upward = jnp.where(
        (row >= d.rows + 2) & (row < d.rows + 4), roll(edges, d.rows), jnp.zeros_like(edges)
    )
    for (ref, first), down in zip(strips(one, two, even, d), (even, jnp.logical_not(even))):
        ref[0:CH, :] = state[first]
        ref[CH : 2 * CH, :] = state[first + 1]
        put_edges(ref, 2 * CH, jnp.where(down, downward, upward), d)


def fetch(sources, targets, sems):
    copies = [
        pltpu.make_async_copy(source, target, sems.at[index])
        for index, (source, target) in enumerate(zip(sources, targets))
    ]
    for copy in copies:
        copy.start()
    return copies


def start_kernel(
    d, flags, far_given, far_surface, far_wet, far_offsets, far_weights,
    state, planes, sides, places, fields, own_edges, one, two,
    raw, tall, turned, given, surface, wet, offsets, weights, sems,
):
    rows = d.rows
    pieces = [pl.ds(at, 16) for at in range(0, CH, 16)]
    copies = fetch(
        [far_given.at[piece] for piece in pieces] + [far_surface, far_wet, far_offsets, far_weights],
        [given.at[piece] for piece in pieces] + [surface, wet, offsets, weights],
        sems,
    )
    edge_places(places, d)
    for index, piece in enumerate(pieces):
        copies[index].wait()
        turned[index * 16 * rows : (index + 1) * 16 * rows, :] = (
            given[piece].astype(F32).reshape(16 * rows, 128)
        )
    for row in range(rows):
        state[row] = turned[pl.ds(row, CH, stride=rows), :].astype(BF16)
    for copy in copies[len(pieces) :]:
        copy.wait()
    emit(state, surface, wet, flags, places, fields, own_edges, one, two, raw, d)
    for k in range(NK):
        code = (offsets[0, k] * SPAN + offsets[1, k]).astype(F32)
        tall[k * rows : (k + 1) * rows, :] = code
        tall[(NK + k) * rows : (NK + k + 1) * rows, :] = weights[k]
        planes[k] = code.astype(BF16)
        planes[NK + k] = weights[k].astype(BF16)
    packed = pack_columns([tall[plane * rows : (plane + 1) * rows, :] for plane in range(2 * NK)], 2)
    sides[...] = packed.astype(BF16)
    even = flags[3] == 0
    for (ref, first), down in zip(strips(one, two, even, d), (even, jnp.logical_not(even))):
        strip = [tall[pl.ds(first + step, 2 * NK, stride=rows), :] for step in range(2)]
        ref[d.strip : d.strip + 16, :] = jnp.concatenate(strip, axis=0).astype(BF16)
        ref[d.strip + 16 : d.strip + 32, :] = jnp.where(
            down, packed[rows - 16 : rows], packed[0:16]
        ).astype(BF16)


def decode(code):
    shifted = code.astype(jnp.int32) + (HW * SPAN + HW)
    rows = lax.shift_right_logical(shifted * 241, 12)
    return rows - HW, shifted - rows * SPAN - HW


def along_lanes(values, index):
    numbers = lax.GatherDimensionNumbers(
        offset_dims=(),
        collapsed_slice_dims=(1,),
        start_index_map=(1,),
        operand_batching_dims=(0,),
        start_indices_batching_dims=(0,),
    )
    return lax.gather(
        values, index[..., None], numbers, (1, 1), mode=lax.GatherScatterMode.PROMISE_IN_BOUNDS
    )


def couple(fields, coupled, rows):
    largest = None
    for field in range(NS):
        here = jnp.max(jnp.abs(fields[field]), axis=0, keepdims=True)
        largest = here if largest is None else jnp.maximum(largest, here)
    largest = jnp.maximum(jnp.max(largest, axis=1, keepdims=True), 1e-30)
    scale = FIXED / largest
    for pair in range(NS // 2):
        high, low = [
            jnp.floor(fields[2 * pair + part] * scale + 0.5).astype(jnp.int32) for part in range(2)
        ]
        coupled[pair] = high * (1 << 16) + (low + (1 << 15))
    return largest * (1 / FIXED)


def uncouple(values):
    high = lax.shift_right_arithmetic(values, 16)
    low = (values & 0xFFFF) - (1 << 15)
    return high.astype(F32), low.astype(F32)


def select_rows(source, start, picks):
    chosen = [[jnp.full((8, 128), 1 << 15, jnp.int32) for _ in range(NS // 2)] for _ in picks]
    for shift in range(-HW, HW + 1):
        at = pl.ds(start + shift, 8)
        values = [source[pair, at, :] for pair in range(NS // 2)]
        for slot, (rows, index, allowed) in enumerate(picks):
            here = (rows == shift) & allowed
            for pair in range(NS // 2):
                picked = along_lanes(values[pair], index)
                chosen[slot][pair] = jnp.where(here, picked, chosen[slot][pair])
    return [[part for values in pairs for part in uncouple(values)] for pairs in chosen]


def regrid_inside(coupled, unit, plan_x, part_x, first, tiles, tall):
    lane = lanes((8, 128))
    for step in range(tiles):
        at = first + step * 8
        picks = []
        weights = []
        for k in range(NK):
            rows, cols = decode(plan_x[pl.ds(k * tall + at, 8), :])
            weights.append(plan_x[pl.ds((NK + k) * tall + at, 8), :] * unit)
            column = lane + cols
            picks.append((rows, column & 127, (column >= 0) & (column < 128)))
        chosen = select_rows(coupled, at + 14, picks)
        for field in range(NS):
            total = chosen[0][field] * weights[0]
            for k in range(1, NK):
                total = total + chosen[k][field] * weights[k]
            part_x[pl.ds(field * tall + at, 8), :] = total


def edge_lanes():
    lane = lanes((8, 128))
    return ((lane + 8) & 127) // 32, ((lane + 8) & 31) - 8


def plan_edges(plan_x, plan_y, plan_e, first, tiles, tall, sides):
    part, place = edge_lanes()
    outer = place >= 8
    for step in range(tiles):
        at = first + step * 8
        code = jnp.zeros((8, 128), F32)
        weight = jnp.zeros((8, 128), F32)
        for k in range(NK):
            edge_code = roll(plan_x[pl.ds(k * tall + at, 8), :], 32 * k)
            edge_weight = roll(plan_x[pl.ds((NK + k) * tall + at, 8), :], 32 * k)
            if sides:
                edge_code = jnp.where(
                    outer, roll(plan_y[pl.ds(k * tall + at, 8), :], 32 * k + 16), edge_code
                )
                edge_weight = jnp.where(
                    outer, roll(plan_y[pl.ds((NK + k) * tall + at, 8), :], 32 * k + 16), edge_weight
                )
            code = jnp.where(part == k, edge_code, code)
            weight = jnp.where(part == k, edge_weight, weight)
        plan_e[pl.ds(at, 8), :] = code
        plan_e[pl.ds(tall + at, 8), :] = weight


def regrid_beside(coupled, unit, plan_e, part_x, forcing_x, forcing_y, first, tiles, tall, sides):
    lane = lanes((8, 128))
    part, place = edge_lanes()
    outer = place >= 8
    inner_column = place & 127
    outer_column = jnp.where(place < 16, place - 16, place + 112)
    edge = (lane < 8) | (lane >= 120)
    for step in range(tiles):
        at = first + step * 8
        rows, cols = decode(plan_e[pl.ds(at, 8), :])
        weight = plan_e[pl.ds(tall + at, 8), :] * unit
        column = jnp.where(outer, outer_column, inner_column) + cols
        within = (column >= 0) & (column < 128)
        index = jnp.where(within, column + 32, column) & 127
        (chosen,) = select_rows(coupled, at + 14, [(rows, index, outer | jnp.logical_not(within))])
        for field in range(NS):
            part_sum = chosen[field] * weight
            extra = part_sum
            for k in range(1, NK):
                extra = extra + roll(part_sum, -32 * k)
            total = part_x[pl.ds(field * tall + at, 8), :] + jnp.where(edge, extra, 0.0)
            forcing_x[pl.ds(at * 8 + field, 8, stride=8), :] = total
            forcing_x[pl.ds(at * 8 + field + 4, 8, stride=8), :] = total
            if sides:
                extra = roll(extra, -16)
                forcing_y[pl.ds(at * 8 + field, 8, stride=8), :] = extra
                forcing_y[pl.ds(at * 8 + field + 4, 8, stride=8), :] = extra


def twice_gelu(x):
    scale = (2 / jnp.pi) ** 0.5
    return x + x * jnp.tanh(x * (scale + (scale * 0.044715) * (x * x)))


def air(state, out, forcing_x, air_in, atm_out, d):
    half = d.rows // 2
    first = subs((8, 128)) < 4
    blank = jnp.zeros((32, 128), BF16)

    def inputs(row):
        at = (row + 2) * 8
        forced = jnp.where(first, forcing_x[at : at + 8, :], 1.0)
        forced = jnp.concatenate([forced, jnp.zeros_like(forced)], axis=0).astype(BF16)
        return jnp.concatenate([state[row], forced, blank], axis=0)

    for step in range(half):
        pair = jnp.concatenate([inputs(step), inputs(step + half)], axis=1)
        hidden = twice_gelu(jnp.dot(air_in[...], pair, preferred_element_type=F32)).astype(BF16)
        update = jnp.dot(atm_out[...], hidden, preferred_element_type=F32)
        for offset in range(2):
            row = step + offset * half
            change = update[:, offset * 128 : (offset + 1) * 128]
            out(row, state[row].astype(F32) + 0.5 * change)


def edge_forcing(forcing_x, forcing_y, d):
    lane = lanes((8, d.edge))
    block = lane // d.block
    row = lane % d.block

    inner = outer = jnp.zeros((8, d.edge), F32)
    for step in range(d.rows + 4):
        at = pl.ds(step * 8, 8)
        pad = [jnp.zeros((8, 128), F32)] * (d.pieces - 1)
        here = jnp.concatenate([forcing_x[at, :]] + pad, axis=1)
        there = jnp.concatenate([forcing_y[at, :]] + pad, axis=1)
        for index, column in enumerate((126, 0, 127, 1)):
            shift = step + index * d.block - column
            match = (block == index) & (row == step)
            if column in (0, 127):
                inner = jnp.where(match, roll(here, shift), inner)
            outer = jnp.where(match, roll(there, shift), outer)
    return inner, outer


def roll_rows(state, upper, lower, rolled, d):
    def put(row, values):
        rolled[row, 0:CH, :] = roll(values, 1)
        rolled[row, CH : 2 * CH, :] = values
        rolled[row, 2 * CH : 3 * CH, :] = roll(values, -1)

    for step in range(2):
        put(step, upper[step * CH : (step + 1) * CH, :])
        put(d.rows + 2 + step, lower[step * CH : (step + 1) * CH, :])
    for row in range(d.rows):
        put(row + 2, state[row])


def sea(
    state, rolled, edges, left, right, out, forcing_x, forcing_y, ocn_in, ocn_out, wet,
    at_top, at_bottom, stack, hidden, side, d,
):
    rows, block = d.rows, d.block
    lane = lanes((CH, 128))
    spot = lanes((CH, d.edge))
    part = spot // block
    inner = edges
    outer = jnp.where((part == 0) | (part == 2), left, right)

    def sides_of(inner, outer, spot):
        first = spot < block
        return (
            jnp.where(first, outer, roll(inner, -block)),
            jnp.where(first, roll(outer, -2 * block), outer),
            jnp.where(first, roll(inner, -block), roll(outer, -2 * block)),
        )

    beside = sides_of(inner, outer, spot)
    middle = beside[1]
    force_in, force_out = edge_forcing(forcing_x, forcing_y, d)
    beside_forcing = sides_of(force_in, force_out, lanes((8, d.edge)))
    sub = subs((8, d.edge))
    ones = jnp.ones((8, d.edge), F32)
    forced = jnp.concatenate(
        [
            jnp.where(sub < 4, beside_forcing[0], beside_forcing[1]),
            jnp.where(sub < 4, beside_forcing[2], ones),
        ],
        axis=0,
    ).astype(BF16)
    columns = jnp.concatenate(list(beside) + [forced], axis=0)
    for tap in range(3):
        side[tap * 256 : (tap + 1) * 256, :] = roll(columns, -tap)

    sub_row = subs((8, 128))
    lane_row = lanes((8, 128))

    for row in range(rows + 4):
        entry = roll(middle, -row)[:, :128]
        stack[row, 0:CH, :] = jnp.where(lane == 0, entry, rolled[row, 0:CH, :])
        stack[row, CH : 2 * CH, :] = rolled[row, CH : 2 * CH, :]
        entry = roll(middle, 127 - block - row)[:, :128]
        stack[row, 2 * CH : 3 * CH, :] = jnp.where(lane == 127, entry, rolled[row, 2 * CH : 3 * CH, :])
        here, there = forcing_x[row * 8 : row * 8 + 8, :], forcing_y[row * 8 : row * 8 + 8, :]
        before = roll(jnp.where(lane_row == 127, there, here), 1)
        after = roll(jnp.where(lane_row == 0, there, here), -1)
        stack[row, 3 * CH : 256, :] = jnp.concatenate(
            [jnp.where(sub_row < 4, before, here), jnp.where(sub_row < 4, after, 1.0)], axis=0
        ).astype(BF16)

    pairs = (rows + 2) // 2

    for step in range(pairs):
        taps = jnp.concatenate(
            [
                stack[step : step + 3].reshape(3 * 256, 128),
                stack[step + pairs : step + pairs + 3].reshape(3 * 256, 128),
            ],
            axis=1,
        )
        active = twice_gelu(jnp.dot(ocn_in[...], taps, preferred_element_type=F32))
        low, high = active[:, :128], active[:, 128:]
        if step == 0:
            low = jnp.where(at_top != 0, 0.0, low)
        if step == pairs - 1:
            high = jnp.where(at_bottom != 0, 0.0, high)
        hidden[step, 0:HIDK, :] = low.astype(BF16)
        hidden[step + pairs, 0:HIDK, :] = high.astype(BF16)
        blank = jnp.zeros((HIDP - HIDK, 128), BF16)
        hidden[step, HIDK:HIDP, :] = blank
        hidden[step + pairs, HIDK:HIDP, :] = blank

    product = jnp.dot(ocn_in[...], side[...], preferred_element_type=F32)
    spot = lanes((1, d.edge)) % block
    gone = ((spot == 0) & (at_top != 0)) | ((spot == rows + 1) & (at_bottom != 0))
    active = jnp.where(gone, 0.0, twice_gelu(product)).astype(BF16)
    active = jnp.concatenate([active, jnp.zeros((HIDP - HIDK, d.edge), BF16)], axis=0)

    def taps_of(slices):
        total = None
        for tap, values in enumerate(slices):
            weights = ocn_out[tap * 3 * CH : (tap + 1) * 3 * CH, :]
            product = jnp.dot(weights, values, preferred_element_type=F32)
            total = product if total is None else total + product
        return total

    partial = taps_of([roll(active, -tap) for tap in range(3)])
    from_left, from_right = partial[0:CH], partial[2 * CH : 3 * CH]
    half = rows // 2
    for step in range(half):
        product = taps_of(
            [
                jnp.concatenate([hidden[step + tap], hidden[step + half + tap]], axis=1)
                for tap in range(3)
            ]
        )
        for offset in range(2):
            row = step + offset * half
            sums = product[:, offset * 128 : (offset + 1) * 128]
            entry = roll(from_left, -row)[:, :128]
            total = sums[CH : 2 * CH] + jnp.where(lane == 0, entry, roll(sums[0:CH], 1))
            entry = roll(from_right, 127 - block - row)[:, :128]
            total = total + jnp.where(lane == 127, entry, roll(sums[2 * CH : 3 * CH], -1))
            update = total * (0.5 * wet[row : row + 1, :].astype(F32))
            out(row, state[row].astype(F32) + update)


def prepare(atm_in, atm_bias, ocn_in, ocn_bias, ocn_out, air_in, first, second, is_ocean):
    def bias_rows(ref, width):
        row = jnp.concatenate([ref[index : index + 1, :] for index in range(ref.shape[0])], axis=1)
        terms = list(split_bf16(row)) + [jnp.zeros_like(row)]
        bias = jnp.concatenate(terms, axis=0)
        return jnp.pad(bias, ((0, 0), (0, width - bias.shape[1])))

    @pl.when(is_ocean == 0)
    def _():
        columns = jnp.concatenate(
            [atm_in[...].astype(F32), bias_rows(atm_bias, HA), jnp.zeros((40, HA), F32)], axis=0
        )
        air_in[...] = columns.T.astype(BF16)

    @pl.when(is_ocean != 0)
    def _():
        bias = bias_rows(ocn_bias, 256)
        count = ocn_in.shape[2]
        for tap in range(3):
            whole = [ocn_in[3 * tap + side].astype(F32) for side in range(3)]
            whole = [jnp.pad(values, ((0, 0), (0, 256 - count))) for values in whole]
            rows = [values[:CH] for values in whole] + [values[CH:] for values in whole]
            rows.append(bias if tap == 0 else jnp.zeros((4, 256), F32))
            columns = jnp.concatenate(rows, axis=0).T
            first[:, tap * 256 : (tap + 1) * 256] = columns[:HIDK].astype(BF16)
        for tap in range(9):
            values = ocn_out[tap].astype(F32)
            second[tap * CH : (tap + 1) * CH, :] = jnp.pad(
                values, ((0, 0), (0, HIDP - count))
            ).astype(BF16)


def ends(flags):
    at_top, at_bottom, even = flags[1] != 0, flags[2] != 0, flags[3] == 0

    def up_and_down(one, two):
        above = jnp.where(even, two, one).astype(F32)
        below = jnp.where(even, one, two).astype(F32)
        return jnp.where(at_top, 0.0, above), jnp.where(at_bottom, 0.0, below)

    return up_and_down


def middle_kernel(d, opening, *refs):
    refs = list(refs)
    take = lambda count: [refs.pop(0) for _ in range(count)]
    flags, state, field_one, beside, field_two, from_one, from_two = take(7)
    if opening:
        planes, *far_weights = take(6)
    else:
        (plan_x,) = take(1)
    part_x, fields_x, rolled = take(3)
    if opening:
        plan_x, *made_weights = take(4)
    (coupled,) = take(1)
    if opening:
        *raw_weights, sems = take(6)
        copies = fetch(far_weights, raw_weights, sems)
    rows, tall = d.rows, d.tall
    is_ocean = flags[0]
    up_and_down = ends(flags)

    if opening:

        @pl.when(is_ocean != 0)
        def _():
            base = d.strip
            pair = up_and_down(from_one[base : base + 16, :], from_two[base : base + 16, :])
            plan_x[...] = jnp.zeros_like(plan_x)
            for step, strip in zip((0, rows + 2), pair):
                for index in range(2):
                    plan_x[pl.ds(step + index, 2 * NK, stride=tall), :] = strip[index * 8 : (index + 1) * 8]

        for plane in range(2 * NK):
            plan_x[plane * tall + 2 : plane * tall + 2 + rows, :] = planes[plane].astype(F32)

    for field in range(NS):
        pair = up_and_down(field_one[field], field_two[field])
        fields_x[field, 0:16, :] = pair[0][rows - 16 : rows]
        fields_x[field, 16 : 16 + rows, :] = beside[field].astype(F32)
        fields_x[field, 16 + rows : 32 + rows, :] = pair[1][0:16]

    unit = couple(fields_x, coupled, rows)

    @pl.when(is_ocean == 0)
    def _():
        regrid_inside(coupled, unit, plan_x, part_x, 2, rows // 8, tall)

    @pl.when(is_ocean != 0)
    def _():
        regrid_inside(coupled, unit, plan_x, part_x, 0, d.tiles, tall)
        upper, lower = up_and_down(from_one[0 : 2 * CH, :], from_two[0 : 2 * CH, :])
        roll_rows(state, upper.astype(BF16), lower.astype(BF16), rolled, d)

    if opening:
        for copy in copies:
            copy.wait()
        prepare(*raw_weights, *made_weights, is_ocean)


def step_kernel(d, opening, closing, *refs):
    refs = list(refs)
    take = lambda count: [refs.pop(0) for _ in range(count)]
    flags, state, wet, from_left, from_right = take(5)
    part_x, fields_x, rolled, edges, plan_x, air_in, first, second, atm_out = take(9)
    if not opening:
        (plan_e,) = take(1)
    if not closing:
        surface, places = take(2)
    (out,) = take(1)
    if not closing:
        fields, new_edges, one, two = take(4)
    if opening:
        (plan_e,) = take(1)
    window, coupled, forcing_x, forcing_y, stack, hidden, side, raw = take(8)
    if opening:
        (plan_y,) = take(1)
    rows, tall = d.rows, d.tall
    is_ocean, at_top, at_bottom = flags[0], flags[1], flags[2]
    up_and_down = ends(flags)

    if opening:

        @pl.when(is_ocean != 0)
        def _():
            plan_y[...] = jnp.zeros_like(plan_y)
            base = d.edge_rows
            parts = [
                (ref[base : base + 16, :], ref[base + 16 + rows : base + 32 + rows, :],
                 ref[base + 16 : base + 16 + rows, :])
                for ref in (from_left, from_right)
            ]
            for plane in range(2 * NK):
                first_end, second_end, own = [
                    unpack_columns(left, right, plane, 2 * NK, 2) for left, right in zip(*parts)
                ]
                above, below = up_and_down(first_end, second_end)
                at = plane * tall
                plan_y[at : at + 2, :] = above[14:16]
                plan_y[at + 2 : at + 2 + rows, :] = own
                plan_y[at + 2 + rows : at + 4 + rows, :] = below[0:2]

    base = d.edge_rows + (rows + 32 if opening else 0)
    parts = [
        (ref[base : base + 16, :], ref[base + 16 + rows : base + 32 + rows, :],
         ref[base + 16 : base + 16 + rows, :])
        for ref in (from_left, from_right)
    ]
    for field in range(NS):
        first_end, second_end, own = [
            unpack_columns(left, right, field, NS, REACH) for left, right in zip(*parts)
        ]
        above, below = up_and_down(first_end, second_end)
        for at, values in ((0, above), (16, own), (16 + rows, below)):
            count = values.shape[0]
            inside = roll(fields_x[field, at : at + count, :], 32)
            lane = lanes(values.shape)
            near = (lane >= 32 - REACH) & (lane < 32 + REACH)
            far = (lane < REACH) | (lane >= 128 - REACH)
            kept = jnp.where(near, inside, jnp.where(far, values, 0.0))
            window[field, at : at + count, :] = kept
    unit = couple(window, coupled, rows)

    def put(row, values):
        if closing:
            raw[pl.ds(row, CH, stride=rows), :] = values
        else:
            out[row] = values.astype(BF16)

    @pl.when(is_ocean == 0)
    def _():
        if opening:
            plan_edges(plan_x, plan_y, plan_e, 2, rows // 8, tall, False)
        regrid_beside(
            coupled, unit, plan_e, part_x, forcing_x, forcing_y, 2, rows // 8, tall, False
        )
        air(state, put, forcing_x, air_in, atm_out, d)

    @pl.when(is_ocean != 0)
    def _():
        if opening:
            plan_edges(plan_x, plan_y, plan_e, 0, d.tiles, tall, True)
        regrid_beside(
            coupled, unit, plan_e, part_x, forcing_x, forcing_y, 0, d.tiles, tall, True
        )
        joined = [get_edges(ref, 0, d) for ref in (from_left, from_right)]
        sea(
            state, rolled, get_edges(edges, 0, d), *joined, put, forcing_x, forcing_y,
            first, second, wet, at_top, at_bottom, stack, hidden, side, d,
        )

    if closing:
        out[...] = raw[...].reshape(CH, rows, 128).astype(BF16)
    else:
        emit(out, surface, wet, flags, places, fields, new_edges, one, two, raw, d)


VMEM = pl.BlockSpec(memory_space=pltpu.VMEM)
HBM = pl.BlockSpec(memory_space=pltpu.HBM)
SMEM = pl.BlockSpec(memory_space=pltpu.SMEM)
PARAMS = pltpu.CompilerParams(vmem_limit_bytes=48 * 1024 * 1024)


def shape(*dims, dtype=BF16):
    return jax.ShapeDtypeStruct(dims, dtype)


def send(x, move):
    names = ("grp", "lat", "lon")
    sizes = [lax.axis_size(name) for name in names]
    pairs = []
    for group in range(sizes[0]):
        for lat in range(sizes[1]):
            for lon in range(sizes[2]):
                to = move(group, lat, lon)
                if to is None or not 0 <= to[1] < sizes[1]:
                    continue
                target = (to[0] * sizes[1] + to[1]) * sizes[2] + to[2] % sizes[2]
                pairs.append(((group * sizes[1] + lat) * sizes[2] + lon, target))
    return lax.ppermute(x, names, pairs)


def swap_rows(x, turn, across):
    count = lax.axis_size("lat")

    def move(group, lat, lon):
        other = ((lat + turn) ^ 1) - turn
        if not 0 <= other < count:
            return 1 - group, lat, lon
        return (1 - group if across else group), other, lon

    return send(x, move)


def exchange(fields, own_edges, one, two, sides, d):
    rows = d.rows
    from_one = swap_rows(one, 0, False)
    from_two = swap_rows(two, 1, False)
    field_one = swap_rows(fields, 0, True)
    field_two = swap_rows(fields, 1, True)
    beside = send(fields, lambda g, i, j: (1 - g, i, j))
    lat, count = lax.axis_index("lat"), lax.axis_size("lat")
    odd = lat % 2 == 1
    edges = own_edges
    for turn, ref in ((0, from_one), (1, from_two)):
        other = ((lat + turn) ^ 1) - turn
        there = (other >= 0) & (other < count)
        edges = edges + jnp.where(there, ref[2 * CH : d.strip], 0)
    edges, beside, field_one, field_two = lax.optimization_barrier(
        (edges, beside, field_one, field_two)
    )
    outer = [field_one[NS], field_two[NS]]
    if rows != 16:
        outer = [
            jnp.where(odd, outer[0][rows - 16 :], outer[0][:16]),
            jnp.where(odd, outer[1][:16], outer[1][rows - 16 :]),
        ]
    packed = [edges]
    if sides is not None:
        packed += [from_one[d.strip + 16 :], sides, from_two[d.strip + 16 :]]
    packed += [outer[0], beside[NS], outer[1]]
    packed = jnp.concatenate(packed, axis=0)
    from_left = send(packed, lambda g, i, j: (g, i, j + 1))
    from_right = send(packed, lambda g, i, j: (g, i, j - 1))
    return (field_one, beside, field_two, from_one, from_two), (from_left, from_right), edges


def local(
    coupled_state, land_mask, regrid_offsets, regrid_weights, surface_proj,
    atm_in, atm_bias, atm_out, ocn_in, ocn_bias, ocn_out,
):
    rows = coupled_state.shape[2]
    assert coupled_state.shape[3] == 128
    d = Dims(rows)
    group = lax.axis_index("grp")
    lat = lax.axis_index("lat")
    flags = jnp.stack(
        [group, lat == 0, lat == lax.axis_size("lat") - 1, lat % 2]
    ).astype(jnp.int32)
    raw_weights = (
        atm_in.T,
        atm_bias.reshape(HA // 128, 128),
        jnp.transpose(ocn_in, (1, 2, 0)),
        ocn_bias[None],
        jnp.transpose(ocn_out, (1, 0, 2)),
    )
    state_shape = shape(rows, CH, 128)
    emitted = [
        shape(NS + 1, rows, 128),
        shape(d.edge_rows, 128),
        shape(d.strip, 128),
        shape(d.strip, 128),
    ]
    raw = pltpu.VMEM((rows * 8, 128), F32)
    turned = pltpu.VMEM((CH * rows, 128), F32)

    def call(kernel, operands, outs, scratch, name, far=()):
        scratch = scratch + [pltpu.VMEM(x.shape, x.dtype) for x in far]
        if far:
            scratch.append(pltpu.SemaphoreType.DMA((len(far) + CH // 16,)))

        far = [pltpu.with_memory_space_constraint(x, pltpu.HBM) for x in far]
        return pl.pallas_call(
            kernel,
            out_shape=outs,
            in_specs=[SMEM] + [VMEM] * len(operands) + [HBM] * len(far),
            out_specs=[VMEM] * len(outs),
            scratch_shapes=scratch,
            compiler_params=PARAMS,
            name=name,
        )(flags, *operands, *far)

    state, planes, sides, places, fields, edges, one, two = call(
        functools.partial(start_kernel, d),
        (),
        [state_shape, shape(2 * NK, rows, 128), shape(rows, 128), shape(rows * 128, d.edge)]
        + emitted[:2]
        + [shape(d.strip + 32, 128)] * 2,
        [raw, pltpu.VMEM((2 * NK * rows, 128), F32), turned],
        "start",
        (coupled_state[0], surface_proj, land_mask, regrid_offsets[0], regrid_weights[0]),
    )

    plan = shape(2 * NK * d.tall, 128, dtype=F32)
    between = [
        shape(NS * d.tall, 128, dtype=F32),
        shape(NS, rows + 32, 128, dtype=F32),
        shape(rows + 4, 3 * CH, 128),
    ]
    made = [shape(HA, 128), shape(HIDK, 768), shape(9 * CH, HIDP)]
    coupled = pltpu.VMEM((NS // 2, rows + 32, 128), jnp.int32)
    scratch = [
        pltpu.VMEM((NS, rows + 32, 128), F32),
        coupled,
        pltpu.VMEM((d.tall * 8, 128), F32),
        pltpu.VMEM((d.tall * 8, 128), F32),
        pltpu.VMEM((rows + 4, 256, 128), BF16),
        pltpu.VMEM((rows + 2, HIDP, 128), BF16),
        pltpu.VMEM((768, d.edge), BF16),
    ]

    vertical, horizontal, edges = exchange(fields, edges, one, two, sides, d)
    *shared, plan_x, air_in, first, second = call(
        functools.partial(middle_kernel, d, True),
        (state, *vertical, planes),
        between + [plan] + made,
        [coupled],
        "first_middle",
        raw_weights,
    )
    weights = (air_in, first, second, atm_out)
    state, fields, edges, one, two, plan_e = call(
        functools.partial(step_kernel, d, True, False),
        (state, land_mask, *horizontal, *shared, edges, plan_x, *weights, surface_proj, places),
        [state_shape] + emitted + [shape(2 * d.tall, 128, dtype=F32)],
        scratch + [raw, pltpu.VMEM(plan.shape, F32)],
        "first_step",
    )

    vertical, horizontal, edges = exchange(fields, edges, one, two, None, d)
    shared = call(
        functools.partial(middle_kernel, d, False),
        (state, *vertical, plan_x),
        between,
        [coupled],
        "second_middle",
    )
    (state,) = call(
        functools.partial(step_kernel, d, False, True),
        (state, land_mask, *horizontal, *shared, edges, plan_x, *weights, plan_e),
        [shape(CH, rows, 128)],
        scratch + [turned],
        "second_step",
    )
    return state[None]


def solution(mesh):
    return jax.shard_map(
        local,
        mesh=mesh,
        in_specs=(
            P("grp", None, "lat", "lon"),
            P("lat", "lon"),
            P("grp", None, None, "lat", "lon"),
            P("grp", None, "lat", "lon"),
            P(),
            P(),
            P(),
            P(),
            P(),
            P(),
            P(),
        ),
        out_specs=P("grp", None, "lat", "lon"),
        check_vma=False,
    )
```

```python
import functools

import jax
import jax.numpy as jnp
from jax import lax
from jax.experimental import pallas as pl
from jax.experimental.pallas import tpu as pltpu
from jax.sharding import PartitionSpec as P

CH = 80
NS = 4
NK = 4
HA = 384
HW = 8
SPAN = 2 * HW + 1
REACH = HW + 2
FIXED = 32767.0
HIDK = 208
HIDP = 256
F32 = jnp.float32
BF16 = jnp.bfloat16


def roll(x, shift, axis=1):
    size = x.shape[axis]
    if isinstance(shift, int):
        shift = shift % size
        if shift == 0:
            return x
    return pltpu.roll(x, shift, axis)


def lanes(shape):
    return lax.broadcasted_iota(jnp.int32, shape, len(shape) - 1)


def subs(shape):
    return lax.broadcasted_iota(jnp.int32, shape, len(shape) - 2)


class Dims:
    def __init__(self, rows):
        self.rows = rows
        self.block = 32 if rows + 4 <= 32 else 64
        self.edge = 4 * self.block
        self.pieces = self.edge // 128
        self.edge_rows = CH * self.pieces
        self.tiles = -(-(rows + 4) // 8)
        self.tall = 8 * self.tiles
        self.strip = 2 * CH + self.edge_rows


def put_edges(ref, at, edges, d):
    for piece in range(d.pieces):
        ref[at + piece * CH : at + (piece + 1) * CH, :] = edges[:, piece * 128 : (piece + 1) * 128]


def get_edges(ref, at, d):
    return jnp.concatenate(
        [ref[at + piece * CH : at + (piece + 1) * CH, :] for piece in range(d.pieces)], axis=1
    )


def edge_places(places, d):
    lane = lanes((1, d.edge))
    block = lane // d.block
    row = lane % d.block - 2
    column = jnp.where(block == 0, 126, jnp.where(block == 1, 0, jnp.where(block == 2, 127, 1)))
    own = (row >= 0) & (row < d.rows)
    target = jnp.where(own, column, -1)
    position = subs((128, d.edge))
    for step in range(d.rows):
        place = (position == jnp.where(row == step, target, -1)).astype(F32).astype(BF16)
        places[step * 128 : (step + 1) * 128, :] = place


def edge_columns(state, places, d):
    whole = jnp.concatenate([state[step] for step in range(d.rows)], axis=1)
    return jnp.dot(whole, places[...], preferred_element_type=F32).astype(BF16)


def pack_columns(values, reach):
    lane = lanes(values[0].shape)
    pitch = 128 // len(values)
    packed = jnp.zeros_like(values[0])
    for index, value in enumerate(values):
        at = index * pitch
        packed = jnp.where((lane >= at) & (lane < at + reach), roll(value, at), packed)
        at += reach
        packed = jnp.where((lane >= at) & (lane < at + reach), roll(value, at + reach - 128), packed)
    return packed


def unpack_columns(left, right, index, count, reach):
    at = index * (128 // count)
    left = roll(left.astype(F32), 128 - at - 2 * reach)
    return jnp.where(lanes(left.shape) < 64, roll(right.astype(F32), -at), left)


def strips(one, two, even, d):
    last = d.rows - 2
    return (one, jnp.where(even, last, 0)), (two, jnp.where(even, 0, last))


def split_bf16(values):
    high = values.astype(BF16).astype(F32)
    mid = (values - high).astype(BF16).astype(F32)
    return high, mid, values - high - mid


class Emission:
    def __init__(self, surface, flags, places, raw, d):
        gap = jnp.zeros((4, CH), F32)
        terms = []
        for term in split_bf16(surface[flags[0]]):
            terms += [term, gap]
        self.proj = jnp.concatenate(terms + [gap, gap], axis=0).astype(BF16)
        self.places, self.raw, self.d, self.flags = places, raw, d, flags
        self.edges = None

    def add(self, step, low, high):
        pair = jnp.concatenate([low, high], axis=1)
        parts = jnp.dot(self.proj, pair, preferred_element_type=F32)
        whole = parts[0:8] + parts[8:16] + parts[16:24]
        other = step + self.d.rows // 2
        self.raw[step * 8 : step * 8 + 8, :] = whole[:, :128]
        self.raw[other * 8 : other * 8 + 8, :] = whole[:, 128:]
        places = [self.places[row * 128 : (row + 1) * 128, :] for row in (step, other)]
        edges = jnp.dot(pair, jnp.concatenate(places, axis=0), preferred_element_type=F32)
        self.edges = edges if self.edges is None else self.edges + edges

    def close(self, state, wet, fields, own_edges, one, two):
        d, even = self.d, self.flags[3] == 0
        keeping = jnp.where(self.flags[0] != 0, wet[...].astype(F32), 1.0)
        whole = [self.raw[pl.ds(field, d.rows, stride=8), :] * keeping for field in range(NS)]
        for field in range(NS):
            fields[field] = whole[field].astype(BF16)
        fields[NS] = pack_columns(whole, REACH).astype(BF16)
        edges = self.edges.astype(BF16)
        put_edges(own_edges, 0, edges, d)
        row = lanes(edges.shape) % d.block
        downward = jnp.where(row < 2, roll(edges, -d.rows), jnp.zeros_like(edges))
        upward = jnp.where(
            (row >= d.rows + 2) & (row < d.rows + 4), roll(edges, d.rows), jnp.zeros_like(edges)
        )
        for (ref, first), down in zip(strips(one, two, even, d), (even, jnp.logical_not(even))):
            ref[0:CH, :] = state[first]
            ref[CH : 2 * CH, :] = state[first + 1]
            put_edges(ref, 2 * CH, jnp.where(down, downward, upward), d)


def fetch(sources, targets, sems):
    copies = [
        pltpu.make_async_copy(source, target, sems.at[index])
        for index, (source, target) in enumerate(zip(sources, targets))
    ]
    for copy in copies:
        copy.start()
    return copies


def start_kernel(
    d, flags, far_given, far_surface, far_wet, far_offsets, far_weights,
    state, planes, sides, places, fields, own_edges, one, two,
    raw, tall, turned, given, surface, wet, offsets, weights, sems,
):
    rows = d.rows
    pieces = [pl.ds(at, 16) for at in range(0, CH, 16)]
    copies = fetch(
        [far_given.at[piece] for piece in pieces] + [far_surface, far_wet, far_offsets, far_weights],
        [given.at[piece] for piece in pieces] + [surface, wet, offsets, weights],
        sems,
    )
    edge_places(places, d)
    for index, piece in enumerate(pieces):
        copies[index].wait()
        turned[index * 16 * rows : (index + 1) * 16 * rows, :] = (
            given[piece].astype(F32).reshape(16 * rows, 128)
        )
    for row in range(rows):
        state[row] = turned[pl.ds(row, CH, stride=rows), :].astype(BF16)
    for copy in copies[len(pieces) :]:
        copy.wait()
    emission = Emission(surface, flags, places, raw, d)
    for step in range(rows // 2):
        emission.add(step, state[step], state[step + rows // 2])
    emission.close(state, wet, fields, own_edges, one, two)
    for k in range(NK):
        code = (offsets[0, k] * SPAN + offsets[1, k]).astype(F32)
        tall[k * rows : (k + 1) * rows, :] = code
        tall[(NK + k) * rows : (NK + k + 1) * rows, :] = weights[k]
        planes[k] = code.astype(BF16)
        planes[NK + k] = weights[k].astype(BF16)
    packed = pack_columns([tall[plane * rows : (plane + 1) * rows, :] for plane in range(2 * NK)], 2)
    sides[...] = packed.astype(BF16)
    even = flags[3] == 0
    for (ref, first), down in zip(strips(one, two, even, d), (even, jnp.logical_not(even))):
        strip = [tall[pl.ds(first + step, 2 * NK, stride=rows), :] for step in range(2)]
        ref[d.strip : d.strip + 16, :] = jnp.concatenate(strip, axis=0).astype(BF16)
        ref[d.strip + 16 : d.strip + 32, :] = jnp.where(
            down, packed[rows - 16 : rows], packed[0:16]
        ).astype(BF16)


def decode(code):
    shifted = code.astype(jnp.int32) + (HW * SPAN + HW)
    rows = lax.shift_right_logical(shifted * 241, 12)
    return rows - HW, shifted - rows * SPAN - HW


def along_lanes(values, index):
    numbers = lax.GatherDimensionNumbers(
        offset_dims=(),
        collapsed_slice_dims=(1,),
        start_index_map=(1,),
        operand_batching_dims=(0,),
        start_indices_batching_dims=(0,),
    )
    return lax.gather(
        values, index[..., None], numbers, (1, 1), mode=lax.GatherScatterMode.PROMISE_IN_BOUNDS
    )


def couple(fields, coupled, rows):
    largest = None
    for field in range(NS):
        here = jnp.max(jnp.abs(fields[field]), axis=0, keepdims=True)
        largest = here if largest is None else jnp.maximum(largest, here)
    largest = jnp.maximum(jnp.max(largest, axis=1, keepdims=True), 1e-30)
    scale = FIXED / largest
    for pair in range(NS // 2):
        high, low = [
            jnp.floor(fields[2 * pair + part] * scale + 0.5).astype(jnp.int32) for part in range(2)
        ]
        coupled[pair] = high * (1 << 16) + (low + (1 << 15))
    return largest * (1 / FIXED)


def uncouple(values):
    high = lax.shift_right_arithmetic(values, 16)
    low = (values & 0xFFFF) - (1 << 15)
    return high.astype(F32), low.astype(F32)


def select_rows(source, start, picks):
    parts = source.shape[0]
    blank = jnp.full((8, 128), 1 << 15, jnp.int32) if parts < NS else jnp.zeros((8, 128), F32)
    chosen = [[blank for _ in range(parts)] for _ in picks]
    for shift in range(-HW, HW + 1):
        at = pl.ds(start + shift, 8)
        values = [source[part, at, :] for part in range(parts)]
        for slot, (rows, index, allowed) in enumerate(picks):
            here = (rows == shift) & allowed
            for part in range(parts):
                picked = along_lanes(values[part], index)
                chosen[slot][part] = jnp.where(here, picked, chosen[slot][part])
    if parts == NS:
        return chosen
    return [[part for values in pairs for part in uncouple(values)] for pairs in chosen]


def regrid_inside(coupled, unit, plan_x, part_x, first, tiles, tall):
    lane = lanes((8, 128))
    for step in range(tiles):
        at = first + step * 8
        picks = []
        weights = []
        for k in range(NK):
            rows, cols = decode(plan_x[pl.ds(k * tall + at, 8), :])
            weights.append(plan_x[pl.ds((NK + k) * tall + at, 8), :] * unit)
            column = lane + cols
            picks.append((rows, column & 127, (column >= 0) & (column < 128)))
        chosen = select_rows(coupled, at + 14, picks)
        for field in range(NS):
            total = chosen[0][field] * weights[0]
            for k in range(1, NK):
                total = total + chosen[k][field] * weights[k]
            part_x[pl.ds(field * tall + at, 8), :] = total


def edge_lanes():
    lane = lanes((8, 128))
    return ((lane + 8) & 127) // 32, ((lane + 8) & 31) - 8


def plan_edges(plan_x, plan_y, plan_e, first, tiles, tall, sides):
    part, place = edge_lanes()
    outer = place >= 8
    for step in range(tiles):
        at = first + step * 8
        code = jnp.zeros((8, 128), F32)
        weight = jnp.zeros((8, 128), F32)
        for k in range(NK):
            edge_code = roll(plan_x[pl.ds(k * tall + at, 8), :], 32 * k)
            edge_weight = roll(plan_x[pl.ds((NK + k) * tall + at, 8), :], 32 * k)
            if sides:
                edge_code = jnp.where(
                    outer, roll(plan_y[pl.ds(k * tall + at, 8), :], 32 * k + 16), edge_code
                )
                edge_weight = jnp.where(
                    outer, roll(plan_y[pl.ds((NK + k) * tall + at, 8), :], 32 * k + 16), edge_weight
                )
            code = jnp.where(part == k, edge_code, code)
            weight = jnp.where(part == k, edge_weight, weight)
        plan_e[pl.ds(at, 8), :] = code
        plan_e[pl.ds(tall + at, 8), :] = weight


def regrid_beside(window, plan_e, part_x, forcing_x, forcing_y, first, tiles, tall, sides):
    lane = lanes((8, 128))
    part, place = edge_lanes()
    outer = place >= 8
    inner_column = place & 127
    outer_column = jnp.where(place < 16, place - 16, place + 112)
    edge = (lane < 8) | (lane >= 120)
    for step in range(tiles):
        at = first + step * 8
        rows, cols = decode(plan_e[pl.ds(at, 8), :])
        weight = plan_e[pl.ds(tall + at, 8), :]
        column = jnp.where(outer, outer_column, inner_column) + cols
        within = (column >= 0) & (column < 128)
        index = jnp.where(within, column + 32, column) & 127
        (chosen,) = select_rows(window, at + 14, [(rows, index, outer | jnp.logical_not(within))])
        for field in range(NS):
            part_sum = chosen[field] * weight
            extra = part_sum
            for k in range(1, NK):
                extra = extra + roll(part_sum, -32 * k)
            total = part_x[pl.ds(field * tall + at, 8), :] + jnp.where(edge, extra, 0.0)
            forcing_x[pl.ds(at * 8 + field, 8, stride=8), :] = total
            forcing_x[pl.ds(at * 8 + field + 4, 8, stride=8), :] = total
            if sides:
                extra = roll(extra, -16)
                forcing_y[pl.ds(at * 8 + field, 8, stride=8), :] = extra
                forcing_y[pl.ds(at * 8 + field + 4, 8, stride=8), :] = extra


def twice_gelu(x):
    scale = (2 / jnp.pi) ** 0.5
    return x + x * jnp.tanh(x * (scale + (scale * 0.044715) * (x * x)))


def air(state, out, forcing_x, air_in, atm_out, d):
    half = d.rows // 2
    first = subs((8, 128)) < 4
    blank = jnp.zeros((32, 128), BF16)

    def inputs(row):
        at = (row + 2) * 8
        forced = jnp.where(first, forcing_x[at : at + 8, :], 1.0)
        forced = jnp.concatenate([forced, jnp.zeros_like(forced)], axis=0).astype(BF16)
        return jnp.concatenate([state[row], forced, blank], axis=0)

    for step in range(half):
        pair = jnp.concatenate([inputs(step), inputs(step + half)], axis=1)
        hidden = twice_gelu(jnp.dot(air_in[...], pair, preferred_element_type=F32)).astype(BF16)
        update = jnp.dot(atm_out[...], hidden, preferred_element_type=F32)
        news = []
        for offset in range(2):
            change = update[:, offset * 128 : (offset + 1) * 128]
            news.append(state[step + offset * half].astype(F32) + 0.5 * change)
        out(step, *news)


def edge_forcing(forcing_x, forcing_y, d):
    lane = lanes((8, d.edge))
    block = lane // d.block
    row = lane % d.block

    inner = outer = jnp.zeros((8, d.edge), F32)
    for step in range(d.rows + 4):
        at = pl.ds(step * 8, 8)
        pad = [jnp.zeros((8, 128), F32)] * (d.pieces - 1)
        here = jnp.concatenate([forcing_x[at, :]] + pad, axis=1)
        there = jnp.concatenate([forcing_y[at, :]] + pad, axis=1)
        for index, column in enumerate((126, 0, 127, 1)):
            shift = step + index * d.block - column
            match = (block == index) & (row == step)
            if column in (0, 127):
                inner = jnp.where(match, roll(here, shift), inner)
            outer = jnp.where(match, roll(there, shift), outer)
    return inner, outer


def roll_rows(state, upper, lower, rolled, d):
    def put(row, values):
        rolled[row, 0:CH, :] = roll(values, 1)
        rolled[row, CH : 2 * CH, :] = values
        rolled[row, 2 * CH : 3 * CH, :] = roll(values, -1)

    for step in range(2):
        put(step, upper[step * CH : (step + 1) * CH, :])
        put(d.rows + 2 + step, lower[step * CH : (step + 1) * CH, :])
    for row in range(d.rows):
        put(row + 2, state[row])


def sea(
    state, rolled, edges, left, right, out, forcing_x, forcing_y, ocn_in, ocn_out, wet,
    at_top, at_bottom, stack, hidden, side, d,
):
    rows, block = d.rows, d.block
    lane = lanes((CH, 128))
    spot = lanes((CH, d.edge))
    part = spot // block
    inner = edges
    outer = jnp.where((part == 0) | (part == 2), left, right)

    def sides_of(inner, outer, spot):
        first = spot < block
        return (
            jnp.where(first, outer, roll(inner, -block)),
            jnp.where(first, roll(outer, -2 * block), outer),
            jnp.where(first, roll(inner, -block), roll(outer, -2 * block)),
        )

    beside = sides_of(inner, outer, spot)
    middle = beside[1]
    force_in, force_out = edge_forcing(forcing_x, forcing_y, d)
    beside_forcing = sides_of(force_in, force_out, lanes((8, d.edge)))
    sub = subs((8, d.edge))
    ones = jnp.ones((8, d.edge), F32)
    forced = jnp.concatenate(
        [
            jnp.where(sub < 4, beside_forcing[0], beside_forcing[1]),
            jnp.where(sub < 4, beside_forcing[2], ones),
        ],
        axis=0,
    ).astype(BF16)
    columns = jnp.concatenate(list(beside) + [forced], axis=0)
    for tap in range(3):
        side[tap * 256 : (tap + 1) * 256, :] = roll(columns, -tap)

    sub_row = subs((8, 128))
    lane_row = lanes((8, 128))

    for row in range(rows + 4):
        entry = roll(middle, -row)[:, :128]
        stack[row, 0:CH, :] = jnp.where(lane == 0, entry, rolled[row, 0:CH, :])
        stack[row, CH : 2 * CH, :] = rolled[row, CH : 2 * CH, :]
        entry = roll(middle, 127 - block - row)[:, :128]
        stack[row, 2 * CH : 3 * CH, :] = jnp.where(lane == 127, entry, rolled[row, 2 * CH : 3 * CH, :])
        here, there = forcing_x[row * 8 : row * 8 + 8, :], forcing_y[row * 8 : row * 8 + 8, :]
        before = roll(jnp.where(lane_row == 127, there, here), 1)
        after = roll(jnp.where(lane_row == 0, there, here), -1)
        stack[row, 3 * CH : 256, :] = jnp.concatenate(
            [jnp.where(sub_row < 4, before, here), jnp.where(sub_row < 4, after, 1.0)], axis=0
        ).astype(BF16)

    pairs = (rows + 2) // 2

    for step in range(pairs):
        taps = jnp.concatenate(
            [
                stack[step : step + 3].reshape(3 * 256, 128),
                stack[step + pairs : step + pairs + 3].reshape(3 * 256, 128),
            ],
            axis=1,
        )
        active = twice_gelu(jnp.dot(ocn_in[...], taps, preferred_element_type=F32))
        low, high = active[:, :128], active[:, 128:]
        if step == 0:
            low = jnp.where(at_top != 0, 0.0, low)
        if step == pairs - 1:
            high = jnp.where(at_bottom != 0, 0.0, high)
        hidden[step, 0:HIDK, :] = low.astype(BF16)
        hidden[step + pairs, 0:HIDK, :] = high.astype(BF16)
        blank = jnp.zeros((HIDP - HIDK, 128), BF16)
        hidden[step, HIDK:HIDP, :] = blank
        hidden[step + pairs, HIDK:HIDP, :] = blank

    product = jnp.dot(ocn_in[...], side[...], preferred_element_type=F32)
    spot = lanes((1, d.edge)) % block
    gone = ((spot == 0) & (at_top != 0)) | ((spot == rows + 1) & (at_bottom != 0))
    active = jnp.where(gone, 0.0, twice_gelu(product)).astype(BF16)
    active = jnp.concatenate([active, jnp.zeros((HIDP - HIDK, d.edge), BF16)], axis=0)

    def taps_of(slices):
        total = None
        for tap, values in enumerate(slices):
            weights = ocn_out[tap * 3 * CH : (tap + 1) * 3 * CH, :]
            product = jnp.dot(weights, values, preferred_element_type=F32)
            total = product if total is None else total + product
        return total

    partial = taps_of([roll(active, -tap) for tap in range(3)])
    from_left, from_right = partial[0:CH], partial[2 * CH : 3 * CH]
    half = rows // 2
    for step in range(half):
        product = taps_of(
            [
                jnp.concatenate([hidden[step + tap], hidden[step + half + tap]], axis=1)
                for tap in range(3)
            ]
        )
        news = []
        for offset in range(2):
            row = step + offset * half
            sums = product[:, offset * 128 : (offset + 1) * 128]
            entry = roll(from_left, -row)[:, :128]
            total = sums[CH : 2 * CH] + jnp.where(lane == 0, entry, roll(sums[0:CH], 1))
            entry = roll(from_right, 127 - block - row)[:, :128]
            total = total + jnp.where(lane == 127, entry, roll(sums[2 * CH : 3 * CH], -1))
            update = total * (0.5 * wet[row : row + 1, :].astype(F32))
            news.append(state[row].astype(F32) + update)
        out(step, *news)


def prepare(atm_in, atm_bias, ocn_in, ocn_bias, ocn_out, air_in, first, second, is_ocean):
    def bias_rows(ref, width):
        row = jnp.concatenate([ref[index : index + 1, :] for index in range(ref.shape[0])], axis=1)
        terms = list(split_bf16(row)) + [jnp.zeros_like(row)]
        bias = jnp.concatenate(terms, axis=0)
        return jnp.pad(bias, ((0, 0), (0, width - bias.shape[1])))

    @pl.when(is_ocean == 0)
    def _():
        columns = jnp.concatenate(
            [atm_in[...].astype(F32), bias_rows(atm_bias, HA), jnp.zeros((40, HA), F32)], axis=0
        )
        air_in[...] = columns.T.astype(BF16)

    @pl.when(is_ocean != 0)
    def _():
        bias = bias_rows(ocn_bias, 256)
        count = ocn_in.shape[2]
        for tap in range(3):
            whole = [ocn_in[3 * tap + side].astype(F32) for side in range(3)]
            whole = [jnp.pad(values, ((0, 0), (0, 256 - count))) for values in whole]
            rows = [values[:CH] for values in whole] + [values[CH:] for values in whole]
            rows.append(bias if tap == 0 else jnp.zeros((4, 256), F32))
            columns = jnp.concatenate(rows, axis=0).T
            first[:, tap * 256 : (tap + 1) * 256] = columns[:HIDK].astype(BF16)
        for tap in range(9):
            values = ocn_out[tap].astype(F32)
            second[tap * CH : (tap + 1) * CH, :] = jnp.pad(
                values, ((0, 0), (0, HIDP - count))
            ).astype(BF16)


def ends(flags):
    at_top, at_bottom, even = flags[1] != 0, flags[2] != 0, flags[3] == 0

    def up_and_down(one, two):
        above = jnp.where(even, two, one).astype(F32)
        below = jnp.where(even, one, two).astype(F32)
        return jnp.where(at_top, 0.0, above), jnp.where(at_bottom, 0.0, below)

    return up_and_down


def middle_kernel(d, opening, *refs):
    refs = list(refs)
    take = lambda count: [refs.pop(0) for _ in range(count)]
    flags, state, field_one, beside, field_two, from_one, from_two = take(7)
    if opening:
        planes, *far_weights = take(6)
    else:
        (plan_x,) = take(1)
    part_x, fields_x, rolled = take(3)
    if opening:
        plan_x, *made_weights = take(4)
    (coupled,) = take(1)
    if opening:
        *raw_weights, sems = take(6)
        copies = fetch(far_weights, raw_weights, sems)
    rows, tall = d.rows, d.tall
    is_ocean = flags[0]
    up_and_down = ends(flags)

    if opening:

        @pl.when(is_ocean != 0)
        def _():
            base = d.strip
            pair = up_and_down(from_one[base : base + 16, :], from_two[base : base + 16, :])
            plan_x[...] = jnp.zeros_like(plan_x)
            for step, strip in zip((0, rows + 2), pair):
                for index in range(2):
                    plan_x[pl.ds(step + index, 2 * NK, stride=tall), :] = strip[index * 8 : (index + 1) * 8]

        for plane in range(2 * NK):
            plan_x[plane * tall + 2 : plane * tall + 2 + rows, :] = planes[plane].astype(F32)

    for field in range(NS):
        pair = up_and_down(field_one[field], field_two[field])
        fields_x[field, 0:16, :] = pair[0][rows - 16 : rows]
        fields_x[field, 16 : 16 + rows, :] = beside[field].astype(F32)
        fields_x[field, 16 + rows : 32 + rows, :] = pair[1][0:16]

    unit = couple(fields_x, coupled, rows)

    @pl.when(is_ocean == 0)
    def _():
        regrid_inside(coupled, unit, plan_x, part_x, 2, rows // 8, tall)

    @pl.when(is_ocean != 0)
    def _():
        regrid_inside(coupled, unit, plan_x, part_x, 0, d.tiles, tall)
        upper, lower = up_and_down(from_one[0 : 2 * CH, :], from_two[0 : 2 * CH, :])
        roll_rows(state, upper.astype(BF16), lower.astype(BF16), rolled, d)

    if opening:
        for copy in copies:
            copy.wait()
        prepare(*raw_weights, *made_weights, is_ocean)


def step_kernel(d, opening, closing, *refs):
    refs = list(refs)
    take = lambda count: [refs.pop(0) for _ in range(count)]
    flags, state, wet, from_left, from_right = take(5)
    part_x, fields_x, rolled, edges, plan_x, air_in, first, second, atm_out = take(9)
    if not opening:
        (plan_e,) = take(1)
    if not closing:
        surface, places = take(2)
    (out,) = take(1)
    if not closing:
        fields, new_edges, one, two = take(4)
    if opening:
        (plan_e,) = take(1)
    window, forcing_x, forcing_y, stack, hidden, side, raw = take(7)
    if opening:
        (plan_y,) = take(1)
    rows, tall = d.rows, d.tall
    is_ocean, at_top, at_bottom = flags[0], flags[1], flags[2]
    up_and_down = ends(flags)

    if opening:

        @pl.when(is_ocean != 0)
        def _():
            plan_y[...] = jnp.zeros_like(plan_y)
            base = d.edge_rows
            parts = [
                (ref[base : base + 16, :], ref[base + 16 + rows : base + 32 + rows, :],
                 ref[base + 16 : base + 16 + rows, :])
                for ref in (from_left, from_right)
            ]
            for plane in range(2 * NK):
                first_end, second_end, own = [
                    unpack_columns(left, right, plane, 2 * NK, 2) for left, right in zip(*parts)
                ]
                above, below = up_and_down(first_end, second_end)
                at = plane * tall
                plan_y[at : at + 2, :] = above[14:16]
                plan_y[at + 2 : at + 2 + rows, :] = own
                plan_y[at + 2 + rows : at + 4 + rows, :] = below[0:2]

    base = d.edge_rows + (rows + 32 if opening else 0)
    parts = [
        (ref[base : base + 16, :], ref[base + 16 + rows : base + 32 + rows, :],
         ref[base + 16 : base + 16 + rows, :])
        for ref in (from_left, from_right)
    ]
    for field in range(NS):
        first_end, second_end, own = [
            unpack_columns(left, right, field, NS, REACH) for left, right in zip(*parts)
        ]
        above, below = up_and_down(first_end, second_end)
        for at, values in ((0, above), (16, own), (16 + rows, below)):
            count = values.shape[0]
            inside = roll(fields_x[field, at : at + count, :], 32)
            lane = lanes(values.shape)
            near = (lane >= 32 - REACH) & (lane < 32 + REACH)
            far = (lane < REACH) | (lane >= 128 - REACH)
            kept = jnp.where(near, inside, jnp.where(far, values, 0.0))
            window[field, at : at + count, :] = kept
    def finished():
        emission = None if closing else Emission(surface, flags, places, raw, d)

        def put(step, low, high):
            if closing:
                for row, values in ((step, low), (step + rows // 2, high)):
                    raw[pl.ds(row, CH, stride=rows), :] = values
                return
            low, high = low.astype(BF16), high.astype(BF16)
            out[step] = low
            out[step + rows // 2] = high
            emission.add(step, low, high)

        def close():
            if not closing:
                emission.close(out, wet, fields, new_edges, one, two)

        return put, close

    @pl.when(is_ocean == 0)
    def _():
        if opening:
            plan_edges(plan_x, plan_y, plan_e, 2, rows // 8, tall, False)
        regrid_beside(
            window, plan_e, part_x, forcing_x, forcing_y, 2, rows // 8, tall, False
        )
        put, close = finished()
        air(state, put, forcing_x, air_in, atm_out, d)
        close()

    @pl.when(is_ocean != 0)
    def _():
        if opening:
            plan_edges(plan_x, plan_y, plan_e, 0, d.tiles, tall, True)
        regrid_beside(
            window, plan_e, part_x, forcing_x, forcing_y, 0, d.tiles, tall, True
        )
        put, close = finished()
        joined = [get_edges(ref, 0, d) for ref in (from_left, from_right)]
        sea(
            state, rolled, get_edges(edges, 0, d), *joined, put, forcing_x, forcing_y,
            first, second, wet, at_top, at_bottom, stack, hidden, side, d,
        )
        close()

    if closing:
        out[...] = raw[...].reshape(CH, rows, 128).astype(BF16)


VMEM = pl.BlockSpec(memory_space=pltpu.VMEM)
HBM = pl.BlockSpec(memory_space=pltpu.HBM)
SMEM = pl.BlockSpec(memory_space=pltpu.SMEM)
PARAMS = pltpu.CompilerParams(vmem_limit_bytes=48 * 1024 * 1024)


def shape(*dims, dtype=BF16):
    return jax.ShapeDtypeStruct(dims, dtype)


def send(x, move):
    names = ("grp", "lat", "lon")
    sizes = [lax.axis_size(name) for name in names]
    pairs = []
    for group in range(sizes[0]):
        for lat in range(sizes[1]):
            for lon in range(sizes[2]):
                to = move(group, lat, lon)
                if to is None or not 0 <= to[1] < sizes[1]:
                    continue
                target = (to[0] * sizes[1] + to[1]) * sizes[2] + to[2] % sizes[2]
                pairs.append(((group * sizes[1] + lat) * sizes[2] + lon, target))
    return lax.ppermute(x, names, pairs)


def swap_rows(x, turn, across):
    count = lax.axis_size("lat")

    def move(group, lat, lon):
        other = ((lat + turn) ^ 1) - turn
        if not 0 <= other < count:
            return 1 - group, lat, lon
        return (1 - group if across else group), other, lon

    return send(x, move)


def exchange(fields, own_edges, one, two, sides, d):
    rows = d.rows
    from_one = swap_rows(one, 0, False)
    from_two = swap_rows(two, 1, False)
    field_one = swap_rows(fields, 0, True)
    field_two = swap_rows(fields, 1, True)
    beside = send(fields, lambda g, i, j: (1 - g, i, j))
    lat, count = lax.axis_index("lat"), lax.axis_size("lat")
    odd = lat % 2 == 1
    edges = own_edges
    for turn, ref in ((0, from_one), (1, from_two)):
        other = ((lat + turn) ^ 1) - turn
        there = (other >= 0) & (other < count)
        edges = edges + jnp.where(there, ref[2 * CH : d.strip], 0)
    edges, beside, field_one, field_two = lax.optimization_barrier(
        (edges, beside, field_one, field_two)
    )
    outer = [field_one[NS], field_two[NS]]
    if rows != 16:
        outer = [
            jnp.where(odd, outer[0][rows - 16 :], outer[0][:16]),
            jnp.where(odd, outer[1][:16], outer[1][rows - 16 :]),
        ]
    packed = [edges]
    if sides is not None:
        packed += [from_one[d.strip + 16 :], sides, from_two[d.strip + 16 :]]
    packed += [outer[0], beside[NS], outer[1]]
    packed = jnp.concatenate(packed, axis=0)
    from_left = send(packed, lambda g, i, j: (g, i, j + 1))
    from_right = send(packed, lambda g, i, j: (g, i, j - 1))
    return (field_one, beside, field_two, from_one, from_two), (from_left, from_right), edges


def local(
    coupled_state, land_mask, regrid_offsets, regrid_weights, surface_proj,
    atm_in, atm_bias, atm_out, ocn_in, ocn_bias, ocn_out,
):
    rows = coupled_state.shape[2]
    assert coupled_state.shape[3] == 128
    d = Dims(rows)
    group = lax.axis_index("grp")
    lat = lax.axis_index("lat")
    flags = jnp.stack(
        [group, lat == 0, lat == lax.axis_size("lat") - 1, lat % 2]
    ).astype(jnp.int32)
    raw_weights = (
        atm_in.T,
        atm_bias.reshape(HA // 128, 128),
        jnp.transpose(ocn_in, (1, 2, 0)),
        ocn_bias[None],
        jnp.transpose(ocn_out, (1, 0, 2)),
    )
    state_shape = shape(rows, CH, 128)
    emitted = [
        shape(NS + 1, rows, 128),
        shape(d.edge_rows, 128),
        shape(d.strip, 128),
        shape(d.strip, 128),
    ]
    raw = pltpu.VMEM((rows * 8, 128), F32)
    turned = pltpu.VMEM((CH * rows, 128), F32)

    def call(kernel, operands, outs, scratch, name, far=()):
        scratch = scratch + [pltpu.VMEM(x.shape, x.dtype) for x in far]
        if far:
            scratch.append(pltpu.SemaphoreType.DMA((len(far) + CH // 16,)))

        far = [pltpu.with_memory_space_constraint(x, pltpu.HBM) for x in far]
        return pl.pallas_call(
            kernel,
            out_shape=outs,
            in_specs=[SMEM] + [VMEM] * len(operands) + [HBM] * len(far),
            out_specs=[VMEM] * len(outs),
            scratch_shapes=scratch,
            compiler_params=PARAMS,
            name=name,
        )(flags, *operands, *far)

    state, planes, sides, places, fields, edges, one, two = call(
        functools.partial(start_kernel, d),
        (),
        [state_shape, shape(2 * NK, rows, 128), shape(rows, 128), shape(rows * 128, d.edge)]
        + emitted[:2]
        + [shape(d.strip + 32, 128)] * 2,
        [raw, pltpu.VMEM((2 * NK * rows, 128), F32), turned],
        "start",
        (coupled_state[0], surface_proj, land_mask, regrid_offsets[0], regrid_weights[0]),
    )

    plan = shape(2 * NK * d.tall, 128, dtype=F32)
    between = [
        shape(NS * d.tall, 128, dtype=F32),
        shape(NS, rows + 32, 128, dtype=F32),
        shape(rows + 4, 3 * CH, 128),
    ]
    made = [shape(HA, 128), shape(HIDK, 768), shape(9 * CH, HIDP)]
    coupled = pltpu.VMEM((NS // 2, rows + 32, 128), jnp.int32)
    scratch = [
        pltpu.VMEM((NS, rows + 32, 128), F32),
        pltpu.VMEM((d.tall * 8, 128), F32),
        pltpu.VMEM((d.tall * 8, 128), F32),
        pltpu.VMEM((rows + 4, 256, 128), BF16),
        pltpu.VMEM((rows + 2, HIDP, 128), BF16),
        pltpu.VMEM((768, d.edge), BF16),
    ]

    vertical, horizontal, edges = exchange(fields, edges, one, two, sides, d)
    *shared, plan_x, air_in, first, second = call(
        functools.partial(middle_kernel, d, True),
        (state, *vertical, planes),
        between + [plan] + made,
        [coupled],
        "first_middle",
        raw_weights,
    )
    weights = (air_in, first, second, atm_out)
    state, fields, edges, one, two, plan_e = call(
        functools.partial(step_kernel, d, True, False),
        (state, land_mask, *horizontal, *shared, edges, plan_x, *weights, surface_proj, places),
        [state_shape] + emitted + [shape(2 * d.tall, 128, dtype=F32)],
        scratch + [raw, pltpu.VMEM(plan.shape, F32)],
        "first_step",
    )

    vertical, horizontal, edges = exchange(fields, edges, one, two, None, d)
    shared = call(
        functools.partial(middle_kernel, d, False),
        (state, *vertical, plan_x),
        between,
        [coupled],
        "second_middle",
    )
    (state,) = call(
        functools.partial(step_kernel, d, False, True),
        (state, land_mask, *horizontal, *shared, edges, plan_x, *weights, plan_e),
        [shape(CH, rows, 128)],
        scratch + [turned],
        "second_step",
    )
    return state[None]


def solution(mesh):
    return jax.shard_map(
        local,
        mesh=mesh,
        in_specs=(
            P("grp", None, "lat", "lon"),
            P("lat", "lon"),
            P("grp", None, None, "lat", "lon"),
            P("grp", None, "lat", "lon"),
            P(),
            P(),
            P(),
            P(),
            P(),
            P(),
            P(),
        ),
        out_specs=P("grp", None, "lat", "lon"),
        check_vma=False,
    )
```

```python
import functools

import jax
import jax.numpy as jnp
from jax import lax
from jax.experimental import pallas as pl
from jax.experimental.pallas import tpu as pltpu
from jax.sharding import PartitionSpec as P

CH = 80
NS = 4
NK = 4
HA = 384
HW = 8
SPAN = 2 * HW + 1
REACH = HW + 2
FIXED = 32767.0
HIDK = 208
HIDP = 256
F32 = jnp.float32
BF16 = jnp.bfloat16


def roll(x, shift, axis=1):
    size = x.shape[axis]
    if isinstance(shift, int):
        shift = shift % size
        if shift == 0:
            return x
    return pltpu.roll(x, shift, axis)


def lanes(shape):
    return lax.broadcasted_iota(jnp.int32, shape, len(shape) - 1)


def subs(shape):
    return lax.broadcasted_iota(jnp.int32, shape, len(shape) - 2)


class Dims:
    def __init__(self, rows):
        self.rows = rows
        self.block = 32 if rows + 4 <= 32 else 64
        self.edge = 4 * self.block
        self.pieces = self.edge // 128
        self.edge_rows = CH * self.pieces
        self.tiles = -(-(rows + 4) // 8)
        self.tall = 8 * self.tiles
        self.strip = 2 * CH + self.edge_rows


def put_edges(ref, at, edges, d):
    for piece in range(d.pieces):
        ref[at + piece * CH : at + (piece + 1) * CH, :] = edges[:, piece * 128 : (piece + 1) * 128]


def get_edges(ref, at, d):
    return jnp.concatenate(
        [ref[at + piece * CH : at + (piece + 1) * CH, :] for piece in range(d.pieces)], axis=1
    )


def edge_places(places, d):
    lane = lanes((1, d.edge))
    block = lane // d.block
    row = lane % d.block - 2
    column = jnp.where(block == 0, 126, jnp.where(block == 1, 0, jnp.where(block == 2, 127, 1)))
    own = (row >= 0) & (row < d.rows)
    target = jnp.where(own, column, -1)
    position = subs((128, d.edge))
    for step in range(d.rows):
        place = (position == jnp.where(row == step, target, -1)).astype(F32).astype(BF16)
        places[step * 128 : (step + 1) * 128, :] = place


def edge_columns(state, places, d):
    whole = jnp.concatenate([state[step] for step in range(d.rows)], axis=1)
    return jnp.dot(whole, places[...], preferred_element_type=F32).astype(BF16)


def pack_columns(values, reach):
    lane = lanes(values[0].shape)
    pitch = 128 // len(values)
    packed = jnp.zeros_like(values[0])
    for index, value in enumerate(values):
        at = index * pitch
        packed = jnp.where((lane >= at) & (lane < at + reach), roll(value, at), packed)
        at += reach
        packed = jnp.where((lane >= at) & (lane < at + reach), roll(value, at + reach - 128), packed)
    return packed


def unpack_columns(left, right, index, count, reach):
    at = index * (128 // count)
    left = roll(left.astype(F32), 128 - at - 2 * reach)
    return jnp.where(lanes(left.shape) < 64, roll(right.astype(F32), -at), left)


def strips(one, two, even, d):
    last = d.rows - 2
    return (one, jnp.where(even, last, 0)), (two, jnp.where(even, 0, last))


def split_bf16(values):
    high = values.astype(BF16).astype(F32)
    mid = (values - high).astype(BF16).astype(F32)
    return high, mid, values - high - mid


class Emission:
    def __init__(self, surface, flags, places, raw, d):
        gap = jnp.zeros((4, CH), F32)
        terms = []
        for term in split_bf16(surface[flags[0]]):
            terms += [term, gap]
        self.proj = jnp.concatenate(terms + [gap, gap], axis=0).astype(BF16)
        self.places, self.raw, self.d, self.flags = places, raw, d, flags

    def project(self, state):
        half = self.d.rows // 2
        products = []
        for step in range(half):
            pair = jnp.concatenate([state[step], state[step + half]], axis=1)
            products.append(jnp.dot(self.proj, pair, preferred_element_type=F32))
        whole = jnp.concatenate([state[step] for step in range(2 * half)], axis=1)
        edges = jnp.dot(whole, self.places[...], preferred_element_type=F32)
        for step, parts in enumerate(products):
            parts = parts[0:8] + parts[8:16] + parts[16:24]
            self.raw[step * 8 : step * 8 + 8, :] = parts[:, :128]
            self.raw[(step + half) * 8 : (step + half) * 8 + 8, :] = parts[:, 128:]
        return edges.astype(BF16)

    def close(self, state, wet, fields, own_edges, one, two):
        d, even = self.d, self.flags[3] == 0
        edges = self.project(state)
        keeping = jnp.where(self.flags[0] != 0, wet[...].astype(F32), 1.0)
        whole = [self.raw[pl.ds(field, d.rows, stride=8), :] * keeping for field in range(NS)]
        for field in range(NS):
            fields[field] = whole[field].astype(BF16)
        fields[NS] = pack_columns(whole, REACH).astype(BF16)
        put_edges(own_edges, 0, edges, d)
        row = lanes(edges.shape) % d.block
        downward = jnp.where(row < 2, roll(edges, -d.rows), jnp.zeros_like(edges))
        upward = jnp.where(
            (row >= d.rows + 2) & (row < d.rows + 4), roll(edges, d.rows), jnp.zeros_like(edges)
        )
        for (ref, first), down in zip(strips(one, two, even, d), (even, jnp.logical_not(even))):
            ref[0:CH, :] = state[first]
            ref[CH : 2 * CH, :] = state[first + 1]
            put_edges(ref, 2 * CH, jnp.where(down, downward, upward), d)


def fetch(sources, targets, sems):
    copies = [
        pltpu.make_async_copy(source, target, sems.at[index])
        for index, (source, target) in enumerate(zip(sources, targets))
    ]
    for copy in copies:
        copy.start()
    return copies


def start_kernel(
    d, flags, far_given, far_surface, far_wet, far_offsets, far_weights,
    state, planes, sides, places, fields, own_edges, one, two,
    raw, tall, turned, given, surface, wet, offsets, weights, sems,
):
    rows = d.rows
    pieces = [pl.ds(at, 16) for at in range(0, CH, 16)]
    copies = fetch(
        [far_given.at[piece] for piece in pieces] + [far_surface, far_wet, far_offsets, far_weights],
        [given.at[piece] for piece in pieces] + [surface, wet, offsets, weights],
        sems,
    )
    edge_places(places, d)
    for index, piece in enumerate(pieces):
        copies[index].wait()
        turned[index * 16 * rows : (index + 1) * 16 * rows, :] = (
            given[piece].astype(F32).reshape(16 * rows, 128)
        )
    for row in range(rows):
        state[row] = turned[pl.ds(row, CH, stride=rows), :].astype(BF16)
    for copy in copies[len(pieces) :]:
        copy.wait()
    emission = Emission(surface, flags, places, raw, d)
    emission.close(state, wet, fields, own_edges, one, two)
    for k in range(NK):
        code = (offsets[0, k] * SPAN + offsets[1, k]).astype(F32)
        tall[k * rows : (k + 1) * rows, :] = code
        tall[(NK + k) * rows : (NK + k + 1) * rows, :] = weights[k]
        planes[k] = code.astype(BF16)
        planes[NK + k] = weights[k].astype(BF16)
    packed = pack_columns([tall[plane * rows : (plane + 1) * rows, :] for plane in range(2 * NK)], 2)
    sides[...] = packed.astype(BF16)
    even = flags[3] == 0
    for (ref, first), down in zip(strips(one, two, even, d), (even, jnp.logical_not(even))):
        strip = [tall[pl.ds(first + step, 2 * NK, stride=rows), :] for step in range(2)]
        ref[d.strip : d.strip + 16, :] = jnp.concatenate(strip, axis=0).astype(BF16)
        ref[d.strip + 16 : d.strip + 32, :] = jnp.where(
            down, packed[rows - 16 : rows], packed[0:16]
        ).astype(BF16)


def decode(code):
    shifted = code.astype(jnp.int32) + (HW * SPAN + HW)
    rows = lax.shift_right_logical(shifted * 241, 12)
    return rows - HW, shifted - rows * SPAN - HW


def along_lanes(values, index):
    numbers = lax.GatherDimensionNumbers(
        offset_dims=(),
        collapsed_slice_dims=(1,),
        start_index_map=(1,),
        operand_batching_dims=(0,),
        start_indices_batching_dims=(0,),
    )
    return lax.gather(
        values, index[..., None], numbers, (1, 1), mode=lax.GatherScatterMode.PROMISE_IN_BOUNDS
    )


def couple(fields, coupled, rows):
    largest = None
    for field in range(NS):
        here = jnp.max(jnp.abs(fields[field]), axis=0, keepdims=True)
        largest = here if largest is None else jnp.maximum(largest, here)
    largest = jnp.maximum(jnp.max(largest, axis=1, keepdims=True), 1e-30)
    scale = FIXED / largest
    for pair in range(NS // 2):
        high, low = [
            jnp.floor(fields[2 * pair + part] * scale + 0.5).astype(jnp.int32) for part in range(2)
        ]
        coupled[pair] = high * (1 << 16) + (low + (1 << 15))
    return largest * (1 / FIXED)


def uncouple(values):
    high = lax.shift_right_arithmetic(values, 16)
    low = (values & 0xFFFF) - (1 << 15)
    return high.astype(F32), low.astype(F32)


def select_rows(source, start, picks):
    parts = source.shape[0]
    blank = jnp.full((8, 128), 1 << 15, jnp.int32) if parts < NS else jnp.zeros((8, 128), F32)
    chosen = [[blank for _ in range(parts)] for _ in picks]
    for shift in range(-HW, HW + 1):
        at = pl.ds(start + shift, 8)
        values = [source[part, at, :] for part in range(parts)]
        for slot, (rows, index, allowed) in enumerate(picks):
            here = (rows == shift) & allowed
            for part in range(parts):
                picked = along_lanes(values[part], index)
                chosen[slot][part] = jnp.where(here, picked, chosen[slot][part])
    if parts == NS:
        return chosen
    return [[part for values in pairs for part in uncouple(values)] for pairs in chosen]


def regrid_inside(coupled, unit, plan_x, part_x, first, tiles, tall):
    lane = lanes((8, 128))
    for step in range(tiles):
        at = first + step * 8
        picks = []
        weights = []
        for k in range(NK):
            rows, cols = decode(plan_x[pl.ds(k * tall + at, 8), :])
            weights.append(plan_x[pl.ds((NK + k) * tall + at, 8), :] * unit)
            column = lane + cols
            picks.append((rows, column & 127, (column >= 0) & (column < 128)))
        chosen = select_rows(coupled, at + 14, picks)
        for field in range(NS):
            total = chosen[0][field] * weights[0]
            for k in range(1, NK):
                total = total + chosen[k][field] * weights[k]
            part_x[pl.ds(field * tall + at, 8), :] = total


def edge_lanes():
    lane = lanes((8, 128))
    return ((lane + 8) & 127) // 32, ((lane + 8) & 31) - 8


def plan_edges(plan_x, plan_y, plan_e, first, tiles, tall, sides):
    part, place = edge_lanes()
    outer = place >= 8
    for step in range(tiles):
        at = first + step * 8
        code = jnp.zeros((8, 128), F32)
        weight = jnp.zeros((8, 128), F32)
        for k in range(NK):
            edge_code = roll(plan_x[pl.ds(k * tall + at, 8), :], 32 * k)
            edge_weight = roll(plan_x[pl.ds((NK + k) * tall + at, 8), :], 32 * k)
            if sides:
                edge_code = jnp.where(
                    outer, roll(plan_y[pl.ds(k * tall + at, 8), :], 32 * k + 16), edge_code
                )
                edge_weight = jnp.where(
                    outer, roll(plan_y[pl.ds((NK + k) * tall + at, 8), :], 32 * k + 16), edge_weight
                )
            code = jnp.where(part == k, edge_code, code)
            weight = jnp.where(part == k, edge_weight, weight)
        plan_e[pl.ds(at, 8), :] = code
        plan_e[pl.ds(tall + at, 8), :] = weight


def regrid_beside(window, plan_e, part_x, forcing_x, forcing_y, first, tiles, tall, sides):
    lane = lanes((8, 128))
    part, place = edge_lanes()
    outer = place >= 8
    inner_column = place & 127
    outer_column = jnp.where(place < 16, place - 16, place + 112)
    edge = (lane < 8) | (lane >= 120)
    for step in range(tiles):
        at = first + step * 8
        rows, cols = decode(plan_e[pl.ds(at, 8), :])
        weight = plan_e[pl.ds(tall + at, 8), :]
        column = jnp.where(outer, outer_column, inner_column) + cols
        within = (column >= 0) & (column < 128)
        index = jnp.where(within, column + 32, column) & 127
        (chosen,) = select_rows(window, at + 14, [(rows, index, outer | jnp.logical_not(within))])
        for field in range(NS):
            part_sum = chosen[field] * weight
            extra = part_sum
            for k in range(1, NK):
                extra = extra + roll(part_sum, -32 * k)
            total = part_x[pl.ds(field * tall + at, 8), :] + jnp.where(edge, extra, 0.0)
            forcing_x[pl.ds(at * 8 + field, 8, stride=8), :] = total
            forcing_x[pl.ds(at * 8 + field + 4, 8, stride=8), :] = total
            if sides:
                extra = roll(extra, -16)
                forcing_y[pl.ds(at * 8 + field, 8, stride=8), :] = extra
                forcing_y[pl.ds(at * 8 + field + 4, 8, stride=8), :] = extra


def twice_gelu(x):
    scale = (2 / jnp.pi) ** 0.5
    return x + x * jnp.tanh(x * (scale + (scale * 0.044715) * (x * x)))


def staggered(count, *stages):
    values = [{} for _ in stages]
    for turn in range(count + len(stages) - 1):
        for index, stage in enumerate(stages):
            step = turn - index
            if 0 <= step < count:
                given = values[index - 1].pop(step) if index else None
                values[index][step] = stage(step, given)


def air(state, out, forcing_x, air_in, atm_out, d):
    half = d.rows // 2
    leading = subs((8, 128)) < 4
    blank = jnp.zeros((32, 128), BF16)

    def inputs(row):
        at = (row + 2) * 8
        forced = jnp.where(leading, forcing_x[at : at + 8, :], 1.0)
        forced = jnp.concatenate([forced, jnp.zeros_like(forced)], axis=0).astype(BF16)
        return jnp.concatenate([state[row], forced, blank], axis=0)

    def first(step, _):
        pair = jnp.concatenate([inputs(step), inputs(step + half)], axis=1)
        return jnp.dot(air_in[...], pair, preferred_element_type=F32)

    def middle(step, product):
        return twice_gelu(product).astype(BF16)

    def second(step, hidden):
        return jnp.dot(atm_out[...], hidden, preferred_element_type=F32)

    def last(step, update):
        news = []
        for offset in range(2):
            change = update[:, offset * 128 : (offset + 1) * 128]
            news.append(state[step + offset * half].astype(F32) + 0.5 * change)
        out(step, *news)

    staggered(half, first, middle, second, last)


def edge_forcing(forcing_x, forcing_y, d):
    lane = lanes((8, d.edge))
    block = lane // d.block
    row = lane % d.block

    inner = outer = jnp.zeros((8, d.edge), F32)
    for step in range(d.rows + 4):
        at = pl.ds(step * 8, 8)
        pad = [jnp.zeros((8, 128), F32)] * (d.pieces - 1)
        here = jnp.concatenate([forcing_x[at, :]] + pad, axis=1)
        there = jnp.concatenate([forcing_y[at, :]] + pad, axis=1)
        for index, column in enumerate((126, 0, 127, 1)):
            shift = step + index * d.block - column
            match = (block == index) & (row == step)
            if column in (0, 127):
                inner = jnp.where(match, roll(here, shift), inner)
            outer = jnp.where(match, roll(there, shift), outer)
    return inner, outer


def roll_rows(state, upper, lower, rolled, d):
    def put(row, values):
        rolled[row, 0:CH, :] = roll(values, 1)
        rolled[row, CH : 2 * CH, :] = values
        rolled[row, 2 * CH : 3 * CH, :] = roll(values, -1)

    for step in range(2):
        put(step, upper[step * CH : (step + 1) * CH, :])
        put(d.rows + 2 + step, lower[step * CH : (step + 1) * CH, :])
    for row in range(d.rows):
        put(row + 2, state[row])


def sea(
    state, rolled, edges, left, right, out, forcing_x, forcing_y, ocn_in, ocn_out, wet,
    at_top, at_bottom, stack, hidden, side, d,
):
    rows, block = d.rows, d.block
    lane = lanes((CH, 128))
    spot = lanes((CH, d.edge))
    part = spot // block
    inner = edges
    outer = jnp.where((part == 0) | (part == 2), left, right)

    def sides_of(inner, outer, spot):
        first = spot < block
        return (
            jnp.where(first, outer, roll(inner, -block)),
            jnp.where(first, roll(outer, -2 * block), outer),
            jnp.where(first, roll(inner, -block), roll(outer, -2 * block)),
        )

    beside = sides_of(inner, outer, spot)
    middle = beside[1]
    force_in, force_out = edge_forcing(forcing_x, forcing_y, d)
    beside_forcing = sides_of(force_in, force_out, lanes((8, d.edge)))
    sub = subs((8, d.edge))
    ones = jnp.ones((8, d.edge), F32)
    forced = jnp.concatenate(
        [
            jnp.where(sub < 4, beside_forcing[0], beside_forcing[1]),
            jnp.where(sub < 4, beside_forcing[2], ones),
        ],
        axis=0,
    ).astype(BF16)
    columns = jnp.concatenate(list(beside) + [forced], axis=0)
    for tap in range(3):
        side[tap * 256 : (tap + 1) * 256, :] = roll(columns, -tap)

    sub_row = subs((8, 128))
    lane_row = lanes((8, 128))

    for row in range(rows + 4):
        entry = roll(middle, -row)[:, :128]
        stack[row, 0:CH, :] = jnp.where(lane == 0, entry, rolled[row, 0:CH, :])
        stack[row, CH : 2 * CH, :] = rolled[row, CH : 2 * CH, :]
        entry = roll(middle, 127 - block - row)[:, :128]
        stack[row, 2 * CH : 3 * CH, :] = jnp.where(lane == 127, entry, rolled[row, 2 * CH : 3 * CH, :])
        here, there = forcing_x[row * 8 : row * 8 + 8, :], forcing_y[row * 8 : row * 8 + 8, :]
        before = roll(jnp.where(lane_row == 127, there, here), 1)
        after = roll(jnp.where(lane_row == 0, there, here), -1)
        stack[row, 3 * CH : 256, :] = jnp.concatenate(
            [jnp.where(sub_row < 4, before, here), jnp.where(sub_row < 4, after, 1.0)], axis=0
        ).astype(BF16)

    pairs = (rows + 2) // 2

    def first(step, _):
        taps = jnp.concatenate(
            [
                stack[step : step + 3].reshape(3 * 256, 128),
                stack[step + pairs : step + pairs + 3].reshape(3 * 256, 128),
            ],
            axis=1,
        )
        return jnp.dot(ocn_in[...], taps, preferred_element_type=F32)

    def activate(step, product):
        active = twice_gelu(product)
        low, high = active[:, :128], active[:, 128:]
        if step == 0:
            low = jnp.where(at_top != 0, 0.0, low)
        if step == pairs - 1:
            high = jnp.where(at_bottom != 0, 0.0, high)
        hidden[step, 0:HIDK, :] = low.astype(BF16)
        hidden[step + pairs, 0:HIDK, :] = high.astype(BF16)
        blank = jnp.zeros((HIDP - HIDK, 128), BF16)
        hidden[step, HIDK:HIDP, :] = blank
        hidden[step + pairs, HIDK:HIDP, :] = blank

    staggered(pairs, first, activate)
    product = jnp.dot(ocn_in[...], side[...], preferred_element_type=F32)
    spot = lanes((1, d.edge)) % block
    gone = ((spot == 0) & (at_top != 0)) | ((spot == rows + 1) & (at_bottom != 0))
    active = jnp.where(gone, 0.0, twice_gelu(product)).astype(BF16)
    active = jnp.concatenate([active, jnp.zeros((HIDP - HIDK, d.edge), BF16)], axis=0)

    def taps_of(slices):
        total = None
        for tap, values in enumerate(slices):
            weights = ocn_out[tap * 3 * CH : (tap + 1) * 3 * CH, :]
            product = jnp.dot(weights, values, preferred_element_type=F32)
            total = product if total is None else total + product
        return total

    partial = taps_of([roll(active, -tap) for tap in range(3)])
    from_left, from_right = partial[0:CH], partial[2 * CH : 3 * CH]
    half = rows // 2

    def second(step, _):
        return taps_of(
            [
                jnp.concatenate([hidden[step + tap], hidden[step + half + tap]], axis=1)
                for tap in range(3)
            ]
        )

    def last(step, product):
        news = []
        for offset in range(2):
            row = step + offset * half
            sums = product[:, offset * 128 : (offset + 1) * 128]
            entry = roll(from_left, -row)[:, :128]
            total = sums[CH : 2 * CH] + jnp.where(lane == 0, entry, roll(sums[0:CH], 1))
            entry = roll(from_right, 127 - block - row)[:, :128]
            total = total + jnp.where(lane == 127, entry, roll(sums[2 * CH : 3 * CH], -1))
            update = total * (0.5 * wet[row : row + 1, :].astype(F32))
            news.append(state[row].astype(F32) + update)
        out(step, *news)

    staggered(half, second, last)


def prepare(atm_in, atm_bias, ocn_in, ocn_bias, ocn_out, air_in, first, second, is_ocean):
    def bias_rows(ref, width):
        row = jnp.concatenate([ref[index : index + 1, :] for index in range(ref.shape[0])], axis=1)
        terms = list(split_bf16(row)) + [jnp.zeros_like(row)]
        bias = jnp.concatenate(terms, axis=0)
        return jnp.pad(bias, ((0, 0), (0, width - bias.shape[1])))

    @pl.when(is_ocean == 0)
    def _():
        columns = jnp.concatenate(
            [atm_in[...].astype(F32), bias_rows(atm_bias, HA), jnp.zeros((40, HA), F32)], axis=0
        )
        air_in[...] = columns.T.astype(BF16)

    @pl.when(is_ocean != 0)
    def _():
        bias = bias_rows(ocn_bias, 256)
        count = ocn_in.shape[2]
        for tap in range(3):
            whole = [ocn_in[3 * tap + side].astype(F32) for side in range(3)]
            whole = [jnp.pad(values, ((0, 0), (0, 256 - count))) for values in whole]
            rows = [values[:CH] for values in whole] + [values[CH:] for values in whole]
            rows.append(bias if tap == 0 else jnp.zeros((4, 256), F32))
            columns = jnp.concatenate(rows, axis=0).T
            first[:, tap * 256 : (tap + 1) * 256] = columns[:HIDK].astype(BF16)
        for tap in range(9):
            values = ocn_out[tap].astype(F32)
            second[tap * CH : (tap + 1) * CH, :] = jnp.pad(
                values, ((0, 0), (0, HIDP - count))
            ).astype(BF16)


def ends(flags):
    at_top, at_bottom, even = flags[1] != 0, flags[2] != 0, flags[3] == 0

    def up_and_down(one, two):
        above = jnp.where(even, two, one).astype(F32)
        below = jnp.where(even, one, two).astype(F32)
        return jnp.where(at_top, 0.0, above), jnp.where(at_bottom, 0.0, below)

    return up_and_down


def middle_kernel(d, opening, *refs):
    refs = list(refs)
    take = lambda count: [refs.pop(0) for _ in range(count)]
    flags, state, field_one, beside, field_two, from_one, from_two = take(7)
    if opening:
        planes, *far_weights = take(6)
    else:
        (plan_x,) = take(1)
    part_x, fields_x, rolled = take(3)
    if opening:
        plan_x, *made_weights = take(4)
    (coupled,) = take(1)
    if opening:
        *raw_weights, sems = take(6)
        copies = fetch(far_weights, raw_weights, sems)
    rows, tall = d.rows, d.tall
    is_ocean = flags[0]
    up_and_down = ends(flags)

    if opening:

        @pl.when(is_ocean != 0)
        def _():
            base = d.strip
            pair = up_and_down(from_one[base : base + 16, :], from_two[base : base + 16, :])
            plan_x[...] = jnp.zeros_like(plan_x)
            for step, strip in zip((0, rows + 2), pair):
                for index in range(2):
                    plan_x[pl.ds(step + index, 2 * NK, stride=tall), :] = strip[index * 8 : (index + 1) * 8]

        for plane in range(2 * NK):
            plan_x[plane * tall + 2 : plane * tall + 2 + rows, :] = planes[plane].astype(F32)

    for field in range(NS):
        pair = up_and_down(field_one[field], field_two[field])
        fields_x[field, 0:16, :] = pair[0][rows - 16 : rows]
        fields_x[field, 16 : 16 + rows, :] = beside[field].astype(F32)
        fields_x[field, 16 + rows : 32 + rows, :] = pair[1][0:16]

    unit = couple(fields_x, coupled, rows)

    @pl.when(is_ocean == 0)
    def _():
        regrid_inside(coupled, unit, plan_x, part_x, 2, rows // 8, tall)

    @pl.when(is_ocean != 0)
    def _():
        regrid_inside(coupled, unit, plan_x, part_x, 0, d.tiles, tall)
        upper, lower = up_and_down(from_one[0 : 2 * CH, :], from_two[0 : 2 * CH, :])
        roll_rows(state, upper.astype(BF16), lower.astype(BF16), rolled, d)

    if opening:
        for copy in copies:
            copy.wait()
        prepare(*raw_weights, *made_weights, is_ocean)


def step_kernel(d, opening, closing, *refs):
    refs = list(refs)
    take = lambda count: [refs.pop(0) for _ in range(count)]
    flags, state, wet, from_left, from_right = take(5)
    part_x, fields_x, rolled, edges, plan_x, air_in, first, second, atm_out = take(9)
    if not opening:
        (plan_e,) = take(1)
    if not closing:
        surface, places = take(2)
    (out,) = take(1)
    if not closing:
        fields, new_edges, one, two = take(4)
    if opening:
        (plan_e,) = take(1)
    window, forcing_x, forcing_y, stack, hidden, side, raw = take(7)
    if opening:
        (plan_y,) = take(1)
    rows, tall = d.rows, d.tall
    is_ocean, at_top, at_bottom = flags[0], flags[1], flags[2]
    up_and_down = ends(flags)

    if opening:

        @pl.when(is_ocean != 0)
        def _():
            plan_y[...] = jnp.zeros_like(plan_y)
            base = d.edge_rows
            parts = [
                (ref[base : base + 16, :], ref[base + 16 + rows : base + 32 + rows, :],
                 ref[base + 16 : base + 16 + rows, :])
                for ref in (from_left, from_right)
            ]
            for plane in range(2 * NK):
                first_end, second_end, own = [
                    unpack_columns(left, right, plane, 2 * NK, 2) for left, right in zip(*parts)
                ]
                above, below = up_and_down(first_end, second_end)
                at = plane * tall
                plan_y[at : at + 2, :] = above[14:16]
                plan_y[at + 2 : at + 2 + rows, :] = own
                plan_y[at + 2 + rows : at + 4 + rows, :] = below[0:2]

    base = d.edge_rows + (rows + 32 if opening else 0)
    parts = [
        (ref[base : base + 16, :], ref[base + 16 + rows : base + 32 + rows, :],
         ref[base + 16 : base + 16 + rows, :])
        for ref in (from_left, from_right)
    ]
    for field in range(NS):
        first_end, second_end, own = [
            unpack_columns(left, right, field, NS, REACH) for left, right in zip(*parts)
        ]
        above, below = up_and_down(first_end, second_end)
        for at, values in ((0, above), (16, own), (16 + rows, below)):
            count = values.shape[0]
            inside = roll(fields_x[field, at : at + count, :], 32)
            lane = lanes(values.shape)
            near = (lane >= 32 - REACH) & (lane < 32 + REACH)
            far = (lane < REACH) | (lane >= 128 - REACH)
            kept = jnp.where(near, inside, jnp.where(far, values, 0.0))
            window[field, at : at + count, :] = kept
    def finished():
        emission = None if closing else Emission(surface, flags, places, raw, d)

        def put(step, low, high):
            if closing:
                for row, values in ((step, low), (step + rows // 2, high)):
                    raw[pl.ds(row, CH, stride=rows), :] = values
                return
            out[step] = low.astype(BF16)
            out[step + rows // 2] = high.astype(BF16)

        def close():
            if not closing:
                emission.close(out, wet, fields, new_edges, one, two)

        return put, close

    @pl.when(is_ocean == 0)
    def _():
        if opening:
            plan_edges(plan_x, plan_y, plan_e, 2, rows // 8, tall, False)
        regrid_beside(
            window, plan_e, part_x, forcing_x, forcing_y, 2, rows // 8, tall, False
        )
        put, close = finished()
        air(state, put, forcing_x, air_in, atm_out, d)
        close()

    @pl.when(is_ocean != 0)
    def _():
        if opening:
            plan_edges(plan_x, plan_y, plan_e, 0, d.tiles, tall, True)
        regrid_beside(
            window, plan_e, part_x, forcing_x, forcing_y, 0, d.tiles, tall, True
        )
        put, close = finished()
        joined = [get_edges(ref, 0, d) for ref in (from_left, from_right)]
        sea(
            state, rolled, get_edges(edges, 0, d), *joined, put, forcing_x, forcing_y,
            first, second, wet, at_top, at_bottom, stack, hidden, side, d,
        )
        close()

    if closing:
        out[...] = raw[...].reshape(CH, rows, 128).astype(BF16)


VMEM = pl.BlockSpec(memory_space=pltpu.VMEM)
HBM = pl.BlockSpec(memory_space=pltpu.HBM)
SMEM = pl.BlockSpec(memory_space=pltpu.SMEM)
PARAMS = pltpu.CompilerParams(vmem_limit_bytes=48 * 1024 * 1024)


def shape(*dims, dtype=BF16):
    return jax.ShapeDtypeStruct(dims, dtype)


def send(x, move):
    names = ("grp", "lat", "lon")
    sizes = [lax.axis_size(name) for name in names]
    pairs = []
    for group in range(sizes[0]):
        for lat in range(sizes[1]):
            for lon in range(sizes[2]):
                to = move(group, lat, lon)
                if to is None or not 0 <= to[1] < sizes[1]:
                    continue
                target = (to[0] * sizes[1] + to[1]) * sizes[2] + to[2] % sizes[2]
                pairs.append(((group * sizes[1] + lat) * sizes[2] + lon, target))
    return lax.ppermute(x, names, pairs)


def swap_rows(x, turn, across):
    count = lax.axis_size("lat")

    def move(group, lat, lon):
        other = ((lat + turn) ^ 1) - turn
        if not 0 <= other < count:
            return 1 - group, lat, lon
        return (1 - group if across else group), other, lon

    return send(x, move)


def exchange(fields, own_edges, one, two, sides, d):
    rows = d.rows
    from_one = swap_rows(one, 0, False)
    from_two = swap_rows(two, 1, False)
    field_one = swap_rows(fields, 0, True)
    field_two = swap_rows(fields, 1, True)
    beside = send(fields, lambda g, i, j: (1 - g, i, j))
    lat, count = lax.axis_index("lat"), lax.axis_size("lat")
    odd = lat % 2 == 1
    edges = own_edges
    for turn, ref in ((0, from_one), (1, from_two)):
        other = ((lat + turn) ^ 1) - turn
        there = (other >= 0) & (other < count)
        edges = edges + jnp.where(there, ref[2 * CH : d.strip], 0)
    edges, beside, field_one, field_two = lax.optimization_barrier(
        (edges, beside, field_one, field_two)
    )
    outer = [field_one[NS], field_two[NS]]
    if rows != 16:
        outer = [
            jnp.where(odd, outer[0][rows - 16 :], outer[0][:16]),
            jnp.where(odd, outer[1][:16], outer[1][rows - 16 :]),
        ]
    packed = [edges]
    if sides is not None:
        packed += [from_one[d.strip + 16 :], sides, from_two[d.strip + 16 :]]
    packed += [outer[0], beside[NS], outer[1]]
    packed = jnp.concatenate(packed, axis=0)
    from_left = send(packed, lambda g, i, j: (g, i, j + 1))
    from_right = send(packed, lambda g, i, j: (g, i, j - 1))
    return (field_one, beside, field_two, from_one, from_two), (from_left, from_right), edges


def local(
    coupled_state, land_mask, regrid_offsets, regrid_weights, surface_proj,
    atm_in, atm_bias, atm_out, ocn_in, ocn_bias, ocn_out,
):
    rows = coupled_state.shape[2]
    assert coupled_state.shape[3] == 128
    d = Dims(rows)
    group = lax.axis_index("grp")
    lat = lax.axis_index("lat")
    flags = jnp.stack(
        [group, lat == 0, lat == lax.axis_size("lat") - 1, lat % 2]
    ).astype(jnp.int32)
    raw_weights = (
        atm_in.T,
        atm_bias.reshape(HA // 128, 128),
        jnp.transpose(ocn_in, (1, 2, 0)),
        ocn_bias[None],
        jnp.transpose(ocn_out, (1, 0, 2)),
    )
    state_shape = shape(rows, CH, 128)
    emitted = [
        shape(NS + 1, rows, 128),
        shape(d.edge_rows, 128),
        shape(d.strip, 128),
        shape(d.strip, 128),
    ]
    raw = pltpu.VMEM((rows * 8, 128), F32)
    turned = pltpu.VMEM((CH * rows, 128), F32)

    def call(kernel, operands, outs, scratch, name, far=()):
        scratch = scratch + [pltpu.VMEM(x.shape, x.dtype) for x in far]
        if far:
            scratch.append(pltpu.SemaphoreType.DMA((len(far) + CH // 16,)))

        far = [pltpu.with_memory_space_constraint(x, pltpu.HBM) for x in far]
        return pl.pallas_call(
            kernel,
            out_shape=outs,
            in_specs=[SMEM] + [VMEM] * len(operands) + [HBM] * len(far),
            out_specs=[VMEM] * len(outs),
            scratch_shapes=scratch,
            compiler_params=PARAMS,
            name=name,
        )(flags, *operands, *far)

    state, planes, sides, places, fields, edges, one, two = call(
        functools.partial(start_kernel, d),
        (),
        [state_shape, shape(2 * NK, rows, 128), shape(rows, 128), shape(rows * 128, d.edge)]
        + emitted[:2]
        + [shape(d.strip + 32, 128)] * 2,
        [raw, pltpu.VMEM((2 * NK * rows, 128), F32), turned],
        "start",
        (coupled_state[0], surface_proj, land_mask, regrid_offsets[0], regrid_weights[0]),
    )

    plan = shape(2 * NK * d.tall, 128, dtype=F32)
    between = [
        shape(NS * d.tall, 128, dtype=F32),
        shape(NS, rows + 32, 128, dtype=F32),
        shape(rows + 4, 3 * CH, 128),
    ]
    made = [shape(HA, 128), shape(HIDK, 768), shape(9 * CH, HIDP)]
    coupled = pltpu.VMEM((NS // 2, rows + 32, 128), jnp.int32)
    scratch = [
        pltpu.VMEM((NS, rows + 32, 128), F32),
        pltpu.VMEM((d.tall * 8, 128), F32),
        pltpu.VMEM((d.tall * 8, 128), F32),
        pltpu.VMEM((rows + 4, 256, 128), BF16),
        pltpu.VMEM((rows + 2, HIDP, 128), BF16),
        pltpu.VMEM((768, d.edge), BF16),
    ]

    vertical, horizontal, edges = exchange(fields, edges, one, two, sides, d)
    *shared, plan_x, air_in, first, second = call(
        functools.partial(middle_kernel, d, True),
        (state, *vertical, planes),
        between + [plan] + made,
        [coupled],
        "first_middle",
        raw_weights,
    )
    weights = (air_in, first, second, atm_out)
    state, fields, edges, one, two, plan_e = call(
        functools.partial(step_kernel, d, True, False),
        (state, land_mask, *horizontal, *shared, edges, plan_x, *weights, surface_proj, places),
        [state_shape] + emitted + [shape(2 * d.tall, 128, dtype=F32)],
        scratch + [raw, pltpu.VMEM(plan.shape, F32)],
        "first_step",
    )

    vertical, horizontal, edges = exchange(fields, edges, one, two, None, d)
    shared = call(
        functools.partial(middle_kernel, d, False),
        (state, *vertical, plan_x),
        between,
        [coupled],
        "second_middle",
    )
    (state,) = call(
        functools.partial(step_kernel, d, False, True),
        (state, land_mask, *horizontal, *shared, edges, plan_x, *weights, plan_e),
        [shape(CH, rows, 128)],
        scratch + [turned],
        "second_step",
    )
    return state[None]


def solution(mesh):
    return jax.shard_map(
        local,
        mesh=mesh,
        in_specs=(
            P("grp", None, "lat", "lon"),
            P("lat", "lon"),
            P("grp", None, None, "lat", "lon"),
            P("grp", None, "lat", "lon"),
            P(),
            P(),
            P(),
            P(),
            P(),
            P(),
            P(),
        ),
        out_specs=P("grp", None, "lat", "lon"),
        check_vma=False,
    )
```

```python
import functools

import jax
import jax.numpy as jnp
from jax import lax
from jax.experimental import pallas as pl
from jax.experimental.pallas import tpu as pltpu
from jax.sharding import PartitionSpec as P

CH = 80
NS = 4
NK = 4
HA = 384
HW = 8
SPAN = 2 * HW + 1
REACH = HW + 2
FIXED = 32767.0
HIDK = 208
HIDP = 256
F32 = jnp.float32
BF16 = jnp.bfloat16


def roll(x, shift, axis=1):
    size = x.shape[axis]
    if isinstance(shift, int):
        shift = shift % size
        if shift == 0:
            return x
    return pltpu.roll(x, shift, axis)


def lanes(shape):
    return lax.broadcasted_iota(jnp.int32, shape, len(shape) - 1)


def subs(shape):
    return lax.broadcasted_iota(jnp.int32, shape, len(shape) - 2)


class Dims:
    def __init__(self, rows):
        self.rows = rows
        self.block = 32 if rows + 4 <= 32 else 64
        self.edge = 4 * self.block
        self.pieces = self.edge // 128
        self.edge_rows = CH * self.pieces
        self.tiles = -(-(rows + 4) // 8)
        self.tall = 8 * self.tiles
        self.strip = 2 * CH + self.edge_rows


def put_edges(ref, at, edges, d):
    for piece in range(d.pieces):
        ref[at + piece * CH : at + (piece + 1) * CH, :] = edges[:, piece * 128 : (piece + 1) * 128]


def get_edges(ref, at, d):
    return jnp.concatenate(
        [ref[at + piece * CH : at + (piece + 1) * CH, :] for piece in range(d.pieces)], axis=1
    )


def edge_places(places, d):
    lane = lanes((1, d.edge))
    block = lane // d.block
    row = lane % d.block - 2
    column = jnp.where(block == 0, 126, jnp.where(block == 1, 0, jnp.where(block == 2, 127, 1)))
    own = (row >= 0) & (row < d.rows)
    target = jnp.where(own, column, -1)
    position = subs((128, d.edge))
    for step in range(d.rows):
        place = (position == jnp.where(row == step, target, -1)).astype(F32).astype(BF16)
        places[step * 128 : (step + 1) * 128, :] = place


def edge_columns(state, places, d):
    whole = jnp.concatenate([state[step] for step in range(d.rows)], axis=1)
    return jnp.dot(whole, places[...], preferred_element_type=F32).astype(BF16)


def pack_columns(values, reach):
    lane = lanes(values[0].shape)
    pitch = 128 // len(values)
    packed = jnp.zeros_like(values[0])
    for index, value in enumerate(values):
        at = index * pitch
        packed = jnp.where((lane >= at) & (lane < at + reach), roll(value, at), packed)
        at += reach
        packed = jnp.where((lane >= at) & (lane < at + reach), roll(value, at + reach - 128), packed)
    return packed


def unpack_columns(left, right, index, count, reach):
    at = index * (128 // count)
    left = roll(left.astype(F32), 128 - at - 2 * reach)
    return jnp.where(lanes(left.shape) < 64, roll(right.astype(F32), -at), left)


def strips(one, two, even, d):
    last = d.rows - 2
    return (one, jnp.where(even, last, 0)), (two, jnp.where(even, 0, last))


def split_bf16(values):
    high = values.astype(BF16).astype(F32)
    mid = (values - high).astype(BF16).astype(F32)
    return high, mid, values - high - mid


class Emission:
    def __init__(self, surface, flags, places, raw, d):
        gap = jnp.zeros((4, CH), F32)
        terms = []
        for term in split_bf16(surface[flags[0]]):
            terms += [term, gap]
        self.proj = jnp.concatenate(terms + [gap, gap], axis=0).astype(BF16)
        self.places, self.raw, self.d, self.flags = places, raw, d, flags

    def project(self, state):
        half = self.d.rows // 2
        products = []
        for step in range(half):
            pair = jnp.concatenate([state[step], state[step + half]], axis=1)
            products.append(jnp.dot(self.proj, pair, preferred_element_type=F32))
        whole = jnp.concatenate([state[step] for step in range(2 * half)], axis=1)
        edges = jnp.dot(whole, self.places[...], preferred_element_type=F32)
        for step, parts in enumerate(products):
            parts = parts[0:8] + parts[8:16] + parts[16:24]
            self.raw[step * 8 : step * 8 + 8, :] = parts[:, :128]
            self.raw[(step + half) * 8 : (step + half) * 8 + 8, :] = parts[:, 128:]
        return edges.astype(BF16)

    def close(self, state, wet, fields, own_edges, one, two):
        d, even = self.d, self.flags[3] == 0
        edges = self.project(state)
        keeping = jnp.where(self.flags[0] != 0, wet[...].astype(F32), 1.0)
        whole = [self.raw[pl.ds(field, d.rows, stride=8), :] * keeping for field in range(NS)]
        for field in range(NS):
            fields[field] = whole[field].astype(BF16)
        fields[NS] = pack_columns(whole, REACH).astype(BF16)
        put_edges(own_edges, 0, edges, d)
        row = lanes(edges.shape) % d.block
        downward = jnp.where(row < 2, roll(edges, -d.rows), jnp.zeros_like(edges))
        upward = jnp.where(
            (row >= d.rows + 2) & (row < d.rows + 4), roll(edges, d.rows), jnp.zeros_like(edges)
        )
        for (ref, first), down in zip(strips(one, two, even, d), (even, jnp.logical_not(even))):
            ref[0:CH, :] = state[first]
            ref[CH : 2 * CH, :] = state[first + 1]
            put_edges(ref, 2 * CH, jnp.where(down, downward, upward), d)


def fetch(sources, targets, sems):
    copies = [
        pltpu.make_async_copy(source, target, sems.at[index])
        for index, (source, target) in enumerate(zip(sources, targets))
    ]
    for copy in copies:
        copy.start()
    return copies


def start_kernel(
    d, flags, far_given, far_surface, far_wet, far_offsets, far_weights,
    state, planes, sides, places, fields, own_edges, one, two,
    raw, tall, turned, given, surface, wet, offsets, weights, sems,
):
    rows = d.rows
    pieces = [pl.ds(at, 16) for at in range(0, CH, 16)]
    copies = fetch(
        [far_given.at[piece] for piece in pieces] + [far_surface, far_wet, far_offsets, far_weights],
        [given.at[piece] for piece in pieces] + [surface, wet, offsets, weights],
        sems,
    )
    edge_places(places, d)
    for index, piece in enumerate(pieces):
        copies[index].wait()
        turned[index * 16 * rows : (index + 1) * 16 * rows, :] = (
            given[piece].astype(F32).reshape(16 * rows, 128)
        )
    for row in range(rows):
        state[row] = turned[pl.ds(row, CH, stride=rows), :].astype(BF16)
    for copy in copies[len(pieces) :]:
        copy.wait()
    emission = Emission(surface, flags, places, raw, d)
    emission.close(state, wet, fields, own_edges, one, two)
    for k in range(NK):
        code = (offsets[0, k] * SPAN + offsets[1, k]).astype(F32)
        tall[k * rows : (k + 1) * rows, :] = code
        tall[(NK + k) * rows : (NK + k + 1) * rows, :] = weights[k]
        planes[k] = code.astype(BF16)
        planes[NK + k] = weights[k].astype(BF16)
    packed = pack_columns([tall[plane * rows : (plane + 1) * rows, :] for plane in range(2 * NK)], 2)
    sides[...] = packed.astype(BF16)
    even = flags[3] == 0
    for (ref, first), down in zip(strips(one, two, even, d), (even, jnp.logical_not(even))):
        strip = [tall[pl.ds(first + step, 2 * NK, stride=rows), :] for step in range(2)]
        ref[d.strip : d.strip + 16, :] = jnp.concatenate(strip, axis=0).astype(BF16)
        ref[d.strip + 16 : d.strip + 32, :] = jnp.where(
            down, packed[rows - 16 : rows], packed[0:16]
        ).astype(BF16)


def decode(code):
    shifted = code.astype(jnp.int32) + (HW * SPAN + HW)
    rows = lax.shift_right_logical(shifted * 241, 12)
    return rows - HW, shifted - rows * SPAN - HW


def along_lanes(values, index):
    numbers = lax.GatherDimensionNumbers(
        offset_dims=(),
        collapsed_slice_dims=(1,),
        start_index_map=(1,),
        operand_batching_dims=(0,),
        start_indices_batching_dims=(0,),
    )
    return lax.gather(
        values, index[..., None], numbers, (1, 1), mode=lax.GatherScatterMode.PROMISE_IN_BOUNDS
    )


def couple(fields, coupled, rows):
    largest = None
    for field in range(NS):
        here = jnp.max(jnp.abs(fields[field]), axis=0, keepdims=True)
        largest = here if largest is None else jnp.maximum(largest, here)
    largest = jnp.maximum(jnp.max(largest, axis=1, keepdims=True), 1e-30)
    scale = FIXED / largest
    for pair in range(NS // 2):
        high, low = [
            jnp.floor(fields[2 * pair + part] * scale + 0.5).astype(jnp.int32) for part in range(2)
        ]
        coupled[pair] = high * (1 << 16) + (low + (1 << 15))
    return largest * (1 / FIXED)


def uncouple(values):
    high = lax.shift_right_arithmetic(values, 16)
    low = (values & 0xFFFF) - (1 << 15)
    return high.astype(F32), low.astype(F32)


def select_rows(source, start, picks):
    parts = source.shape[0]
    blank = jnp.full((8, 128), 1 << 15, jnp.int32) if parts < NS else jnp.zeros((8, 128), F32)
    chosen = [[blank for _ in range(parts)] for _ in picks]
    for shift in range(-HW, HW + 1):
        at = pl.ds(start + shift, 8)
        values = [source[part, at, :] for part in range(parts)]
        for slot, (rows, index, allowed) in enumerate(picks):
            here = (rows == shift) & allowed
            for part in range(parts):
                picked = along_lanes(values[part], index)
                chosen[slot][part] = jnp.where(here, picked, chosen[slot][part])
    if parts == NS:
        return chosen
    return [[part for values in pairs for part in uncouple(values)] for pairs in chosen]


def regrid_inside(coupled, unit, plan_x, part_x, first, tiles, tall):
    lane = lanes((8, 128))
    for step in range(tiles):
        at = first + step * 8
        picks = []
        weights = []
        for k in range(NK):
            rows, cols = decode(plan_x[pl.ds(k * tall + at, 8), :])
            weights.append(plan_x[pl.ds((NK + k) * tall + at, 8), :] * unit)
            column = lane + cols
            picks.append((rows, column & 127, (column >= 0) & (column < 128)))
        chosen = select_rows(coupled, at + 14, picks)
        for field in range(NS):
            total = chosen[0][field] * weights[0]
            for k in range(1, NK):
                total = total + chosen[k][field] * weights[k]
            part_x[pl.ds(field * tall + at, 8), :] = total


def edge_lanes():
    lane = lanes((8, 128))
    return ((lane + 8) & 127) // 32, ((lane + 8) & 31) - 8


def plan_edges(plan_x, plan_y, plan_e, first, tiles, tall, sides):
    part, place = edge_lanes()
    outer = place >= 8
    for step in range(tiles):
        at = first + step * 8
        code = jnp.zeros((8, 128), F32)
        weight = jnp.zeros((8, 128), F32)
        for k in range(NK):
            edge_code = roll(plan_x[pl.ds(k * tall + at, 8), :], 32 * k)
            edge_weight = roll(plan_x[pl.ds((NK + k) * tall + at, 8), :], 32 * k)
            if sides:
                edge_code = jnp.where(
                    outer, roll(plan_y[pl.ds(k * tall + at, 8), :], 32 * k + 16), edge_code
                )
                edge_weight = jnp.where(
                    outer, roll(plan_y[pl.ds((NK + k) * tall + at, 8), :], 32 * k + 16), edge_weight
                )
            code = jnp.where(part == k, edge_code, code)
            weight = jnp.where(part == k, edge_weight, weight)
        plan_e[pl.ds(at, 8), :] = code
        plan_e[pl.ds(tall + at, 8), :] = weight


def regrid_beside(window, plan_e, part_x, forcing_x, forcing_y, first, tiles, tall, sides):
    lane = lanes((8, 128))
    part, place = edge_lanes()
    outer = place >= 8
    inner_column = place & 127
    outer_column = jnp.where(place < 16, place - 16, place + 112)
    edge = (lane < 8) | (lane >= 120)
    for step in range(tiles):
        at = first + step * 8
        rows, cols = decode(plan_e[pl.ds(at, 8), :])
        weight = plan_e[pl.ds(tall + at, 8), :]
        column = jnp.where(outer, outer_column, inner_column) + cols
        within = (column >= 0) & (column < 128)
        index = jnp.where(within, column + 32, column) & 127
        (chosen,) = select_rows(window, at + 14, [(rows, index, outer | jnp.logical_not(within))])
        for field in range(NS):
            part_sum = chosen[field] * weight
            extra = part_sum
            for k in range(1, NK):
                extra = extra + roll(part_sum, -32 * k)
            total = part_x[pl.ds(field * tall + at, 8), :] + jnp.where(edge, extra, 0.0)
            forcing_x[pl.ds(at * 8 + field, 8, stride=8), :] = total
            forcing_x[pl.ds(at * 8 + field + 4, 8, stride=8), :] = total
            if sides:
                extra = roll(extra, -16)
                forcing_y[pl.ds(at * 8 + field, 8, stride=8), :] = extra
                forcing_y[pl.ds(at * 8 + field + 4, 8, stride=8), :] = extra


def twice_gelu(x):
    scale = (2 / jnp.pi) ** 0.5
    return x + x * jnp.tanh(x * (scale + (scale * 0.044715) * (x * x)))


def staggered(count, *stages):
    values = [{} for _ in stages]
    for turn in range(count + len(stages) - 1):
        for index, stage in enumerate(stages):
            step = turn - index
            if 0 <= step < count:
                given = values[index - 1].pop(step) if index else None
                values[index][step] = stage(step, given)


def air(state, out, forcing_x, air_in, atm_out, d):
    half = d.rows // 2
    leading = subs((8, 128)) < 4
    blank = jnp.zeros((32, 128), BF16)

    def inputs(row):
        at = (row + 2) * 8
        forced = jnp.where(leading, forcing_x[at : at + 8, :], 1.0)
        forced = jnp.concatenate([forced, jnp.zeros_like(forced)], axis=0).astype(BF16)
        return jnp.concatenate([state[row], forced, blank], axis=0)

    def first(step, _):
        pair = jnp.concatenate([inputs(step), inputs(step + half)], axis=1)
        return jnp.dot(air_in[...], pair, preferred_element_type=F32)

    def middle(step, product):
        return twice_gelu(product).astype(BF16)

    def second(step, hidden):
        return jnp.dot(atm_out[...], hidden, preferred_element_type=F32)

    def last(step, update):
        news = []
        for offset in range(2):
            change = update[:, offset * 128 : (offset + 1) * 128]
            news.append(state[step + offset * half].astype(F32) + 0.5 * change)
        out(step, *news)

    staggered(half, first, middle, second, last)


def edge_forcing(forcing_x, forcing_y, d):
    lane = lanes((8, d.edge))
    block = lane // d.block
    row = lane % d.block

    inner = outer = jnp.zeros((8, d.edge), F32)
    for step in range(d.rows + 4):
        at = pl.ds(step * 8, 8)
        pad = [jnp.zeros((8, 128), F32)] * (d.pieces - 1)
        here = jnp.concatenate([forcing_x[at, :]] + pad, axis=1)
        there = jnp.concatenate([forcing_y[at, :]] + pad, axis=1)
        for index, column in enumerate((126, 0, 127, 1)):
            shift = step + index * d.block - column
            match = (block == index) & (row == step)
            if column in (0, 127):
                inner = jnp.where(match, roll(here, shift), inner)
            outer = jnp.where(match, roll(there, shift), outer)
    return inner, outer


def roll_rows(state, upper, lower, rolled, d):
    def put(row, values):
        rolled[row, 0:CH, :] = roll(values, 1)
        rolled[row, CH : 2 * CH, :] = values
        rolled[row, 2 * CH : 3 * CH, :] = roll(values, -1)

    for step in range(2):
        put(step, upper[step * CH : (step + 1) * CH, :])
        put(d.rows + 2 + step, lower[step * CH : (step + 1) * CH, :])
    for row in range(d.rows):
        put(row + 2, state[row])


def sea(
    state, rolled, edges, left, right, out, forcing_x, forcing_y, ocn_in, ocn_out, wet,
    at_top, at_bottom, stack, hidden, side, d,
):
    rows, block = d.rows, d.block
    lane = lanes((CH, 128))
    spot = lanes((CH, d.edge))
    part = spot // block
    inner = edges
    outer = jnp.where((part == 0) | (part == 2), left, right)

    def sides_of(inner, outer, spot):
        first = spot < block
        return (
            jnp.where(first, outer, roll(inner, -block)),
            jnp.where(first, roll(outer, -2 * block), outer),
            jnp.where(first, roll(inner, -block), roll(outer, -2 * block)),
        )

    beside = sides_of(inner, outer, spot)
    middle = beside[1]
    force_in, force_out = edge_forcing(forcing_x, forcing_y, d)
    beside_forcing = sides_of(force_in, force_out, lanes((8, d.edge)))
    sub = subs((8, d.edge))
    ones = jnp.ones((8, d.edge), F32)
    forced = jnp.concatenate(
        [
            jnp.where(sub < 4, beside_forcing[0], beside_forcing[1]),
            jnp.where(sub < 4, beside_forcing[2], ones),
        ],
        axis=0,
    ).astype(BF16)
    columns = jnp.concatenate(list(beside) + [forced], axis=0)
    for tap in range(3):
        side[tap * 256 : (tap + 1) * 256, :] = roll(columns, -tap)

    sub_row = subs((8, 128))
    lane_row = lanes((8, 128))

    for row in range(rows + 4):
        entry = roll(middle, -row)[:, :128]
        stack[row, 0:CH, :] = jnp.where(lane == 0, entry, rolled[row, 0:CH, :])
        stack[row, CH : 2 * CH, :] = rolled[row, CH : 2 * CH, :]
        entry = roll(middle, 127 - block - row)[:, :128]
        stack[row, 2 * CH : 3 * CH, :] = jnp.where(lane == 127, entry, rolled[row, 2 * CH : 3 * CH, :])
        here, there = forcing_x[row * 8 : row * 8 + 8, :], forcing_y[row * 8 : row * 8 + 8, :]
        before = roll(jnp.where(lane_row == 127, there, here), 1)
        after = roll(jnp.where(lane_row == 0, there, here), -1)
        stack[row, 3 * CH : 256, :] = jnp.concatenate(
            [jnp.where(sub_row < 4, before, here), jnp.where(sub_row < 4, after, 1.0)], axis=0
        ).astype(BF16)

    pairs = (rows + 2) // 2

    def first(step, _):
        taps = jnp.concatenate(
            [
                stack[step : step + 3].reshape(3 * 256, 128),
                stack[step + pairs : step + pairs + 3].reshape(3 * 256, 128),
            ],
            axis=1,
        )
        return jnp.dot(ocn_in[...], taps, preferred_element_type=F32)

    def activate(step, product):
        active = twice_gelu(product)
        low, high = active[:, :128], active[:, 128:]
        if step == 0:
            low = jnp.where(at_top != 0, 0.0, low)
        if step == pairs - 1:
            high = jnp.where(at_bottom != 0, 0.0, high)
        hidden[step, 0:HIDK, :] = low.astype(BF16)
        hidden[step + pairs, 0:HIDK, :] = high.astype(BF16)
        blank = jnp.zeros((HIDP - HIDK, 128), BF16)
        hidden[step, HIDK:HIDP, :] = blank
        hidden[step + pairs, HIDK:HIDP, :] = blank

    staggered(pairs, first, activate)
    product = jnp.dot(ocn_in[...], side[...], preferred_element_type=F32)
    spot = lanes((1, d.edge)) % block
    gone = ((spot == 0) & (at_top != 0)) | ((spot == rows + 1) & (at_bottom != 0))
    active = jnp.where(gone, 0.0, twice_gelu(product)).astype(BF16)
    active = jnp.concatenate([active, jnp.zeros((HIDP - HIDK, d.edge), BF16)], axis=0)

    def taps_of(slices):
        total = None
        for tap, values in enumerate(slices):
            weights = ocn_out[tap * 3 * CH : (tap + 1) * 3 * CH, :]
            product = jnp.dot(weights, values, preferred_element_type=F32)
            total = product if total is None else total + product
        return total

    partial = taps_of([roll(active, -tap) for tap in range(3)])
    from_left, from_right = partial[0:CH], partial[2 * CH : 3 * CH]
    half = rows // 2

    def second(step, _):
        return taps_of(
            [
                jnp.concatenate([hidden[step + tap], hidden[step + half + tap]], axis=1)
                for tap in range(3)
            ]
        )

    def last(step, product):
        news = []
        for offset in range(2):
            row = step + offset * half
            sums = product[:, offset * 128 : (offset + 1) * 128]
            entry = roll(from_left, -row)[:, :128]
            total = sums[CH : 2 * CH] + jnp.where(lane == 0, entry, roll(sums[0:CH], 1))
            entry = roll(from_right, 127 - block - row)[:, :128]
            total = total + jnp.where(lane == 127, entry, roll(sums[2 * CH : 3 * CH], -1))
            update = total * (0.5 * wet[row : row + 1, :].astype(F32))
            news.append(state[row].astype(F32) + update)
        out(step, *news)

    staggered(half, second, last)


def prepare(atm_in, atm_bias, ocn_in, ocn_bias, ocn_out, air_in, first, second, is_ocean):
    def bias_rows(ref, width):
        row = jnp.concatenate([ref[index : index + 1, :] for index in range(ref.shape[0])], axis=1)
        terms = list(split_bf16(row)) + [jnp.zeros_like(row)]
        bias = jnp.concatenate(terms, axis=0)
        return jnp.pad(bias, ((0, 0), (0, width - bias.shape[1])))

    @pl.when(is_ocean == 0)
    def _():
        columns = jnp.concatenate(
            [atm_in[...].astype(F32), bias_rows(atm_bias, HA), jnp.zeros((40, HA), F32)], axis=0
        )
        air_in[...] = columns.T.astype(BF16)

    @pl.when(is_ocean != 0)
    def _():
        bias = bias_rows(ocn_bias, 256)
        count = ocn_in.shape[2]
        for tap in range(3):
            whole = [ocn_in[3 * tap + side].astype(F32) for side in range(3)]
            whole = [jnp.pad(values, ((0, 0), (0, 256 - count))) for values in whole]
            rows = [values[:CH] for values in whole] + [values[CH:] for values in whole]
            rows.append(bias if tap == 0 else jnp.zeros((4, 256), F32))
            columns = jnp.concatenate(rows, axis=0).T
            first[:, tap * 256 : (tap + 1) * 256] = columns[:HIDK].astype(BF16)
        for tap in range(9):
            values = ocn_out[tap].astype(F32)
            second[tap * CH : (tap + 1) * CH, :] = jnp.pad(
                values, ((0, 0), (0, HIDP - count))
            ).astype(BF16)


def ends(flags):
    at_top, at_bottom, even = flags[1] != 0, flags[2] != 0, flags[3] == 0

    def up_and_down(one, two):
        above = jnp.where(even, two, one).astype(F32)
        below = jnp.where(even, one, two).astype(F32)
        return jnp.where(at_top, 0.0, above), jnp.where(at_bottom, 0.0, below)

    return up_and_down


def middle_kernel(d, opening, *refs):
    refs = list(refs)
    take = lambda count: [refs.pop(0) for _ in range(count)]
    flags, state, field_one, beside, field_two, from_one, from_two = take(7)
    if opening:
        planes, *far_weights = take(6)
    else:
        (plan_x,) = take(1)
    part_x, fields_x, rolled = take(3)
    if opening:
        plan_x, *made_weights = take(4)
    (coupled,) = take(1)
    if opening:
        *raw_weights, sems = take(6)
        copies = fetch(far_weights, raw_weights, sems)
    rows, tall = d.rows, d.tall
    is_ocean = flags[0]
    up_and_down = ends(flags)

    if opening:

        @pl.when(is_ocean != 0)
        def _():
            base = d.strip
            pair = up_and_down(from_one[base : base + 16, :], from_two[base : base + 16, :])
            plan_x[...] = jnp.zeros_like(plan_x)
            for step, strip in zip((0, rows + 2), pair):
                for index in range(2):
                    plan_x[pl.ds(step + index, 2 * NK, stride=tall), :] = strip[index * 8 : (index + 1) * 8]

        for plane in range(2 * NK):
            plan_x[plane * tall + 2 : plane * tall + 2 + rows, :] = planes[plane].astype(F32)

    for field in range(NS):
        pair = up_and_down(field_one[field], field_two[field])
        fields_x[field, 0:16, :] = pair[0][rows - 16 : rows]
        fields_x[field, 16 : 16 + rows, :] = beside[field].astype(F32)
        fields_x[field, 16 + rows : 32 + rows, :] = pair[1][0:16]

    unit = couple(fields_x, coupled, rows)

    @pl.when(is_ocean == 0)
    def _():
        regrid_inside(coupled, unit, plan_x, part_x, 2, rows // 8, tall)

    @pl.when(is_ocean != 0)
    def _():
        regrid_inside(coupled, unit, plan_x, part_x, 0, d.tiles, tall)
        upper, lower = up_and_down(from_one[0 : 2 * CH, :], from_two[0 : 2 * CH, :])
        roll_rows(state, upper.astype(BF16), lower.astype(BF16), rolled, d)

    if opening:
        for copy in copies:
            copy.wait()
        prepare(*raw_weights, *made_weights, is_ocean)


def step_kernel(d, opening, closing, *refs):
    refs = list(refs)
    take = lambda count: [refs.pop(0) for _ in range(count)]
    flags, state, wet, from_left, from_right = take(5)
    part_x, fields_x, rolled, edges, plan_x, air_in, first, second, atm_out = take(9)
    if not opening:
        (plan_e,) = take(1)
    if not closing:
        surface, places = take(2)
    (out,) = take(1)
    if not closing:
        fields, new_edges, one, two = take(4)
    if opening:
        (plan_e,) = take(1)
    window, forcing_x, forcing_y, stack, hidden, side, raw = take(7)
    if opening:
        (plan_y,) = take(1)
    rows, tall = d.rows, d.tall
    is_ocean, at_top, at_bottom = flags[0], flags[1], flags[2]
    up_and_down = ends(flags)

    if opening:

        @pl.when(is_ocean != 0)
        def _():
            plan_y[...] = jnp.zeros_like(plan_y)
            base = d.edge_rows
            parts = [
                (ref[base : base + 16, :], ref[base + 16 + rows : base + 32 + rows, :],
                 ref[base + 16 : base + 16 + rows, :])
                for ref in (from_left, from_right)
            ]
            for plane in range(2 * NK):
                first_end, second_end, own = [
                    unpack_columns(left, right, plane, 2 * NK, 2) for left, right in zip(*parts)
                ]
                above, below = up_and_down(first_end, second_end)
                at = plane * tall
                plan_y[at : at + 2, :] = above[14:16]
                plan_y[at + 2 : at + 2 + rows, :] = own
                plan_y[at + 2 + rows : at + 4 + rows, :] = below[0:2]

    base = d.edge_rows + (rows + 32 if opening else 0)
    parts = [
        (ref[base : base + 16, :], ref[base + 16 + rows : base + 32 + rows, :],
         ref[base + 16 : base + 16 + rows, :])
        for ref in (from_left, from_right)
    ]
    for field in range(NS):
        first_end, second_end, own = [
            unpack_columns(left, right, field, NS, REACH) for left, right in zip(*parts)
        ]
        above, below = up_and_down(first_end, second_end)
        for at, values in ((0, above), (16, own), (16 + rows, below)):
            count = values.shape[0]
            inside = roll(fields_x[field, at : at + count, :], 32)
            lane = lanes(values.shape)
            near = (lane >= 32 - REACH) & (lane < 32 + REACH)
            far = (lane < REACH) | (lane >= 128 - REACH)
            kept = jnp.where(near, inside, jnp.where(far, values, 0.0))
            window[field, at : at + count, :] = kept
    def finished():
        emission = None if closing else Emission(surface, flags, places, raw, d)

        def put(step, low, high):
            if closing:
                for row, values in ((step, low), (step + rows // 2, high)):
                    raw[pl.ds(row, CH, stride=rows), :] = values
                return
            out[step] = low.astype(BF16)
            out[step + rows // 2] = high.astype(BF16)

        def close():
            if not closing:
                emission.close(out, wet, fields, new_edges, one, two)

        return put, close

    @pl.when(is_ocean == 0)
    def _():
        if opening:
            plan_edges(plan_x, plan_y, plan_e, 2, rows // 8, tall, False)
        regrid_beside(
            window, plan_e, part_x, forcing_x, forcing_y, 2, rows // 8, tall, False
        )
        put, close = finished()
        air(state, put, forcing_x, air_in, atm_out, d)
        close()

    @pl.when(is_ocean != 0)
    def _():
        if opening:
            plan_edges(plan_x, plan_y, plan_e, 0, d.tiles, tall, True)
        regrid_beside(
            window, plan_e, part_x, forcing_x, forcing_y, 0, d.tiles, tall, True
        )
        put, close = finished()
        joined = [get_edges(ref, 0, d) for ref in (from_left, from_right)]
        sea(
            state, rolled, get_edges(edges, 0, d), *joined, put, forcing_x, forcing_y,
            first, second, wet, at_top, at_bottom, stack, hidden, side, d,
        )
        close()

    if closing:
        out[...] = raw[...].reshape(CH, rows, 128).astype(BF16)


VMEM = pl.BlockSpec(memory_space=pltpu.VMEM)
HBM = pl.BlockSpec(memory_space=pltpu.HBM)
SMEM = pl.BlockSpec(memory_space=pltpu.SMEM)
PARAMS = pltpu.CompilerParams(vmem_limit_bytes=48 * 1024 * 1024)


def shape(*dims, dtype=BF16):
    return jax.ShapeDtypeStruct(dims, dtype)


def send(x, move):
    names = ("grp", "lat", "lon")
    sizes = [lax.axis_size(name) for name in names]
    pairs = []
    for group in range(sizes[0]):
        for lat in range(sizes[1]):
            for lon in range(sizes[2]):
                to = move(group, lat, lon)
                if to is None or not 0 <= to[1] < sizes[1]:
                    continue
                target = (to[0] * sizes[1] + to[1]) * sizes[2] + to[2] % sizes[2]
                pairs.append(((group * sizes[1] + lat) * sizes[2] + lon, target))
    return lax.ppermute(x, names, pairs)


def swap_rows(x, turn, across):
    count, columns = lax.axis_size("lat"), lax.axis_size("lon")

    def move(group, lat, lon):
        other = ((lat + turn) ^ 1) - turn
        if 0 <= other < count and (across or group == 1):
            return (1 - group if across else group), other, lon
        beside = lon ^ 1
        return group, lat, beside if beside < columns else lon

    return send(x, move)


def exchange(fields, own_edges, one, two, sides, d):
    rows = d.rows
    from_one = swap_rows(one, 0, False)
    from_two = swap_rows(two, 1, False)
    field_one = swap_rows(fields, 0, True)
    field_two = swap_rows(fields, 1, True)
    beside = send(fields, lambda g, i, j: (1 - g, i, j))
    lat, count = lax.axis_index("lat"), lax.axis_size("lat")
    odd = lat % 2 == 1
    edges = own_edges
    for turn, ref in ((0, from_one), (1, from_two)):
        other = ((lat + turn) ^ 1) - turn
        there = (other >= 0) & (other < count)
        edges = edges + jnp.where(there, ref[2 * CH : d.strip], 0)
    edges, beside, field_one, field_two = lax.optimization_barrier(
        (edges, beside, field_one, field_two)
    )
    outer = [field_one[NS], field_two[NS]]
    if rows != 16:
        outer = [
            jnp.where(odd, outer[0][rows - 16 :], outer[0][:16]),
            jnp.where(odd, outer[1][:16], outer[1][rows - 16 :]),
        ]
    packed = [edges]
    if sides is not None:
        packed += [from_one[d.strip + 16 :], sides, from_two[d.strip + 16 :]]
    packed += [outer[0], beside[NS], outer[1]]
    packed = jnp.concatenate(packed, axis=0)
    from_left = send(packed, lambda g, i, j: (g, i, j + 1))
    from_right = send(packed, lambda g, i, j: (g, i, j - 1))
    return (field_one, beside, field_two, from_one, from_two), (from_left, from_right), edges


def local(
    coupled_state, land_mask, regrid_offsets, regrid_weights, surface_proj,
    atm_in, atm_bias, atm_out, ocn_in, ocn_bias, ocn_out,
):
    rows = coupled_state.shape[2]
    assert coupled_state.shape[3] == 128
    d = Dims(rows)
    group = lax.axis_index("grp")
    lat = lax.axis_index("lat")
    flags = jnp.stack(
        [group, lat == 0, lat == lax.axis_size("lat") - 1, lat % 2]
    ).astype(jnp.int32)
    raw_weights = (
        atm_in.T,
        atm_bias.reshape(HA // 128, 128),
        jnp.transpose(ocn_in, (1, 2, 0)),
        ocn_bias[None],
        jnp.transpose(ocn_out, (1, 0, 2)),
    )
    state_shape = shape(rows, CH, 128)
    emitted = [
        shape(NS + 1, rows, 128),
        shape(d.edge_rows, 128),
        shape(d.strip, 128),
        shape(d.strip, 128),
    ]
    raw = pltpu.VMEM((rows * 8, 128), F32)
    turned = pltpu.VMEM((CH * rows, 128), F32)

    def call(kernel, operands, outs, scratch, name, far=()):
        scratch = scratch + [pltpu.VMEM(x.shape, x.dtype) for x in far]
        if far:
            scratch.append(pltpu.SemaphoreType.DMA((len(far) + CH // 16,)))

        far = [pltpu.with_memory_space_constraint(x, pltpu.HBM) for x in far]
        return pl.pallas_call(
            kernel,
            out_shape=outs,
            in_specs=[SMEM] + [VMEM] * len(operands) + [HBM] * len(far),
            out_specs=[VMEM] * len(outs),
            scratch_shapes=scratch,
            compiler_params=PARAMS,
            name=name,
        )(flags, *operands, *far)

    state, planes, sides, places, fields, edges, one, two = call(
        functools.partial(start_kernel, d),
        (),
        [state_shape, shape(2 * NK, rows, 128), shape(rows, 128), shape(rows * 128, d.edge)]
        + emitted[:2]
        + [shape(d.strip + 32, 128)] * 2,
        [raw, pltpu.VMEM((2 * NK * rows, 128), F32), turned],
        "start",
        (coupled_state[0], surface_proj, land_mask, regrid_offsets[0], regrid_weights[0]),
    )

    plan = shape(2 * NK * d.tall, 128, dtype=F32)
    between = [
        shape(NS * d.tall, 128, dtype=F32),
        shape(NS, rows + 32, 128, dtype=F32),
        shape(rows + 4, 3 * CH, 128),
    ]
    made = [shape(HA, 128), shape(HIDK, 768), shape(9 * CH, HIDP)]
    coupled = pltpu.VMEM((NS // 2, rows + 32, 128), jnp.int32)
    scratch = [
        pltpu.VMEM((NS, rows + 32, 128), F32),
        pltpu.VMEM((d.tall * 8, 128), F32),
        pltpu.VMEM((d.tall * 8, 128), F32),
        pltpu.VMEM((rows + 4, 256, 128), BF16),
        pltpu.VMEM((rows + 2, HIDP, 128), BF16),
        pltpu.VMEM((768, d.edge), BF16),
    ]

    vertical, horizontal, edges = exchange(fields, edges, one, two, sides, d)
    *shared, plan_x, air_in, first, second = call(
        functools.partial(middle_kernel, d, True),
        (state, *vertical, planes),
        between + [plan] + made,
        [coupled],
        "first_middle",
        raw_weights,
    )
    weights = (air_in, first, second, atm_out)
    state, fields, edges, one, two, plan_e = call(
        functools.partial(step_kernel, d, True, False),
        (state, land_mask, *horizontal, *shared, edges, plan_x, *weights, surface_proj, places),
        [state_shape] + emitted + [shape(2 * d.tall, 128, dtype=F32)],
        scratch + [raw, pltpu.VMEM(plan.shape, F32)],
        "first_step",
    )

    vertical, horizontal, edges = exchange(fields, edges, one, two, None, d)
    shared = call(
        functools.partial(middle_kernel, d, False),
        (state, *vertical, plan_x),
        between,
        [coupled],
        "second_middle",
    )
    (state,) = call(
        functools.partial(step_kernel, d, False, True),
        (state, land_mask, *horizontal, *shared, edges, plan_x, *weights, plan_e),
        [shape(CH, rows, 128)],
        scratch + [turned],
        "second_step",
    )
    return state[None]


def solution(mesh):
    return jax.shard_map(
        local,
        mesh=mesh,
        in_specs=(
            P("grp", None, "lat", "lon"),
            P("lat", "lon"),
            P("grp", None, None, "lat", "lon"),
            P("grp", None, "lat", "lon"),
            P(),
            P(),
            P(),
            P(),
            P(),
            P(),
            P(),
        ),
        out_specs=P("grp", None, "lat", "lon"),
        check_vma=False,
    )
```

```python
import functools

import jax
import jax.numpy as jnp
from jax import lax
from jax.experimental import pallas as pl
from jax.experimental.pallas import tpu as pltpu
from jax.sharding import PartitionSpec as P

CH = 80
NS = 4
NK = 4
HA = 384
HW = 8
SPAN = 2 * HW + 1
REACH = HW + 2
FIXED = 32767.0
HIDK = 208
HIDP = 256
F32 = jnp.float32
BF16 = jnp.bfloat16


def roll(x, shift, axis=1):
    size = x.shape[axis]
    if isinstance(shift, int):
        shift = shift % size
        if shift == 0:
            return x
    return pltpu.roll(x, shift, axis)


def lanes(shape):
    return lax.broadcasted_iota(jnp.int32, shape, len(shape) - 1)


def subs(shape):
    return lax.broadcasted_iota(jnp.int32, shape, len(shape) - 2)


class Dims:
    def __init__(self, rows):
        self.rows = rows
        self.block = 32 if rows + 4 <= 32 else 64
        self.edge = 4 * self.block
        self.pieces = self.edge // 128
        self.edge_rows = CH * self.pieces
        self.tiles = -(-(rows + 4) // 8)
        self.tall = 8 * self.tiles
        self.strip = 2 * CH + self.edge_rows


def put_edges(ref, at, edges, d):
    for piece in range(d.pieces):
        ref[at + piece * CH : at + (piece + 1) * CH, :] = edges[:, piece * 128 : (piece + 1) * 128]


def get_edges(ref, at, d):
    return jnp.concatenate(
        [ref[at + piece * CH : at + (piece + 1) * CH, :] for piece in range(d.pieces)], axis=1
    )


def edge_places(places, d):
    lane = lanes((1, d.edge))
    block = lane // d.block
    row = lane % d.block
    target = jnp.where(block == 0, 126, jnp.where(block == 1, 0, jnp.where(block == 2, 127, 1)))
    position = subs((128, d.edge))
    for step in range(d.rows + 4):
        place = (position == jnp.where(row == step, target, -1)).astype(F32).astype(BF16)
        places[step * 128 : (step + 1) * 128, :] = place


def edge_columns(state, places, d):
    whole = jnp.concatenate([state[step] for step in range(d.rows)], axis=1)
    return jnp.dot(whole, places[...], preferred_element_type=F32).astype(BF16)


def pack_columns(values, reach):
    lane = lanes(values[0].shape)
    pitch = 128 // len(values)
    packed = jnp.zeros_like(values[0])
    for index, value in enumerate(values):
        at = index * pitch
        packed = jnp.where((lane >= at) & (lane < at + reach), roll(value, at), packed)
        at += reach
        packed = jnp.where((lane >= at) & (lane < at + reach), roll(value, at + reach - 128), packed)
    return packed


def unpack_columns(left, right, index, count, reach):
    at = index * (128 // count)
    left = roll(left.astype(F32), 128 - at - 2 * reach)
    return jnp.where(lanes(left.shape) < 64, roll(right.astype(F32), -at), left)


def strips(one, two, even, d):
    last = d.rows - 2
    return (one, jnp.where(even, last, 0)), (two, jnp.where(even, 0, last))


def split_bf16(values):
    high = values.astype(BF16).astype(F32)
    mid = (values - high).astype(BF16).astype(F32)
    return high, mid, values - high - mid


class Emission:
    def __init__(self, surface, flags, places, raw, d):
        gap = jnp.zeros((4, CH), F32)
        terms = []
        for term in split_bf16(surface[flags[0]]):
            terms += [term, gap]
        self.proj = jnp.concatenate(terms + [gap, gap], axis=0).astype(BF16)
        self.places, self.raw, self.d, self.flags = places, raw, d, flags

    def project(self, state):
        half = self.d.rows // 2
        products = []
        for step in range(half):
            pair = jnp.concatenate([state[step], state[step + half]], axis=1)
            products.append(jnp.dot(self.proj, pair, preferred_element_type=F32))
        whole = jnp.concatenate([state[step] for step in range(2 * half)], axis=1)
        own = self.places[256 : 256 + 256 * half, :]
        edges = jnp.dot(whole, own, preferred_element_type=F32)
        for step, parts in enumerate(products):
            parts = parts[0:8] + parts[8:16] + parts[16:24]
            self.raw[step * 8 : step * 8 + 8, :] = parts[:, :128]
            self.raw[(step + half) * 8 : (step + half) * 8 + 8, :] = parts[:, 128:]
        return edges.astype(BF16)

    def close(self, state, wet, fields, own_edges, one, two):
        d, even = self.d, self.flags[3] == 0
        edges = self.project(state)
        keeping = jnp.where(self.flags[0] != 0, wet[...].astype(F32), 1.0)
        whole = [self.raw[pl.ds(field, d.rows, stride=8), :] * keeping for field in range(NS)]
        for field in range(NS):
            fields[field] = whole[field].astype(BF16)
        fields[NS] = pack_columns(whole, REACH).astype(BF16)
        put_edges(own_edges, 0, edges, d)
        row = lanes(edges.shape) % d.block
        downward = jnp.where(row < 2, roll(edges, -d.rows), jnp.zeros_like(edges))
        upward = jnp.where(
            (row >= d.rows + 2) & (row < d.rows + 4), roll(edges, d.rows), jnp.zeros_like(edges)
        )
        for (ref, first), down in zip(strips(one, two, even, d), (even, jnp.logical_not(even))):
            ref[0:CH, :] = state[first]
            ref[CH : 2 * CH, :] = state[first + 1]
            put_edges(ref, 2 * CH, jnp.where(down, downward, upward), d)


def fetch(sources, targets, sems):
    copies = [
        pltpu.make_async_copy(source, target, sems.at[index])
        for index, (source, target) in enumerate(zip(sources, targets))
    ]
    for copy in copies:
        copy.start()
    return copies


def start_kernel(
    d, flags, far_given, far_surface, far_wet, far_offsets, far_weights,
    state, planes, sides, places, fields, own_edges, one, two,
    raw, tall, turned, given, surface, wet, offsets, weights, sems,
):
    rows = d.rows
    pieces = [pl.ds(at, 16) for at in range(0, CH, 16)]
    copies = fetch(
        [far_given.at[piece] for piece in pieces] + [far_surface, far_wet, far_offsets, far_weights],
        [given.at[piece] for piece in pieces] + [surface, wet, offsets, weights],
        sems,
    )
    edge_places(places, d)
    for index, piece in enumerate(pieces):
        copies[index].wait()
        turned[index * 16 * rows : (index + 1) * 16 * rows, :] = (
            given[piece].astype(F32).reshape(16 * rows, 128)
        )
    for row in range(rows):
        state[row] = turned[pl.ds(row, CH, stride=rows), :].astype(BF16)
    for copy in copies[len(pieces) :]:
        copy.wait()
    emission = Emission(surface, flags, places, raw, d)
    emission.close(state, wet, fields, own_edges, one, two)
    for k in range(NK):
        code = (offsets[0, k] * SPAN + offsets[1, k]).astype(F32)
        tall[k * rows : (k + 1) * rows, :] = code
        tall[(NK + k) * rows : (NK + k + 1) * rows, :] = weights[k]
        planes[k] = code.astype(BF16)
        planes[NK + k] = weights[k].astype(BF16)
    packed = pack_columns([tall[plane * rows : (plane + 1) * rows, :] for plane in range(2 * NK)], 2)
    sides[...] = packed.astype(BF16)
    even = flags[3] == 0
    for (ref, first), down in zip(strips(one, two, even, d), (even, jnp.logical_not(even))):
        strip = [tall[pl.ds(first + step, 2 * NK, stride=rows), :] for step in range(2)]
        ref[d.strip : d.strip + 16, :] = jnp.concatenate(strip, axis=0).astype(BF16)
        ref[d.strip + 16 : d.strip + 32, :] = jnp.where(
            down, packed[rows - 16 : rows], packed[0:16]
        ).astype(BF16)


def decode(code):
    shifted = code.astype(jnp.int32) + (HW * SPAN + HW)
    rows = lax.shift_right_logical(shifted * 241, 12)
    return rows - HW, shifted - rows * SPAN - HW


def along_lanes(values, index):
    numbers = lax.GatherDimensionNumbers(
        offset_dims=(),
        collapsed_slice_dims=(1,),
        start_index_map=(1,),
        operand_batching_dims=(0,),
        start_indices_batching_dims=(0,),
    )
    return lax.gather(
        values, index[..., None], numbers, (1, 1), mode=lax.GatherScatterMode.PROMISE_IN_BOUNDS
    )


def couple(fields, coupled, rows):
    largest = None
    for field in range(NS):
        here = jnp.max(jnp.abs(fields[field]), axis=0, keepdims=True)
        largest = here if largest is None else jnp.maximum(largest, here)
    largest = jnp.maximum(jnp.max(largest, axis=1, keepdims=True), 1e-30)
    scale = FIXED / largest
    for pair in range(NS // 2):
        high, low = [
            jnp.floor(fields[2 * pair + part] * scale + 0.5).astype(jnp.int32) for part in range(2)
        ]
        coupled[pair] = high * (1 << 16) + (low + (1 << 15))
    return largest * (1 / FIXED)


def uncouple(values):
    high = lax.shift_right_arithmetic(values, 16)
    low = (values & 0xFFFF) - (1 << 15)
    return high.astype(F32), low.astype(F32)


def select_rows(source, start, picks):
    parts = source.shape[0]
    blank = jnp.full((8, 128), 1 << 15, jnp.int32) if parts < NS else jnp.zeros((8, 128), F32)
    chosen = [[blank for _ in range(parts)] for _ in picks]
    for shift in range(-HW, HW + 1):
        at = pl.ds(start + shift, 8)
        values = [source[part, at, :] for part in range(parts)]
        for slot, (rows, index, allowed) in enumerate(picks):
            here = (rows == shift) & allowed
            for part in range(parts):
                picked = along_lanes(values[part], index)
                chosen[slot][part] = jnp.where(here, picked, chosen[slot][part])
    if parts == NS:
        return chosen
    return [[part for values in pairs for part in uncouple(values)] for pairs in chosen]


def regrid_inside(coupled, unit, plan_x, part_x, first, tiles, tall):
    lane = lanes((8, 128))
    for step in range(tiles):
        at = first + step * 8
        picks = []
        weights = []
        for k in range(NK):
            rows, cols = decode(plan_x[pl.ds(k * tall + at, 8), :])
            weights.append(plan_x[pl.ds((NK + k) * tall + at, 8), :] * unit)
            column = lane + cols
            picks.append((rows, column & 127, (column >= 0) & (column < 128)))
        chosen = select_rows(coupled, at + 14, picks)
        for field in range(NS):
            total = chosen[0][field] * weights[0]
            for k in range(1, NK):
                total = total + chosen[k][field] * weights[k]
            part_x[pl.ds(field * tall + at, 8), :] = total


def edge_lanes():
    lane = lanes((8, 128))
    return ((lane + 8) & 127) // 32, ((lane + 8) & 31) - 8


def plan_edges(plan_x, plan_y, plan_e, first, tiles, tall, sides):
    part, place = edge_lanes()
    outer = place >= 8
    for step in range(tiles):
        at = first + step * 8
        code = jnp.zeros((8, 128), F32)
        weight = jnp.zeros((8, 128), F32)
        for k in range(NK):
            edge_code = roll(plan_x[pl.ds(k * tall + at, 8), :], 32 * k)
            edge_weight = roll(plan_x[pl.ds((NK + k) * tall + at, 8), :], 32 * k)
            if sides:
                edge_code = jnp.where(
                    outer, roll(plan_y[pl.ds(k * tall + at, 8), :], 32 * k + 16), edge_code
                )
                edge_weight = jnp.where(
                    outer, roll(plan_y[pl.ds((NK + k) * tall + at, 8), :], 32 * k + 16), edge_weight
                )
            code = jnp.where(part == k, edge_code, code)
            weight = jnp.where(part == k, edge_weight, weight)
        plan_e[pl.ds(at, 8), :] = code
        plan_e[pl.ds(tall + at, 8), :] = weight


def regrid_beside(window, plan_e, part_x, forcing_x, forcing_y, first, tiles, tall, sides):
    lane = lanes((8, 128))
    part, place = edge_lanes()
    outer = place >= 8
    inner_column = place & 127
    outer_column = jnp.where(place < 16, place - 16, place + 112)
    edge = (lane < 8) | (lane >= 120)
    for step in range(tiles):
        at = first + step * 8
        rows, cols = decode(plan_e[pl.ds(at, 8), :])
        weight = plan_e[pl.ds(tall + at, 8), :]
        column = jnp.where(outer, outer_column, inner_column) + cols
        within = (column >= 0) & (column < 128)
        index = jnp.where(within, column + 32, column) & 127
        (chosen,) = select_rows(window, at + 14, [(rows, index, outer | jnp.logical_not(within))])
        for field in range(NS):
            part_sum = chosen[field] * weight
            extra = part_sum
            for k in range(1, NK):
                extra = extra + roll(part_sum, -32 * k)
            total = part_x[pl.ds(field * tall + at, 8), :] + jnp.where(edge, extra, 0.0)
            forcing_x[pl.ds(at * 8 + field, 8, stride=8), :] = total
            forcing_x[pl.ds(at * 8 + field + 4, 8, stride=8), :] = total
            if sides:
                extra = roll(extra, -16)
                forcing_y[pl.ds(at * 8 + field, 8, stride=8), :] = extra
                forcing_y[pl.ds(at * 8 + field + 4, 8, stride=8), :] = extra


def twice_gelu(x):
    scale = (2 / jnp.pi) ** 0.5
    return x + x * jnp.tanh(x * (scale + (scale * 0.044715) * (x * x)))


def staggered(count, *stages, between=()):
    between = list(between)
    values = [{} for _ in stages]
    for turn in range(count + len(stages) - 1):
        for index, stage in enumerate(stages):
            step = turn - index
            if 0 <= step < count:
                given = values[index - 1].pop(step) if index else None
                values[index][step] = stage(step, given)
        if between:
            between.pop(0)()
    for extra in between:
        extra()


def air(state, out, forcing_x, air_in, atm_out, d):
    half = d.rows // 2
    leading = subs((8, 128)) < 4
    blank = jnp.zeros((32, 128), BF16)

    def inputs(row):
        at = (row + 2) * 8
        forced = jnp.where(leading, forcing_x[at : at + 8, :], 1.0)
        forced = jnp.concatenate([forced, jnp.zeros_like(forced)], axis=0).astype(BF16)
        return jnp.concatenate([state[row], forced, blank], axis=0)

    def first(step, _):
        pair = jnp.concatenate([inputs(step), inputs(step + half)], axis=1)
        return jnp.dot(air_in[...], pair, preferred_element_type=F32)

    def middle(step, product):
        return twice_gelu(product).astype(BF16)

    def second(step, hidden):
        return jnp.dot(atm_out[...], hidden, preferred_element_type=F32)

    def last(step, update):
        news = []
        for offset in range(2):
            change = update[:, offset * 128 : (offset + 1) * 128]
            news.append(state[step + offset * half].astype(F32) + 0.5 * change)
        out(step, *news)

    staggered(half, first, middle, second, last)


def spread(edges, places, first, second):
    chosen = [places[row * 128 : (row + 1) * 128, :] for row in (first, second)]
    terms = edges.shape[1] // places.shape[1]
    chosen = jnp.concatenate([jnp.concatenate(chosen, axis=0)] * terms, axis=1)
    return lax.dot_general(
        edges, chosen, (((1,), (1,)), ((), ())), preferred_element_type=F32
    )


def edge_forcing(forcing_x, forcing_y, places, d):
    rows = []
    for step in range(d.rows + 4):
        at = pl.ds(step * 8, 8)
        rows.append(jnp.concatenate([forcing_x[at, :], forcing_y[at, :]], axis=0).astype(BF16))
    whole = jnp.concatenate(rows, axis=1)
    edges = jnp.dot(whole, places[...], preferred_element_type=F32)
    return edges[0:8], edges[8:16]


def roll_rows(state, upper, lower, rolled, d):
    def put(row, values):
        rolled[row, 0:CH, :] = roll(values, 1)
        rolled[row, CH : 2 * CH, :] = values
        rolled[row, 2 * CH : 3 * CH, :] = roll(values, -1)

    for step in range(2):
        put(step, upper[step * CH : (step + 1) * CH, :])
        put(d.rows + 2 + step, lower[step * CH : (step + 1) * CH, :])
    for row in range(d.rows):
        put(row + 2, state[row])


def sea(
    state, rolled, edges, left, right, out, forcing_x, forcing_y, ocn_in, ocn_out, wet,
    at_top, at_bottom, stack, hidden, side, places, d,
):
    rows, block = d.rows, d.block
    lane = lanes((CH, 128))
    spot = lanes((CH, d.edge))
    part = spot // block
    inner = edges
    outer = jnp.where((part == 0) | (part == 2), left, right)

    def sides_of(inner, outer, spot):
        first = spot < block
        return (
            jnp.where(first, outer, roll(inner, -block)),
            jnp.where(first, roll(outer, -2 * block), outer),
            jnp.where(first, roll(inner, -block), roll(outer, -2 * block)),
        )

    beside = sides_of(inner, outer, spot)
    middle = jnp.where((spot >= block) & (spot < 3 * block), roll(beside[1], block), 0)
    entries = []
    for row in range(0, rows + 4, 2):
        pair = spread(middle, places, row, row + 1).astype(BF16)
        entries += [pair[:, :128], pair[:, 128:]]
    force_in, force_out = edge_forcing(forcing_x, forcing_y, places, d)
    beside_forcing = sides_of(force_in, force_out, lanes((8, d.edge)))
    sub = subs((8, d.edge))
    ones = jnp.ones((8, d.edge), F32)
    forced = jnp.concatenate(
        [
            jnp.where(sub < 4, beside_forcing[0], beside_forcing[1]),
            jnp.where(sub < 4, beside_forcing[2], ones),
        ],
        axis=0,
    ).astype(BF16)
    columns = jnp.concatenate(list(beside) + [forced], axis=0)
    for tap in range(3):
        side[tap * 256 : (tap + 1) * 256, :] = roll(columns, -tap)

    sub_row = subs((8, 128))
    lane_row = lanes((8, 128))

    for row in range(rows + 4):
        entry = entries[row]
        stack[row, 0:CH, :] = jnp.where(lane == 0, entry, rolled[row, 0:CH, :])
        stack[row, CH : 2 * CH, :] = rolled[row, CH : 2 * CH, :]
        stack[row, 2 * CH : 3 * CH, :] = jnp.where(lane == 127, entry, rolled[row, 2 * CH : 3 * CH, :])
        here, there = forcing_x[row * 8 : row * 8 + 8, :], forcing_y[row * 8 : row * 8 + 8, :]
        before = roll(jnp.where(lane_row == 127, there, here), 1)
        after = roll(jnp.where(lane_row == 0, there, here), -1)
        stack[row, 3 * CH : 256, :] = jnp.concatenate(
            [jnp.where(sub_row < 4, before, here), jnp.where(sub_row < 4, after, 1.0)], axis=0
        ).astype(BF16)

    pairs = (rows + 2) // 2

    def first(step, _):
        taps = jnp.concatenate(
            [
                stack[step : step + 3].reshape(3 * 256, 128),
                stack[step + pairs : step + pairs + 3].reshape(3 * 256, 128),
            ],
            axis=1,
        )
        return jnp.dot(ocn_in[...], taps, preferred_element_type=F32)

    def activate(step, product):
        active = twice_gelu(product)
        low, high = active[:, :128], active[:, 128:]
        if step == 0:
            low = jnp.where(at_top != 0, 0.0, low)
        if step == pairs - 1:
            high = jnp.where(at_bottom != 0, 0.0, high)
        hidden[step, 0:HIDK, :] = low.astype(BF16)
        hidden[step + pairs, 0:HIDK, :] = high.astype(BF16)
        blank = jnp.zeros((HIDP - HIDK, 128), BF16)
        hidden[step, HIDK:HIDP, :] = blank
        hidden[step + pairs, HIDK:HIDP, :] = blank

    held = {}

    def edge_first():
        held["product"] = jnp.dot(ocn_in[...], side[...], preferred_element_type=F32)

    def edge_activate():
        spot = lanes((1, d.edge)) % block
        gone = ((spot == 0) & (at_top != 0)) | ((spot == rows + 1) & (at_bottom != 0))
        active = jnp.where(gone, 0.0, twice_gelu(held["product"])).astype(BF16)
        active = jnp.concatenate([active, jnp.zeros((HIDP - HIDK, d.edge), BF16)], axis=0)
        held["taps"] = [roll(active, -tap) for tap in range(3)]

    def edge_second():
        held["partial"] = taps_of(held["taps"])

    def edge_spread():
        spot = lanes((CH, d.edge))
        row = spot % block - 2
        inside = (row >= 0) & (row < rows)
        left = (spot >= block) & (spot < 2 * block) & inside
        right = (spot >= 2 * block) & (spot < 3 * block) & inside
        from_left = roll(held["partial"][0:CH], block + 2)
        from_right = roll(held["partial"][2 * CH : 3 * CH], block + 2)
        sums = jnp.where(left, from_left, jnp.where(right, from_right, 0.0))
        high = sums.astype(BF16)
        held["sums"] = jnp.concatenate([high, (sums - high.astype(F32)).astype(BF16)], axis=1)

    def taps_of(slices):
        total = None
        for tap, values in enumerate(slices):
            weights = ocn_out[tap * 3 * CH : (tap + 1) * 3 * CH, :]
            product = jnp.dot(weights, values, preferred_element_type=F32)
            total = product if total is None else total + product
        return total

    wait = lambda: None
    staggered(
        pairs, first, activate,
        between=(edge_first, wait, edge_activate, wait, edge_second, wait, edge_spread),
    )
    half = rows // 2

    def second(step, _):
        product = taps_of(
            [
                jnp.concatenate([hidden[step + tap], hidden[step + half + tap]], axis=1)
                for tap in range(3)
            ]
        )
        return product, spread(held["sums"], places, step + 2, step + half + 2)

    def last(step, products):
        product, entries = products
        news = []
        for offset in range(2):
            row = step + offset * half
            sums = product[:, offset * 128 : (offset + 1) * 128]
            total = sums[CH : 2 * CH] + entries[:, offset * 128 : (offset + 1) * 128]
            total = total + jnp.where(lane == 0, 0.0, roll(sums[0:CH], 1))
            total = total + jnp.where(lane == 127, 0.0, roll(sums[2 * CH : 3 * CH], -1))
            update = total * (0.5 * wet[row : row + 1, :].astype(F32))
            news.append(state[row].astype(F32) + update)
        out(step, *news)

    staggered(half, second, last)


def prepare(atm_in, atm_bias, ocn_in, ocn_bias, ocn_out, air_in, first, second, is_ocean):
    def bias_rows(ref, width):
        row = jnp.concatenate([ref[index : index + 1, :] for index in range(ref.shape[0])], axis=1)
        terms = list(split_bf16(row)) + [jnp.zeros_like(row)]
        bias = jnp.concatenate(terms, axis=0)
        return jnp.pad(bias, ((0, 0), (0, width - bias.shape[1])))

    @pl.when(is_ocean == 0)
    def _():
        columns = jnp.concatenate(
            [atm_in[...].astype(F32), bias_rows(atm_bias, HA), jnp.zeros((40, HA), F32)], axis=0
        )
        air_in[...] = columns.T.astype(BF16)

    @pl.when(is_ocean != 0)
    def _():
        bias = bias_rows(ocn_bias, 256)
        count = ocn_in.shape[2]
        for tap in range(3):
            whole = [ocn_in[3 * tap + side].astype(F32) for side in range(3)]
            whole = [jnp.pad(values, ((0, 0), (0, 256 - count))) for values in whole]
            rows = [values[:CH] for values in whole] + [values[CH:] for values in whole]
            rows.append(bias if tap == 0 else jnp.zeros((4, 256), F32))
            columns = jnp.concatenate(rows, axis=0).T
            first[:, tap * 256 : (tap + 1) * 256] = columns[:HIDK].astype(BF16)
        for tap in range(9):
            values = ocn_out[tap].astype(F32)
            second[tap * CH : (tap + 1) * CH, :] = jnp.pad(
                values, ((0, 0), (0, HIDP - count))
            ).astype(BF16)


def ends(flags):
    at_top, at_bottom, even = flags[1] != 0, flags[2] != 0, flags[3] == 0

    def up_and_down(one, two):
        above = jnp.where(even, two, one).astype(F32)
        below = jnp.where(even, one, two).astype(F32)
        return jnp.where(at_top, 0.0, above), jnp.where(at_bottom, 0.0, below)

    return up_and_down


def middle_kernel(d, opening, *refs):
    refs = list(refs)
    take = lambda count: [refs.pop(0) for _ in range(count)]
    flags, state, field_one, beside, field_two, from_one, from_two = take(7)
    if opening:
        planes, *far_weights = take(6)
    else:
        (plan_x,) = take(1)
    part_x, fields_x, rolled = take(3)
    if opening:
        plan_x, *made_weights = take(4)
    (coupled,) = take(1)
    if opening:
        *raw_weights, sems = take(6)
        copies = fetch(far_weights, raw_weights, sems)
    rows, tall = d.rows, d.tall
    is_ocean = flags[0]
    up_and_down = ends(flags)

    if opening:

        @pl.when(is_ocean != 0)
        def _():
            base = d.strip
            pair = up_and_down(from_one[base : base + 16, :], from_two[base : base + 16, :])
            plan_x[...] = jnp.zeros_like(plan_x)
            for step, strip in zip((0, rows + 2), pair):
                for index in range(2):
                    plan_x[pl.ds(step + index, 2 * NK, stride=tall), :] = strip[index * 8 : (index + 1) * 8]

        for plane in range(2 * NK):
            plan_x[plane * tall + 2 : plane * tall + 2 + rows, :] = planes[plane].astype(F32)

    for field in range(NS):
        pair = up_and_down(field_one[field], field_two[field])
        fields_x[field, 0:16, :] = pair[0][rows - 16 : rows]
        fields_x[field, 16 : 16 + rows, :] = beside[field].astype(F32)
        fields_x[field, 16 + rows : 32 + rows, :] = pair[1][0:16]

    unit = couple(fields_x, coupled, rows)

    @pl.when(is_ocean == 0)
    def _():
        regrid_inside(coupled, unit, plan_x, part_x, 2, rows // 8, tall)

    @pl.when(is_ocean != 0)
    def _():
        regrid_inside(coupled, unit, plan_x, part_x, 0, d.tiles, tall)
        upper, lower = up_and_down(from_one[0 : 2 * CH, :], from_two[0 : 2 * CH, :])
        roll_rows(state, upper.astype(BF16), lower.astype(BF16), rolled, d)

    if opening:
        for copy in copies:
            copy.wait()
        prepare(*raw_weights, *made_weights, is_ocean)


def step_kernel(d, opening, closing, *refs):
    refs = list(refs)
    take = lambda count: [refs.pop(0) for _ in range(count)]
    flags, state, wet, from_left, from_right = take(5)
    part_x, fields_x, rolled, edges, plan_x, air_in, first, second, atm_out = take(9)
    if not opening:
        (plan_e,) = take(1)
    (places,) = take(1)
    if not closing:
        (surface,) = take(1)
    (out,) = take(1)
    if not closing:
        fields, new_edges, one, two = take(4)
    if opening:
        (plan_e,) = take(1)
    window, forcing_x, forcing_y, stack, hidden, side, raw = take(7)
    if opening:
        (plan_y,) = take(1)
    rows, tall = d.rows, d.tall
    is_ocean, at_top, at_bottom = flags[0], flags[1], flags[2]
    up_and_down = ends(flags)

    if opening:

        @pl.when(is_ocean != 0)
        def _():
            plan_y[...] = jnp.zeros_like(plan_y)
            base = d.edge_rows
            parts = [
                (ref[base : base + 16, :], ref[base + 16 + rows : base + 32 + rows, :],
                 ref[base + 16 : base + 16 + rows, :])
                for ref in (from_left, from_right)
            ]
            for plane in range(2 * NK):
                first_end, second_end, own = [
                    unpack_columns(left, right, plane, 2 * NK, 2) for left, right in zip(*parts)
                ]
                above, below = up_and_down(first_end, second_end)
                at = plane * tall
                plan_y[at : at + 2, :] = above[14:16]
                plan_y[at + 2 : at + 2 + rows, :] = own
                plan_y[at + 2 + rows : at + 4 + rows, :] = below[0:2]

    base = d.edge_rows + (rows + 32 if opening else 0)
    parts = [
        (ref[base : base + 16, :], ref[base + 16 + rows : base + 32 + rows, :],
         ref[base + 16 : base + 16 + rows, :])
        for ref in (from_left, from_right)
    ]
    for field in range(NS):
        first_end, second_end, own = [
            unpack_columns(left, right, field, NS, REACH) for left, right in zip(*parts)
        ]
        above, below = up_and_down(first_end, second_end)
        for at, values in ((0, above), (16, own), (16 + rows, below)):
            count = values.shape[0]
            inside = roll(fields_x[field, at : at + count, :], 32)
            lane = lanes(values.shape)
            near = (lane >= 32 - REACH) & (lane < 32 + REACH)
            far = (lane < REACH) | (lane >= 128 - REACH)
            kept = jnp.where(near, inside, jnp.where(far, values, 0.0))
            window[field, at : at + count, :] = kept
    def finished():
        emission = None if closing else Emission(surface, flags, places, raw, d)

        def put(step, low, high):
            if closing:
                for row, values in ((step, low), (step + rows // 2, high)):
                    raw[pl.ds(row, CH, stride=rows), :] = values
                return
            out[step] = low.astype(BF16)
            out[step + rows // 2] = high.astype(BF16)

        def close():
            if not closing:
                emission.close(out, wet, fields, new_edges, one, two)

        return put, close

    @pl.when(is_ocean == 0)
    def _():
        if opening:
            plan_edges(plan_x, plan_y, plan_e, 2, rows // 8, tall, False)
        regrid_beside(
            window, plan_e, part_x, forcing_x, forcing_y, 2, rows // 8, tall, False
        )
        put, close = finished()
        air(state, put, forcing_x, air_in, atm_out, d)
        close()

    @pl.when(is_ocean != 0)
    def _():
        if opening:
            plan_edges(plan_x, plan_y, plan_e, 0, d.tiles, tall, True)
        regrid_beside(
            window, plan_e, part_x, forcing_x, forcing_y, 0, d.tiles, tall, True
        )
        put, close = finished()
        joined = [get_edges(ref, 0, d) for ref in (from_left, from_right)]
        sea(
            state, rolled, get_edges(edges, 0, d), *joined, put, forcing_x, forcing_y,
            first, second, wet, at_top, at_bottom, stack, hidden, side, places, d,
        )
        close()

    if closing:
        out[...] = raw[...].reshape(CH, rows, 128).astype(BF16)


VMEM = pl.BlockSpec(memory_space=pltpu.VMEM)
HBM = pl.BlockSpec(memory_space=pltpu.HBM)
SMEM = pl.BlockSpec(memory_space=pltpu.SMEM)
PARAMS = pltpu.CompilerParams(vmem_limit_bytes=48 * 1024 * 1024)


def shape(*dims, dtype=BF16):
    return jax.ShapeDtypeStruct(dims, dtype)


def send(x, move):
    names = ("grp", "lat", "lon")
    sizes = [lax.axis_size(name) for name in names]
    pairs = []
    for group in range(sizes[0]):
        for lat in range(sizes[1]):
            for lon in range(sizes[2]):
                to = move(group, lat, lon)
                if to is None or not 0 <= to[1] < sizes[1]:
                    continue
                target = (to[0] * sizes[1] + to[1]) * sizes[2] + to[2] % sizes[2]
                pairs.append(((group * sizes[1] + lat) * sizes[2] + lon, target))
    return lax.ppermute(x, names, pairs)


def swap_rows(x, turn, across):
    count, columns = lax.axis_size("lat"), lax.axis_size("lon")

    def move(group, lat, lon):
        other = ((lat + turn) ^ 1) - turn
        if 0 <= other < count and (across or group == 1):
            return (1 - group if across else group), other, lon
        beside = lon ^ 1
        return group, lat, beside if beside < columns else lon

    return send(x, move)


def exchange(fields, own_edges, one, two, sides, d):
    rows = d.rows
    from_one = swap_rows(one, 0, False)
    from_two = swap_rows(two, 1, False)
    field_one = swap_rows(fields, 0, True)
    field_two = swap_rows(fields, 1, True)
    beside = send(fields, lambda g, i, j: (1 - g, i, j))
    lat, count = lax.axis_index("lat"), lax.axis_size("lat")
    odd = lat % 2 == 1
    edges = own_edges
    for turn, ref in ((0, from_one), (1, from_two)):
        other = ((lat + turn) ^ 1) - turn
        there = (other >= 0) & (other < count)
        edges = edges + jnp.where(there, ref[2 * CH : d.strip], 0)
    edges, beside, field_one, field_two = lax.optimization_barrier(
        (edges, beside, field_one, field_two)
    )
    outer = [field_one[NS], field_two[NS]]
    if rows != 16:
        outer = [
            jnp.where(odd, outer[0][rows - 16 :], outer[0][:16]),
            jnp.where(odd, outer[1][:16], outer[1][rows - 16 :]),
        ]
    packed = [edges]
    if sides is not None:
        packed += [from_one[d.strip + 16 :], sides, from_two[d.strip + 16 :]]
    packed += [outer[0], beside[NS], outer[1]]
    packed = jnp.concatenate(packed, axis=0)
    from_left = send(packed, lambda g, i, j: (g, i, j + 1))
    from_right = send(packed, lambda g, i, j: (g, i, j - 1))
    return (field_one, beside, field_two, from_one, from_two), (from_left, from_right), edges


def local(
    coupled_state, land_mask, regrid_offsets, regrid_weights, surface_proj,
    atm_in, atm_bias, atm_out, ocn_in, ocn_bias, ocn_out,
):
    rows = coupled_state.shape[2]
    assert coupled_state.shape[3] == 128
    d = Dims(rows)
    group = lax.axis_index("grp")
    lat = lax.axis_index("lat")
    flags = jnp.stack(
        [group, lat == 0, lat == lax.axis_size("lat") - 1, lat % 2]
    ).astype(jnp.int32)
    raw_weights = (
        atm_in.T,
        atm_bias.reshape(HA // 128, 128),
        jnp.transpose(ocn_in, (1, 2, 0)),
        ocn_bias[None],
        jnp.transpose(ocn_out, (1, 0, 2)),
    )
    state_shape = shape(rows, CH, 128)
    emitted = [
        shape(NS + 1, rows, 128),
        shape(d.edge_rows, 128),
        shape(d.strip, 128),
        shape(d.strip, 128),
    ]
    raw = pltpu.VMEM((rows * 8, 128), F32)
    turned = pltpu.VMEM((CH * rows, 128), F32)

    def call(kernel, operands, outs, scratch, name, far=()):
        scratch = scratch + [pltpu.VMEM(x.shape, x.dtype) for x in far]
        if far:
            scratch.append(pltpu.SemaphoreType.DMA((len(far) + CH // 16,)))

        far = [pltpu.with_memory_space_constraint(x, pltpu.HBM) for x in far]
        return pl.pallas_call(
            kernel,
            out_shape=outs,
            in_specs=[SMEM] + [VMEM] * len(operands) + [HBM] * len(far),
            out_specs=[VMEM] * len(outs),
            scratch_shapes=scratch,
            compiler_params=PARAMS,
            name=name,
        )(flags, *operands, *far)

    state, planes, sides, places, fields, edges, one, two = call(
        functools.partial(start_kernel, d),
        (),
        [state_shape, shape(2 * NK, rows, 128), shape(rows, 128), shape((rows + 4) * 128, d.edge)]
        + emitted[:2]
        + [shape(d.strip + 32, 128)] * 2,
        [raw, pltpu.VMEM((2 * NK * rows, 128), F32), turned],
        "start",
        (coupled_state[0], surface_proj, land_mask, regrid_offsets[0], regrid_weights[0]),
    )

    plan = shape(2 * NK * d.tall, 128, dtype=F32)
    between = [
        shape(NS * d.tall, 128, dtype=F32),
        shape(NS, rows + 32, 128, dtype=F32),
        shape(rows + 4, 3 * CH, 128),
    ]
    made = [shape(HA, 128), shape(HIDK, 768), shape(9 * CH, HIDP)]
    coupled = pltpu.VMEM((NS // 2, rows + 32, 128), jnp.int32)
    scratch = [
        pltpu.VMEM((NS, rows + 32, 128), F32),
        pltpu.VMEM((d.tall * 8, 128), F32),
        pltpu.VMEM((d.tall * 8, 128), F32),
        pltpu.VMEM((rows + 4, 256, 128), BF16),
        pltpu.VMEM((rows + 2, HIDP, 128), BF16),
        pltpu.VMEM((768, d.edge), BF16),
    ]

    vertical, horizontal, edges = exchange(fields, edges, one, two, sides, d)
    *shared, plan_x, air_in, first, second = call(
        functools.partial(middle_kernel, d, True),
        (state, *vertical, planes),
        between + [plan] + made,
        [coupled],
        "first_middle",
        raw_weights,
    )
    weights = (air_in, first, second, atm_out)
    state, fields, edges, one, two, plan_e = call(
        functools.partial(step_kernel, d, True, False),
        (state, land_mask, *horizontal, *shared, edges, plan_x, *weights, places, surface_proj),
        [state_shape] + emitted + [shape(2 * d.tall, 128, dtype=F32)],
        scratch + [raw, pltpu.VMEM(plan.shape, F32)],
        "first_step",
    )

    vertical, horizontal, edges = exchange(fields, edges, one, two, None, d)
    shared = call(
        functools.partial(middle_kernel, d, False),
        (state, *vertical, plan_x),
        between,
        [coupled],
        "second_middle",
    )
    (state,) = call(
        functools.partial(step_kernel, d, False, True),
        (state, land_mask, *horizontal, *shared, edges, plan_x, *weights, plan_e, places),
        [shape(CH, rows, 128)],
        scratch + [turned],
        "second_step",
    )
    return state[None]


def solution(mesh):
    return jax.shard_map(
        local,
        mesh=mesh,
        in_specs=(
            P("grp", None, "lat", "lon"),
            P("lat", "lon"),
            P("grp", None, None, "lat", "lon"),
            P("grp", None, "lat", "lon"),
            P(),
            P(),
            P(),
            P(),
            P(),
            P(),
            P(),
        ),
        out_specs=P("grp", None, "lat", "lon"),
        check_vma=False,
    )
```

```python
import functools

import jax
import jax.numpy as jnp
from jax import lax
from jax.experimental import pallas as pl
from jax.experimental.pallas import tpu as pltpu
from jax.sharding import PartitionSpec as P

CH = 80
NS = 4
NK = 4
HA = 384
HW = 8
SPAN = 2 * HW + 1
REACH = HW + 2
FIXED = 32767.0
HIDK = 208
HIDP = 256
F32 = jnp.float32
BF16 = jnp.bfloat16


def roll(x, shift, axis=1):
    size = x.shape[axis]
    if isinstance(shift, int):
        shift = shift % size
        if shift == 0:
            return x
    return pltpu.roll(x, shift, axis)


def lanes(shape):
    return lax.broadcasted_iota(jnp.int32, shape, len(shape) - 1)


def subs(shape):
    return lax.broadcasted_iota(jnp.int32, shape, len(shape) - 2)


class Dims:
    def __init__(self, rows):
        self.rows = rows
        self.block = 32 if rows + 4 <= 32 else 64
        self.edge = 4 * self.block
        self.pieces = self.edge // 128
        self.edge_rows = CH * self.pieces
        self.tiles = -(-(rows + 4) // 8)
        self.tall = 8 * self.tiles
        self.strip = 2 * CH + self.edge_rows


def put_edges(ref, at, edges, d):
    for piece in range(d.pieces):
        ref[at + piece * CH : at + (piece + 1) * CH, :] = edges[:, piece * 128 : (piece + 1) * 128]


def get_edges(ref, at, d):
    return jnp.concatenate(
        [ref[at + piece * CH : at + (piece + 1) * CH, :] for piece in range(d.pieces)], axis=1
    )


def edge_places(places, d):
    lane = lanes((1, d.edge))
    block = lane // d.block
    row = lane % d.block - 2
    column = jnp.where(block == 0, 126, jnp.where(block == 1, 0, jnp.where(block == 2, 127, 1)))
    own = (row >= 0) & (row < d.rows)
    target = jnp.where(own, column, -1)
    position = subs((128, d.edge))
    for step in range(d.rows):
        place = (position == jnp.where(row == step, target, -1)).astype(F32).astype(BF16)
        places[step * 128 : (step + 1) * 128, :] = place


def edge_columns(state, places, d):
    whole = jnp.concatenate([state[step] for step in range(d.rows)], axis=1)
    return jnp.dot(whole, places[...], preferred_element_type=F32).astype(BF16)


def pack_columns(values, reach):
    lane = lanes(values[0].shape)
    pitch = 128 // len(values)
    packed = jnp.zeros_like(values[0])
    for index, value in enumerate(values):
        at = index * pitch
        packed = jnp.where((lane >= at) & (lane < at + reach), roll(value, at), packed)
        at += reach
        packed = jnp.where((lane >= at) & (lane < at + reach), roll(value, at + reach - 128), packed)
    return packed


def unpack_columns(left, right, index, count, reach):
    at = index * (128 // count)
    left = roll(left.astype(F32), 128 - at - 2 * reach)
    return jnp.where(lanes(left.shape) < 64, roll(right.astype(F32), -at), left)


def strips(one, two, even, d):
    last = d.rows - 2
    return (one, jnp.where(even, last, 0)), (two, jnp.where(even, 0, last))


def split_bf16(values):
    high = values.astype(BF16).astype(F32)
    mid = (values - high).astype(BF16).astype(F32)
    return high, mid, values - high - mid


class Emission:
    def __init__(self, surface, flags, places, raw, d):
        gap = jnp.zeros((4, CH), F32)
        terms = []
        for term in split_bf16(surface[flags[0]]):
            terms += [term, gap]
        self.proj = jnp.concatenate(terms + [gap, gap], axis=0).astype(BF16)
        self.places, self.raw, self.d, self.flags = places, raw, d, flags

    def project(self, state):
        half = self.d.rows // 2
        products = []
        for step in range(half):
            pair = jnp.concatenate([state[step], state[step + half]], axis=1)
            products.append(jnp.dot(self.proj, pair, preferred_element_type=F32))
        whole = jnp.concatenate([state[step] for step in range(2 * half)], axis=1)
        edges = jnp.dot(whole, self.places[...], preferred_element_type=F32)
        for step, parts in enumerate(products):
            parts = parts[0:8] + parts[8:16] + parts[16:24]
            self.raw[step * 8 : step * 8 + 8, :] = parts[:, :128]
            self.raw[(step + half) * 8 : (step + half) * 8 + 8, :] = parts[:, 128:]
        return edges.astype(BF16)

    def close(self, state, wet, fields, own_edges, one, two):
        d, even = self.d, self.flags[3] == 0
        edges = self.project(state)
        keeping = jnp.where(self.flags[0] != 0, wet[...].astype(F32), 1.0)
        whole = [self.raw[pl.ds(field, d.rows, stride=8), :] * keeping for field in range(NS)]
        for field in range(NS):
            fields[field] = whole[field].astype(BF16)
        fields[NS] = pack_columns(whole, REACH).astype(BF16)
        put_edges(own_edges, 0, edges, d)
        row = lanes(edges.shape) % d.block
        downward = jnp.where(row < 2, roll(edges, -d.rows), jnp.zeros_like(edges))
        upward = jnp.where(
            (row >= d.rows + 2) & (row < d.rows + 4), roll(edges, d.rows), jnp.zeros_like(edges)
        )
        for (ref, first), down in zip(strips(one, two, even, d), (even, jnp.logical_not(even))):
            ref[0:CH, :] = state[first]
            ref[CH : 2 * CH, :] = state[first + 1]
            put_edges(ref, 2 * CH, jnp.where(down, downward, upward), d)


def fetch(sources, targets, sems):
    copies = [
        pltpu.make_async_copy(source, target, sems.at[index])
        for index, (source, target) in enumerate(zip(sources, targets))
    ]
    for copy in copies:
        copy.start()
    return copies


def start_kernel(
    d, flags, far_given, far_surface, far_wet, far_offsets, far_weights,
    state, planes, sides, places, fields, own_edges, one, two,
    raw, tall, turned, given, surface, wet, offsets, weights, sems,
):
    rows = d.rows
    pieces = [pl.ds(at, 16) for at in range(0, CH, 16)]
    copies = fetch(
        [far_given.at[piece] for piece in pieces] + [far_surface, far_wet, far_offsets, far_weights],
        [given.at[piece] for piece in pieces] + [surface, wet, offsets, weights],
        sems,
    )
    edge_places(places, d)
    for index, piece in enumerate(pieces):
        copies[index].wait()
        turned[index * 16 * rows : (index + 1) * 16 * rows, :] = (
            given[piece].astype(F32).reshape(16 * rows, 128)
        )
    for row in range(rows):
        state[row] = turned[pl.ds(row, CH, stride=rows), :].astype(BF16)
    for copy in copies[len(pieces) :]:
        copy.wait()
    emission = Emission(surface, flags, places, raw, d)
    emission.close(state, wet, fields, own_edges, one, two)
    for k in range(NK):
        code = (offsets[0, k] * SPAN + offsets[1, k]).astype(F32)
        tall[k * rows : (k + 1) * rows, :] = code
        tall[(NK + k) * rows : (NK + k + 1) * rows, :] = weights[k]
        planes[k] = code.astype(BF16)
        planes[NK + k] = weights[k].astype(BF16)
    packed = pack_columns([tall[plane * rows : (plane + 1) * rows, :] for plane in range(2 * NK)], 2)
    sides[...] = packed.astype(BF16)
    even = flags[3] == 0
    for (ref, first), down in zip(strips(one, two, even, d), (even, jnp.logical_not(even))):
        strip = [tall[pl.ds(first + step, 2 * NK, stride=rows), :] for step in range(2)]
        ref[d.strip : d.strip + 16, :] = jnp.concatenate(strip, axis=0).astype(BF16)
        ref[d.strip + 16 : d.strip + 32, :] = jnp.where(
            down, packed[rows - 16 : rows], packed[0:16]
        ).astype(BF16)


def decode(code):
    shifted = code.astype(jnp.int32) + (HW * SPAN + HW)
    rows = lax.shift_right_logical(shifted * 241, 12)
    return rows - HW, shifted - rows * SPAN - HW


def along_lanes(values, index):
    numbers = lax.GatherDimensionNumbers(
        offset_dims=(),
        collapsed_slice_dims=(1,),
        start_index_map=(1,),
        operand_batching_dims=(0,),
        start_indices_batching_dims=(0,),
    )
    return lax.gather(
        values, index[..., None], numbers, (1, 1), mode=lax.GatherScatterMode.PROMISE_IN_BOUNDS
    )


def couple(fields, coupled, rows):
    largest = None
    for field in range(NS):
        here = jnp.max(jnp.abs(fields[field]), axis=0, keepdims=True)
        largest = here if largest is None else jnp.maximum(largest, here)
    largest = jnp.maximum(jnp.max(largest, axis=1, keepdims=True), 1e-30)
    scale = FIXED / largest
    for pair in range(NS // 2):
        high, low = [
            jnp.floor(fields[2 * pair + part] * scale + 0.5).astype(jnp.int32) for part in range(2)
        ]
        coupled[pair] = high * (1 << 16) + (low + (1 << 15))
    return largest * (1 / FIXED)


def uncouple(values):
    high = lax.shift_right_arithmetic(values, 16)
    low = (values & 0xFFFF) - (1 << 15)
    return high.astype(F32), low.astype(F32)


def select_rows(source, start, picks):
    parts = source.shape[0]
    blank = jnp.full((8, 128), 1 << 15, jnp.int32) if parts < NS else jnp.zeros((8, 128), F32)
    chosen = [[blank for _ in range(parts)] for _ in picks]
    for shift in range(-HW, HW + 1):
        at = pl.ds(start + shift, 8)
        values = [source[part, at, :] for part in range(parts)]
        for slot, (rows, index, allowed) in enumerate(picks):
            here = (rows == shift) & allowed
            for part in range(parts):
                picked = along_lanes(values[part], index)
                chosen[slot][part] = jnp.where(here, picked, chosen[slot][part])
    if parts == NS:
        return chosen
    return [[part for values in pairs for part in uncouple(values)] for pairs in chosen]


def regrid_inside(coupled, unit, plan_x, part_x, first, tiles, tall):
    lane = lanes((8, 128))
    for step in range(tiles):
        at = first + step * 8
        picks = []
        weights = []
        for k in range(NK):
            rows, cols = decode(plan_x[pl.ds(k * tall + at, 8), :])
            weights.append(plan_x[pl.ds((NK + k) * tall + at, 8), :] * unit)
            column = lane + cols
            picks.append((rows, column & 127, (column >= 0) & (column < 128)))
        chosen = select_rows(coupled, at + 14, picks)
        for field in range(NS):
            total = chosen[0][field] * weights[0]
            for k in range(1, NK):
                total = total + chosen[k][field] * weights[k]
            part_x[pl.ds(field * tall + at, 8), :] = total


def edge_lanes():
    lane = lanes((8, 128))
    return ((lane + 8) & 127) // 32, ((lane + 8) & 31) - 8


def plan_edges(plan_x, plan_y, plan_e, first, tiles, tall, sides):
    part, place = edge_lanes()
    outer = place >= 8
    for step in range(tiles):
        at = first + step * 8
        code = jnp.zeros((8, 128), F32)
        weight = jnp.zeros((8, 128), F32)
        for k in range(NK):
            edge_code = roll(plan_x[pl.ds(k * tall + at, 8), :], 32 * k)
            edge_weight = roll(plan_x[pl.ds((NK + k) * tall + at, 8), :], 32 * k)
            if sides:
                edge_code = jnp.where(
                    outer, roll(plan_y[pl.ds(k * tall + at, 8), :], 32 * k + 16), edge_code
                )
                edge_weight = jnp.where(
                    outer, roll(plan_y[pl.ds((NK + k) * tall + at, 8), :], 32 * k + 16), edge_weight
                )
            code = jnp.where(part == k, edge_code, code)
            weight = jnp.where(part == k, edge_weight, weight)
        plan_e[pl.ds(at, 8), :] = code
        plan_e[pl.ds(tall + at, 8), :] = weight


def regrid_beside(window, plan_e, part_x, forcing_x, forcing_y, first, tiles, tall, sides):
    lane = lanes((8, 128))
    part, place = edge_lanes()
    outer = place >= 8
    inner_column = place & 127
    outer_column = jnp.where(place < 16, place - 16, place + 112)
    edge = (lane < 8) | (lane >= 120)
    for step in range(tiles):
        at = first + step * 8
        rows, cols = decode(plan_e[pl.ds(at, 8), :])
        weight = plan_e[pl.ds(tall + at, 8), :]
        column = jnp.where(outer, outer_column, inner_column) + cols
        within = (column >= 0) & (column < 128)
        index = jnp.where(within, column + 32, column) & 127
        (chosen,) = select_rows(window, at + 14, [(rows, index, outer | jnp.logical_not(within))])
        for field in range(NS):
            part_sum = chosen[field] * weight
            extra = part_sum
            for k in range(1, NK):
                extra = extra + roll(part_sum, -32 * k)
            total = part_x[pl.ds(field * tall + at, 8), :] + jnp.where(edge, extra, 0.0)
            forcing_x[pl.ds(at * 8 + field, 8, stride=8), :] = total
            forcing_x[pl.ds(at * 8 + field + 4, 8, stride=8), :] = total
            if sides:
                extra = roll(extra, -16)
                forcing_y[pl.ds(at * 8 + field, 8, stride=8), :] = extra
                forcing_y[pl.ds(at * 8 + field + 4, 8, stride=8), :] = extra


def twice_gelu(x):
    scale = (2 / jnp.pi) ** 0.5
    return x + x * jnp.tanh(x * (scale + (scale * 0.044715) * (x * x)))


def staggered(count, *stages):
    values = [{} for _ in stages]
    for turn in range(count + len(stages) - 1):
        for index, stage in enumerate(stages):
            step = turn - index
            if 0 <= step < count:
                given = values[index - 1].pop(step) if index else None
                values[index][step] = stage(step, given)


def air(state, out, forcing_x, air_in, atm_out, d):
    half = d.rows // 2
    leading = subs((8, 128)) < 4
    blank = jnp.zeros((32, 128), BF16)

    def inputs(row):
        at = (row + 2) * 8
        forced = jnp.where(leading, forcing_x[at : at + 8, :], 1.0)
        forced = jnp.concatenate([forced, jnp.zeros_like(forced)], axis=0).astype(BF16)
        return jnp.concatenate([state[row], forced, blank], axis=0)

    def first(step, _):
        pair = jnp.concatenate([inputs(step), inputs(step + half)], axis=1)
        return jnp.dot(air_in[...], pair, preferred_element_type=F32)

    def middle(step, product):
        return twice_gelu(product).astype(BF16)

    def second(step, hidden):
        return jnp.dot(atm_out[...], hidden, preferred_element_type=F32)

    def last(step, update):
        news = []
        for offset in range(2):
            change = update[:, offset * 128 : (offset + 1) * 128]
            news.append(state[step + offset * half].astype(F32) + 0.5 * change)
        out(step, *news)

    staggered(half, first, middle, second, last)


def edge_forcing(forcing_x, forcing_y, d):
    lane = lanes((8, d.edge))
    block = lane // d.block
    row = lane % d.block

    inner = outer = jnp.zeros((8, d.edge), F32)
    for step in range(d.rows + 4):
        at = pl.ds(step * 8, 8)
        pad = [jnp.zeros((8, 128), F32)] * (d.pieces - 1)
        here = jnp.concatenate([forcing_x[at, :]] + pad, axis=1)
        there = jnp.concatenate([forcing_y[at, :]] + pad, axis=1)
        for index, column in enumerate((126, 0, 127, 1)):
            shift = step + index * d.block - column
            match = (block == index) & (row == step)
            if column in (0, 127):
                inner = jnp.where(match, roll(here, shift), inner)
            outer = jnp.where(match, roll(there, shift), outer)
    return inner, outer


def roll_rows(state, upper, lower, rolled, d):
    def put(row, values):
        rolled[row, 0:CH, :] = roll(values, 1)
        rolled[row, CH : 2 * CH, :] = values
        rolled[row, 2 * CH : 3 * CH, :] = roll(values, -1)

    for step in range(2):
        put(step, upper[step * CH : (step + 1) * CH, :])
        put(d.rows + 2 + step, lower[step * CH : (step + 1) * CH, :])
    for row in range(d.rows):
        put(row + 2, state[row])


def sea(
    state, rolled, edges, left, right, out, forcing_x, forcing_y, ocn_in, ocn_out, wet,
    at_top, at_bottom, stack, hidden, side, d,
):
    rows, block = d.rows, d.block
    lane = lanes((CH, 128))
    spot = lanes((CH, d.edge))
    part = spot // block
    inner = edges
    outer = jnp.where((part == 0) | (part == 2), left, right)

    def sides_of(inner, outer, spot):
        first = spot < block
        return (
            jnp.where(first, outer, roll(inner, -block)),
            jnp.where(first, roll(outer, -2 * block), outer),
            jnp.where(first, roll(inner, -block), roll(outer, -2 * block)),
        )

    beside = sides_of(inner, outer, spot)
    middle = beside[1]
    force_in, force_out = edge_forcing(forcing_x, forcing_y, d)
    beside_forcing = sides_of(force_in, force_out, lanes((8, d.edge)))
    sub = subs((8, d.edge))
    ones = jnp.ones((8, d.edge), F32)
    forced = jnp.concatenate(
        [
            jnp.where(sub < 4, beside_forcing[0], beside_forcing[1]),
            jnp.where(sub < 4, beside_forcing[2], ones),
        ],
        axis=0,
    ).astype(BF16)
    columns = jnp.concatenate(list(beside) + [forced], axis=0)
    for tap in range(3):
        side[tap * 256 : (tap + 1) * 256, :] = roll(columns, -tap)

    sub_row = subs((8, 128))
    lane_row = lanes((8, 128))

    for row in range(rows + 4):
        entry = roll(middle, -row)[:, :128]
        stack[row, 0:CH, :] = jnp.where(lane == 0, entry, rolled[row, 0:CH, :])
        stack[row, CH : 2 * CH, :] = rolled[row, CH : 2 * CH, :]
        entry = roll(middle, 127 - block - row)[:, :128]
        stack[row, 2 * CH : 3 * CH, :] = jnp.where(lane == 127, entry, rolled[row, 2 * CH : 3 * CH, :])
        here, there = forcing_x[row * 8 : row * 8 + 8, :], forcing_y[row * 8 : row * 8 + 8, :]
        before = roll(jnp.where(lane_row == 127, there, here), 1)
        after = roll(jnp.where(lane_row == 0, there, here), -1)
        stack[row, 3 * CH : 256, :] = jnp.concatenate(
            [jnp.where(sub_row < 4, before, here), jnp.where(sub_row < 4, after, 1.0)], axis=0
        ).astype(BF16)

    pairs = (rows + 2) // 2

    def first(step, _):
        taps = jnp.concatenate(
            [
                stack[step : step + 3].reshape(3 * 256, 128),
                stack[step + pairs : step + pairs + 3].reshape(3 * 256, 128),
            ],
            axis=1,
        )
        return jnp.dot(ocn_in[...], taps, preferred_element_type=F32)

    def activate(step, product):
        active = twice_gelu(product)
        low, high = active[:, :128], active[:, 128:]
        if step == 0:
            low = jnp.where(at_top != 0, 0.0, low)
        if step == pairs - 1:
            high = jnp.where(at_bottom != 0, 0.0, high)
        hidden[step, 0:HIDK, :] = low.astype(BF16)
        hidden[step + pairs, 0:HIDK, :] = high.astype(BF16)
        blank = jnp.zeros((HIDP - HIDK, 128), BF16)
        hidden[step, HIDK:HIDP, :] = blank
        hidden[step + pairs, HIDK:HIDP, :] = blank

    staggered(pairs, first, activate)
    product = jnp.dot(ocn_in[...], side[...], preferred_element_type=F32)
    spot = lanes((1, d.edge)) % block
    gone = ((spot == 0) & (at_top != 0)) | ((spot == rows + 1) & (at_bottom != 0))
    active = jnp.where(gone, 0.0, twice_gelu(product)).astype(BF16)
    active = jnp.concatenate([active, jnp.zeros((HIDP - HIDK, d.edge), BF16)], axis=0)

    def taps_of(slices):
        total = None
        for tap, values in enumerate(slices):
            weights = ocn_out[tap * 3 * CH : (tap + 1) * 3 * CH, :]
            product = jnp.dot(weights, values, preferred_element_type=F32)
            total = product if total is None else total + product
        return total

    partial = taps_of([roll(active, -tap) for tap in range(3)])
    from_left, from_right = partial[0:CH], partial[2 * CH : 3 * CH]
    half = rows // 2

    def second(step, _):
        return taps_of(
            [
                jnp.concatenate([hidden[step + tap], hidden[step + half + tap]], axis=1)
                for tap in range(3)
            ]
        )

    def last(step, product):
        news = []
        for offset in range(2):
            row = step + offset * half
            sums = product[:, offset * 128 : (offset + 1) * 128]
            entry = roll(from_left, -row)[:, :128]
            total = sums[CH : 2 * CH] + jnp.where(lane == 0, entry, roll(sums[0:CH], 1))
            entry = roll(from_right, 127 - block - row)[:, :128]
            total = total + jnp.where(lane == 127, entry, roll(sums[2 * CH : 3 * CH], -1))
            update = total * (0.5 * wet[row : row + 1, :].astype(F32))
            news.append(state[row].astype(F32) + update)
        out(step, *news)

    staggered(half, second, last)


def prepare(atm_in, atm_bias, ocn_in, ocn_bias, ocn_out, air_in, first, second, is_ocean):
    def bias_rows(ref, width):
        row = jnp.concatenate([ref[index : index + 1, :] for index in range(ref.shape[0])], axis=1)
        terms = list(split_bf16(row)) + [jnp.zeros_like(row)]
        bias = jnp.concatenate(terms, axis=0)
        return jnp.pad(bias, ((0, 0), (0, width - bias.shape[1])))

    @pl.when(is_ocean == 0)
    def _():
        columns = jnp.concatenate(
            [atm_in[...].astype(F32), bias_rows(atm_bias, HA), jnp.zeros((40, HA), F32)], axis=0
        )
        air_in[...] = columns.T.astype(BF16)

    @pl.when(is_ocean != 0)
    def _():
        bias = bias_rows(ocn_bias, 256)
        count = ocn_in.shape[2]
        for tap in range(3):
            whole = [ocn_in[3 * tap + side].astype(F32) for side in range(3)]
            whole = [jnp.pad(values, ((0, 0), (0, 256 - count))) for values in whole]
            rows = [values[:CH] for values in whole] + [values[CH:] for values in whole]
            rows.append(bias if tap == 0 else jnp.zeros((4, 256), F32))
            columns = jnp.concatenate(rows, axis=0).T
            first[:, tap * 256 : (tap + 1) * 256] = columns[:HIDK].astype(BF16)
        for tap in range(9):
            values = ocn_out[tap].astype(F32)
            second[tap * CH : (tap + 1) * CH, :] = jnp.pad(
                values, ((0, 0), (0, HIDP - count))
            ).astype(BF16)


def ends(flags):
    at_top, at_bottom, even = flags[1] != 0, flags[2] != 0, flags[3] == 0

    def up_and_down(one, two):
        above = jnp.where(even, two, one).astype(F32)
        below = jnp.where(even, one, two).astype(F32)
        return jnp.where(at_top, 0.0, above), jnp.where(at_bottom, 0.0, below)

    return up_and_down


def middle_kernel(d, opening, *refs):
    refs = list(refs)
    take = lambda count: [refs.pop(0) for _ in range(count)]
    flags, state, field_one, beside, field_two, from_one, from_two = take(7)
    if opening:
        planes, *far_weights = take(6)
    else:
        (plan_x,) = take(1)
    part_x, fields_x, rolled = take(3)
    if opening:
        plan_x, *made_weights = take(4)
    (coupled,) = take(1)
    if opening:
        *raw_weights, sems = take(6)
        copies = fetch(far_weights, raw_weights, sems)
    rows, tall = d.rows, d.tall
    is_ocean = flags[0]
    up_and_down = ends(flags)

    if opening:

        @pl.when(is_ocean != 0)
        def _():
            base = d.strip
            pair = up_and_down(from_one[base : base + 16, :], from_two[base : base + 16, :])
            plan_x[...] = jnp.zeros_like(plan_x)
            for step, strip in zip((0, rows + 2), pair):
                for index in range(2):
                    plan_x[pl.ds(step + index, 2 * NK, stride=tall), :] = strip[index * 8 : (index + 1) * 8]

        for plane in range(2 * NK):
            plan_x[plane * tall + 2 : plane * tall + 2 + rows, :] = planes[plane].astype(F32)

    for field in range(NS):
        pair = up_and_down(field_one[field], field_two[field])
        fields_x[field, 0:16, :] = pair[0][rows - 16 : rows]
        fields_x[field, 16 : 16 + rows, :] = beside[field].astype(F32)
        fields_x[field, 16 + rows : 32 + rows, :] = pair[1][0:16]

    unit = couple(fields_x, coupled, rows)

    @pl.when(is_ocean == 0)
    def _():
        regrid_inside(coupled, unit, plan_x, part_x, 2, rows // 8, tall)

    @pl.when(is_ocean != 0)
    def _():
        regrid_inside(coupled, unit, plan_x, part_x, 0, d.tiles, tall)
        upper, lower = up_and_down(from_one[0 : 2 * CH, :], from_two[0 : 2 * CH, :])
        roll_rows(state, upper.astype(BF16), lower.astype(BF16), rolled, d)

    if opening:
        for copy in copies:
            copy.wait()
        prepare(*raw_weights, *made_weights, is_ocean)


def step_kernel(d, opening, closing, *refs):
    refs = list(refs)
    take = lambda count: [refs.pop(0) for _ in range(count)]
    flags, state, wet, from_left, from_right = take(5)
    part_x, fields_x, rolled, edges, plan_x, air_in, first, second, atm_out = take(9)
    if not opening:
        (plan_e,) = take(1)
    if not closing:
        surface, places = take(2)
    (out,) = take(1)
    if not closing:
        fields, new_edges, one, two = take(4)
    if opening:
        (plan_e,) = take(1)
    window, forcing_x, forcing_y, stack, hidden, side, raw = take(7)
    if opening:
        (plan_y,) = take(1)
    rows, tall = d.rows, d.tall
    is_ocean, at_top, at_bottom = flags[0], flags[1], flags[2]
    up_and_down = ends(flags)

    if opening:

        @pl.when(is_ocean != 0)
        def _():
            plan_y[...] = jnp.zeros_like(plan_y)
            base = d.edge_rows
            parts = [
                (ref[base : base + 16, :], ref[base + 16 + rows : base + 32 + rows, :],
                 ref[base + 16 : base + 16 + rows, :])
                for ref in (from_left, from_right)
            ]
            for plane in range(2 * NK):
                first_end, second_end, own = [
                    unpack_columns(left, right, plane, 2 * NK, 2) for left, right in zip(*parts)
                ]
                above, below = up_and_down(first_end, second_end)
                at = plane * tall
                plan_y[at : at + 2, :] = above[14:16]
                plan_y[at + 2 : at + 2 + rows, :] = own
                plan_y[at + 2 + rows : at + 4 + rows, :] = below[0:2]

    base = d.edge_rows + (rows + 32 if opening else 0)
    parts = [
        (ref[base : base + 16, :], ref[base + 16 + rows : base + 32 + rows, :],
         ref[base + 16 : base + 16 + rows, :])
        for ref in (from_left, from_right)
    ]
    for field in range(NS):
        first_end, second_end, own = [
            unpack_columns(left, right, field, NS, REACH) for left, right in zip(*parts)
        ]
        above, below = up_and_down(first_end, second_end)
        for at, values in ((0, above), (16, own), (16 + rows, below)):
            count = values.shape[0]
            inside = roll(fields_x[field, at : at + count, :], 32)
            lane = lanes(values.shape)
            near = (lane >= 32 - REACH) & (lane < 32 + REACH)
            far = (lane < REACH) | (lane >= 128 - REACH)
            kept = jnp.where(near, inside, jnp.where(far, values, 0.0))
            window[field, at : at + count, :] = kept
    def finished():
        emission = None if closing else Emission(surface, flags, places, raw, d)

        def put(step, low, high):
            if closing:
                for row, values in ((step, low), (step + rows // 2, high)):
                    raw[pl.ds(row, CH, stride=rows), :] = values
                return
            out[step] = low.astype(BF16)
            out[step + rows // 2] = high.astype(BF16)

        def close():
            if not closing:
                emission.close(out, wet, fields, new_edges, one, two)

        return put, close

    @pl.when(is_ocean == 0)
    def _():
        if opening:
            plan_edges(plan_x, plan_y, plan_e, 2, rows // 8, tall, False)
        regrid_beside(
            window, plan_e, part_x, forcing_x, forcing_y, 2, rows // 8, tall, False
        )
        put, close = finished()
        air(state, put, forcing_x, air_in, atm_out, d)
        close()

    @pl.when(is_ocean != 0)
    def _():
        if opening:
            plan_edges(plan_x, plan_y, plan_e, 0, d.tiles, tall, True)
        regrid_beside(
            window, plan_e, part_x, forcing_x, forcing_y, 0, d.tiles, tall, True
        )
        put, close = finished()
        joined = [get_edges(ref, 0, d) for ref in (from_left, from_right)]
        sea(
            state, rolled, get_edges(edges, 0, d), *joined, put, forcing_x, forcing_y,
            first, second, wet, at_top, at_bottom, stack, hidden, side, d,
        )
        close()

    if closing:
        out[...] = raw[...].reshape(CH, rows, 128).astype(BF16)


VMEM = pl.BlockSpec(memory_space=pltpu.VMEM)
HBM = pl.BlockSpec(memory_space=pltpu.HBM)
SMEM = pl.BlockSpec(memory_space=pltpu.SMEM)
PARAMS = pltpu.CompilerParams(vmem_limit_bytes=48 * 1024 * 1024)


def shape(*dims, dtype=BF16):
    return jax.ShapeDtypeStruct(dims, dtype)


def send(x, move):
    names = ("grp", "lat", "lon")
    sizes = [lax.axis_size(name) for name in names]
    pairs = []
    for group in range(sizes[0]):
        for lat in range(sizes[1]):
            for lon in range(sizes[2]):
                to = move(group, lat, lon)
                if to is None or not 0 <= to[1] < sizes[1]:
                    continue
                target = (to[0] * sizes[1] + to[1]) * sizes[2] + to[2] % sizes[2]
                pairs.append(((group * sizes[1] + lat) * sizes[2] + lon, target))
    return lax.ppermute(x, names, pairs)


def swap_rows(x, turn, across):
    count, columns = lax.axis_size("lat"), lax.axis_size("lon")

    def move(group, lat, lon):
        other = ((lat + turn) ^ 1) - turn
        if 0 <= other < count and (across or group == 1):
            return (1 - group if across else group), other, lon
        beside = lon ^ 1
        return group, lat, beside if beside < columns else lon

    return send(x, move)


def exchange(fields, own_edges, one, two, sides, d):
    rows = d.rows
    scale = jnp.where(lax.axis_index("grp") > 1, 0, 1).astype(BF16)
    from_one = swap_rows(one, 0, False)
    field_one = swap_rows(fields, 0, True)
    from_two = swap_rows(two * scale, 1, False)
    fields = fields * scale
    field_two = swap_rows(fields, 1, True)
    beside = send(fields, lambda g, i, j: (1 - g, i, j))
    field_one, from_one = lax.optimization_barrier((field_one, from_one))
    from_two, field_one = lax.optimization_barrier((from_two, field_one))
    field_two, from_two = lax.optimization_barrier((field_two, from_two))
    beside, field_two = lax.optimization_barrier((beside, field_two))
    lat, count = lax.axis_index("lat"), lax.axis_size("lat")
    odd = lat % 2 == 1
    edges = own_edges
    for turn, ref in ((0, from_one), (1, from_two)):
        other = ((lat + turn) ^ 1) - turn
        there = (other >= 0) & (other < count)
        edges = edges + jnp.where(there, ref[2 * CH : d.strip], 0)
    outer = [field_one[NS], field_two[NS]]
    if rows != 16:
        outer = [
            jnp.where(odd, outer[0][rows - 16 :], outer[0][:16]),
            jnp.where(odd, outer[1][:16], outer[1][rows - 16 :]),
        ]
    packed = [edges]
    if sides is not None:
        packed += [from_one[d.strip + 16 :], sides, from_two[d.strip + 16 :]]
    packed += [outer[0], beside[NS], outer[1]]
    packed = jnp.concatenate(packed, axis=0)
    from_left = send(packed, lambda g, i, j: (g, i, j + 1))
    from_right = send(packed, lambda g, i, j: (g, i, j - 1))
    return (field_one, beside, field_two, from_one, from_two), (from_left, from_right), edges


def local(
    coupled_state, land_mask, regrid_offsets, regrid_weights, surface_proj,
    atm_in, atm_bias, atm_out, ocn_in, ocn_bias, ocn_out,
):
    rows = coupled_state.shape[2]
    assert coupled_state.shape[3] == 128
    d = Dims(rows)
    group = lax.axis_index("grp")
    lat = lax.axis_index("lat")
    flags = jnp.stack(
        [group, lat == 0, lat == lax.axis_size("lat") - 1, lat % 2]
    ).astype(jnp.int32)
    raw_weights = (
        atm_in.T,
        atm_bias.reshape(HA // 128, 128),
        jnp.transpose(ocn_in, (1, 2, 0)),
        ocn_bias[None],
        jnp.transpose(ocn_out, (1, 0, 2)),
    )
    state_shape = shape(rows, CH, 128)
    emitted = [
        shape(NS + 1, rows, 128),
        shape(d.edge_rows, 128),
        shape(d.strip, 128),
        shape(d.strip, 128),
    ]
    raw = pltpu.VMEM((rows * 8, 128), F32)
    turned = pltpu.VMEM((CH * rows, 128), F32)

    def call(kernel, operands, outs, scratch, name, far=()):
        scratch = scratch + [pltpu.VMEM(x.shape, x.dtype) for x in far]
        if far:
            scratch.append(pltpu.SemaphoreType.DMA((len(far) + CH // 16,)))

        far = [pltpu.with_memory_space_constraint(x, pltpu.HBM) for x in far]
        return pl.pallas_call(
            kernel,
            out_shape=outs,
            in_specs=[SMEM] + [VMEM] * len(operands) + [HBM] * len(far),
            out_specs=[VMEM] * len(outs),
            scratch_shapes=scratch,
            compiler_params=PARAMS,
            name=name,
        )(flags, *operands, *far)

    state, planes, sides, places, fields, edges, one, two = call(
        functools.partial(start_kernel, d),
        (),
        [state_shape, shape(2 * NK, rows, 128), shape(rows, 128), shape(rows * 128, d.edge)]
        + emitted[:2]
        + [shape(d.strip + 32, 128)] * 2,
        [raw, pltpu.VMEM((2 * NK * rows, 128), F32), turned],
        "start",
        (coupled_state[0], surface_proj, land_mask, regrid_offsets[0], regrid_weights[0]),
    )

    plan = shape(2 * NK * d.tall, 128, dtype=F32)
    between = [
        shape(NS * d.tall, 128, dtype=F32),
        shape(NS, rows + 32, 128, dtype=F32),
        shape(rows + 4, 3 * CH, 128),
    ]
    made = [shape(HA, 128), shape(HIDK, 768), shape(9 * CH, HIDP)]
    coupled = pltpu.VMEM((NS // 2, rows + 32, 128), jnp.int32)
    scratch = [
        pltpu.VMEM((NS, rows + 32, 128), F32),
        pltpu.VMEM((d.tall * 8, 128), F32),
        pltpu.VMEM((d.tall * 8, 128), F32),
        pltpu.VMEM((rows + 4, 256, 128), BF16),
        pltpu.VMEM((rows + 2, HIDP, 128), BF16),
        pltpu.VMEM((768, d.edge), BF16),
    ]

    vertical, horizontal, edges = exchange(fields, edges, one, two, sides, d)
    *shared, plan_x, air_in, first, second = call(
        functools.partial(middle_kernel, d, True),
        (state, *vertical, planes),
        between + [plan] + made,
        [coupled],
        "first_middle",
        raw_weights,
    )
    weights = (air_in, first, second, atm_out)
    state, fields, edges, one, two, plan_e = call(
        functools.partial(step_kernel, d, True, False),
        (state, land_mask, *horizontal, *shared, edges, plan_x, *weights, surface_proj, places),
        [state_shape] + emitted + [shape(2 * d.tall, 128, dtype=F32)],
        scratch + [raw, pltpu.VMEM(plan.shape, F32)],
        "first_step",
    )

    vertical, horizontal, edges = exchange(fields, edges, one, two, None, d)
    shared = call(
        functools.partial(middle_kernel, d, False),
        (state, *vertical, plan_x),
        between,
        [coupled],
        "second_middle",
    )
    (state,) = call(
        functools.partial(step_kernel, d, False, True),
        (state, land_mask, *horizontal, *shared, edges, plan_x, *weights, plan_e),
        [shape(CH, rows, 128)],
        scratch + [turned],
        "second_step",
    )
    return state[None]


def solution(mesh):
    return jax.shard_map(
        local,
        mesh=mesh,
        in_specs=(
            P("grp", None, "lat", "lon"),
            P("lat", "lon"),
            P("grp", None, None, "lat", "lon"),
            P("grp", None, "lat", "lon"),
            P(),
            P(),
            P(),
            P(),
            P(),
            P(),
            P(),
        ),
        out_specs=P("grp", None, "lat", "lon"),
        check_vma=False,
    )
```

```python
import functools

import jax
import jax.numpy as jnp
from jax import lax
from jax.experimental import pallas as pl
from jax.experimental.pallas import tpu as pltpu
from jax.sharding import PartitionSpec as P

CH = 80
NS = 4
NK = 4
HA = 384
HW = 8
SPAN = 2 * HW + 1
REACH = HW + 2
FIXED = 32767.0
HIDK = 208
HIDP = 256
F32 = jnp.float32
BF16 = jnp.bfloat16


def roll(x, shift, axis=1):
    size = x.shape[axis]
    if isinstance(shift, int):
        shift = shift % size
        if shift == 0:
            return x
    return pltpu.roll(x, shift, axis)


def lanes(shape):
    return lax.broadcasted_iota(jnp.int32, shape, len(shape) - 1)


def subs(shape):
    return lax.broadcasted_iota(jnp.int32, shape, len(shape) - 2)


class Dims:
    def __init__(self, rows):
        self.rows = rows
        self.block = 32 if rows + 4 <= 32 else 64
        self.edge = 4 * self.block
        self.pieces = self.edge // 128
        self.edge_rows = CH * self.pieces
        self.tiles = -(-(rows + 4) // 8)
        self.tall = 8 * self.tiles
        self.strip = 2 * CH + self.edge_rows


def put_edges(ref, at, edges, d):
    for piece in range(d.pieces):
        ref[at + piece * CH : at + (piece + 1) * CH, :] = edges[:, piece * 128 : (piece + 1) * 128]


def get_edges(ref, at, d):
    return jnp.concatenate(
        [ref[at + piece * CH : at + (piece + 1) * CH, :] for piece in range(d.pieces)], axis=1
    )


def edge_places(places, d):
    lane = lanes((1, d.edge))
    block = lane // d.block
    row = lane % d.block - 2
    column = jnp.where(block == 0, 126, jnp.where(block == 1, 0, jnp.where(block == 2, 127, 1)))
    own = (row >= 0) & (row < d.rows)
    target = jnp.where(own, column, -1)
    position = subs((128, d.edge))
    for step in range(d.rows):
        place = (position == jnp.where(row == step, target, -1)).astype(F32).astype(BF16)
        places[step * 128 : (step + 1) * 128, :] = place


def edge_columns(state, places, d):
    whole = jnp.concatenate([state[step] for step in range(d.rows)], axis=1)
    return jnp.dot(whole, places[...], preferred_element_type=F32).astype(BF16)


def pack_columns(values, reach):
    lane = lanes(values[0].shape)
    pitch = 128 // len(values)
    packed = jnp.zeros_like(values[0])
    for index, value in enumerate(values):
        at = index * pitch
        packed = jnp.where((lane >= at) & (lane < at + reach), roll(value, at), packed)
        at += reach
        packed = jnp.where((lane >= at) & (lane < at + reach), roll(value, at + reach - 128), packed)
    return packed


def unpack_columns(left, right, index, count, reach):
    at = index * (128 // count)
    left = roll(left.astype(F32), 128 - at - 2 * reach)
    return jnp.where(lanes(left.shape) < 64, roll(right.astype(F32), -at), left)


def strips(one, two, even, d):
    last = d.rows - 2
    return (one, jnp.where(even, last, 0)), (two, jnp.where(even, 0, last))


def split_bf16(values):
    high = values.astype(BF16).astype(F32)
    mid = (values - high).astype(BF16).astype(F32)
    return high, mid, values - high - mid


class Emission:
    def __init__(self, surface, flags, places, raw, d):
        gap = jnp.zeros((4, CH), F32)
        terms = []
        for term in split_bf16(surface[flags[0]]):
            terms += [term, gap]
        self.proj = jnp.concatenate(terms + [gap, gap], axis=0).astype(BF16)
        self.places, self.raw, self.d, self.flags = places, raw, d, flags

    def project(self, state):
        half = self.d.rows // 2
        products = []
        for step in range(half):
            pair = jnp.concatenate([state[step], state[step + half]], axis=1)
            products.append(jnp.dot(self.proj, pair, preferred_element_type=F32))
        whole = jnp.concatenate([state[step] for step in range(2 * half)], axis=1)
        edges = jnp.dot(whole, self.places[...], preferred_element_type=F32)
        for step, parts in enumerate(products):
            parts = parts[0:8] + parts[8:16] + parts[16:24]
            self.raw[step * 8 : step * 8 + 8, :] = parts[:, :128]
            self.raw[(step + half) * 8 : (step + half) * 8 + 8, :] = parts[:, 128:]
        return edges.astype(BF16)

    def close(self, state, wet, fields, own_edges, one, two):
        d, even = self.d, self.flags[3] == 0
        edges = self.project(state)
        keeping = jnp.where(self.flags[0] != 0, wet[...].astype(F32), 1.0)
        whole = [self.raw[pl.ds(field, d.rows, stride=8), :] * keeping for field in range(NS)]
        for field in range(NS):
            fields[field] = whole[field].astype(BF16)
        fields[NS] = pack_columns(whole, REACH).astype(BF16)
        put_edges(own_edges, 0, edges, d)
        row = lanes(edges.shape) % d.block
        downward = jnp.where(row < 2, roll(edges, -d.rows), jnp.zeros_like(edges))
        upward = jnp.where(
            (row >= d.rows + 2) & (row < d.rows + 4), roll(edges, d.rows), jnp.zeros_like(edges)
        )
        for (ref, first), down in zip(strips(one, two, even, d), (even, jnp.logical_not(even))):
            ref[0:CH, :] = state[first]
            ref[CH : 2 * CH, :] = state[first + 1]
            put_edges(ref, 2 * CH, jnp.where(down, downward, upward), d)


def fetch(sources, targets, sems):
    copies = [
        pltpu.make_async_copy(source, target, sems.at[index])
        for index, (source, target) in enumerate(zip(sources, targets))
    ]
    for copy in copies:
        copy.start()
    return copies


def start_kernel(
    d, flags, far_given, far_surface, far_wet, far_offsets, far_weights,
    state, planes, sides, places, fields, own_edges, one, two,
    raw, tall, turned, given, surface, wet, offsets, weights, sems,
):
    rows = d.rows
    pieces = [pl.ds(at, 16) for at in range(0, CH, 16)]
    copies = fetch(
        [far_given.at[piece] for piece in pieces] + [far_surface, far_wet, far_offsets, far_weights],
        [given.at[piece] for piece in pieces] + [surface, wet, offsets, weights],
        sems,
    )
    edge_places(places, d)
    for index, piece in enumerate(pieces):
        copies[index].wait()
        turned[index * 16 * rows : (index + 1) * 16 * rows, :] = (
            given[piece].astype(F32).reshape(16 * rows, 128)
        )
    for row in range(rows):
        state[row] = turned[pl.ds(row, CH, stride=rows), :].astype(BF16)
    for copy in copies[len(pieces) :]:
        copy.wait()
    emission = Emission(surface, flags, places, raw, d)
    emission.close(state, wet, fields, own_edges, one, two)
    for k in range(NK):
        code = (offsets[0, k] * SPAN + offsets[1, k]).astype(F32)
        tall[k * rows : (k + 1) * rows, :] = code
        tall[(NK + k) * rows : (NK + k + 1) * rows, :] = weights[k]
        planes[k] = code.astype(BF16)
        planes[NK + k] = weights[k].astype(BF16)
    packed = pack_columns([tall[plane * rows : (plane + 1) * rows, :] for plane in range(2 * NK)], 2)
    sides[...] = packed.astype(BF16)
    even = flags[3] == 0
    for (ref, first), down in zip(strips(one, two, even, d), (even, jnp.logical_not(even))):
        strip = [tall[pl.ds(first + step, 2 * NK, stride=rows), :] for step in range(2)]
        ref[d.strip : d.strip + 16, :] = jnp.concatenate(strip, axis=0).astype(BF16)
        ref[d.strip + 16 : d.strip + 32, :] = jnp.where(
            down, packed[rows - 16 : rows], packed[0:16]
        ).astype(BF16)


def decode(code):
    shifted = code.astype(jnp.int32) + (HW * SPAN + HW)
    rows = lax.shift_right_logical(shifted * 241, 12)
    return rows - HW, shifted - rows * SPAN - HW


def along_lanes(values, index):
    numbers = lax.GatherDimensionNumbers(
        offset_dims=(),
        collapsed_slice_dims=(1,),
        start_index_map=(1,),
        operand_batching_dims=(0,),
        start_indices_batching_dims=(0,),
    )
    return lax.gather(
        values, index[..., None], numbers, (1, 1), mode=lax.GatherScatterMode.PROMISE_IN_BOUNDS
    )


def couple(fields, coupled, rows):
    largest = None
    for field in range(NS):
        here = jnp.max(jnp.abs(fields[field]), axis=0, keepdims=True)
        largest = here if largest is None else jnp.maximum(largest, here)
    largest = jnp.maximum(jnp.max(largest, axis=1, keepdims=True), 1e-30)
    scale = FIXED / largest
    for pair in range(NS // 2):
        high, low = [
            jnp.floor(fields[2 * pair + part] * scale + 0.5).astype(jnp.int32) for part in range(2)
        ]
        coupled[pair] = high * (1 << 16) + (low + (1 << 15))
    return largest * (1 / FIXED)


def uncouple(values):
    high = lax.shift_right_arithmetic(values, 16)
    low = (values & 0xFFFF) - (1 << 15)
    return high.astype(F32), low.astype(F32)


def select_rows(source, start, picks):
    parts = source.shape[0]
    blank = jnp.full((8, 128), 1 << 15, jnp.int32) if parts < NS else jnp.zeros((8, 128), F32)
    chosen = [[blank for _ in range(parts)] for _ in picks]
    for shift in range(-HW, HW + 1):
        at = pl.ds(start + shift, 8)
        values = [source[part, at, :] for part in range(parts)]
        for slot, (rows, index, allowed) in enumerate(picks):
            here = (rows == shift) & allowed
            for part in range(parts):
                picked = along_lanes(values[part], index)
                chosen[slot][part] = jnp.where(here, picked, chosen[slot][part])
    if parts == NS:
        return chosen
    return [[part for values in pairs for part in uncouple(values)] for pairs in chosen]


def regrid_inside(coupled, unit, plan_x, part_x, first, tiles, tall):
    lane = lanes((8, 128))
    for step in range(tiles):
        at = first + step * 8
        picks = []
        weights = []
        for k in range(NK):
            rows, cols = decode(plan_x[pl.ds(k * tall + at, 8), :])
            weights.append(plan_x[pl.ds((NK + k) * tall + at, 8), :] * unit)
            column = lane + cols
            picks.append((rows, column & 127, (column >= 0) & (column < 128)))
        chosen = select_rows(coupled, at + 14, picks)
        for field in range(NS):
            total = chosen[0][field] * weights[0]
            for k in range(1, NK):
                total = total + chosen[k][field] * weights[k]
            part_x[pl.ds(field * tall + at, 8), :] = total


def edge_lanes():
    lane = lanes((8, 128))
    return ((lane + 8) & 127) // 32, ((lane + 8) & 31) - 8


def plan_edges(plan_x, plan_y, plan_e, first, tiles, tall, sides):
    part, place = edge_lanes()
    outer = place >= 8
    for step in range(tiles):
        at = first + step * 8
        code = jnp.zeros((8, 128), F32)
        weight = jnp.zeros((8, 128), F32)
        for k in range(NK):
            edge_code = roll(plan_x[pl.ds(k * tall + at, 8), :], 32 * k)
            edge_weight = roll(plan_x[pl.ds((NK + k) * tall + at, 8), :], 32 * k)
            if sides:
                edge_code = jnp.where(
                    outer, roll(plan_y[pl.ds(k * tall + at, 8), :], 32 * k + 16), edge_code
                )
                edge_weight = jnp.where(
                    outer, roll(plan_y[pl.ds((NK + k) * tall + at, 8), :], 32 * k + 16), edge_weight
                )
            code = jnp.where(part == k, edge_code, code)
            weight = jnp.where(part == k, edge_weight, weight)
        plan_e[pl.ds(at, 8), :] = code
        plan_e[pl.ds(tall + at, 8), :] = weight


def regrid_beside(window, plan_e, part_x, forcing_x, forcing_y, first, tiles, tall, sides):
    lane = lanes((8, 128))
    part, place = edge_lanes()
    outer = place >= 8
    inner_column = place & 127
    outer_column = jnp.where(place < 16, place - 16, place + 112)
    edge = (lane < 8) | (lane >= 120)
    for step in range(tiles):
        at = first + step * 8
        rows, cols = decode(plan_e[pl.ds(at, 8), :])
        weight = plan_e[pl.ds(tall + at, 8), :]
        column = jnp.where(outer, outer_column, inner_column) + cols
        within = (column >= 0) & (column < 128)
        index = jnp.where(within, column + 32, column) & 127
        (chosen,) = select_rows(window, at + 14, [(rows, index, outer | jnp.logical_not(within))])
        for field in range(NS):
            part_sum = chosen[field] * weight
            extra = part_sum
            for k in range(1, NK):
                extra = extra + roll(part_sum, -32 * k)
            total = part_x[pl.ds(field * tall + at, 8), :] + jnp.where(edge, extra, 0.0)
            forcing_x[pl.ds(at * 8 + field, 8, stride=8), :] = total
            forcing_x[pl.ds(at * 8 + field + 4, 8, stride=8), :] = total
            if sides:
                extra = roll(extra, -16)
                forcing_y[pl.ds(at * 8 + field, 8, stride=8), :] = extra
                forcing_y[pl.ds(at * 8 + field + 4, 8, stride=8), :] = extra


def twice_gelu(x):
    scale = (2 / jnp.pi) ** 0.5
    return x + x * jnp.tanh(x * (scale + (scale * 0.044715) * (x * x)))


def staggered(count, *stages):
    values = [{} for _ in stages]
    for turn in range(count + len(stages) - 1):
        for index, stage in enumerate(stages):
            step = turn - index
            if 0 <= step < count:
                given = values[index - 1].pop(step) if index else None
                values[index][step] = stage(step, given)


def air(state, out, forcing_x, air_in, atm_out, d):
    half = d.rows // 2
    leading = subs((8, 128)) < 4
    blank = jnp.zeros((32, 128), BF16)

    def inputs(row):
        at = (row + 2) * 8
        forced = jnp.where(leading, forcing_x[at : at + 8, :], 1.0)
        forced = jnp.concatenate([forced, jnp.zeros_like(forced)], axis=0).astype(BF16)
        return jnp.concatenate([state[row], forced, blank], axis=0)

    def first(step, _):
        pair = jnp.concatenate([inputs(step), inputs(step + half)], axis=1)
        return jnp.dot(air_in[...], pair, preferred_element_type=F32)

    def middle(step, product):
        return twice_gelu(product).astype(BF16)

    def second(step, hidden):
        return jnp.dot(atm_out[...], hidden, preferred_element_type=F32)

    def last(step, update):
        news = []
        for offset in range(2):
            change = update[:, offset * 128 : (offset + 1) * 128]
            news.append(state[step + offset * half].astype(F32) + 0.5 * change)
        out(step, *news)

    staggered(half, first, middle, second, last)


def edge_forcing(forcing_x, forcing_y, d):
    lane = lanes((8, d.edge))
    block = lane // d.block
    row = lane % d.block

    inner = outer = jnp.zeros((8, d.edge), F32)
    for step in range(d.rows + 4):
        at = pl.ds(step * 8, 8)
        pad = [jnp.zeros((8, 128), F32)] * (d.pieces - 1)
        here = jnp.concatenate([forcing_x[at, :]] + pad, axis=1)
        there = jnp.concatenate([forcing_y[at, :]] + pad, axis=1)
        for index, column in enumerate((126, 0, 127, 1)):
            shift = step + index * d.block - column
            match = (block == index) & (row == step)
            if column in (0, 127):
                inner = jnp.where(match, roll(here, shift), inner)
            outer = jnp.where(match, roll(there, shift), outer)
    return inner, outer


def roll_rows(state, upper, lower, rolled, d):
    def put(row, values):
        rolled[row, 0:CH, :] = roll(values, 1)
        rolled[row, CH : 2 * CH, :] = values
        rolled[row, 2 * CH : 3 * CH, :] = roll(values, -1)

    for step in range(2):
        put(step, upper[step * CH : (step + 1) * CH, :])
        put(d.rows + 2 + step, lower[step * CH : (step + 1) * CH, :])
    for row in range(d.rows):
        put(row + 2, state[row])


def sea(
    state, rolled, edges, left, right, out, forcing_x, forcing_y, ocn_in, ocn_out, wet,
    at_top, at_bottom, stack, hidden, side, d,
):
    rows, block = d.rows, d.block
    lane = lanes((CH, 128))
    spot = lanes((CH, d.edge))
    part = spot // block
    inner = edges
    outer = jnp.where((part == 0) | (part == 2), left, right)

    def sides_of(inner, outer, spot):
        first = spot < block
        return (
            jnp.where(first, outer, roll(inner, -block)),
            jnp.where(first, roll(outer, -2 * block), outer),
            jnp.where(first, roll(inner, -block), roll(outer, -2 * block)),
        )

    beside = sides_of(inner, outer, spot)
    middle = beside[1]
    force_in, force_out = edge_forcing(forcing_x, forcing_y, d)
    beside_forcing = sides_of(force_in, force_out, lanes((8, d.edge)))
    sub = subs((8, d.edge))
    ones = jnp.ones((8, d.edge), F32)
    forced = jnp.concatenate(
        [
            jnp.where(sub < 4, beside_forcing[0], beside_forcing[1]),
            jnp.where(sub < 4, beside_forcing[2], ones),
        ],
        axis=0,
    ).astype(BF16)
    columns = jnp.concatenate(list(beside) + [forced], axis=0)
    for tap in range(3):
        side[tap * 256 : (tap + 1) * 256, :] = roll(columns, -tap)

    sub_row = subs((8, 128))
    lane_row = lanes((8, 128))

    for row in range(rows + 4):
        entry = roll(middle, -row)[:, :128]
        stack[row, 0:CH, :] = jnp.where(lane == 0, entry, rolled[row, 0:CH, :])
        stack[row, CH : 2 * CH, :] = rolled[row, CH : 2 * CH, :]
        entry = roll(middle, 127 - block - row)[:, :128]
        stack[row, 2 * CH : 3 * CH, :] = jnp.where(lane == 127, entry, rolled[row, 2 * CH : 3 * CH, :])
        here, there = forcing_x[row * 8 : row * 8 + 8, :], forcing_y[row * 8 : row * 8 + 8, :]
        before = roll(jnp.where(lane_row == 127, there, here), 1)
        after = roll(jnp.where(lane_row == 0, there, here), -1)
        stack[row, 3 * CH : 256, :] = jnp.concatenate(
            [jnp.where(sub_row < 4, before, here), jnp.where(sub_row < 4, after, 1.0)], axis=0
        ).astype(BF16)

    pairs = (rows + 2) // 2

    def first(step, _):
        taps = jnp.concatenate(
            [
                stack[step : step + 3].reshape(3 * 256, 128),
                stack[step + pairs : step + pairs + 3].reshape(3 * 256, 128),
            ],
            axis=1,
        )
        return jnp.dot(ocn_in[...], taps, preferred_element_type=F32)

    def activate(step, product):
        active = twice_gelu(product)
        low, high = active[:, :128], active[:, 128:]
        if step == 0:
            low = jnp.where(at_top != 0, 0.0, low)
        if step == pairs - 1:
            high = jnp.where(at_bottom != 0, 0.0, high)
        hidden[step, 0:HIDK, :] = low.astype(BF16)
        hidden[step + pairs, 0:HIDK, :] = high.astype(BF16)
        blank = jnp.zeros((HIDP - HIDK, 128), BF16)
        hidden[step, HIDK:HIDP, :] = blank
        hidden[step + pairs, HIDK:HIDP, :] = blank

    staggered(pairs, first, activate)
    product = jnp.dot(ocn_in[...], side[...], preferred_element_type=F32)
    spot = lanes((1, d.edge)) % block
    gone = ((spot == 0) & (at_top != 0)) | ((spot == rows + 1) & (at_bottom != 0))
    active = jnp.where(gone, 0.0, twice_gelu(product)).astype(BF16)
    active = jnp.concatenate([active, jnp.zeros((HIDP - HIDK, d.edge), BF16)], axis=0)

    def taps_of(slices):
        total = None
        for tap, values in enumerate(slices):
            weights = ocn_out[tap * 3 * CH : (tap + 1) * 3 * CH, :]
            product = jnp.dot(weights, values, preferred_element_type=F32)
            total = product if total is None else total + product
        return total

    partial = taps_of([roll(active, -tap) for tap in range(3)])
    from_left, from_right = partial[0:CH], partial[2 * CH : 3 * CH]
    half = rows // 2

    def second(step, _):
        return taps_of(
            [
                jnp.concatenate([hidden[step + tap], hidden[step + half + tap]], axis=1)
                for tap in range(3)
            ]
        )

    def last(step, product):
        news = []
        for offset in range(2):
            row = step + offset * half
            sums = product[:, offset * 128 : (offset + 1) * 128]
            entry = roll(from_left, -row)[:, :128]
            total = sums[CH : 2 * CH] + jnp.where(lane == 0, entry, roll(sums[0:CH], 1))
            entry = roll(from_right, 127 - block - row)[:, :128]
            total = total + jnp.where(lane == 127, entry, roll(sums[2 * CH : 3 * CH], -1))
            update = total * (0.5 * wet[row : row + 1, :].astype(F32))
            news.append(state[row].astype(F32) + update)
        out(step, *news)

    staggered(half, second, last)


def prepare(atm_in, atm_bias, ocn_in, ocn_bias, ocn_out, air_in, first, second, is_ocean):
    def bias_rows(ref, width):
        row = jnp.concatenate([ref[index : index + 1, :] for index in range(ref.shape[0])], axis=1)
        terms = list(split_bf16(row)) + [jnp.zeros_like(row)]
        bias = jnp.concatenate(terms, axis=0)
        return jnp.pad(bias, ((0, 0), (0, width - bias.shape[1])))

    @pl.when(is_ocean == 0)
    def _():
        columns = jnp.concatenate(
            [atm_in[...].astype(F32), bias_rows(atm_bias, HA), jnp.zeros((40, HA), F32)], axis=0
        )
        air_in[...] = columns.T.astype(BF16)

    @pl.when(is_ocean != 0)
    def _():
        bias = bias_rows(ocn_bias, 256)
        count = ocn_in.shape[2]
        for tap in range(3):
            whole = [ocn_in[3 * tap + side].astype(F32) for side in range(3)]
            whole = [jnp.pad(values, ((0, 0), (0, 256 - count))) for values in whole]
            rows = [values[:CH] for values in whole] + [values[CH:] for values in whole]
            rows.append(bias if tap == 0 else jnp.zeros((4, 256), F32))
            columns = jnp.concatenate(rows, axis=0).T
            first[:, tap * 256 : (tap + 1) * 256] = columns[:HIDK].astype(BF16)
        for tap in range(9):
            values = ocn_out[tap].astype(F32)
            second[tap * CH : (tap + 1) * CH, :] = jnp.pad(
                values, ((0, 0), (0, HIDP - count))
            ).astype(BF16)


def ends(flags):
    at_top, at_bottom, even = flags[1] != 0, flags[2] != 0, flags[3] == 0

    def up_and_down(one, two):
        above = jnp.where(even, two, one).astype(F32)
        below = jnp.where(even, one, two).astype(F32)
        return jnp.where(at_top, 0.0, above), jnp.where(at_bottom, 0.0, below)

    return up_and_down


def middle_kernel(d, opening, *refs):
    refs = list(refs)
    take = lambda count: [refs.pop(0) for _ in range(count)]
    flags, state, field_one, beside, field_two, from_one, from_two = take(7)
    if opening:
        planes, *far_weights = take(6)
    else:
        (plan_x,) = take(1)
    part_x, fields_x, rolled = take(3)
    if opening:
        plan_x, *made_weights = take(4)
    (coupled,) = take(1)
    if opening:
        *raw_weights, sems = take(6)
        copies = fetch(far_weights, raw_weights, sems)
    rows, tall = d.rows, d.tall
    is_ocean = flags[0]
    up_and_down = ends(flags)

    if opening:

        @pl.when(is_ocean != 0)
        def _():
            base = d.strip
            pair = up_and_down(from_one[base : base + 16, :], from_two[base : base + 16, :])
            plan_x[...] = jnp.zeros_like(plan_x)
            for step, strip in zip((0, rows + 2), pair):
                for index in range(2):
                    plan_x[pl.ds(step + index, 2 * NK, stride=tall), :] = strip[index * 8 : (index + 1) * 8]

        for plane in range(2 * NK):
            plan_x[plane * tall + 2 : plane * tall + 2 + rows, :] = planes[plane].astype(F32)

    for field in range(NS):
        pair = up_and_down(field_one[field], field_two[field])
        fields_x[field, 0:16, :] = pair[0][rows - 16 : rows]
        fields_x[field, 16 : 16 + rows, :] = beside[field].astype(F32)
        fields_x[field, 16 + rows : 32 + rows, :] = pair[1][0:16]

    unit = couple(fields_x, coupled, rows)

    @pl.when(is_ocean == 0)
    def _():
        regrid_inside(coupled, unit, plan_x, part_x, 2, rows // 8, tall)

    @pl.when(is_ocean != 0)
    def _():
        regrid_inside(coupled, unit, plan_x, part_x, 0, d.tiles, tall)
        upper, lower = up_and_down(from_one[0 : 2 * CH, :], from_two[0 : 2 * CH, :])
        roll_rows(state, upper.astype(BF16), lower.astype(BF16), rolled, d)

    if opening:
        for copy in copies:
            copy.wait()
        prepare(*raw_weights, *made_weights, is_ocean)


def step_kernel(d, opening, closing, *refs):
    refs = list(refs)
    take = lambda count: [refs.pop(0) for _ in range(count)]
    flags, state, wet, from_left, from_right = take(5)
    part_x, fields_x, rolled, edges, plan_x, air_in, first, second, atm_out = take(9)
    if not opening:
        (plan_e,) = take(1)
    if not closing:
        surface, places = take(2)
    (out,) = take(1)
    if not closing:
        fields, new_edges, one, two = take(4)
    if opening:
        (plan_e,) = take(1)
    window, forcing_x, forcing_y, stack, hidden, side, raw = take(7)
    if opening:
        (plan_y,) = take(1)
    rows, tall = d.rows, d.tall
    is_ocean, at_top, at_bottom = flags[0], flags[1], flags[2]
    up_and_down = ends(flags)

    if opening:

        @pl.when(is_ocean != 0)
        def _():
            plan_y[...] = jnp.zeros_like(plan_y)
            base = d.edge_rows
            parts = [
                (ref[base : base + 16, :], ref[base + 16 + rows : base + 32 + rows, :],
                 ref[base + 16 : base + 16 + rows, :])
                for ref in (from_left, from_right)
            ]
            for plane in range(2 * NK):
                first_end, second_end, own = [
                    unpack_columns(left, right, plane, 2 * NK, 2) for left, right in zip(*parts)
                ]
                above, below = up_and_down(first_end, second_end)
                at = plane * tall
                plan_y[at : at + 2, :] = above[14:16]
                plan_y[at + 2 : at + 2 + rows, :] = own
                plan_y[at + 2 + rows : at + 4 + rows, :] = below[0:2]

    base = d.edge_rows + (rows + 32 if opening else 0)
    parts = [
        (ref[base : base + 16, :], ref[base + 16 + rows : base + 32 + rows, :],
         ref[base + 16 : base + 16 + rows, :])
        for ref in (from_left, from_right)
    ]
    for field in range(NS):
        first_end, second_end, own = [
            unpack_columns(left, right, field, NS, REACH) for left, right in zip(*parts)
        ]
        above, below = up_and_down(first_end, second_end)
        for at, values in ((0, above), (16, own), (16 + rows, below)):
            count = values.shape[0]
            inside = roll(fields_x[field, at : at + count, :], 32)
            lane = lanes(values.shape)
            near = (lane >= 32 - REACH) & (lane < 32 + REACH)
            far = (lane < REACH) | (lane >= 128 - REACH)
            kept = jnp.where(near, inside, jnp.where(far, values, 0.0))
            window[field, at : at + count, :] = kept
    def finished():
        emission = None if closing else Emission(surface, flags, places, raw, d)

        def put(step, low, high):
            if closing:
                for row, values in ((step, low), (step + rows // 2, high)):
                    raw[pl.ds(row, CH, stride=rows), :] = values
                return
            out[step] = low.astype(BF16)
            out[step + rows // 2] = high.astype(BF16)

        def close():
            if not closing:
                emission.close(out, wet, fields, new_edges, one, two)

        return put, close

    @pl.when(is_ocean == 0)
    def _():
        if opening:
            plan_edges(plan_x, plan_y, plan_e, 2, rows // 8, tall, False)
        regrid_beside(
            window, plan_e, part_x, forcing_x, forcing_y, 2, rows // 8, tall, False
        )
        put, close = finished()
        air(state, put, forcing_x, air_in, atm_out, d)
        close()

    @pl.when(is_ocean != 0)
    def _():
        if opening:
            plan_edges(plan_x, plan_y, plan_e, 0, d.tiles, tall, True)
        regrid_beside(
            window, plan_e, part_x, forcing_x, forcing_y, 0, d.tiles, tall, True
        )
        put, close = finished()
        joined = [get_edges(ref, 0, d) for ref in (from_left, from_right)]
        sea(
            state, rolled, get_edges(edges, 0, d), *joined, put, forcing_x, forcing_y,
            first, second, wet, at_top, at_bottom, stack, hidden, side, d,
        )
        close()

    if closing:
        out[...] = raw[...].reshape(CH, rows, 128).astype(BF16)


VMEM = pl.BlockSpec(memory_space=pltpu.VMEM)
HBM = pl.BlockSpec(memory_space=pltpu.HBM)
SMEM = pl.BlockSpec(memory_space=pltpu.SMEM)
PARAMS = pltpu.CompilerParams(vmem_limit_bytes=48 * 1024 * 1024)


def shape(*dims, dtype=BF16):
    return jax.ShapeDtypeStruct(dims, dtype)


def send(x, move):
    names = ("grp", "lat", "lon")
    sizes = [lax.axis_size(name) for name in names]
    pairs = []
    for group in range(sizes[0]):
        for lat in range(sizes[1]):
            for lon in range(sizes[2]):
                to = move(group, lat, lon)
                if to is None or not 0 <= to[1] < sizes[1]:
                    continue
                target = (to[0] * sizes[1] + to[1]) * sizes[2] + to[2] % sizes[2]
                pairs.append(((group * sizes[1] + lat) * sizes[2] + lon, target))
    return lax.ppermute(x, names, pairs)


def swap_rows(x, turn, across):
    count, columns = lax.axis_size("lat"), lax.axis_size("lon")

    def move(group, lat, lon):
        other = ((lat + turn) ^ 1) - turn
        if 0 <= other < count and (across or group == 1):
            return (1 - group if across else group), other, lon
        beside = lon ^ 1
        return group, lat, beside if beside < columns else lon

    return send(x, move)


def exchange(fields, own_edges, one, two, sides, d):
    rows = d.rows
    scale = jnp.where(lax.axis_index("grp") > 1, 0, 1).astype(BF16)
    later = fields * scale
    beside = send(fields, lambda g, i, j: (1 - g, i, j))
    from_one = swap_rows(one, 0, False)
    from_two = swap_rows(two, 1, False)
    field_one = swap_rows(later, 0, True)
    field_two = swap_rows(later, 1, True)
    beside, from_one = lax.optimization_barrier((beside, from_one))
    from_two, beside = lax.optimization_barrier((from_two, beside))
    field_one, from_two = lax.optimization_barrier((field_one, from_two))
    field_two, field_one = lax.optimization_barrier((field_two, field_one))
    lat, count = lax.axis_index("lat"), lax.axis_size("lat")
    odd = lat % 2 == 1
    edges = own_edges
    for turn, ref in ((0, from_one), (1, from_two)):
        other = ((lat + turn) ^ 1) - turn
        there = (other >= 0) & (other < count)
        edges = edges + jnp.where(there, ref[2 * CH : d.strip], 0)
    outer = [field_one[NS], field_two[NS]]
    if rows != 16:
        outer = [
            jnp.where(odd, outer[0][rows - 16 :], outer[0][:16]),
            jnp.where(odd, outer[1][:16], outer[1][rows - 16 :]),
        ]
    packed = [edges]
    if sides is not None:
        packed += [from_one[d.strip + 16 :], sides, from_two[d.strip + 16 :]]
    packed += [outer[0], beside[NS], outer[1]]
    packed = jnp.concatenate(packed, axis=0)
    from_left = send(packed, lambda g, i, j: (g, i, j + 1))
    from_right = send(packed, lambda g, i, j: (g, i, j - 1))
    return (field_one, beside, field_two, from_one, from_two), (from_left, from_right), edges


def local(
    coupled_state, land_mask, regrid_offsets, regrid_weights, surface_proj,
    atm_in, atm_bias, atm_out, ocn_in, ocn_bias, ocn_out,
):
    rows = coupled_state.shape[2]
    assert coupled_state.shape[3] == 128
    d = Dims(rows)
    group = lax.axis_index("grp")
    lat = lax.axis_index("lat")
    flags = jnp.stack(
        [group, lat == 0, lat == lax.axis_size("lat") - 1, lat % 2]
    ).astype(jnp.int32)
    raw_weights = (
        atm_in.T,
        atm_bias.reshape(HA // 128, 128),
        jnp.transpose(ocn_in, (1, 2, 0)),
        ocn_bias[None],
        jnp.transpose(ocn_out, (1, 0, 2)),
    )
    state_shape = shape(rows, CH, 128)
    emitted = [
        shape(NS + 1, rows, 128),
        shape(d.edge_rows, 128),
        shape(d.strip, 128),
        shape(d.strip, 128),
    ]
    raw = pltpu.VMEM((rows * 8, 128), F32)
    turned = pltpu.VMEM((CH * rows, 128), F32)

    def call(kernel, operands, outs, scratch, name, far=()):
        scratch = scratch + [pltpu.VMEM(x.shape, x.dtype) for x in far]
        if far:
            scratch.append(pltpu.SemaphoreType.DMA((len(far) + CH // 16,)))

        far = [pltpu.with_memory_space_constraint(x, pltpu.HBM) for x in far]
        return pl.pallas_call(
            kernel,
            out_shape=outs,
            in_specs=[SMEM] + [VMEM] * len(operands) + [HBM] * len(far),
            out_specs=[VMEM] * len(outs),
            scratch_shapes=scratch,
            compiler_params=PARAMS,
            name=name,
        )(flags, *operands, *far)

    state, planes, sides, places, fields, edges, one, two = call(
        functools.partial(start_kernel, d),
        (),
        [state_shape, shape(2 * NK, rows, 128), shape(rows, 128), shape(rows * 128, d.edge)]
        + emitted[:2]
        + [shape(d.strip + 32, 128)] * 2,
        [raw, pltpu.VMEM((2 * NK * rows, 128), F32), turned],
        "start",
        (coupled_state[0], surface_proj, land_mask, regrid_offsets[0], regrid_weights[0]),
    )

    plan = shape(2 * NK * d.tall, 128, dtype=F32)
    between = [
        shape(NS * d.tall, 128, dtype=F32),
        shape(NS, rows + 32, 128, dtype=F32),
        shape(rows + 4, 3 * CH, 128),
    ]
    made = [shape(HA, 128), shape(HIDK, 768), shape(9 * CH, HIDP)]
    coupled = pltpu.VMEM((NS // 2, rows + 32, 128), jnp.int32)
    scratch = [
        pltpu.VMEM((NS, rows + 32, 128), F32),
        pltpu.VMEM((d.tall * 8, 128), F32),
        pltpu.VMEM((d.tall * 8, 128), F32),
        pltpu.VMEM((rows + 4, 256, 128), BF16),
        pltpu.VMEM((rows + 2, HIDP, 128), BF16),
        pltpu.VMEM((768, d.edge), BF16),
    ]

    vertical, horizontal, edges = exchange(fields, edges, one, two, sides, d)
    *shared, plan_x, air_in, first, second = call(
        functools.partial(middle_kernel, d, True),
        (state, *vertical, planes),
        between + [plan] + made,
        [coupled],
        "first_middle",
        raw_weights,
    )
    weights = (air_in, first, second, atm_out)
    state, fields, edges, one, two, plan_e = call(
        functools.partial(step_kernel, d, True, False),
        (state, land_mask, *horizontal, *shared, edges, plan_x, *weights, surface_proj, places),
        [state_shape] + emitted + [shape(2 * d.tall, 128, dtype=F32)],
        scratch + [raw, pltpu.VMEM(plan.shape, F32)],
        "first_step",
    )

    vertical, horizontal, edges = exchange(fields, edges, one, two, None, d)
    shared = call(
        functools.partial(middle_kernel, d, False),
        (state, *vertical, plan_x),
        between,
        [coupled],
        "second_middle",
    )
    (state,) = call(
        functools.partial(step_kernel, d, False, True),
        (state, land_mask, *horizontal, *shared, edges, plan_x, *weights, plan_e),
        [shape(CH, rows, 128)],
        scratch + [turned],
        "second_step",
    )
    return state[None]


def solution(mesh):
    return jax.shard_map(
        local,
        mesh=mesh,
        in_specs=(
            P("grp", None, "lat", "lon"),
            P("lat", "lon"),
            P("grp", None, None, "lat", "lon"),
            P("grp", None, "lat", "lon"),
            P(),
            P(),
            P(),
            P(),
            P(),
            P(),
            P(),
        ),
        out_specs=P("grp", None, "lat", "lon"),
        check_vma=False,
    )
```

```python
import functools

import jax
import jax.numpy as jnp
from jax import lax
from jax.experimental import pallas as pl
from jax.experimental.pallas import tpu as pltpu
from jax.sharding import PartitionSpec as P

CH = 80
NS = 4
NK = 4
HA = 384
HW = 8
SPAN = 2 * HW + 1
REACH = HW + 2
FIXED = 32767.0
HIDK = 208
HIDP = 256
F32 = jnp.float32
BF16 = jnp.bfloat16


def roll(x, shift, axis=1):
    size = x.shape[axis]
    if isinstance(shift, int):
        shift = shift % size
        if shift == 0:
            return x
    return pltpu.roll(x, shift, axis)


def lanes(shape):
    return lax.broadcasted_iota(jnp.int32, shape, len(shape) - 1)


def subs(shape):
    return lax.broadcasted_iota(jnp.int32, shape, len(shape) - 2)


class Dims:
    def __init__(self, rows):
        self.rows = rows
        self.block = 32 if rows + 4 <= 32 else 64
        self.edge = 4 * self.block
        self.pieces = self.edge // 128
        self.edge_rows = CH * self.pieces
        self.tiles = -(-(rows + 4) // 8)
        self.tall = 8 * self.tiles
        self.strip = 2 * CH + 16
        self.lead = self.edge_rows + 32


def put_edges(ref, at, edges, d):
    for piece in range(d.pieces):
        ref[at + piece * CH : at + (piece + 1) * CH, :] = edges[:, piece * 128 : (piece + 1) * 128]


def get_edges(ref, at, d):
    return jnp.concatenate(
        [ref[at + piece * CH : at + (piece + 1) * CH, :] for piece in range(d.pieces)], axis=1
    )


def edge_places(places, d):
    lane = lanes((1, d.edge))
    block = lane // d.block
    row = lane % d.block - 2
    column = jnp.where(block == 0, 126, jnp.where(block == 1, 0, jnp.where(block == 2, 127, 1)))
    own = (row >= 0) & (row < d.rows)
    target = jnp.where(own, column, -1)
    position = subs((128, d.edge))
    for step in range(d.rows):
        place = (position == jnp.where(row == step, target, -1)).astype(F32).astype(BF16)
        places[step * 128 : (step + 1) * 128, :] = place


def edge_columns(state, places, d):
    whole = jnp.concatenate([state[step] for step in range(d.rows)], axis=1)
    return jnp.dot(whole, places[...], preferred_element_type=F32).astype(BF16)


def pack_columns(values, reach):
    lane = lanes(values[0].shape)
    pitch = 128 // len(values)
    packed = jnp.zeros_like(values[0])
    for index, value in enumerate(values):
        at = index * pitch
        packed = jnp.where((lane >= at) & (lane < at + reach), roll(value, at), packed)
        at += reach
        packed = jnp.where((lane >= at) & (lane < at + reach), roll(value, at + reach - 128), packed)
    return packed


def unpack_columns(left, right, index, count, reach):
    at = index * (128 // count)
    left = roll(left.astype(F32), 128 - at - 2 * reach)
    return jnp.where(lanes(left.shape) < 64, roll(right.astype(F32), -at), left)


def corner_lane(index):
    block = index // 2
    column = jnp.where(block == 0, 126, jnp.where(block == 1, 0, jnp.where(block == 2, 127, 1)))
    return jnp.where(index < 8, column + 128 * (index % 2), -1)


def join_corners(own, above, below, d):
    index = subs((16, d.edge))
    spot = (index % 8 // 2) * d.block + index % 2 + jnp.where(index < 8, 0, d.rows + 2)
    place = (lanes((16, d.edge)) == spot).astype(F32).astype(BF16)
    corners = jnp.concatenate([above[0:8], below[0:8]], axis=0).astype(BF16)
    corners = lax.dot_general(
        corners, place, (((0,), (0,)), ((), ())), preferred_element_type=F32
    )
    return own + corners[:CH].astype(BF16)


def strips(one, two, even, d):
    last = d.rows - 2
    return (one, jnp.where(even, last, 0)), (two, jnp.where(even, 0, last))


def split_bf16(values):
    high = values.astype(BF16).astype(F32)
    mid = (values - high).astype(BF16).astype(F32)
    return high, mid, values - high - mid


class Emission:
    def __init__(self, surface, flags, places, raw, d):
        gap = jnp.zeros((4, CH), F32)
        terms = []
        for term in split_bf16(surface[flags[0]]):
            terms += [term, gap]
        self.proj = jnp.concatenate(terms + [gap, gap], axis=0).astype(BF16)
        self.places, self.raw, self.d, self.flags = places, raw, d, flags

    def project(self, state):
        half = self.d.rows // 2
        products = []
        for step in range(half):
            pair = jnp.concatenate([state[step], state[step + half]], axis=1)
            products.append(jnp.dot(self.proj, pair, preferred_element_type=F32))
        whole = jnp.concatenate([state[step] for step in range(2 * half)], axis=1)
        edges = jnp.dot(whole, self.places[...], preferred_element_type=F32)
        for step, parts in enumerate(products):
            parts = parts[0:8] + parts[8:16] + parts[16:24]
            self.raw[step * 8 : step * 8 + 8, :] = parts[:, :128]
            self.raw[(step + half) * 8 : (step + half) * 8 + 8, :] = parts[:, 128:]
        return edges.astype(BF16)

    def close(self, state, wet, fields, own_edges, one, two):
        d, even = self.d, self.flags[3] == 0
        edges = self.project(state)
        keeping = jnp.where(self.flags[0] != 0, wet[...].astype(F32), 1.0)
        whole = [self.raw[pl.ds(field, d.rows, stride=8), :] * keeping for field in range(NS)]
        for field in range(NS):
            fields[field] = whole[field].astype(BF16)
        fields[NS] = pack_columns(whole, REACH).astype(BF16)
        put_edges(own_edges, 0, edges, d)
        pick = (lanes((16, 256)) == corner_lane(subs((16, 256)))).astype(F32).astype(BF16)
        rest = jnp.zeros((128 - CH, 256), BF16)
        for ref, first in strips(one, two, even, d):
            ref[0:CH, :] = state[first]
            ref[CH : 2 * CH, :] = state[first + 1]
            pair = jnp.concatenate([state[first], state[first + 1]], axis=1)
            corners = lax.dot_general(
                pick,
                jnp.concatenate([pair, rest], axis=0),
                (((1,), (1,)), ((), ())),
                preferred_element_type=F32,
            )
            ref[2 * CH : d.strip, :] = corners.astype(BF16)


def fetch(sources, targets, sems):
    copies = [
        pltpu.make_async_copy(source, target, sems.at[index])
        for index, (source, target) in enumerate(zip(sources, targets))
    ]
    for copy in copies:
        copy.start()
    return copies


def start_kernel(
    d, flags, far_given, far_surface, far_wet, far_offsets, far_weights,
    state, planes, sides, places, fields, own_edges, one, two,
    raw, tall, turned, given, surface, wet, offsets, weights, sems,
):
    rows = d.rows
    pieces = [pl.ds(at, 16) for at in range(0, CH, 16)]
    copies = fetch(
        [far_offsets, far_weights, far_surface, far_wet] + [far_given.at[piece] for piece in pieces],
        [offsets, weights, surface, wet] + [given.at[piece] for piece in pieces],
        sems,
    )
    edge_places(places, d)
    for copy in copies[:4]:
        copy.wait()
    for k in range(NK):
        code = (offsets[0, k] * SPAN + offsets[1, k]).astype(F32)
        tall[k * rows : (k + 1) * rows, :] = code
        tall[(NK + k) * rows : (NK + k + 1) * rows, :] = weights[k]
        planes[k] = code.astype(BF16)
        planes[NK + k] = weights[k].astype(BF16)
    packed = pack_columns([tall[plane * rows : (plane + 1) * rows, :] for plane in range(2 * NK)], 2)
    sides[...] = packed.astype(BF16)
    even = flags[3] == 0
    for (ref, first), down in zip(strips(one, two, even, d), (even, jnp.logical_not(even))):
        strip = [tall[pl.ds(first + step, 2 * NK, stride=rows), :] for step in range(2)]
        ref[d.strip : d.strip + 16, :] = jnp.concatenate(strip, axis=0).astype(BF16)
        ref[d.strip + 16 : d.strip + 32, :] = jnp.where(
            down, packed[rows - 16 : rows], packed[0:16]
        ).astype(BF16)
    for index, piece in enumerate(pieces):
        copies[4 + index].wait()
        turned[index * 16 * rows : (index + 1) * 16 * rows, :] = (
            given[piece].astype(F32).reshape(16 * rows, 128)
        )
    for row in range(rows):
        state[row] = turned[pl.ds(row, CH, stride=rows), :].astype(BF16)
    emission = Emission(surface, flags, places, raw, d)
    emission.close(state, wet, fields, own_edges, one, two)


def decode(code):
    shifted = code.astype(jnp.int32) + (HW * SPAN + HW)
    rows = lax.shift_right_logical(shifted * 241, 12)
    return rows - HW, shifted - rows * SPAN - HW


def along_lanes(values, index):
    numbers = lax.GatherDimensionNumbers(
        offset_dims=(),
        collapsed_slice_dims=(1,),
        start_index_map=(1,),
        operand_batching_dims=(0,),
        start_indices_batching_dims=(0,),
    )
    return lax.gather(
        values, index[..., None], numbers, (1, 1), mode=lax.GatherScatterMode.PROMISE_IN_BOUNDS
    )


def couple(fields, coupled, rows):
    largest = None
    for field in range(NS):
        here = jnp.max(jnp.abs(fields[field]), axis=0, keepdims=True)
        largest = here if largest is None else jnp.maximum(largest, here)
    largest = jnp.maximum(jnp.max(largest, axis=1, keepdims=True), 1e-30)
    scale = FIXED / largest
    for pair in range(NS // 2):
        high, low = [
            jnp.floor(fields[2 * pair + part] * scale + 0.5).astype(jnp.int32) for part in range(2)
        ]
        coupled[pair] = high * (1 << 16) + (low + (1 << 15))
    return largest * (1 / FIXED)


def uncouple(values):
    high = lax.shift_right_arithmetic(values, 16)
    low = (values & 0xFFFF) - (1 << 15)
    return high.astype(F32), low.astype(F32)


def select_rows(source, start, picks):
    parts = source.shape[0]
    blank = jnp.full((8, 128), 1 << 15, jnp.int32) if parts < NS else jnp.zeros((8, 128), F32)
    chosen = [[blank for _ in range(parts)] for _ in picks]
    for shift in range(-HW, HW + 1):
        at = pl.ds(start + shift, 8)
        values = [source[part, at, :] for part in range(parts)]
        for slot, (rows, index, allowed) in enumerate(picks):
            here = (rows == shift) & allowed
            for part in range(parts):
                picked = along_lanes(values[part], index)
                chosen[slot][part] = jnp.where(here, picked, chosen[slot][part])
    if parts == NS:
        return chosen
    return [[part for values in pairs for part in uncouple(values)] for pairs in chosen]


def regrid_inside(coupled, unit, plan_x, part_x, first, tiles, tall):
    lane = lanes((8, 128))
    for step in range(tiles):
        at = first + step * 8
        picks = []
        weights = []
        for k in range(NK):
            rows, cols = decode(plan_x[pl.ds(k * tall + at, 8), :])
            weights.append(plan_x[pl.ds((NK + k) * tall + at, 8), :] * unit)
            column = lane + cols
            picks.append((rows, column & 127, (column >= 0) & (column < 128)))
        chosen = select_rows(coupled, at + 14, picks)
        for field in range(NS):
            total = chosen[0][field] * weights[0]
            for k in range(1, NK):
                total = total + chosen[k][field] * weights[k]
            part_x[pl.ds(field * tall + at, 8), :] = total


def edge_lanes():
    lane = lanes((8, 128))
    return ((lane + 8) & 127) // 32, ((lane + 8) & 31) - 8


def plan_edges(plan_x, plan_y, plan_e, first, tiles, tall, sides):
    part, place = edge_lanes()
    outer = place >= 8
    for step in range(tiles):
        at = first + step * 8
        code = jnp.zeros((8, 128), F32)
        weight = jnp.zeros((8, 128), F32)
        for k in range(NK):
            edge_code = roll(plan_x[pl.ds(k * tall + at, 8), :], 32 * k)
            edge_weight = roll(plan_x[pl.ds((NK + k) * tall + at, 8), :], 32 * k)
            if sides:
                edge_code = jnp.where(
                    outer, roll(plan_y[pl.ds(k * tall + at, 8), :], 32 * k + 16), edge_code
                )
                edge_weight = jnp.where(
                    outer, roll(plan_y[pl.ds((NK + k) * tall + at, 8), :], 32 * k + 16), edge_weight
                )
            code = jnp.where(part == k, edge_code, code)
            weight = jnp.where(part == k, edge_weight, weight)
        plan_e[pl.ds(at, 8), :] = code
        plan_e[pl.ds(tall + at, 8), :] = weight


def regrid_beside(window, plan_e, part_x, forcing_x, forcing_y, first, tiles, tall, sides):
    lane = lanes((8, 128))
    part, place = edge_lanes()
    outer = place >= 8
    inner_column = place & 127
    outer_column = jnp.where(place < 16, place - 16, place + 112)
    edge = (lane < 8) | (lane >= 120)
    for step in range(tiles):
        at = first + step * 8
        rows, cols = decode(plan_e[pl.ds(at, 8), :])
        weight = plan_e[pl.ds(tall + at, 8), :]
        column = jnp.where(outer, outer_column, inner_column) + cols
        within = (column >= 0) & (column < 128)
        index = jnp.where(within, column + 32, column) & 127
        (chosen,) = select_rows(window, at + 14, [(rows, index, outer | jnp.logical_not(within))])
        for field in range(NS):
            part_sum = chosen[field] * weight
            extra = part_sum
            for k in range(1, NK):
                extra = extra + roll(part_sum, -32 * k)
            total = part_x[pl.ds(field * tall + at, 8), :] + jnp.where(edge, extra, 0.0)
            forcing_x[pl.ds(at * 8 + field, 8, stride=8), :] = total
            forcing_x[pl.ds(at * 8 + field + 4, 8, stride=8), :] = total
            if sides:
                extra = roll(extra, -16)
                forcing_y[pl.ds(at * 8 + field, 8, stride=8), :] = extra
                forcing_y[pl.ds(at * 8 + field + 4, 8, stride=8), :] = extra


def twice_gelu(x):
    scale = (2 / jnp.pi) ** 0.5
    return x + x * jnp.tanh(x * (scale + (scale * 0.044715) * (x * x)))


def staggered(count, *stages):
    values = [{} for _ in stages]
    for turn in range(count + len(stages) - 1):
        for index, stage in enumerate(stages):
            step = turn - index
            if 0 <= step < count:
                given = values[index - 1].pop(step) if index else None
                values[index][step] = stage(step, given)


def air(state, out, forcing_x, air_in, atm_out, d):
    half = d.rows // 2
    leading = subs((8, 128)) < 4
    blank = jnp.zeros((32, 128), BF16)

    def inputs(row):
        at = (row + 2) * 8
        forced = jnp.where(leading, forcing_x[at : at + 8, :], 1.0)
        forced = jnp.concatenate([forced, jnp.zeros_like(forced)], axis=0).astype(BF16)
        return jnp.concatenate([state[row], forced, blank], axis=0)

    def first(step, _):
        pair = jnp.concatenate([inputs(step), inputs(step + half)], axis=1)
        return jnp.dot(air_in[...], pair, preferred_element_type=F32)

    def middle(step, product):
        return twice_gelu(product).astype(BF16)

    def second(step, hidden):
        return jnp.dot(atm_out[...], hidden, preferred_element_type=F32)

    def last(step, update):
        news = []
        for offset in range(2):
            change = update[:, offset * 128 : (offset + 1) * 128]
            news.append(state[step + offset * half].astype(F32) + 0.5 * change)
        out(step, *news)

    staggered(half, first, middle, second, last)


def edge_forcing(forcing_x, forcing_y, d):
    lane = lanes((8, d.edge))
    block = lane // d.block
    row = lane % d.block

    inner = outer = jnp.zeros((8, d.edge), F32)
    for step in range(d.rows + 4):
        at = pl.ds(step * 8, 8)
        pad = [jnp.zeros((8, 128), F32)] * (d.pieces - 1)
        here = jnp.concatenate([forcing_x[at, :]] + pad, axis=1)
        there = jnp.concatenate([forcing_y[at, :]] + pad, axis=1)
        for index, column in enumerate((126, 0, 127, 1)):
            shift = step + index * d.block - column
            match = (block == index) & (row == step)
            if column in (0, 127):
                inner = jnp.where(match, roll(here, shift), inner)
            outer = jnp.where(match, roll(there, shift), outer)
    return inner, outer


def roll_rows(state, upper, lower, rolled, d):
    def put(row, values):
        rolled[row, 0:CH, :] = roll(values, 1)
        rolled[row, CH : 2 * CH, :] = values
        rolled[row, 2 * CH : 3 * CH, :] = roll(values, -1)

    for step in range(2):
        put(step, upper[step * CH : (step + 1) * CH, :])
        put(d.rows + 2 + step, lower[step * CH : (step + 1) * CH, :])
    for row in range(d.rows):
        put(row + 2, state[row])


def sea(
    state, rolled, edges, left, right, out, forcing_x, forcing_y, ocn_in, ocn_out, wet,
    at_top, at_bottom, stack, hidden, side, d,
):
    rows, block = d.rows, d.block
    lane = lanes((CH, 128))
    spot = lanes((CH, d.edge))
    part = spot // block
    inner = edges
    outer = jnp.where((part == 0) | (part == 2), left, right)

    def sides_of(inner, outer, spot):
        first = spot < block
        return (
            jnp.where(first, outer, roll(inner, -block)),
            jnp.where(first, roll(outer, -2 * block), outer),
            jnp.where(first, roll(inner, -block), roll(outer, -2 * block)),
        )

    beside = sides_of(inner, outer, spot)
    middle = beside[1]
    force_in, force_out = edge_forcing(forcing_x, forcing_y, d)
    beside_forcing = sides_of(force_in, force_out, lanes((8, d.edge)))
    sub = subs((8, d.edge))
    ones = jnp.ones((8, d.edge), F32)
    forced = jnp.concatenate(
        [
            jnp.where(sub < 4, beside_forcing[0], beside_forcing[1]),
            jnp.where(sub < 4, beside_forcing[2], ones),
        ],
        axis=0,
    ).astype(BF16)
    columns = jnp.concatenate(list(beside) + [forced], axis=0)
    for tap in range(3):
        side[tap * 256 : (tap + 1) * 256, :] = roll(columns, -tap)

    sub_row = subs((8, 128))
    lane_row = lanes((8, 128))

    for row in range(rows + 4):
        entry = roll(middle, -row)[:, :128]
        stack[row, 0:CH, :] = jnp.where(lane == 0, entry, rolled[row, 0:CH, :])
        stack[row, CH : 2 * CH, :] = rolled[row, CH : 2 * CH, :]
        entry = roll(middle, 127 - block - row)[:, :128]
        stack[row, 2 * CH : 3 * CH, :] = jnp.where(lane == 127, entry, rolled[row, 2 * CH : 3 * CH, :])
        here, there = forcing_x[row * 8 : row * 8 + 8, :], forcing_y[row * 8 : row * 8 + 8, :]
        before = roll(jnp.where(lane_row == 127, there, here), 1)
        after = roll(jnp.where(lane_row == 0, there, here), -1)
        stack[row, 3 * CH : 256, :] = jnp.concatenate(
            [jnp.where(sub_row < 4, before, here), jnp.where(sub_row < 4, after, 1.0)], axis=0
        ).astype(BF16)

    pairs = (rows + 2) // 2

    def first(step, _):
        taps = jnp.concatenate(
            [
                stack[step : step + 3].reshape(3 * 256, 128),
                stack[step + pairs : step + pairs + 3].reshape(3 * 256, 128),
            ],
            axis=1,
        )
        return jnp.dot(ocn_in[...], taps, preferred_element_type=F32)

    def activate(step, product):
        active = twice_gelu(product)
        low, high = active[:, :128], active[:, 128:]
        if step == 0:
            low = jnp.where(at_top != 0, 0.0, low)
        if step == pairs - 1:
            high = jnp.where(at_bottom != 0, 0.0, high)
        hidden[step, 0:HIDK, :] = low.astype(BF16)
        hidden[step + pairs, 0:HIDK, :] = high.astype(BF16)
        blank = jnp.zeros((HIDP - HIDK, 128), BF16)
        hidden[step, HIDK:HIDP, :] = blank
        hidden[step + pairs, HIDK:HIDP, :] = blank

    staggered(pairs, first, activate)
    product = jnp.dot(ocn_in[...], side[...], preferred_element_type=F32)
    spot = lanes((1, d.edge)) % block
    gone = ((spot == 0) & (at_top != 0)) | ((spot == rows + 1) & (at_bottom != 0))
    active = jnp.where(gone, 0.0, twice_gelu(product)).astype(BF16)
    active = jnp.concatenate([active, jnp.zeros((HIDP - HIDK, d.edge), BF16)], axis=0)

    def taps_of(slices):
        total = None
        for tap, values in enumerate(slices):
            weights = ocn_out[tap * 3 * CH : (tap + 1) * 3 * CH, :]
            product = jnp.dot(weights, values, preferred_element_type=F32)
            total = product if total is None else total + product
        return total

    partial = taps_of([roll(active, -tap) for tap in range(3)])
    from_left, from_right = partial[0:CH], partial[2 * CH : 3 * CH]
    half = rows // 2

    def second(step, _):
        return taps_of(
            [
                jnp.concatenate([hidden[step + tap], hidden[step + half + tap]], axis=1)
                for tap in range(3)
            ]
        )

    def last(step, product):
        news = []
        for offset in range(2):
            row = step + offset * half
            sums = product[:, offset * 128 : (offset + 1) * 128]
            entry = roll(from_left, -row)[:, :128]
            total = sums[CH : 2 * CH] + jnp.where(lane == 0, entry, roll(sums[0:CH], 1))
            entry = roll(from_right, 127 - block - row)[:, :128]
            total = total + jnp.where(lane == 127, entry, roll(sums[2 * CH : 3 * CH], -1))
            update = total * (0.5 * wet[row : row + 1, :].astype(F32))
            news.append(state[row].astype(F32) + update)
        out(step, *news)

    staggered(half, second, last)


def prepare(atm_in, atm_bias, ocn_in, ocn_bias, ocn_out, air_in, first, second, is_ocean):
    def bias_rows(ref, width):
        row = jnp.concatenate([ref[index : index + 1, :] for index in range(ref.shape[0])], axis=1)
        terms = list(split_bf16(row)) + [jnp.zeros_like(row)]
        bias = jnp.concatenate(terms, axis=0)
        return jnp.pad(bias, ((0, 0), (0, width - bias.shape[1])))

    @pl.when(is_ocean == 0)
    def _():
        columns = jnp.concatenate(
            [atm_in[...].astype(F32), bias_rows(atm_bias, HA), jnp.zeros((40, HA), F32)], axis=0
        )
        air_in[...] = columns.T.astype(BF16)

    @pl.when(is_ocean != 0)
    def _():
        bias = bias_rows(ocn_bias, 256)
        count = ocn_in.shape[2]
        for tap in range(3):
            whole = [ocn_in[3 * tap + side].astype(F32) for side in range(3)]
            whole = [jnp.pad(values, ((0, 0), (0, 256 - count))) for values in whole]
            rows = [values[:CH] for values in whole] + [values[CH:] for values in whole]
            rows.append(bias if tap == 0 else jnp.zeros((4, 256), F32))
            columns = jnp.concatenate(rows, axis=0).T
            first[:, tap * 256 : (tap + 1) * 256] = columns[:HIDK].astype(BF16)
        for tap in range(9):
            values = ocn_out[tap].astype(F32)
            second[tap * CH : (tap + 1) * CH, :] = jnp.pad(
                values, ((0, 0), (0, HIDP - count))
            ).astype(BF16)


def ends(flags):
    at_top, at_bottom, even = flags[1] != 0, flags[2] != 0, flags[3] == 0

    def up_and_down(one, two):
        above = jnp.where(even, two, one).astype(F32)
        below = jnp.where(even, one, two).astype(F32)
        return jnp.where(at_top, 0.0, above), jnp.where(at_bottom, 0.0, below)

    return up_and_down


def middle_kernel(d, opening, *refs):
    refs = list(refs)
    take = lambda count: [refs.pop(0) for _ in range(count)]
    flags, state, field_one, beside, field_two, from_one, from_two = take(7)
    if opening:
        planes, *far_weights = take(6)
    else:
        (plan_x,) = take(1)
    part_x, fields_x, rolled = take(3)
    if opening:
        plan_x, *made_weights = take(4)
    (coupled,) = take(1)
    if opening:
        *raw_weights, sems = take(6)
        copies = fetch(far_weights, raw_weights, sems)
    rows, tall = d.rows, d.tall
    is_ocean = flags[0]
    up_and_down = ends(flags)

    if opening:

        @pl.when(is_ocean != 0)
        def _():
            base = d.strip
            pair = up_and_down(from_one[base : base + 16, :], from_two[base : base + 16, :])
            plan_x[...] = jnp.zeros_like(plan_x)
            for step, strip in zip((0, rows + 2), pair):
                for index in range(2):
                    plan_x[pl.ds(step + index, 2 * NK, stride=tall), :] = strip[index * 8 : (index + 1) * 8]

        for plane in range(2 * NK):
            plan_x[plane * tall + 2 : plane * tall + 2 + rows, :] = planes[plane].astype(F32)

    for field in range(NS):
        pair = up_and_down(field_one[field], field_two[field])
        fields_x[field, 0:16, :] = pair[0][rows - 16 : rows]
        fields_x[field, 16 : 16 + rows, :] = beside[field].astype(F32)
        fields_x[field, 16 + rows : 32 + rows, :] = pair[1][0:16]

    unit = couple(fields_x, coupled, rows)

    @pl.when(is_ocean == 0)
    def _():
        regrid_inside(coupled, unit, plan_x, part_x, 2, rows // 8, tall)

    @pl.when(is_ocean != 0)
    def _():
        regrid_inside(coupled, unit, plan_x, part_x, 0, d.tiles, tall)
        upper, lower = up_and_down(from_one[0 : 2 * CH, :], from_two[0 : 2 * CH, :])
        roll_rows(state, upper.astype(BF16), lower.astype(BF16), rolled, d)

    if opening:
        for copy in copies:
            copy.wait()
        prepare(*raw_weights, *made_weights, is_ocean)


def step_kernel(d, opening, closing, *refs):
    refs = list(refs)
    take = lambda count: [refs.pop(0) for _ in range(count)]
    flags, state, wet, from_one, from_two, from_left, from_right = take(7)
    part_x, fields_x, rolled, edges, plan_x, air_in, first, second, atm_out = take(9)
    if not opening:
        (plan_e,) = take(1)
    if not closing:
        surface, places = take(2)
    (out,) = take(1)
    if not closing:
        fields, new_edges, one, two = take(4)
    if opening:
        (plan_e,) = take(1)
    window, forcing_x, forcing_y, stack, hidden, side, raw = take(7)
    if opening:
        (plan_y,) = take(1)
    rows, tall = d.rows, d.tall
    is_ocean, at_top, at_bottom = flags[0], flags[1], flags[2]
    up_and_down = ends(flags)

    if opening:

        @pl.when(is_ocean != 0)
        def _():
            plan_y[...] = jnp.zeros_like(plan_y)
            base = d.lead
            parts = [
                (ref[base : base + 16, :], ref[base + 16 + rows : base + 32 + rows, :],
                 ref[base + 16 : base + 16 + rows, :])
                for ref in (from_left, from_right)
            ]
            for plane in range(2 * NK):
                first_end, second_end, own = [
                    unpack_columns(left, right, plane, 2 * NK, 2) for left, right in zip(*parts)
                ]
                above, below = up_and_down(first_end, second_end)
                at = plane * tall
                plan_y[at : at + 2, :] = above[14:16]
                plan_y[at + 2 : at + 2 + rows, :] = own
                plan_y[at + 2 + rows : at + 4 + rows, :] = below[0:2]

    base = d.lead + (rows + 32 if opening else 0)
    parts = [
        (ref[base : base + 16, :], ref[base + 16 + rows : base + 32 + rows, :],
         ref[base + 16 : base + 16 + rows, :])
        for ref in (from_left, from_right)
    ]
    for field in range(NS):
        first_end, second_end, own = [
            unpack_columns(left, right, field, NS, REACH) for left, right in zip(*parts)
        ]
        above, below = up_and_down(first_end, second_end)
        for at, values in ((0, above), (16, own), (16 + rows, below)):
            count = values.shape[0]
            inside = roll(fields_x[field, at : at + count, :], 32)
            lane = lanes(values.shape)
            near = (lane >= 32 - REACH) & (lane < 32 + REACH)
            far = (lane < REACH) | (lane >= 128 - REACH)
            kept = jnp.where(near, inside, jnp.where(far, values, 0.0))
            window[field, at : at + count, :] = kept
    def finished():
        emission = None if closing else Emission(surface, flags, places, raw, d)

        def put(step, low, high):
            if closing:
                for row, values in ((step, low), (step + rows // 2, high)):
                    raw[pl.ds(row, CH, stride=rows), :] = values
                return
            out[step] = low.astype(BF16)
            out[step + rows // 2] = high.astype(BF16)

        def close():
            if not closing:
                emission.close(out, wet, fields, new_edges, one, two)

        return put, close

    @pl.when(is_ocean == 0)
    def _():
        if opening:
            plan_edges(plan_x, plan_y, plan_e, 2, rows // 8, tall, False)
        regrid_beside(
            window, plan_e, part_x, forcing_x, forcing_y, 2, rows // 8, tall, False
        )
        put, close = finished()
        air(state, put, forcing_x, air_in, atm_out, d)
        close()

    @pl.when(is_ocean != 0)
    def _():
        if opening:
            plan_edges(plan_x, plan_y, plan_e, 0, d.tiles, tall, True)
        regrid_beside(
            window, plan_e, part_x, forcing_x, forcing_y, 0, d.tiles, tall, True
        )
        put, close = finished()
        at, end = d.edge_rows, d.edge_rows + 16
        joined = [
            join_corners(
                get_edges(ref, 0, d), *up_and_down(ref[at:end, :], ref[end : end + 16, :]), d
            )
            for ref in (from_left, from_right)
        ]
        corners = up_and_down(from_one[2 * CH : d.strip, :], from_two[2 * CH : d.strip, :])
        own = join_corners(get_edges(edges, 0, d), *corners, d)
        sea(
            state, rolled, own, *joined, put, forcing_x, forcing_y,
            first, second, wet, at_top, at_bottom, stack, hidden, side, d,
        )
        close()

    if closing:
        out[...] = raw[...].reshape(CH, rows, 128).astype(BF16)


VMEM = pl.BlockSpec(memory_space=pltpu.VMEM)
HBM = pl.BlockSpec(memory_space=pltpu.HBM)
SMEM = pl.BlockSpec(memory_space=pltpu.SMEM)
PARAMS = pltpu.CompilerParams(vmem_limit_bytes=48 * 1024 * 1024)


def shape(*dims, dtype=BF16):
    return jax.ShapeDtypeStruct(dims, dtype)


def send(x, move):
    names = ("grp", "lat", "lon")
    sizes = [lax.axis_size(name) for name in names]
    pairs = []
    for group in range(sizes[0]):
        for lat in range(sizes[1]):
            for lon in range(sizes[2]):
                to = move(group, lat, lon)
                if to is None or not 0 <= to[1] < sizes[1]:
                    continue
                target = (to[0] * sizes[1] + to[1]) * sizes[2] + to[2] % sizes[2]
                pairs.append(((group * sizes[1] + lat) * sizes[2] + lon, target))
    return lax.ppermute(x, names, pairs)


def swap_rows(x, turn, across):
    count, columns = lax.axis_size("lat"), lax.axis_size("lon")

    def move(group, lat, lon):
        other = ((lat + turn) ^ 1) - turn
        if 0 <= other < count and (across or group == 1):
            return (1 - group if across else group), other, lon
        beside = lon ^ 1
        return group, lat, beside if beside < columns else lon

    return send(x, move)


def exchange(fields, own_edges, one, two, sides, d):
    rows = d.rows
    rest = fields * jnp.where(lax.axis_index("grp") > 1, 0, 1).astype(BF16)
    if sides is not None:
        field_two = swap_rows(fields, 1, True)
        from_one = swap_rows(one, 0, False)
        from_two = swap_rows(two, 1, False)
        field_one = swap_rows(rest, 0, True)
        beside = send(rest, lambda g, i, j: (1 - g, i, j))
        from_one, field_two = lax.optimization_barrier((from_one, field_two))
        from_two, from_one = lax.optimization_barrier((from_two, from_one))
        field_one, from_two = lax.optimization_barrier((field_one, from_two))
        beside, field_one, own_edges = lax.optimization_barrier((beside, field_one, own_edges))
    else:
        field_one = swap_rows(fields, 0, True)
        from_two = swap_rows(two, 1, False)
        from_one = swap_rows(one, 0, False)
        field_two = swap_rows(rest, 1, True)
        beside = send(rest, lambda g, i, j: (1 - g, i, j))
        from_two, field_one = lax.optimization_barrier((from_two, field_one))
        from_one, from_two = lax.optimization_barrier((from_one, from_two))
        field_two, from_one = lax.optimization_barrier((field_two, from_one))
        beside, field_two, own_edges = lax.optimization_barrier((beside, field_two, own_edges))
    odd = lax.axis_index("lat") % 2 == 1
    outer = [field_one[NS], field_two[NS]]
    if rows != 16:
        outer = [
            jnp.where(odd, outer[0][rows - 16 :], outer[0][:16]),
            jnp.where(odd, outer[1][:16], outer[1][rows - 16 :]),
        ]
    packed = [own_edges, from_one[2 * CH : d.strip], from_two[2 * CH : d.strip]]
    if sides is not None:
        packed += [from_one[d.strip + 16 :], sides, from_two[d.strip + 16 :]]
    packed += [outer[0], beside[NS], outer[1]]
    packed = jnp.concatenate(packed, axis=0)
    from_left = send(packed, lambda g, i, j: (g, i, j + 1))
    from_right = send(packed, lambda g, i, j: (g, i, j - 1))
    return (field_one, beside, field_two, from_one, from_two), (from_one, from_two, from_left, from_right)


def local(
    coupled_state, land_mask, regrid_offsets, regrid_weights, surface_proj,
    atm_in, atm_bias, atm_out, ocn_in, ocn_bias, ocn_out,
):
    rows = coupled_state.shape[2]
    assert coupled_state.shape[3] == 128
    d = Dims(rows)
    group = lax.axis_index("grp")
    lat = lax.axis_index("lat")
    flags = jnp.stack(
        [group, lat == 0, lat == lax.axis_size("lat") - 1, lat % 2]
    ).astype(jnp.int32)
    raw_weights = (
        atm_in.T,
        atm_bias.reshape(HA // 128, 128),
        jnp.transpose(ocn_in, (1, 2, 0)),
        ocn_bias[None],
        jnp.transpose(ocn_out, (1, 0, 2)),
    )
    state_shape = shape(rows, CH, 128)
    emitted = [
        shape(NS + 1, rows, 128),
        shape(d.edge_rows, 128),
        shape(d.strip, 128),
        shape(d.strip, 128),
    ]
    raw = pltpu.VMEM((rows * 8, 128), F32)
    turned = pltpu.VMEM((CH * rows, 128), F32)

    def call(kernel, operands, outs, scratch, name, far=()):
        scratch = scratch + [pltpu.VMEM(x.shape, x.dtype) for x in far]
        if far:
            scratch.append(pltpu.SemaphoreType.DMA((len(far) + CH // 16,)))

        far = [pltpu.with_memory_space_constraint(x, pltpu.HBM) for x in far]
        return pl.pallas_call(
            kernel,
            out_shape=outs,
            in_specs=[SMEM] + [VMEM] * len(operands) + [HBM] * len(far),
            out_specs=[VMEM] * len(outs),
            scratch_shapes=scratch,
            compiler_params=PARAMS,
            name=name,
        )(flags, *operands, *far)

    state, planes, sides, places, fields, edges, one, two = call(
        functools.partial(start_kernel, d),
        (),
        [state_shape, shape(2 * NK, rows, 128), shape(rows, 128), shape(rows * 128, d.edge)]
        + emitted[:2]
        + [shape(d.strip + 32, 128)] * 2,
        [raw, pltpu.VMEM((2 * NK * rows, 128), F32), turned],
        "start",
        (coupled_state[0], surface_proj, land_mask, regrid_offsets[0], regrid_weights[0]),
    )

    plan = shape(2 * NK * d.tall, 128, dtype=F32)
    between = [
        shape(NS * d.tall, 128, dtype=F32),
        shape(NS, rows + 32, 128, dtype=F32),
        shape(rows + 4, 3 * CH, 128),
    ]
    made = [shape(HA, 128), shape(HIDK, 768), shape(9 * CH, HIDP)]
    coupled = pltpu.VMEM((NS // 2, rows + 32, 128), jnp.int32)
    scratch = [
        pltpu.VMEM((NS, rows + 32, 128), F32),
        pltpu.VMEM((d.tall * 8, 128), F32),
        pltpu.VMEM((d.tall * 8, 128), F32),
        pltpu.VMEM((rows + 4, 256, 128), BF16),
        pltpu.VMEM((rows + 2, HIDP, 128), BF16),
        pltpu.VMEM((768, d.edge), BF16),
    ]

    vertical, horizontal = exchange(fields, edges, one, two, sides, d)
    *shared, plan_x, air_in, first, second = call(
        functools.partial(middle_kernel, d, True),
        (state, *vertical, planes),
        between + [plan] + made,
        [coupled],
        "first_middle",
        raw_weights,
    )
    weights = (air_in, first, second, atm_out)
    state, fields, edges, one, two, plan_e = call(
        functools.partial(step_kernel, d, True, False),
        (state, land_mask, *horizontal, *shared, edges, plan_x, *weights, surface_proj, places),
        [state_shape] + emitted + [shape(2 * d.tall, 128, dtype=F32)],
        scratch + [raw, pltpu.VMEM(plan.shape, F32)],
        "first_step",
    )

    vertical, horizontal = exchange(fields, edges, one, two, None, d)
    shared = call(
        functools.partial(middle_kernel, d, False),
        (state, *vertical, plan_x),
        between,
        [coupled],
        "second_middle",
    )
    (state,) = call(
        functools.partial(step_kernel, d, False, True),
        (state, land_mask, *horizontal, *shared, edges, plan_x, *weights, plan_e),
        [shape(CH, rows, 128)],
        scratch + [turned],
        "second_step",
    )
    return state[None]


def solution(mesh):
    return jax.shard_map(
        local,
        mesh=mesh,
        in_specs=(
            P("grp", None, "lat", "lon"),
            P("lat", "lon"),
            P("grp", None, None, "lat", "lon"),
            P("grp", None, "lat", "lon"),
            P(),
            P(),
            P(),
            P(),
            P(),
            P(),
            P(),
        ),
        out_specs=P("grp", None, "lat", "lon"),
        check_vma=False,
    )
```

```python
import functools

import jax
import jax.numpy as jnp
from jax import lax
from jax.experimental import pallas as pl
from jax.experimental.pallas import tpu as pltpu
from jax.sharding import PartitionSpec as P

CH = 80
NS = 4
NK = 4
HA = 384
HW = 8
SPAN = 2 * HW + 1
REACH = HW + 2
FIXED = 32767.0
HIDK = 208
HIDP = 256
F32 = jnp.float32
BF16 = jnp.bfloat16


def roll(x, shift, axis=1):
    size = x.shape[axis]
    if isinstance(shift, int):
        shift = shift % size
        if shift == 0:
            return x
    return pltpu.roll(x, shift, axis)


def lanes(shape):
    return lax.broadcasted_iota(jnp.int32, shape, len(shape) - 1)


def subs(shape):
    return lax.broadcasted_iota(jnp.int32, shape, len(shape) - 2)


class Dims:
    def __init__(self, rows):
        self.rows = rows
        self.block = 32 if rows + 4 <= 32 else 64
        self.edge = 4 * self.block
        self.pieces = self.edge // 128
        self.edge_rows = CH * self.pieces
        self.tiles = -(-(rows + 4) // 8)
        self.tall = 8 * self.tiles
        self.strip = 2 * CH + self.edge_rows


def put_edges(ref, at, edges, d):
    for piece in range(d.pieces):
        ref[at + piece * CH : at + (piece + 1) * CH, :] = edges[:, piece * 128 : (piece + 1) * 128]


def get_edges(ref, at, d):
    return jnp.concatenate(
        [ref[at + piece * CH : at + (piece + 1) * CH, :] for piece in range(d.pieces)], axis=1
    )


def edge_places(places, d):
    lane = lanes((1, d.edge))
    block = lane // d.block
    row = lane % d.block - 2
    column = jnp.where(block == 0, 126, jnp.where(block == 1, 0, jnp.where(block == 2, 127, 1)))
    own = (row >= 0) & (row < d.rows)
    target = jnp.where(own, column, -1)
    position = subs((128, d.edge))
    for step in range(d.rows):
        place = (position == jnp.where(row == step, target, -1)).astype(F32).astype(BF16)
        places[step * 128 : (step + 1) * 128, :] = place


def edge_columns(state, places, d):
    whole = jnp.concatenate([state[step] for step in range(d.rows)], axis=1)
    return jnp.dot(whole, places[...], preferred_element_type=F32).astype(BF16)


def pack_columns(values, reach):
    lane = lanes(values[0].shape)
    pitch = 128 // len(values)
    packed = jnp.zeros_like(values[0])
    for index, value in enumerate(values):
        at = index * pitch
        packed = jnp.where((lane >= at) & (lane < at + reach), roll(value, at), packed)
        at += reach
        packed = jnp.where((lane >= at) & (lane < at + reach), roll(value, at + reach - 128), packed)
    return packed


def unpack_columns(left, right, index, count, reach):
    at = index * (128 // count)
    left = roll(left.astype(F32), 128 - at - 2 * reach)
    return jnp.where(lanes(left.shape) < 64, roll(right.astype(F32), -at), left)


def strips(one, two, even, d):
    last = d.rows - 2
    return (one, jnp.where(even, last, 0)), (two, jnp.where(even, 0, last))


def split_bf16(values):
    high = values.astype(BF16).astype(F32)
    mid = (values - high).astype(BF16).astype(F32)
    return high, mid, values - high - mid


class Emission:
    def __init__(self, surface, flags, places, raw, d):
        gap = jnp.zeros((4, CH), F32)
        terms = []
        for term in split_bf16(surface[flags[0]]):
            terms += [term, gap]
        self.proj = jnp.concatenate(terms + [gap, gap], axis=0).astype(BF16)
        self.places, self.raw, self.d, self.flags = places, raw, d, flags

    def project(self, state):
        half = self.d.rows // 2
        products = []
        for step in range(half):
            pair = jnp.concatenate([state[step], state[step + half]], axis=1)
            products.append(jnp.dot(self.proj, pair, preferred_element_type=F32))
        whole = jnp.concatenate([state[step] for step in range(2 * half)], axis=1)
        edges = jnp.dot(whole, self.places[...], preferred_element_type=F32)
        for step, parts in enumerate(products):
            parts = parts[0:8] + parts[8:16] + parts[16:24]
            self.raw[step * 8 : step * 8 + 8, :] = parts[:, :128]
            self.raw[(step + half) * 8 : (step + half) * 8 + 8, :] = parts[:, 128:]
        return edges.astype(BF16)

    def close(self, state, wet, fields, own_edges, one, two):
        d, even = self.d, self.flags[3] == 0
        edges = self.project(state)
        keeping = jnp.where(self.flags[0] != 0, wet[...].astype(F32), 1.0)
        whole = [self.raw[pl.ds(field, d.rows, stride=8), :] * keeping for field in range(NS)]
        for field in range(NS):
            fields[field] = whole[field].astype(BF16)
        fields[NS] = pack_columns(whole, REACH).astype(BF16)
        put_edges(own_edges, 0, edges, d)
        row = lanes(edges.shape) % d.block
        downward = jnp.where(row < 2, roll(edges, -d.rows), jnp.zeros_like(edges))
        upward = jnp.where(
            (row >= d.rows + 2) & (row < d.rows + 4), roll(edges, d.rows), jnp.zeros_like(edges)
        )
        for (ref, first), down in zip(strips(one, two, even, d), (even, jnp.logical_not(even))):
            ref[0:CH, :] = state[first]
            ref[CH : 2 * CH, :] = state[first + 1]
            put_edges(ref, 2 * CH, jnp.where(down, downward, upward), d)


def fetch(sources, targets, sems):
    copies = [
        pltpu.make_async_copy(source, target, sems.at[index])
        for index, (source, target) in enumerate(zip(sources, targets))
    ]
    for copy in copies:
        copy.start()
    return copies


def start_kernel(
    d, flags, far_given, far_surface, far_wet, far_offsets, far_weights,
    state, planes, sides, places, fields, own_edges, one, two,
    raw, tall, turned, given, surface, wet, offsets, weights, sems,
):
    rows = d.rows
    pieces = [pl.ds(at, 16) for at in range(0, CH, 16)]
    copies = fetch(
        [far_given.at[piece] for piece in pieces] + [far_surface, far_wet, far_offsets, far_weights],
        [given.at[piece] for piece in pieces] + [surface, wet, offsets, weights],
        sems,
    )
    edge_places(places, d)
    for index, piece in enumerate(pieces):
        copies[index].wait()
        turned[index * 16 * rows : (index + 1) * 16 * rows, :] = (
            given[piece].astype(F32).reshape(16 * rows, 128)
        )
    for row in range(rows):
        state[row] = turned[pl.ds(row, CH, stride=rows), :].astype(BF16)
    for copy in copies[len(pieces) :]:
        copy.wait()
    emission = Emission(surface, flags, places, raw, d)
    emission.close(state, wet, fields, own_edges, one, two)
    for k in range(NK):
        code = (offsets[0, k] * SPAN + offsets[1, k]).astype(F32)
        tall[k * rows : (k + 1) * rows, :] = code
        tall[(NK + k) * rows : (NK + k + 1) * rows, :] = weights[k]
        planes[k] = code.astype(BF16)
        planes[NK + k] = weights[k].astype(BF16)
    packed = pack_columns([tall[plane * rows : (plane + 1) * rows, :] for plane in range(2 * NK)], 2)
    sides[...] = packed.astype(BF16)
    even = flags[3] == 0
    for (ref, first), down in zip(strips(one, two, even, d), (even, jnp.logical_not(even))):
        strip = [tall[pl.ds(first + step, 2 * NK, stride=rows), :] for step in range(2)]
        ref[d.strip : d.strip + 16, :] = jnp.concatenate(strip, axis=0).astype(BF16)
        ref[d.strip + 16 : d.strip + 32, :] = jnp.where(
            down, packed[rows - 16 : rows], packed[0:16]
        ).astype(BF16)


def decode(code):
    shifted = code.astype(jnp.int32) + (HW * SPAN + HW)
    rows = lax.shift_right_logical(shifted * 241, 12)
    return rows - HW, shifted - rows * SPAN - HW


def along_lanes(values, index):
    numbers = lax.GatherDimensionNumbers(
        offset_dims=(),
        collapsed_slice_dims=(1,),
        start_index_map=(1,),
        operand_batching_dims=(0,),
        start_indices_batching_dims=(0,),
    )
    return lax.gather(
        values, index[..., None], numbers, (1, 1), mode=lax.GatherScatterMode.PROMISE_IN_BOUNDS
    )


def couple(fields, coupled, rows):
    largest = None
    for field in range(NS):
        here = jnp.max(jnp.abs(fields[field]), axis=0, keepdims=True)
        largest = here if largest is None else jnp.maximum(largest, here)
    largest = jnp.maximum(jnp.max(largest, axis=1, keepdims=True), 1e-30)
    scale = FIXED / largest
    for pair in range(NS // 2):
        high, low = [
            jnp.floor(fields[2 * pair + part] * scale + 0.5).astype(jnp.int32) for part in range(2)
        ]
        coupled[pair] = high * (1 << 16) + (low + (1 << 15))
    return largest * (1 / FIXED)


def uncouple(values):
    high = lax.shift_right_arithmetic(values, 16)
    low = (values & 0xFFFF) - (1 << 15)
    return high.astype(F32), low.astype(F32)


def select_rows(source, start, picks):
    parts = source.shape[0]
    blank = jnp.full((8, 128), 1 << 15, jnp.int32) if parts < NS else jnp.zeros((8, 128), F32)
    chosen = [[blank for _ in range(parts)] for _ in picks]
    for shift in range(-HW, HW + 1):
        at = pl.ds(start + shift, 8)
        values = [source[part, at, :] for part in range(parts)]
        for slot, (rows, index, allowed) in enumerate(picks):
            here = (rows == shift) & allowed
            for part in range(parts):
                picked = along_lanes(values[part], index)
                chosen[slot][part] = jnp.where(here, picked, chosen[slot][part])
    if parts == NS:
        return chosen
    return [[part for values in pairs for part in uncouple(values)] for pairs in chosen]


def regrid_inside(coupled, unit, plan_x, part_x, first, tiles, tall):
    lane = lanes((8, 128))
    for step in range(tiles):
        at = first + step * 8
        picks = []
        weights = []
        for k in range(NK):
            rows, cols = decode(plan_x[pl.ds(k * tall + at, 8), :])
            weights.append(plan_x[pl.ds((NK + k) * tall + at, 8), :] * unit)
            column = lane + cols
            picks.append((rows, column & 127, (column >= 0) & (column < 128)))
        chosen = select_rows(coupled, at + 14, picks)
        for field in range(NS):
            total = chosen[0][field] * weights[0]
            for k in range(1, NK):
                total = total + chosen[k][field] * weights[k]
            part_x[pl.ds(field * tall + at, 8), :] = total


def edge_lanes():
    lane = lanes((8, 128))
    return ((lane + 8) & 127) // 32, ((lane + 8) & 31) - 8


def plan_edges(plan_x, plan_y, plan_e, first, tiles, tall, sides):
    part, place = edge_lanes()
    outer = place >= 8
    for step in range(tiles):
        at = first + step * 8
        code = jnp.zeros((8, 128), F32)
        weight = jnp.zeros((8, 128), F32)
        for k in range(NK):
            edge_code = roll(plan_x[pl.ds(k * tall + at, 8), :], 32 * k)
            edge_weight = roll(plan_x[pl.ds((NK + k) * tall + at, 8), :], 32 * k)
            if sides:
                edge_code = jnp.where(
                    outer, roll(plan_y[pl.ds(k * tall + at, 8), :], 32 * k + 16), edge_code
                )
                edge_weight = jnp.where(
                    outer, roll(plan_y[pl.ds((NK + k) * tall + at, 8), :], 32 * k + 16), edge_weight
                )
            code = jnp.where(part == k, edge_code, code)
            weight = jnp.where(part == k, edge_weight, weight)
        plan_e[pl.ds(at, 8), :] = code
        plan_e[pl.ds(tall + at, 8), :] = weight


def regrid_beside(window, plan_e, part_x, forcing_x, forcing_y, first, tiles, tall, sides):
    lane = lanes((8, 128))
    part, place = edge_lanes()
    outer = place >= 8
    inner_column = place & 127
    outer_column = jnp.where(place < 16, place - 16, place + 112)
    edge = (lane < 8) | (lane >= 120)
    for step in range(tiles):
        at = first + step * 8
        rows, cols = decode(plan_e[pl.ds(at, 8), :])
        weight = plan_e[pl.ds(tall + at, 8), :]
        column = jnp.where(outer, outer_column, inner_column) + cols
        within = (column >= 0) & (column < 128)
        index = jnp.where(within, column + 32, column) & 127
        (chosen,) = select_rows(window, at + 14, [(rows, index, outer | jnp.logical_not(within))])
        for field in range(NS):
            part_sum = chosen[field] * weight
            extra = part_sum
            for k in range(1, NK):
                extra = extra + roll(part_sum, -32 * k)
            total = part_x[pl.ds(field * tall + at, 8), :] + jnp.where(edge, extra, 0.0)
            forcing_x[pl.ds(at * 8 + field, 8, stride=8), :] = total
            forcing_x[pl.ds(at * 8 + field + 4, 8, stride=8), :] = total
            if sides:
                extra = roll(extra, -16)
                forcing_y[pl.ds(at * 8 + field, 8, stride=8), :] = extra
                forcing_y[pl.ds(at * 8 + field + 4, 8, stride=8), :] = extra


def twice_gelu(x):
    scale = (2 / jnp.pi) ** 0.5
    return x + x * jnp.tanh(x * (scale + (scale * 0.044715) * (x * x)))


def staggered(count, *stages):
    values = [{} for _ in stages]
    for turn in range(count + len(stages) - 1):
        for index, stage in enumerate(stages):
            step = turn - index
            if 0 <= step < count:
                given = values[index - 1].pop(step) if index else None
                values[index][step] = stage(step, given)


def air(state, out, forcing_x, air_in, atm_out, d):
    half = d.rows // 2
    leading = subs((8, 128)) < 4
    blank = jnp.zeros((32, 128), BF16)

    def inputs(row):
        at = (row + 2) * 8
        forced = jnp.where(leading, forcing_x[at : at + 8, :], 1.0)
        forced = jnp.concatenate([forced, jnp.zeros_like(forced)], axis=0).astype(BF16)
        return jnp.concatenate([state[row], forced, blank], axis=0)

    def first(step, _):
        pair = jnp.concatenate([inputs(step), inputs(step + half)], axis=1)
        return jnp.dot(air_in[...], pair, preferred_element_type=F32)

    def middle(step, product):
        return twice_gelu(product).astype(BF16)

    def second(step, hidden):
        return jnp.dot(atm_out[...], hidden, preferred_element_type=F32)

    def last(step, update):
        news = []
        for offset in range(2):
            change = update[:, offset * 128 : (offset + 1) * 128]
            news.append(state[step + offset * half].astype(F32) + 0.5 * change)
        out(step, *news)

    staggered(half, first, middle, second, last)


def edge_forcing(forcing_x, forcing_y, d):
    lane = lanes((8, d.edge))
    block = lane // d.block
    row = lane % d.block

    inner = outer = jnp.zeros((8, d.edge), F32)
    for step in range(d.rows + 4):
        at = pl.ds(step * 8, 8)
        pad = [jnp.zeros((8, 128), F32)] * (d.pieces - 1)
        here = jnp.concatenate([forcing_x[at, :]] + pad, axis=1)
        there = jnp.concatenate([forcing_y[at, :]] + pad, axis=1)
        for index, column in enumerate((126, 0, 127, 1)):
            shift = step + index * d.block - column
            match = (block == index) & (row == step)
            if column in (0, 127):
                inner = jnp.where(match, roll(here, shift), inner)
            outer = jnp.where(match, roll(there, shift), outer)
    return inner, outer


def roll_rows(state, upper, lower, rolled, d):
    def put(row, values):
        rolled[row, 0:CH, :] = roll(values, 1)
        rolled[row, CH : 2 * CH, :] = values
        rolled[row, 2 * CH : 3 * CH, :] = roll(values, -1)

    for step in range(2):
        put(step, upper[step * CH : (step + 1) * CH, :])
        put(d.rows + 2 + step, lower[step * CH : (step + 1) * CH, :])
    for row in range(d.rows):
        put(row + 2, state[row])


def sea(
    state, rolled, edges, left, right, out, forcing_x, forcing_y, ocn_in, ocn_out, wet,
    at_top, at_bottom, stack, hidden, side, d,
):
    rows, block = d.rows, d.block
    lane = lanes((CH, 128))
    spot = lanes((CH, d.edge))
    part = spot // block
    inner = edges
    outer = jnp.where((part == 0) | (part == 2), left, right)

    def sides_of(inner, outer, spot):
        first = spot < block
        return (
            jnp.where(first, outer, roll(inner, -block)),
            jnp.where(first, roll(outer, -2 * block), outer),
            jnp.where(first, roll(inner, -block), roll(outer, -2 * block)),
        )

    beside = sides_of(inner, outer, spot)
    middle = beside[1]
    force_in, force_out = edge_forcing(forcing_x, forcing_y, d)
    beside_forcing = sides_of(force_in, force_out, lanes((8, d.edge)))
    sub = subs((8, d.edge))
    ones = jnp.ones((8, d.edge), F32)
    forced = jnp.concatenate(
        [
            jnp.where(sub < 4, beside_forcing[0], beside_forcing[1]),
            jnp.where(sub < 4, beside_forcing[2], ones),
        ],
        axis=0,
    ).astype(BF16)
    columns = jnp.concatenate(list(beside) + [forced], axis=0)
    for tap in range(3):
        side[tap * 256 : (tap + 1) * 256, :] = roll(columns, -tap)

    sub_row = subs((8, 128))
    lane_row = lanes((8, 128))

    for row in range(rows + 4):
        entry = roll(middle, -row)[:, :128]
        stack[row, 0:CH, :] = jnp.where(lane == 0, entry, rolled[row, 0:CH, :])
        stack[row, CH : 2 * CH, :] = rolled[row, CH : 2 * CH, :]
        entry = roll(middle, 127 - block - row)[:, :128]
        stack[row, 2 * CH : 3 * CH, :] = jnp.where(lane == 127, entry, rolled[row, 2 * CH : 3 * CH, :])
        here, there = forcing_x[row * 8 : row * 8 + 8, :], forcing_y[row * 8 : row * 8 + 8, :]
        before = roll(jnp.where(lane_row == 127, there, here), 1)
        after = roll(jnp.where(lane_row == 0, there, here), -1)
        stack[row, 3 * CH : 256, :] = jnp.concatenate(
            [jnp.where(sub_row < 4, before, here), jnp.where(sub_row < 4, after, 1.0)], axis=0
        ).astype(BF16)

    pairs = (rows + 2) // 2

    def first(step, _):
        taps = jnp.concatenate(
            [
                stack[step : step + 3].reshape(3 * 256, 128),
                stack[step + pairs : step + pairs + 3].reshape(3 * 256, 128),
            ],
            axis=1,
        )
        return jnp.dot(ocn_in[...], taps, preferred_element_type=F32)

    def activate(step, product):
        active = twice_gelu(product)
        low, high = active[:, :128], active[:, 128:]
        if step == 0:
            low = jnp.where(at_top != 0, 0.0, low)
        if step == pairs - 1:
            high = jnp.where(at_bottom != 0, 0.0, high)
        hidden[step, 0:HIDK, :] = low.astype(BF16)
        hidden[step + pairs, 0:HIDK, :] = high.astype(BF16)
        blank = jnp.zeros((HIDP - HIDK, 128), BF16)
        hidden[step, HIDK:HIDP, :] = blank
        hidden[step + pairs, HIDK:HIDP, :] = blank

    staggered(pairs, first, activate)
    product = jnp.dot(ocn_in[...], side[...], preferred_element_type=F32)
    spot = lanes((1, d.edge)) % block
    gone = ((spot == 0) & (at_top != 0)) | ((spot == rows + 1) & (at_bottom != 0))
    active = jnp.where(gone, 0.0, twice_gelu(product)).astype(BF16)
    active = jnp.concatenate([active, jnp.zeros((HIDP - HIDK, d.edge), BF16)], axis=0)

    taps = jnp.concatenate([roll(active, -tap) for tap in range(3)], axis=0)
    from_left = jnp.dot(ocn_out[0:CH, :], taps, preferred_element_type=F32)
    from_right = jnp.dot(ocn_out[2 * CH : 3 * CH, :], taps, preferred_element_type=F32)
    half = rows // 2

    def second(step, _):
        taps = jnp.concatenate(
            [
                hidden[step : step + 3].reshape(3 * HIDP, 128),
                hidden[step + half : step + half + 3].reshape(3 * HIDP, 128),
            ],
            axis=1,
        )
        return jnp.dot(ocn_out[...], taps, preferred_element_type=F32)

    def last(step, product):
        news = []
        for offset in range(2):
            row = step + offset * half
            sums = product[:, offset * 128 : (offset + 1) * 128]
            entry = roll(from_left, -row)[:, :128]
            total = sums[CH : 2 * CH] + jnp.where(lane == 0, entry, roll(sums[0:CH], 1))
            entry = roll(from_right, 127 - block - row)[:, :128]
            total = total + jnp.where(lane == 127, entry, roll(sums[2 * CH : 3 * CH], -1))
            update = total * (0.5 * wet[row : row + 1, :].astype(F32))
            news.append(state[row].astype(F32) + update)
        out(step, *news)

    staggered(half, second, last)


def prepare(atm_in, atm_bias, ocn_in, ocn_bias, ocn_out, air_in, first, second, is_ocean):
    def bias_rows(ref, width):
        row = jnp.concatenate([ref[index : index + 1, :] for index in range(ref.shape[0])], axis=1)
        terms = list(split_bf16(row)) + [jnp.zeros_like(row)]
        bias = jnp.concatenate(terms, axis=0)
        return jnp.pad(bias, ((0, 0), (0, width - bias.shape[1])))

    @pl.when(is_ocean == 0)
    def _():
        columns = jnp.concatenate(
            [atm_in[...].astype(F32), bias_rows(atm_bias, HA), jnp.zeros((40, HA), F32)], axis=0
        )
        air_in[...] = columns.T.astype(BF16)

    @pl.when(is_ocean != 0)
    def _():
        bias = bias_rows(ocn_bias, 256)
        count = ocn_in.shape[2]
        for tap in range(3):
            whole = [ocn_in[3 * tap + side].astype(F32) for side in range(3)]
            whole = [jnp.pad(values, ((0, 0), (0, 256 - count))) for values in whole]
            rows = [values[:CH] for values in whole] + [values[CH:] for values in whole]
            rows.append(bias if tap == 0 else jnp.zeros((4, 256), F32))
            columns = jnp.concatenate(rows, axis=0).T
            first[:, tap * 256 : (tap + 1) * 256] = columns[:HIDK].astype(BF16)
        for tap in range(9):
            values = ocn_out[tap].astype(F32)
            at, column = tap // 3 * HIDP, tap % 3
            second[column * CH : (column + 1) * CH, at : at + HIDP] = jnp.pad(
                values, ((0, 0), (0, HIDP - count))
            ).astype(BF16)


def ends(flags):
    at_top, at_bottom, even = flags[1] != 0, flags[2] != 0, flags[3] == 0

    def up_and_down(one, two):
        above = jnp.where(even, two, one).astype(F32)
        below = jnp.where(even, one, two).astype(F32)
        return jnp.where(at_top, 0.0, above), jnp.where(at_bottom, 0.0, below)

    return up_and_down


def middle_kernel(d, opening, *refs):
    refs = list(refs)
    take = lambda count: [refs.pop(0) for _ in range(count)]
    flags, state, field_one, beside, field_two, from_one, from_two = take(7)
    if opening:
        planes, *far_weights = take(6)
    else:
        (plan_x,) = take(1)
    part_x, fields_x, rolled = take(3)
    if opening:
        plan_x, *made_weights = take(4)
    (coupled,) = take(1)
    if opening:
        *raw_weights, sems = take(6)
        copies = fetch(far_weights, raw_weights, sems)
    rows, tall = d.rows, d.tall
    is_ocean = flags[0]
    up_and_down = ends(flags)

    if opening:

        @pl.when(is_ocean != 0)
        def _():
            base = d.strip
            pair = up_and_down(from_one[base : base + 16, :], from_two[base : base + 16, :])
            plan_x[...] = jnp.zeros_like(plan_x)
            for step, strip in zip((0, rows + 2), pair):
                for index in range(2):
                    plan_x[pl.ds(step + index, 2 * NK, stride=tall), :] = strip[index * 8 : (index + 1) * 8]

        for plane in range(2 * NK):
            plan_x[plane * tall + 2 : plane * tall + 2 + rows, :] = planes[plane].astype(F32)

    for field in range(NS):
        pair = up_and_down(field_one[field], field_two[field])
        fields_x[field, 0:16, :] = pair[0][rows - 16 : rows]
        fields_x[field, 16 : 16 + rows, :] = beside[field].astype(F32)
        fields_x[field, 16 + rows : 32 + rows, :] = pair[1][0:16]

    unit = couple(fields_x, coupled, rows)

    @pl.when(is_ocean == 0)
    def _():
        regrid_inside(coupled, unit, plan_x, part_x, 2, rows // 8, tall)

    @pl.when(is_ocean != 0)
    def _():
        regrid_inside(coupled, unit, plan_x, part_x, 0, d.tiles, tall)
        upper, lower = up_and_down(from_one[0 : 2 * CH, :], from_two[0 : 2 * CH, :])
        roll_rows(state, upper.astype(BF16), lower.astype(BF16), rolled, d)

    if opening:
        for copy in copies:
            copy.wait()
        prepare(*raw_weights, *made_weights, is_ocean)


def step_kernel(d, opening, closing, *refs):
    refs = list(refs)
    take = lambda count: [refs.pop(0) for _ in range(count)]
    flags, state, wet, from_left, from_right = take(5)
    part_x, fields_x, rolled, edges, plan_x, air_in, first, second, atm_out = take(9)
    if not opening:
        (plan_e,) = take(1)
    if not closing:
        surface, places = take(2)
    (out,) = take(1)
    if not closing:
        fields, new_edges, one, two = take(4)
    if opening:
        (plan_e,) = take(1)
    window, forcing_x, forcing_y, stack, hidden, side, raw = take(7)
    if opening:
        (plan_y,) = take(1)
    rows, tall = d.rows, d.tall
    is_ocean, at_top, at_bottom = flags[0], flags[1], flags[2]
    up_and_down = ends(flags)

    if opening:

        @pl.when(is_ocean != 0)
        def _():
            plan_y[...] = jnp.zeros_like(plan_y)
            base = d.edge_rows
            parts = [
                (ref[base : base + 16, :], ref[base + 16 + rows : base + 32 + rows, :],
                 ref[base + 16 : base + 16 + rows, :])
                for ref in (from_left, from_right)
            ]
            for plane in range(2 * NK):
                first_end, second_end, own = [
                    unpack_columns(left, right, plane, 2 * NK, 2) for left, right in zip(*parts)
                ]
                above, below = up_and_down(first_end, second_end)
                at = plane * tall
                plan_y[at : at + 2, :] = above[14:16]
                plan_y[at + 2 : at + 2 + rows, :] = own
                plan_y[at + 2 + rows : at + 4 + rows, :] = below[0:2]

    base = d.edge_rows + (rows + 32 if opening else 0)
    parts = [
        (ref[base : base + 16, :], ref[base + 16 + rows : base + 32 + rows, :],
         ref[base + 16 : base + 16 + rows, :])
        for ref in (from_left, from_right)
    ]
    for field in range(NS):
        first_end, second_end, own = [
            unpack_columns(left, right, field, NS, REACH) for left, right in zip(*parts)
        ]
        above, below = up_and_down(first_end, second_end)
        for at, values in ((0, above), (16, own), (16 + rows, below)):
            count = values.shape[0]
            inside = roll(fields_x[field, at : at + count, :], 32)
            lane = lanes(values.shape)
            near = (lane >= 32 - REACH) & (lane < 32 + REACH)
            far = (lane < REACH) | (lane >= 128 - REACH)
            kept = jnp.where(near, inside, jnp.where(far, values, 0.0))
            window[field, at : at + count, :] = kept
    def finished():
        emission = None if closing else Emission(surface, flags, places, raw, d)

        def put(step, low, high):
            if closing:
                for row, values in ((step, low), (step + rows // 2, high)):
                    raw[pl.ds(row, CH, stride=rows), :] = values
                return
            out[step] = low.astype(BF16)
            out[step + rows // 2] = high.astype(BF16)

        def close():
            if not closing:
                emission.close(out, wet, fields, new_edges, one, two)

        return put, close

    @pl.when(is_ocean == 0)
    def _():
        if opening:
            plan_edges(plan_x, plan_y, plan_e, 2, rows // 8, tall, False)
        regrid_beside(
            window, plan_e, part_x, forcing_x, forcing_y, 2, rows // 8, tall, False
        )
        put, close = finished()
        air(state, put, forcing_x, air_in, atm_out, d)
        close()

    @pl.when(is_ocean != 0)
    def _():
        if opening:
            plan_edges(plan_x, plan_y, plan_e, 0, d.tiles, tall, True)
        regrid_beside(
            window, plan_e, part_x, forcing_x, forcing_y, 0, d.tiles, tall, True
        )
        put, close = finished()
        joined = [get_edges(ref, 0, d) for ref in (from_left, from_right)]
        sea(
            state, rolled, get_edges(edges, 0, d), *joined, put, forcing_x, forcing_y,
            first, second, wet, at_top, at_bottom, stack, hidden, side, d,
        )
        close()

    if closing:
        out[...] = raw[...].reshape(CH, rows, 128).astype(BF16)


VMEM = pl.BlockSpec(memory_space=pltpu.VMEM)
HBM = pl.BlockSpec(memory_space=pltpu.HBM)
SMEM = pl.BlockSpec(memory_space=pltpu.SMEM)
PARAMS = pltpu.CompilerParams(vmem_limit_bytes=48 * 1024 * 1024)


def shape(*dims, dtype=BF16):
    return jax.ShapeDtypeStruct(dims, dtype)


def send(x, move):
    names = ("grp", "lat", "lon")
    sizes = [lax.axis_size(name) for name in names]
    pairs = []
    for group in range(sizes[0]):
        for lat in range(sizes[1]):
            for lon in range(sizes[2]):
                to = move(group, lat, lon)
                if to is None or not 0 <= to[1] < sizes[1]:
                    continue
                target = (to[0] * sizes[1] + to[1]) * sizes[2] + to[2] % sizes[2]
                pairs.append(((group * sizes[1] + lat) * sizes[2] + lon, target))
    return lax.ppermute(x, names, pairs)


def swap_rows(x, turn, across):
    count, columns = lax.axis_size("lat"), lax.axis_size("lon")

    def move(group, lat, lon):
        other = ((lat + turn) ^ 1) - turn
        if 0 <= other < count and (across or group == 1):
            return (1 - group if across else group), other, lon
        beside = lon ^ 1
        return group, lat, beside if beside < columns else lon

    return send(x, move)


def exchange(fields, own_edges, one, two, sides, d):
    rows = d.rows
    scale = jnp.where(lax.axis_index("grp") > 1, 0, 1).astype(BF16)
    later = fields * scale
    beside = send(fields, lambda g, i, j: (1 - g, i, j))
    from_one = swap_rows(one, 0, False)
    from_two = swap_rows(two, 1, False)
    field_one = swap_rows(later, 0, True)
    field_two = swap_rows(later, 1, True)
    beside, from_one = lax.optimization_barrier((beside, from_one))
    from_two, beside = lax.optimization_barrier((from_two, beside))
    field_one, from_two = lax.optimization_barrier((field_one, from_two))
    field_two, field_one = lax.optimization_barrier((field_two, field_one))
    lat, count = lax.axis_index("lat"), lax.axis_size("lat")
    odd = lat % 2 == 1
    edges = own_edges
    for turn, ref in ((0, from_one), (1, from_two)):
        other = ((lat + turn) ^ 1) - turn
        there = (other >= 0) & (other < count)
        edges = edges + jnp.where(there, ref[2 * CH : d.strip], 0)
    outer = [field_one[NS], field_two[NS]]
    if rows != 16:
        outer = [
            jnp.where(odd, outer[0][rows - 16 :], outer[0][:16]),
            jnp.where(odd, outer[1][:16], outer[1][rows - 16 :]),
        ]
    packed = [edges]
    if sides is not None:
        packed += [from_one[d.strip + 16 :], sides, from_two[d.strip + 16 :]]
    packed += [outer[0], beside[NS], outer[1]]
    packed = jnp.concatenate(packed, axis=0)
    from_left = send(packed, lambda g, i, j: (g, i, j + 1))
    from_right = send(packed, lambda g, i, j: (g, i, j - 1))
    return (field_one, beside, field_two, from_one, from_two), (from_left, from_right), edges


def local(
    coupled_state, land_mask, regrid_offsets, regrid_weights, surface_proj,
    atm_in, atm_bias, atm_out, ocn_in, ocn_bias, ocn_out,
):
    rows = coupled_state.shape[2]
    assert coupled_state.shape[3] == 128
    d = Dims(rows)
    group = lax.axis_index("grp")
    lat = lax.axis_index("lat")
    flags = jnp.stack(
        [group, lat == 0, lat == lax.axis_size("lat") - 1, lat % 2]
    ).astype(jnp.int32)
    raw_weights = (
        atm_in.T,
        atm_bias.reshape(HA // 128, 128),
        jnp.transpose(ocn_in, (1, 2, 0)),
        ocn_bias[None],
        jnp.transpose(ocn_out, (1, 0, 2)),
    )
    state_shape = shape(rows, CH, 128)
    emitted = [
        shape(NS + 1, rows, 128),
        shape(d.edge_rows, 128),
        shape(d.strip, 128),
        shape(d.strip, 128),
    ]
    raw = pltpu.VMEM((rows * 8, 128), F32)
    turned = pltpu.VMEM((CH * rows, 128), F32)

    def call(kernel, operands, outs, scratch, name, far=()):
        scratch = scratch + [pltpu.VMEM(x.shape, x.dtype) for x in far]
        if far:
            scratch.append(pltpu.SemaphoreType.DMA((len(far) + CH // 16,)))

        far = [pltpu.with_memory_space_constraint(x, pltpu.HBM) for x in far]
        return pl.pallas_call(
            kernel,
            out_shape=outs,
            in_specs=[SMEM] + [VMEM] * len(operands) + [HBM] * len(far),
            out_specs=[VMEM] * len(outs),
            scratch_shapes=scratch,
            compiler_params=PARAMS,
            name=name,
        )(flags, *operands, *far)

    state, planes, sides, places, fields, edges, one, two = call(
        functools.partial(start_kernel, d),
        (),
        [state_shape, shape(2 * NK, rows, 128), shape(rows, 128), shape(rows * 128, d.edge)]
        + emitted[:2]
        + [shape(d.strip + 32, 128)] * 2,
        [raw, pltpu.VMEM((2 * NK * rows, 128), F32), turned],
        "start",
        (coupled_state[0], surface_proj, land_mask, regrid_offsets[0], regrid_weights[0]),
    )

    plan = shape(2 * NK * d.tall, 128, dtype=F32)
    between = [
        shape(NS * d.tall, 128, dtype=F32),
        shape(NS, rows + 32, 128, dtype=F32),
        shape(rows + 4, 3 * CH, 128),
    ]
    made = [shape(HA, 128), shape(HIDK, 768), shape(3 * CH, 3 * HIDP)]
    coupled = pltpu.VMEM((NS // 2, rows + 32, 128), jnp.int32)
    scratch = [
        pltpu.VMEM((NS, rows + 32, 128), F32),
        pltpu.VMEM((d.tall * 8, 128), F32),
        pltpu.VMEM((d.tall * 8, 128), F32),
        pltpu.VMEM((rows + 4, 256, 128), BF16),
        pltpu.VMEM((rows + 2, HIDP, 128), BF16),
        pltpu.VMEM((768, d.edge), BF16),
    ]

    vertical, horizontal, edges = exchange(fields, edges, one, two, sides, d)
    *shared, plan_x, air_in, first, second = call(
        functools.partial(middle_kernel, d, True),
        (state, *vertical, planes),
        between + [plan] + made,
        [coupled],
        "first_middle",
        raw_weights,
    )
    weights = (air_in, first, second, atm_out)
    state, fields, edges, one, two, plan_e = call(
        functools.partial(step_kernel, d, True, False),
        (state, land_mask, *horizontal, *shared, edges, plan_x, *weights, surface_proj, places),
        [state_shape] + emitted + [shape(2 * d.tall, 128, dtype=F32)],
        scratch + [raw, pltpu.VMEM(plan.shape, F32)],
        "first_step",
    )

    vertical, horizontal, edges = exchange(fields, edges, one, two, None, d)
    shared = call(
        functools.partial(middle_kernel, d, False),
        (state, *vertical, plan_x),
        between,
        [coupled],
        "second_middle",
    )
    (state,) = call(
        functools.partial(step_kernel, d, False, True),
        (state, land_mask, *horizontal, *shared, edges, plan_x, *weights, plan_e),
        [shape(CH, rows, 128)],
        scratch + [turned],
        "second_step",
    )
    return state[None]


def solution(mesh):
    return jax.shard_map(
        local,
        mesh=mesh,
        in_specs=(
            P("grp", None, "lat", "lon"),
            P("lat", "lon"),
            P("grp", None, None, "lat", "lon"),
            P("grp", None, "lat", "lon"),
            P(),
            P(),
            P(),
            P(),
            P(),
            P(),
            P(),
        ),
        out_specs=P("grp", None, "lat", "lon"),
        check_vma=False,
    )
```

```python
import functools

import jax
import jax.numpy as jnp
from jax import lax
from jax.experimental import pallas as pl
from jax.experimental.pallas import tpu as pltpu
from jax.sharding import PartitionSpec as P

CH = 80
NS = 4
NK = 4
HA = 384
HW = 8
SPAN = 2 * HW + 1
REACH = HW + 2
FIXED = 32767.0
HIDK = 208
HIDP = 256
F32 = jnp.float32
BF16 = jnp.bfloat16


def roll(x, shift, axis=1):
    size = x.shape[axis]
    if isinstance(shift, int):
        shift = shift % size
        if shift == 0:
            return x
    return pltpu.roll(x, shift, axis)


def lanes(shape):
    return lax.broadcasted_iota(jnp.int32, shape, len(shape) - 1)


def subs(shape):
    return lax.broadcasted_iota(jnp.int32, shape, len(shape) - 2)


class Dims:
    def __init__(self, rows):
        self.rows = rows
        self.block = 32 if rows + 4 <= 32 else 64
        self.edge = 4 * self.block
        self.pieces = self.edge // 128
        self.edge_rows = CH * self.pieces
        self.tiles = -(-(rows + 4) // 8)
        self.tall = 8 * self.tiles
        self.strip = 2 * CH + self.edge_rows


def put_edges(ref, at, edges, d):
    for piece in range(d.pieces):
        ref[at + piece * CH : at + (piece + 1) * CH, :] = edges[:, piece * 128 : (piece + 1) * 128]


def get_edges(ref, at, d):
    return jnp.concatenate(
        [ref[at + piece * CH : at + (piece + 1) * CH, :] for piece in range(d.pieces)], axis=1
    )


def edge_places(places, d):
    lane = lanes((1, d.edge))
    block = lane // d.block
    row = lane % d.block - 2
    column = jnp.where(block == 0, 126, jnp.where(block == 1, 0, jnp.where(block == 2, 127, 1)))
    own = (row >= 0) & (row < d.rows)
    target = jnp.where(own, column, -1)
    position = subs((128, d.edge))
    for step in range(d.rows):
        place = (position == jnp.where(row == step, target, -1)).astype(F32).astype(BF16)
        places[step * 128 : (step + 1) * 128, :] = place


def edge_columns(state, places, d):
    whole = jnp.concatenate([state[step] for step in range(d.rows)], axis=1)
    return jnp.dot(whole, places[...], preferred_element_type=F32).astype(BF16)


def pack_columns(values, reach):
    lane = lanes(values[0].shape)
    pitch = 128 // len(values)
    packed = jnp.zeros_like(values[0])
    for index, value in enumerate(values):
        at = index * pitch
        packed = jnp.where((lane >= at) & (lane < at + reach), roll(value, at), packed)
        at += reach
        packed = jnp.where((lane >= at) & (lane < at + reach), roll(value, at + reach - 128), packed)
    return packed


def unpack_columns(left, right, index, count, reach):
    at = index * (128 // count)
    left = roll(left.astype(F32), 128 - at - 2 * reach)
    return jnp.where(lanes(left.shape) < 64, roll(right.astype(F32), -at), left)


def strips(one, two, even, d):
    last = d.rows - 2
    return (one, jnp.where(even, last, 0)), (two, jnp.where(even, 0, last))


def split_bf16(values):
    high = values.astype(BF16).astype(F32)
    mid = (values - high).astype(BF16).astype(F32)
    return high, mid, values - high - mid


class Emission:
    def __init__(self, surface, flags, places, raw, d):
        gap = jnp.zeros((4, CH), F32)
        terms = []
        for term in split_bf16(surface[flags[0]]):
            terms += [term, gap]
        self.proj = jnp.concatenate(terms + [gap, gap], axis=0).astype(BF16)
        self.places, self.raw, self.d, self.flags = places, raw, d, flags

    def project(self, state):
        half = self.d.rows // 2
        products = []
        for step in range(half):
            pair = jnp.concatenate([state[step], state[step + half]], axis=1)
            products.append(jnp.dot(self.proj, pair, preferred_element_type=F32))
        whole = jnp.concatenate([state[step] for step in range(2 * half)], axis=1)
        edges = jnp.dot(whole, self.places[...], preferred_element_type=F32)
        for step, parts in enumerate(products):
            parts = parts[0:8] + parts[8:16] + parts[16:24]
            self.raw[step * 8 : step * 8 + 8, :] = parts[:, :128]
            self.raw[(step + half) * 8 : (step + half) * 8 + 8, :] = parts[:, 128:]
        return edges.astype(BF16)

    def close(self, state, wet, fields, own_edges, one, two):
        d, even = self.d, self.flags[3] == 0
        edges = self.project(state)
        keeping = jnp.where(self.flags[0] != 0, wet[...].astype(F32), 1.0)
        whole = [self.raw[pl.ds(field, d.rows, stride=8), :] * keeping for field in range(NS)]
        for field in range(NS):
            fields[field] = whole[field].astype(BF16)
        fields[NS] = pack_columns(whole, REACH).astype(BF16)
        put_edges(own_edges, 0, edges, d)
        row = lanes(edges.shape) % d.block
        downward = jnp.where(row < 2, roll(edges, -d.rows), jnp.zeros_like(edges))
        upward = jnp.where(
            (row >= d.rows + 2) & (row < d.rows + 4), roll(edges, d.rows), jnp.zeros_like(edges)
        )
        for (ref, first), down in zip(strips(one, two, even, d), (even, jnp.logical_not(even))):
            ref[0:CH, :] = state[first]
            ref[CH : 2 * CH, :] = state[first + 1]
            put_edges(ref, 2 * CH, jnp.where(down, downward, upward), d)


def fetch(sources, targets, sems):
    copies = [
        pltpu.make_async_copy(source, target, sems.at[index])
        for index, (source, target) in enumerate(zip(sources, targets))
    ]
    for copy in copies:
        copy.start()
    return copies


def start_kernel(
    d, flags, far_given, far_surface, far_wet, far_offsets, far_weights,
    state, planes, sides, places, fields, own_edges, one, two,
    raw, tall, turned, given, surface, wet, offsets, weights, sems,
):
    rows = d.rows
    pieces = [pl.ds(at, 16) for at in range(0, CH, 16)]
    copies = fetch(
        [far_given.at[piece] for piece in pieces] + [far_surface, far_wet, far_offsets, far_weights],
        [given.at[piece] for piece in pieces] + [surface, wet, offsets, weights],
        sems,
    )
    edge_places(places, d)
    for index, piece in enumerate(pieces):
        copies[index].wait()
        turned[index * 16 * rows : (index + 1) * 16 * rows, :] = (
            given[piece].astype(F32).reshape(16 * rows, 128)
        )
    for row in range(rows):
        state[row] = turned[pl.ds(row, CH, stride=rows), :].astype(BF16)
    for copy in copies[len(pieces) :]:
        copy.wait()
    emission = Emission(surface, flags, places, raw, d)
    emission.close(state, wet, fields, own_edges, one, two)
    for k in range(NK):
        code = (offsets[0, k] * SPAN + offsets[1, k]).astype(F32)
        tall[k * rows : (k + 1) * rows, :] = code
        tall[(NK + k) * rows : (NK + k + 1) * rows, :] = weights[k]
        planes[k] = code.astype(BF16)
        planes[NK + k] = weights[k].astype(BF16)
    packed = pack_columns([tall[plane * rows : (plane + 1) * rows, :] for plane in range(2 * NK)], 2)
    sides[...] = packed.astype(BF16)
    even = flags[3] == 0
    for (ref, first), down in zip(strips(one, two, even, d), (even, jnp.logical_not(even))):
        strip = [tall[pl.ds(first + step, 2 * NK, stride=rows), :] for step in range(2)]
        ref[d.strip : d.strip + 16, :] = jnp.concatenate(strip, axis=0).astype(BF16)
        ref[d.strip + 16 : d.strip + 32, :] = jnp.where(
            down, packed[rows - 16 : rows], packed[0:16]
        ).astype(BF16)


def decode(code):
    shifted = code.astype(jnp.int32) + (HW * SPAN + HW)
    rows = lax.shift_right_logical(shifted * 241, 12)
    return rows - HW, shifted - rows * SPAN - HW


def along_lanes(values, index):
    numbers = lax.GatherDimensionNumbers(
        offset_dims=(),
        collapsed_slice_dims=(1,),
        start_index_map=(1,),
        operand_batching_dims=(0,),
        start_indices_batching_dims=(0,),
    )
    return lax.gather(
        values, index[..., None], numbers, (1, 1), mode=lax.GatherScatterMode.PROMISE_IN_BOUNDS
    )


def couple(fields, coupled, rows):
    largest = None
    for field in range(NS):
        here = jnp.max(jnp.abs(fields[field]), axis=0, keepdims=True)
        largest = here if largest is None else jnp.maximum(largest, here)
    largest = jnp.maximum(jnp.max(largest, axis=1, keepdims=True), 1e-30)
    scale = FIXED / largest
    for pair in range(NS // 2):
        high, low = [
            jnp.floor(fields[2 * pair + part] * scale + 0.5).astype(jnp.int32) for part in range(2)
        ]
        coupled[pair] = high * (1 << 16) + (low + (1 << 15))
    return largest * (1 / FIXED)


def uncouple(values):
    high = lax.shift_right_arithmetic(values, 16)
    low = (values & 0xFFFF) - (1 << 15)
    return high.astype(F32), low.astype(F32)


def select_rows(source, start, picks):
    parts = source.shape[0]
    blank = jnp.full((8, 128), 1 << 15, jnp.int32) if parts < NS else jnp.zeros((8, 128), F32)
    chosen = [[blank for _ in range(parts)] for _ in picks]
    for shift in range(-HW, HW + 1):
        at = pl.ds(start + shift, 8)
        values = [source[part, at, :] for part in range(parts)]
        for slot, (rows, index, allowed) in enumerate(picks):
            here = (rows == shift) & allowed
            for part in range(parts):
                picked = along_lanes(values[part], index)
                chosen[slot][part] = jnp.where(here, picked, chosen[slot][part])
    if parts == NS:
        return chosen
    return [[part for values in pairs for part in uncouple(values)] for pairs in chosen]


def regrid_inside(coupled, unit, plan_x, part_x, first, tiles, tall):
    lane = lanes((8, 128))
    for step in range(tiles):
        at = first + step * 8
        picks = []
        weights = []
        for k in range(NK):
            rows, cols = decode(plan_x[pl.ds(k * tall + at, 8), :])
            weights.append(plan_x[pl.ds((NK + k) * tall + at, 8), :] * unit)
            column = lane + cols
            picks.append((rows, column & 127, (column >= 0) & (column < 128)))
        chosen = select_rows(coupled, at + 14, picks)
        for field in range(NS):
            total = chosen[0][field] * weights[0]
            for k in range(1, NK):
                total = total + chosen[k][field] * weights[k]
            part_x[pl.ds(field * tall + at, 8), :] = total


def edge_lanes():
    lane = lanes((8, 128))
    return ((lane + 8) & 127) // 32, ((lane + 8) & 31) - 8


def plan_edges(plan_x, plan_y, plan_e, first, tiles, tall, sides):
    part, place = edge_lanes()
    outer = place >= 8
    for step in range(tiles):
        at = first + step * 8
        code = jnp.zeros((8, 128), F32)
        weight = jnp.zeros((8, 128), F32)
        for k in range(NK):
            edge_code = roll(plan_x[pl.ds(k * tall + at, 8), :], 32 * k)
            edge_weight = roll(plan_x[pl.ds((NK + k) * tall + at, 8), :], 32 * k)
            if sides:
                edge_code = jnp.where(
                    outer, roll(plan_y[pl.ds(k * tall + at, 8), :], 32 * k + 16), edge_code
                )
                edge_weight = jnp.where(
                    outer, roll(plan_y[pl.ds((NK + k) * tall + at, 8), :], 32 * k + 16), edge_weight
                )
            code = jnp.where(part == k, edge_code, code)
            weight = jnp.where(part == k, edge_weight, weight)
        plan_e[pl.ds(at, 8), :] = code
        plan_e[pl.ds(tall + at, 8), :] = weight


def regrid_beside(window, plan_e, part_x, forcing_x, forcing_y, first, tiles, tall, sides):
    lane = lanes((8, 128))
    part, place = edge_lanes()
    outer = place >= 8
    inner_column = place & 127
    outer_column = jnp.where(place < 16, place - 16, place + 112)
    edge = (lane < 8) | (lane >= 120)
    for step in range(tiles):
        at = first + step * 8
        rows, cols = decode(plan_e[pl.ds(at, 8), :])
        weight = plan_e[pl.ds(tall + at, 8), :]
        column = jnp.where(outer, outer_column, inner_column) + cols
        within = (column >= 0) & (column < 128)
        index = jnp.where(within, column + 32, column) & 127
        (chosen,) = select_rows(window, at + 14, [(rows, index, outer | jnp.logical_not(within))])
        for field in range(NS):
            part_sum = chosen[field] * weight
            extra = part_sum
            for k in range(1, NK):
                extra = extra + roll(part_sum, -32 * k)
            total = part_x[pl.ds(field * tall + at, 8), :] + jnp.where(edge, extra, 0.0)
            forcing_x[pl.ds(at * 8 + field, 8, stride=8), :] = total
            forcing_x[pl.ds(at * 8 + field + 4, 8, stride=8), :] = total
            if sides:
                extra = roll(extra, -16)
                forcing_y[pl.ds(at * 8 + field, 8, stride=8), :] = extra
                forcing_y[pl.ds(at * 8 + field + 4, 8, stride=8), :] = extra


def twice_gelu(x):
    scale = (2 / jnp.pi) ** 0.5
    return x + x * jnp.tanh(x * (scale + (scale * 0.044715) * (x * x)))


def staggered(count, *stages, between=()):
    between = list(between)
    values = [{} for _ in stages]
    for turn in range(count + len(stages) - 1):
        for index, stage in enumerate(stages):
            step = turn - index
            if 0 <= step < count:
                given = values[index - 1].pop(step) if index else None
                values[index][step] = stage(step, given)
        if between:
            between.pop(0)()
    for extra in between:
        extra()


def air(state, out, forcing_x, air_in, atm_out, d):
    half = d.rows // 2
    leading = subs((8, 128)) < 4
    blank = jnp.zeros((32, 128), BF16)

    def inputs(row):
        at = (row + 2) * 8
        forced = jnp.where(leading, forcing_x[at : at + 8, :], 1.0)
        forced = jnp.concatenate([forced, jnp.zeros_like(forced)], axis=0).astype(BF16)
        return jnp.concatenate([state[row], forced, blank], axis=0)

    def first(step, _):
        pair = jnp.concatenate([inputs(step), inputs(step + half)], axis=1)
        return jnp.dot(air_in[...], pair, preferred_element_type=F32)

    def middle(step, product):
        return twice_gelu(product).astype(BF16)

    def second(step, hidden):
        return jnp.dot(atm_out[...], hidden, preferred_element_type=F32)

    def last(step, update):
        news = []
        for offset in range(2):
            change = update[:, offset * 128 : (offset + 1) * 128]
            news.append(state[step + offset * half].astype(F32) + 0.5 * change)
        out(step, *news)

    staggered(half, first, middle, second, last)


def edge_forcing(forcing_x, forcing_y, d):
    lane = lanes((8, d.edge))
    block = lane // d.block
    row = lane % d.block

    inner = outer = jnp.zeros((8, d.edge), F32)
    for step in range(d.rows + 4):
        at = pl.ds(step * 8, 8)
        pad = [jnp.zeros((8, 128), F32)] * (d.pieces - 1)
        here = jnp.concatenate([forcing_x[at, :]] + pad, axis=1)
        there = jnp.concatenate([forcing_y[at, :]] + pad, axis=1)
        for index, column in enumerate((126, 0, 127, 1)):
            shift = step + index * d.block - column
            match = (block == index) & (row == step)
            if column in (0, 127):
                inner = jnp.where(match, roll(here, shift), inner)
            outer = jnp.where(match, roll(there, shift), outer)
    return inner, outer


def roll_rows(state, upper, lower, rolled, d):
    def put(row, values):
        rolled[row, 0:CH, :] = roll(values, 1)
        rolled[row, CH : 2 * CH, :] = values
        rolled[row, 2 * CH : 3 * CH, :] = roll(values, -1)

    for step in range(2):
        put(step, upper[step * CH : (step + 1) * CH, :])
        put(d.rows + 2 + step, lower[step * CH : (step + 1) * CH, :])
    for row in range(d.rows):
        put(row + 2, state[row])


def sea(
    state, rolled, edges, left, right, out, forcing_x, forcing_y, ocn_in, ocn_out, wet,
    at_top, at_bottom, stack, hidden, side, d,
):
    rows, block = d.rows, d.block
    lane = lanes((CH, 128))
    spot = lanes((CH, d.edge))
    part = spot // block
    inner = edges
    outer = jnp.where((part == 0) | (part == 2), left, right)

    def sides_of(inner, outer, spot):
        first = spot < block
        return (
            jnp.where(first, outer, roll(inner, -block)),
            jnp.where(first, roll(outer, -2 * block), outer),
            jnp.where(first, roll(inner, -block), roll(outer, -2 * block)),
        )

    beside = sides_of(inner, outer, spot)
    middle = beside[1]
    force_in, force_out = edge_forcing(forcing_x, forcing_y, d)
    beside_forcing = sides_of(force_in, force_out, lanes((8, d.edge)))
    sub = subs((8, d.edge))
    ones = jnp.ones((8, d.edge), F32)
    forced = jnp.concatenate(
        [
            jnp.where(sub < 4, beside_forcing[0], beside_forcing[1]),
            jnp.where(sub < 4, beside_forcing[2], ones),
        ],
        axis=0,
    ).astype(BF16)
    columns = jnp.concatenate(list(beside) + [forced], axis=0)
    for tap in range(3):
        side[tap * 256 : (tap + 1) * 256, :] = roll(columns, -tap)

    sub_row = subs((8, 128))
    lane_row = lanes((8, 128))

    for row in range(rows + 4):
        entry = roll(middle, -row)[:, :128]
        stack[row, 0:CH, :] = jnp.where(lane == 0, entry, rolled[row, 0:CH, :])
        stack[row, CH : 2 * CH, :] = rolled[row, CH : 2 * CH, :]
        entry = roll(middle, 127 - block - row)[:, :128]
        stack[row, 2 * CH : 3 * CH, :] = jnp.where(lane == 127, entry, rolled[row, 2 * CH : 3 * CH, :])
        here, there = forcing_x[row * 8 : row * 8 + 8, :], forcing_y[row * 8 : row * 8 + 8, :]
        before = roll(jnp.where(lane_row == 127, there, here), 1)
        after = roll(jnp.where(lane_row == 0, there, here), -1)
        stack[row, 3 * CH : 256, :] = jnp.concatenate(
            [jnp.where(sub_row < 4, before, here), jnp.where(sub_row < 4, after, 1.0)], axis=0
        ).astype(BF16)

    pairs = (rows + 2) // 2

    def first(step, _):
        taps = jnp.concatenate(
            [
                stack[step : step + 3].reshape(3 * 256, 128),
                stack[step + pairs : step + pairs + 3].reshape(3 * 256, 128),
            ],
            axis=1,
        )
        return jnp.dot(ocn_in[...], taps, preferred_element_type=F32)

    def activate(step, product):
        active = twice_gelu(product)
        low, high = active[:, :128], active[:, 128:]
        if step == 0:
            low = jnp.where(at_top != 0, 0.0, low)
        if step == pairs - 1:
            high = jnp.where(at_bottom != 0, 0.0, high)
        hidden[step, 0:HIDK, :] = low.astype(BF16)
        hidden[step + pairs, 0:HIDK, :] = high.astype(BF16)
        blank = jnp.zeros((HIDP - HIDK, 128), BF16)
        hidden[step, HIDK:HIDP, :] = blank
        hidden[step + pairs, HIDK:HIDP, :] = blank

    held = {}

    def edge_first():
        held["product"] = jnp.dot(ocn_in[...], side[...], preferred_element_type=F32)

    def edge_activate():
        spot = lanes((1, d.edge)) % block
        gone = ((spot == 0) & (at_top != 0)) | ((spot == rows + 1) & (at_bottom != 0))
        active = jnp.where(gone, 0.0, twice_gelu(held["product"])).astype(BF16)
        active = jnp.concatenate([active, jnp.zeros((HIDP - HIDK, d.edge), BF16)], axis=0)
        held["taps"] = jnp.concatenate([roll(active, -tap) for tap in range(3)], axis=0)

    def edge_second():
        held["left"] = jnp.dot(ocn_out[0:CH, :], held["taps"], preferred_element_type=F32)
        held["right"] = jnp.dot(
            ocn_out[2 * CH : 3 * CH, :], held["taps"], preferred_element_type=F32
        )

    wait = lambda: None
    staggered(
        pairs, first, activate, between=(edge_first, wait, edge_activate, wait, edge_second)
    )
    from_left, from_right = held["left"], held["right"]
    half = rows // 2

    def second(step, _):
        taps = jnp.concatenate(
            [
                hidden[step : step + 3].reshape(3 * HIDP, 128),
                hidden[step + half : step + half + 3].reshape(3 * HIDP, 128),
            ],
            axis=1,
        )
        return jnp.dot(ocn_out[...], taps, preferred_element_type=F32)

    def last(step, product):
        news = []
        for offset in range(2):
            row = step + offset * half
            sums = product[:, offset * 128 : (offset + 1) * 128]
            entry = roll(from_left, -row)[:, :128]
            total = sums[CH : 2 * CH] + jnp.where(lane == 0, entry, roll(sums[0:CH], 1))
            entry = roll(from_right, 127 - block - row)[:, :128]
            total = total + jnp.where(lane == 127, entry, roll(sums[2 * CH : 3 * CH], -1))
            update = total * (0.5 * wet[row : row + 1, :].astype(F32))
            news.append(state[row].astype(F32) + update)
        out(step, *news)

    staggered(half, second, last)


def prepare(atm_in, atm_bias, ocn_in, ocn_bias, ocn_out, air_in, first, second, is_ocean):
    def bias_rows(ref, width):
        row = jnp.concatenate([ref[index : index + 1, :] for index in range(ref.shape[0])], axis=1)
        terms = list(split_bf16(row)) + [jnp.zeros_like(row)]
        bias = jnp.concatenate(terms, axis=0)
        return jnp.pad(bias, ((0, 0), (0, width - bias.shape[1])))

    @pl.when(is_ocean == 0)
    def _():
        columns = jnp.concatenate(
            [atm_in[...].astype(F32), bias_rows(atm_bias, HA), jnp.zeros((40, HA), F32)], axis=0
        )
        air_in[...] = columns.T.astype(BF16)

    @pl.when(is_ocean != 0)
    def _():
        bias = bias_rows(ocn_bias, 256)
        count = ocn_in.shape[2]
        for tap in range(3):
            whole = [ocn_in[3 * tap + side].astype(F32) for side in range(3)]
            whole = [jnp.pad(values, ((0, 0), (0, 256 - count))) for values in whole]
            rows = [values[:CH] for values in whole] + [values[CH:] for values in whole]
            rows.append(bias if tap == 0 else jnp.zeros((4, 256), F32))
            columns = jnp.concatenate(rows, axis=0).T
            first[:, tap * 256 : (tap + 1) * 256] = columns[:HIDK].astype(BF16)
        for tap in range(9):
            values = ocn_out[tap].astype(F32)
            at, column = tap // 3 * HIDP, tap % 3
            second[column * CH : (column + 1) * CH, at : at + HIDP] = jnp.pad(
                values, ((0, 0), (0, HIDP - count))
            ).astype(BF16)


def ends(flags):
    at_top, at_bottom, even = flags[1] != 0, flags[2] != 0, flags[3] == 0

    def up_and_down(one, two):
        above = jnp.where(even, two, one).astype(F32)
        below = jnp.where(even, one, two).astype(F32)
        return jnp.where(at_top, 0.0, above), jnp.where(at_bottom, 0.0, below)

    return up_and_down


def middle_kernel(d, opening, *refs):
    refs = list(refs)
    take = lambda count: [refs.pop(0) for _ in range(count)]
    flags, state, field_one, beside, field_two, from_one, from_two = take(7)
    if opening:
        planes, *far_weights = take(6)
    else:
        (plan_x,) = take(1)
    part_x, fields_x, rolled = take(3)
    if opening:
        plan_x, *made_weights = take(4)
    (coupled,) = take(1)
    if opening:
        *raw_weights, sems = take(6)
        copies = fetch(far_weights, raw_weights, sems)
    rows, tall = d.rows, d.tall
    is_ocean = flags[0]
    up_and_down = ends(flags)

    if opening:

        @pl.when(is_ocean != 0)
        def _():
            base = d.strip
            pair = up_and_down(from_one[base : base + 16, :], from_two[base : base + 16, :])
            plan_x[...] = jnp.zeros_like(plan_x)
            for step, strip in zip((0, rows + 2), pair):
                for index in range(2):
                    plan_x[pl.ds(step + index, 2 * NK, stride=tall), :] = strip[index * 8 : (index + 1) * 8]

        for plane in range(2 * NK):
            plan_x[plane * tall + 2 : plane * tall + 2 + rows, :] = planes[plane].astype(F32)

    for field in range(NS):
        pair = up_and_down(field_one[field], field_two[field])
        fields_x[field, 0:16, :] = pair[0][rows - 16 : rows]
        fields_x[field, 16 : 16 + rows, :] = beside[field].astype(F32)
        fields_x[field, 16 + rows : 32 + rows, :] = pair[1][0:16]

    unit = couple(fields_x, coupled, rows)

    @pl.when(is_ocean == 0)
    def _():
        regrid_inside(coupled, unit, plan_x, part_x, 2, rows // 8, tall)

    @pl.when(is_ocean != 0)
    def _():
        regrid_inside(coupled, unit, plan_x, part_x, 0, d.tiles, tall)
        upper, lower = up_and_down(from_one[0 : 2 * CH, :], from_two[0 : 2 * CH, :])
        roll_rows(state, upper.astype(BF16), lower.astype(BF16), rolled, d)

    if opening:
        for copy in copies:
            copy.wait()
        prepare(*raw_weights, *made_weights, is_ocean)


def step_kernel(d, opening, closing, *refs):
    refs = list(refs)
    take = lambda count: [refs.pop(0) for _ in range(count)]
    flags, state, wet, from_left, from_right = take(5)
    part_x, fields_x, rolled, edges, plan_x, air_in, first, second, atm_out = take(9)
    if not opening:
        (plan_e,) = take(1)
    if not closing:
        surface, places = take(2)
    (out,) = take(1)
    if not closing:
        fields, new_edges, one, two = take(4)
    if opening:
        (plan_e,) = take(1)
    window, forcing_x, forcing_y, stack, hidden, side, raw = take(7)
    if opening:
        (plan_y,) = take(1)
    rows, tall = d.rows, d.tall
    is_ocean, at_top, at_bottom = flags[0], flags[1], flags[2]
    up_and_down = ends(flags)

    if opening:

        @pl.when(is_ocean != 0)
        def _():
            plan_y[...] = jnp.zeros_like(plan_y)
            base = d.edge_rows
            parts = [
                (ref[base : base + 16, :], ref[base + 16 + rows : base + 32 + rows, :],
                 ref[base + 16 : base + 16 + rows, :])
                for ref in (from_left, from_right)
            ]
            for plane in range(2 * NK):
                first_end, second_end, own = [
                    unpack_columns(left, right, plane, 2 * NK, 2) for left, right in zip(*parts)
                ]
                above, below = up_and_down(first_end, second_end)
                at = plane * tall
                plan_y[at : at + 2, :] = above[14:16]
                plan_y[at + 2 : at + 2 + rows, :] = own
                plan_y[at + 2 + rows : at + 4 + rows, :] = below[0:2]

    base = d.edge_rows + (rows + 32 if opening else 0)
    parts = [
        (ref[base : base + 16, :], ref[base + 16 + rows : base + 32 + rows, :],
         ref[base + 16 : base + 16 + rows, :])
        for ref in (from_left, from_right)
    ]
    for field in range(NS):
        first_end, second_end, own = [
            unpack_columns(left, right, field, NS, REACH) for left, right in zip(*parts)
        ]
        above, below = up_and_down(first_end, second_end)
        for at, values in ((0, above), (16, own), (16 + rows, below)):
            count = values.shape[0]
            inside = roll(fields_x[field, at : at + count, :], 32)
            lane = lanes(values.shape)
            near = (lane >= 32 - REACH) & (lane < 32 + REACH)
            far = (lane < REACH) | (lane >= 128 - REACH)
            kept = jnp.where(near, inside, jnp.where(far, values, 0.0))
            window[field, at : at + count, :] = kept
    def finished():
        emission = None if closing else Emission(surface, flags, places, raw, d)

        def put(step, low, high):
            if closing:
                for row, values in ((step, low), (step + rows // 2, high)):
                    raw[pl.ds(row, CH, stride=rows), :] = values
                return
            out[step] = low.astype(BF16)
            out[step + rows // 2] = high.astype(BF16)

        def close():
            if not closing:
                emission.close(out, wet, fields, new_edges, one, two)

        return put, close

    @pl.when(is_ocean == 0)
    def _():
        if opening:
            plan_edges(plan_x, plan_y, plan_e, 2, rows // 8, tall, False)
        regrid_beside(
            window, plan_e, part_x, forcing_x, forcing_y, 2, rows // 8, tall, False
        )
        put, close = finished()
        air(state, put, forcing_x, air_in, atm_out, d)
        close()

    @pl.when(is_ocean != 0)
    def _():
        if opening:
            plan_edges(plan_x, plan_y, plan_e, 0, d.tiles, tall, True)
        regrid_beside(
            window, plan_e, part_x, forcing_x, forcing_y, 0, d.tiles, tall, True
        )
        put, close = finished()
        joined = [get_edges(ref, 0, d) for ref in (from_left, from_right)]
        sea(
            state, rolled, get_edges(edges, 0, d), *joined, put, forcing_x, forcing_y,
            first, second, wet, at_top, at_bottom, stack, hidden, side, d,
        )
        close()

    if closing:
        out[...] = raw[...].reshape(CH, rows, 128).astype(BF16)


VMEM = pl.BlockSpec(memory_space=pltpu.VMEM)
HBM = pl.BlockSpec(memory_space=pltpu.HBM)
SMEM = pl.BlockSpec(memory_space=pltpu.SMEM)
PARAMS = pltpu.CompilerParams(vmem_limit_bytes=48 * 1024 * 1024)


def shape(*dims, dtype=BF16):
    return jax.ShapeDtypeStruct(dims, dtype)


def send(x, move):
    names = ("grp", "lat", "lon")
    sizes = [lax.axis_size(name) for name in names]
    pairs = []
    for group in range(sizes[0]):
        for lat in range(sizes[1]):
            for lon in range(sizes[2]):
                to = move(group, lat, lon)
                if to is None or not 0 <= to[1] < sizes[1]:
                    continue
                target = (to[0] * sizes[1] + to[1]) * sizes[2] + to[2] % sizes[2]
                pairs.append(((group * sizes[1] + lat) * sizes[2] + lon, target))
    return lax.ppermute(x, names, pairs)


def swap_rows(x, turn, across):
    count, columns = lax.axis_size("lat"), lax.axis_size("lon")

    def move(group, lat, lon):
        other = ((lat + turn) ^ 1) - turn
        if 0 <= other < count and (across or group == 1):
            return (1 - group if across else group), other, lon
        beside = lon ^ 1
        return group, lat, beside if beside < columns else lon

    return send(x, move)


def exchange(fields, own_edges, one, two, sides, d):
    rows = d.rows
    scale = jnp.where(lax.axis_index("grp") > 1, 0, 1).astype(BF16)
    later = fields * scale
    beside = send(fields, lambda g, i, j: (1 - g, i, j))
    from_one = swap_rows(one, 0, False)
    from_two = swap_rows(two, 1, False)
    field_one = swap_rows(later, 0, True)
    field_two = swap_rows(later, 1, True)
    beside, from_one = lax.optimization_barrier((beside, from_one))
    from_two, beside = lax.optimization_barrier((from_two, beside))
    field_one, from_two = lax.optimization_barrier((field_one, from_two))
    field_two, field_one = lax.optimization_barrier((field_two, field_one))
    lat, count = lax.axis_index("lat"), lax.axis_size("lat")
    odd = lat % 2 == 1
    edges = own_edges
    for turn, ref in ((0, from_one), (1, from_two)):
        other = ((lat + turn) ^ 1) - turn
        there = (other >= 0) & (other < count)
        edges = edges + jnp.where(there, ref[2 * CH : d.strip], 0)
    outer = [field_one[NS], field_two[NS]]
    if rows != 16:
        outer = [
            jnp.where(odd, outer[0][rows - 16 :], outer[0][:16]),
            jnp.where(odd, outer[1][:16], outer[1][rows - 16 :]),
        ]
    packed = [edges]
    if sides is not None:
        packed += [from_one[d.strip + 16 :], sides, from_two[d.strip + 16 :]]
    packed += [outer[0], beside[NS], outer[1]]
    packed = jnp.concatenate(packed, axis=0)
    from_left = send(packed, lambda g, i, j: (g, i, j + 1))
    from_right = send(packed, lambda g, i, j: (g, i, j - 1))
    return (field_one, beside, field_two, from_one, from_two), (from_left, from_right), edges


def local(
    coupled_state, land_mask, regrid_offsets, regrid_weights, surface_proj,
    atm_in, atm_bias, atm_out, ocn_in, ocn_bias, ocn_out,
):
    rows = coupled_state.shape[2]
    assert coupled_state.shape[3] == 128
    d = Dims(rows)
    group = lax.axis_index("grp")
    lat = lax.axis_index("lat")
    flags = jnp.stack(
        [group, lat == 0, lat == lax.axis_size("lat") - 1, lat % 2]
    ).astype(jnp.int32)
    raw_weights = (
        atm_in.T,
        atm_bias.reshape(HA // 128, 128),
        jnp.transpose(ocn_in, (1, 2, 0)),
        ocn_bias[None],
        jnp.transpose(ocn_out, (1, 0, 2)),
    )
    state_shape = shape(rows, CH, 128)
    emitted = [
        shape(NS + 1, rows, 128),
        shape(d.edge_rows, 128),
        shape(d.strip, 128),
        shape(d.strip, 128),
    ]
    raw = pltpu.VMEM((rows * 8, 128), F32)
    turned = pltpu.VMEM((CH * rows, 128), F32)

    def call(kernel, operands, outs, scratch, name, far=()):
        scratch = scratch + [pltpu.VMEM(x.shape, x.dtype) for x in far]
        if far:
            scratch.append(pltpu.SemaphoreType.DMA((len(far) + CH // 16,)))

        far = [pltpu.with_memory_space_constraint(x, pltpu.HBM) for x in far]
        return pl.pallas_call(
            kernel,
            out_shape=outs,
            in_specs=[SMEM] + [VMEM] * len(operands) + [HBM] * len(far),
            out_specs=[VMEM] * len(outs),
            scratch_shapes=scratch,
            compiler_params=PARAMS,
            name=name,
        )(flags, *operands, *far)

    state, planes, sides, places, fields, edges, one, two = call(
        functools.partial(start_kernel, d),
        (),
        [state_shape, shape(2 * NK, rows, 128), shape(rows, 128), shape(rows * 128, d.edge)]
        + emitted[:2]
        + [shape(d.strip + 32, 128)] * 2,
        [raw, pltpu.VMEM((2 * NK * rows, 128), F32), turned],
        "start",
        (coupled_state[0], surface_proj, land_mask, regrid_offsets[0], regrid_weights[0]),
    )

    plan = shape(2 * NK * d.tall, 128, dtype=F32)
    between = [
        shape(NS * d.tall, 128, dtype=F32),
        shape(NS, rows + 32, 128, dtype=F32),
        shape(rows + 4, 3 * CH, 128),
    ]
    made = [shape(HA, 128), shape(HIDK, 768), shape(3 * CH, 3 * HIDP)]
    coupled = pltpu.VMEM((NS // 2, rows + 32, 128), jnp.int32)
    scratch = [
        pltpu.VMEM((NS, rows + 32, 128), F32),
        pltpu.VMEM((d.tall * 8, 128), F32),
        pltpu.VMEM((d.tall * 8, 128), F32),
        pltpu.VMEM((rows + 4, 256, 128), BF16),
        pltpu.VMEM((rows + 2, HIDP, 128), BF16),
        pltpu.VMEM((768, d.edge), BF16),
    ]

    vertical, horizontal, edges = exchange(fields, edges, one, two, sides, d)
    *shared, plan_x, air_in, first, second = call(
        functools.partial(middle_kernel, d, True),
        (state, *vertical, planes),
        between + [plan] + made,
        [coupled],
        "first_middle",
        raw_weights,
    )
    weights = (air_in, first, second, atm_out)
    state, fields, edges, one, two, plan_e = call(
        functools.partial(step_kernel, d, True, False),
        (state, land_mask, *horizontal, *shared, edges, plan_x, *weights, surface_proj, places),
        [state_shape] + emitted + [shape(2 * d.tall, 128, dtype=F32)],
        scratch + [raw, pltpu.VMEM(plan.shape, F32)],
        "first_step",
    )

    vertical, horizontal, edges = exchange(fields, edges, one, two, None, d)
    shared = call(
        functools.partial(middle_kernel, d, False),
        (state, *vertical, plan_x),
        between,
        [coupled],
        "second_middle",
    )
    (state,) = call(
        functools.partial(step_kernel, d, False, True),
        (state, land_mask, *horizontal, *shared, edges, plan_x, *weights, plan_e),
        [shape(CH, rows, 128)],
        scratch + [turned],
        "second_step",
    )
    return state[None]


def solution(mesh):
    return jax.shard_map(
        local,
        mesh=mesh,
        in_specs=(
            P("grp", None, "lat", "lon"),
            P("lat", "lon"),
            P("grp", None, None, "lat", "lon"),
            P("grp", None, "lat", "lon"),
            P(),
            P(),
            P(),
            P(),
            P(),
            P(),
            P(),
        ),
        out_specs=P("grp", None, "lat", "lon"),
        check_vma=False,
    )
```

```python
import functools

import jax
import jax.numpy as jnp
from jax import lax
from jax.experimental import pallas as pl
from jax.experimental.pallas import tpu as pltpu
from jax.sharding import PartitionSpec as P

CH = 80
NS = 4
NK = 4
HA = 384
HW = 8
SPAN = 2 * HW + 1
REACH = HW + 2
FIXED = 32767.0
HIDK = 208
HIDP = 256
F32 = jnp.float32
BF16 = jnp.bfloat16


def roll(x, shift, axis=1):
    size = x.shape[axis]
    if isinstance(shift, int):
        shift = shift % size
        if shift == 0:
            return x
    return pltpu.roll(x, shift, axis)


def lanes(shape):
    return lax.broadcasted_iota(jnp.int32, shape, len(shape) - 1)


def subs(shape):
    return lax.broadcasted_iota(jnp.int32, shape, len(shape) - 2)


class Dims:
    def __init__(self, rows):
        self.rows = rows
        self.block = 32 if rows + 4 <= 32 else 64
        self.edge = 4 * self.block
        self.pieces = self.edge // 128
        self.edge_rows = CH * self.pieces
        self.tiles = -(-(rows + 4) // 8)
        self.tall = 8 * self.tiles
        self.strip = 2 * CH + self.edge_rows


def put_edges(ref, at, edges, d):
    for piece in range(d.pieces):
        ref[at + piece * CH : at + (piece + 1) * CH, :] = edges[:, piece * 128 : (piece + 1) * 128]


def get_edges(ref, at, d):
    return jnp.concatenate(
        [ref[at + piece * CH : at + (piece + 1) * CH, :] for piece in range(d.pieces)], axis=1
    )


def edge_places(places, d):
    lane = lanes((1, d.edge))
    block = lane // d.block
    row = lane % d.block - 2
    column = jnp.where(block == 0, 126, jnp.where(block == 1, 0, jnp.where(block == 2, 127, 1)))
    own = (row >= 0) & (row < d.rows)
    target = jnp.where(own, column, -1)
    position = subs((128, d.edge))
    for step in range(d.rows):
        place = (position == jnp.where(row == step, target, -1)).astype(F32).astype(BF16)
        places[step * 128 : (step + 1) * 128, :] = place


def edge_columns(state, places, d):
    whole = jnp.concatenate([state[step] for step in range(d.rows)], axis=1)
    return jnp.dot(whole, places[...], preferred_element_type=F32).astype(BF16)


def pack_columns(values, reach):
    lane = lanes(values[0].shape)
    pitch = 128 // len(values)
    packed = jnp.zeros_like(values[0])
    for index, value in enumerate(values):
        at = index * pitch
        packed = jnp.where((lane >= at) & (lane < at + reach), roll(value, at), packed)
        at += reach
        packed = jnp.where((lane >= at) & (lane < at + reach), roll(value, at + reach - 128), packed)
    return packed


def unpack_columns(left, right, index, count, reach):
    at = index * (128 // count)
    left = roll(left.astype(F32), 128 - at - 2 * reach)
    return jnp.where(lanes(left.shape) < 64, roll(right.astype(F32), -at), left)


def strips(one, two, even, d):
    last = d.rows - 2
    return (one, jnp.where(even, last, 0)), (two, jnp.where(even, 0, last))


def split_bf16(values):
    high = values.astype(BF16).astype(F32)
    mid = (values - high).astype(BF16).astype(F32)
    return high, mid, values - high - mid


class Emission:
    def __init__(self, surface, flags, places, raw, d):
        gap = jnp.zeros((4, CH), F32)
        terms = []
        for term in split_bf16(surface[flags[0]]):
            terms += [term, gap]
        self.proj = jnp.concatenate(terms + [gap, gap], axis=0).astype(BF16)
        self.places, self.raw, self.d, self.flags = places, raw, d, flags

    def project(self, state):
        half = self.d.rows // 2
        products = []
        for step in range(half):
            pair = jnp.concatenate([state[step], state[step + half]], axis=1)
            products.append(jnp.dot(self.proj, pair, preferred_element_type=F32))
        whole = jnp.concatenate([state[step] for step in range(2 * half)], axis=1)
        edges = jnp.dot(whole, self.places[...], preferred_element_type=F32)
        for step, parts in enumerate(products):
            parts = parts[0:8] + parts[8:16] + parts[16:24]
            self.raw[step * 8 : step * 8 + 8, :] = parts[:, :128]
            self.raw[(step + half) * 8 : (step + half) * 8 + 8, :] = parts[:, 128:]
        return edges.astype(BF16)

    def close(self, state, wet, fields, own_edges, one, two):
        d, even = self.d, self.flags[3] == 0
        edges = self.project(state)
        keeping = jnp.where(self.flags[0] != 0, wet[...].astype(F32), 1.0)
        whole = [self.raw[pl.ds(field, d.rows, stride=8), :] * keeping for field in range(NS)]
        for field in range(NS):
            fields[field] = whole[field].astype(BF16)
        fields[NS] = pack_columns(whole, REACH).astype(BF16)
        put_edges(own_edges, 0, edges, d)
        row = lanes(edges.shape) % d.block
        downward = jnp.where(row < 2, roll(edges, -d.rows), jnp.zeros_like(edges))
        upward = jnp.where(
            (row >= d.rows + 2) & (row < d.rows + 4), roll(edges, d.rows), jnp.zeros_like(edges)
        )
        for (ref, first), down in zip(strips(one, two, even, d), (even, jnp.logical_not(even))):
            ref[0:CH, :] = state[first]
            ref[CH : 2 * CH, :] = state[first + 1]
            put_edges(ref, 2 * CH, jnp.where(down, downward, upward), d)


def fetch(sources, targets, sems):
    copies = [
        pltpu.make_async_copy(source, target, sems.at[index])
        for index, (source, target) in enumerate(zip(sources, targets))
    ]
    for copy in copies:
        copy.start()
    return copies


def start_kernel(
    d, flags, far_given, far_surface, far_wet, far_offsets, far_weights,
    state, planes, sides, places, fields, own_edges, one, two,
    raw, tall, turned, given, surface, wet, offsets, weights, sems,
):
    rows = d.rows
    pieces = [pl.ds(at, 16) for at in range(0, CH, 16)]
    copies = fetch(
        [far_given.at[piece] for piece in pieces] + [far_surface, far_wet, far_offsets, far_weights],
        [given.at[piece] for piece in pieces] + [surface, wet, offsets, weights],
        sems,
    )
    edge_places(places, d)
    for index, piece in enumerate(pieces):
        copies[index].wait()
        turned[index * 16 * rows : (index + 1) * 16 * rows, :] = (
            given[piece].astype(F32).reshape(16 * rows, 128)
        )
    for row in range(rows):
        state[row] = turned[pl.ds(row, CH, stride=rows), :].astype(BF16)
    for copy in copies[len(pieces) :]:
        copy.wait()
    emission = Emission(surface, flags, places, raw, d)
    emission.close(state, wet, fields, own_edges, one, two)
    for k in range(NK):
        code = (offsets[0, k] * SPAN + offsets[1, k]).astype(F32)
        tall[k * rows : (k + 1) * rows, :] = code
        tall[(NK + k) * rows : (NK + k + 1) * rows, :] = weights[k]
        planes[k] = code.astype(BF16)
        planes[NK + k] = weights[k].astype(BF16)
    packed = pack_columns([tall[plane * rows : (plane + 1) * rows, :] for plane in range(2 * NK)], 2)
    sides[...] = packed.astype(BF16)
    even = flags[3] == 0
    for (ref, first), down in zip(strips(one, two, even, d), (even, jnp.logical_not(even))):
        strip = [tall[pl.ds(first + step, 2 * NK, stride=rows), :] for step in range(2)]
        ref[d.strip : d.strip + 16, :] = jnp.concatenate(strip, axis=0).astype(BF16)
        ref[d.strip + 16 : d.strip + 32, :] = jnp.where(
            down, packed[rows - 16 : rows], packed[0:16]
        ).astype(BF16)


def decode(code):
    shifted = code.astype(jnp.int32) + (HW * SPAN + HW)
    rows = lax.shift_right_logical(shifted * 241, 12)
    return rows - HW, shifted - rows * SPAN - HW


def along_lanes(values, index):
    numbers = lax.GatherDimensionNumbers(
        offset_dims=(),
        collapsed_slice_dims=(1,),
        start_index_map=(1,),
        operand_batching_dims=(0,),
        start_indices_batching_dims=(0,),
    )
    return lax.gather(
        values, index[..., None], numbers, (1, 1), mode=lax.GatherScatterMode.PROMISE_IN_BOUNDS
    )


def couple(fields, coupled, rows):
    largest = None
    for field in range(NS):
        here = jnp.max(jnp.abs(fields[field]), axis=0, keepdims=True)
        largest = here if largest is None else jnp.maximum(largest, here)
    largest = jnp.maximum(jnp.max(largest, axis=1, keepdims=True), 1e-30)
    scale = FIXED / largest
    for pair in range(NS // 2):
        high, low = [
            jnp.floor(fields[2 * pair + part] * scale + 0.5).astype(jnp.int32) for part in range(2)
        ]
        coupled[pair] = high * (1 << 16) + (low + (1 << 15))
    return largest * (1 / FIXED)


def uncouple(values):
    high = lax.shift_right_arithmetic(values, 16)
    low = (values & 0xFFFF) - (1 << 15)
    return high.astype(F32), low.astype(F32)


def select_rows(source, start, picks):
    parts = source.shape[0]
    blank = jnp.full((8, 128), 1 << 15, jnp.int32) if parts < NS else jnp.zeros((8, 128), F32)
    chosen = [[blank for _ in range(parts)] for _ in picks]
    for shift in range(-HW, HW + 1):
        at = pl.ds(start + shift, 8)
        values = [source[part, at, :] for part in range(parts)]
        for slot, (rows, index, allowed) in enumerate(picks):
            here = (rows == shift) & allowed
            for part in range(parts):
                picked = along_lanes(values[part], index)
                chosen[slot][part] = jnp.where(here, picked, chosen[slot][part])
    if parts == NS:
        return chosen
    return [[part for values in pairs for part in uncouple(values)] for pairs in chosen]


def regrid_inside(coupled, unit, plan_x, part_x, first, tiles, tall):
    lane = lanes((8, 128))
    for step in range(tiles):
        at = first + step * 8
        picks = []
        weights = []
        for k in range(NK):
            rows, cols = decode(plan_x[pl.ds(k * tall + at, 8), :])
            weights.append(plan_x[pl.ds((NK + k) * tall + at, 8), :] * unit)
            column = lane + cols
            picks.append((rows, column & 127, (column >= 0) & (column < 128)))
        chosen = select_rows(coupled, at + 14, picks)
        for field in range(NS):
            total = chosen[0][field] * weights[0]
            for k in range(1, NK):
                total = total + chosen[k][field] * weights[k]
            part_x[pl.ds(field * tall + at, 8), :] = total


def edge_lanes():
    lane = lanes((8, 128))
    return ((lane + 8) & 127) // 32, ((lane + 8) & 31) - 8


def plan_edges(plan_x, plan_y, plan_e, first, tiles, tall, sides):
    part, place = edge_lanes()
    outer = place >= 8
    for step in range(tiles):
        at = first + step * 8
        code = jnp.zeros((8, 128), F32)
        weight = jnp.zeros((8, 128), F32)
        for k in range(NK):
            edge_code = roll(plan_x[pl.ds(k * tall + at, 8), :], 32 * k)
            edge_weight = roll(plan_x[pl.ds((NK + k) * tall + at, 8), :], 32 * k)
            if sides:
                edge_code = jnp.where(
                    outer, roll(plan_y[pl.ds(k * tall + at, 8), :], 32 * k + 16), edge_code
                )
                edge_weight = jnp.where(
                    outer, roll(plan_y[pl.ds((NK + k) * tall + at, 8), :], 32 * k + 16), edge_weight
                )
            code = jnp.where(part == k, edge_code, code)
            weight = jnp.where(part == k, edge_weight, weight)
        plan_e[pl.ds(at, 8), :] = code
        plan_e[pl.ds(tall + at, 8), :] = weight


def regrid_beside(window, plan_e, part_x, forcing_x, forcing_y, first, tiles, tall, sides):
    lane = lanes((8, 128))
    part, place = edge_lanes()
    outer = place >= 8
    inner_column = place & 127
    outer_column = jnp.where(place < 16, place - 16, place + 112)
    edge = (lane < 8) | (lane >= 120)
    for step in range(tiles):
        at = first + step * 8
        rows, cols = decode(plan_e[pl.ds(at, 8), :])
        weight = plan_e[pl.ds(tall + at, 8), :]
        column = jnp.where(outer, outer_column, inner_column) + cols
        within = (column >= 0) & (column < 128)
        index = jnp.where(within, column + 32, column) & 127
        (chosen,) = select_rows(window, at + 14, [(rows, index, outer | jnp.logical_not(within))])
        for field in range(NS):
            part_sum = chosen[field] * weight
            extra = part_sum
            for k in range(1, NK):
                extra = extra + roll(part_sum, -32 * k)
            total = part_x[pl.ds(field * tall + at, 8), :] + jnp.where(edge, extra, 0.0)
            forcing_x[pl.ds(at * 8 + field, 8, stride=8), :] = total
            forcing_x[pl.ds(at * 8 + field + 4, 8, stride=8), :] = total
            if sides:
                extra = roll(extra, -16)
                forcing_y[pl.ds(at * 8 + field, 8, stride=8), :] = extra
                forcing_y[pl.ds(at * 8 + field + 4, 8, stride=8), :] = extra


def twice_gelu(x):
    scale = (2 / jnp.pi) ** 0.5
    return x + x * jnp.tanh(x * (scale + (scale * 0.044715) * (x * x)))


def staggered(count, *stages):
    values = [{} for _ in stages]
    for turn in range(count + len(stages) - 1):
        for index, stage in enumerate(stages):
            step = turn - index
            if 0 <= step < count:
                given = values[index - 1].pop(step) if index else None
                values[index][step] = stage(step, given)


def air(state, out, forcing_x, air_in, atm_out, d):
    half = d.rows // 2
    leading = subs((8, 128)) < 4
    blank = jnp.zeros((32, 128), BF16)

    def inputs(row):
        at = (row + 2) * 8
        forced = jnp.where(leading, forcing_x[at : at + 8, :], 1.0)
        forced = jnp.concatenate([forced, jnp.zeros_like(forced)], axis=0).astype(BF16)
        return jnp.concatenate([state[row], forced, blank], axis=0)

    def first(step, _):
        pair = jnp.concatenate([inputs(step), inputs(step + half)], axis=1)
        return jnp.dot(air_in[...], pair, preferred_element_type=F32)

    def middle(step, product):
        return twice_gelu(product).astype(BF16)

    def second(step, hidden):
        return jnp.dot(atm_out[...], hidden, preferred_element_type=F32)

    def last(step, update):
        news = []
        for offset in range(2):
            change = update[:, offset * 128 : (offset + 1) * 128]
            news.append(state[step + offset * half].astype(F32) + 0.5 * change)
        out(step, *news)

    staggered(half, first, middle, second, last)


def edge_forcing(forcing_x, forcing_y, d):
    lane = lanes((8, d.edge))
    block = lane // d.block
    row = lane % d.block

    inner = outer = jnp.zeros((8, d.edge), F32)
    for step in range(d.rows + 4):
        at = pl.ds(step * 8, 8)
        pad = [jnp.zeros((8, 128), F32)] * (d.pieces - 1)
        here = jnp.concatenate([forcing_x[at, :]] + pad, axis=1)
        there = jnp.concatenate([forcing_y[at, :]] + pad, axis=1)
        for index, column in enumerate((126, 0, 127, 1)):
            shift = step + index * d.block - column
            match = (block == index) & (row == step)
            if column in (0, 127):
                inner = jnp.where(match, roll(here, shift), inner)
            outer = jnp.where(match, roll(there, shift), outer)
    return inner, outer


def roll_rows(state, upper, lower, rolled, d):
    def put(row, values):
        rolled[row, 0:CH, :] = roll(values, 1)
        rolled[row, CH : 2 * CH, :] = values
        rolled[row, 2 * CH : 3 * CH, :] = roll(values, -1)

    for step in range(2):
        put(step, upper[step * CH : (step + 1) * CH, :])
        put(d.rows + 2 + step, lower[step * CH : (step + 1) * CH, :])
    for row in range(d.rows):
        put(row + 2, state[row])


def sea(
    state, rolled, edges, left, right, out, forcing_x, forcing_y, ocn_in, ocn_out, wet,
    at_top, at_bottom, stack, hidden, side, d,
):
    rows, block = d.rows, d.block
    lane = lanes((CH, 128))
    spot = lanes((CH, d.edge))
    part = spot // block
    inner = edges
    outer = jnp.where((part == 0) | (part == 2), left, right)

    def sides_of(inner, outer, spot):
        first = spot < block
        return (
            jnp.where(first, outer, roll(inner, -block)),
            jnp.where(first, roll(outer, -2 * block), outer),
            jnp.where(first, roll(inner, -block), roll(outer, -2 * block)),
        )

    beside = sides_of(inner, outer, spot)
    middle = beside[1]
    force_in, force_out = edge_forcing(forcing_x, forcing_y, d)
    beside_forcing = sides_of(force_in, force_out, lanes((8, d.edge)))
    sub = subs((8, d.edge))
    ones = jnp.ones((8, d.edge), F32)
    forced = jnp.concatenate(
        [
            jnp.where(sub < 4, beside_forcing[0], beside_forcing[1]),
            jnp.where(sub < 4, beside_forcing[2], ones),
        ],
        axis=0,
    ).astype(BF16)
    columns = jnp.concatenate(list(beside) + [forced], axis=0)
    for tap in range(3):
        side[tap * 256 : (tap + 1) * 256, :] = roll(columns, -tap)

    sub_row = subs((8, 128))
    lane_row = lanes((8, 128))

    for row in range(rows + 4):
        entry = roll(middle, -row)[:, :128]
        stack[row, 0:CH, :] = jnp.where(lane == 0, entry, rolled[row, 0:CH, :])
        stack[row, CH : 2 * CH, :] = rolled[row, CH : 2 * CH, :]
        entry = roll(middle, 127 - block - row)[:, :128]
        stack[row, 2 * CH : 3 * CH, :] = jnp.where(lane == 127, entry, rolled[row, 2 * CH : 3 * CH, :])
        here, there = forcing_x[row * 8 : row * 8 + 8, :], forcing_y[row * 8 : row * 8 + 8, :]
        before = roll(jnp.where(lane_row == 127, there, here), 1)
        after = roll(jnp.where(lane_row == 0, there, here), -1)
        stack[row, 3 * CH : 256, :] = jnp.concatenate(
            [jnp.where(sub_row < 4, before, here), jnp.where(sub_row < 4, after, 1.0)], axis=0
        ).astype(BF16)

    pairs = (rows + 2) // 2

    def first(step, _):
        taps = jnp.concatenate(
            [
                stack[step : step + 3].reshape(3 * 256, 128),
                stack[step + pairs : step + pairs + 3].reshape(3 * 256, 128),
            ],
            axis=1,
        )
        return jnp.dot(ocn_in[...], taps, preferred_element_type=F32)

    def activate(step, product):
        active = twice_gelu(product)
        low, high = active[:, :128], active[:, 128:]
        if step == 0:
            low = jnp.where(at_top != 0, 0.0, low)
        if step == pairs - 1:
            high = jnp.where(at_bottom != 0, 0.0, high)
        hidden[step, 0:HIDK, :] = low.astype(BF16)
        hidden[step + pairs, 0:HIDK, :] = high.astype(BF16)
        blank = jnp.zeros((HIDP - HIDK, 128), BF16)
        hidden[step, HIDK:HIDP, :] = blank
        hidden[step + pairs, HIDK:HIDP, :] = blank

    staggered(pairs, first, activate)
    product = jnp.dot(ocn_in[...], side[...], preferred_element_type=F32)
    spot = lanes((1, d.edge)) % block
    gone = ((spot == 0) & (at_top != 0)) | ((spot == rows + 1) & (at_bottom != 0))
    active = jnp.where(gone, 0.0, twice_gelu(product)).astype(BF16)
    active = jnp.concatenate([active, jnp.zeros((HIDP - HIDK, d.edge), BF16)], axis=0)

    taps = jnp.concatenate([roll(active, -tap) for tap in range(3)], axis=0)
    from_left = jnp.dot(ocn_out[0:CH, :], taps, preferred_element_type=F32)
    from_right = jnp.dot(ocn_out[2 * CH : 3 * CH, :], taps, preferred_element_type=F32)
    half = rows // 2

    def second(step, _):
        taps = jnp.concatenate(
            [
                hidden[step : step + 3].reshape(3 * HIDP, 128),
                hidden[step + half : step + half + 3].reshape(3 * HIDP, 128),
            ],
            axis=1,
        )
        return jnp.dot(ocn_out[...], taps, preferred_element_type=F32)

    def last(step, product):
        news = []
        for offset in range(2):
            row = step + offset * half
            sums = product[:, offset * 128 : (offset + 1) * 128]
            entry = roll(from_left, -row)[:, :128]
            total = sums[CH : 2 * CH] + jnp.where(lane == 0, entry, roll(sums[0:CH], 1))
            entry = roll(from_right, 127 - block - row)[:, :128]
            total = total + jnp.where(lane == 127, entry, roll(sums[2 * CH : 3 * CH], -1))
            update = total * (0.5 * wet[row : row + 1, :].astype(F32))
            news.append(state[row].astype(F32) + update)
        out(step, *news)

    staggered(half, second, last)


def prepare(atm_in, atm_bias, ocn_in, ocn_bias, ocn_out, air_in, first, second, is_ocean):
    def bias_rows(ref, width):
        row = jnp.concatenate([ref[index : index + 1, :] for index in range(ref.shape[0])], axis=1)
        terms = list(split_bf16(row)) + [jnp.zeros_like(row)]
        bias = jnp.concatenate(terms, axis=0)
        return jnp.pad(bias, ((0, 0), (0, width - bias.shape[1])))

    @pl.when(is_ocean == 0)
    def _():
        columns = jnp.concatenate(
            [atm_in[...].astype(F32), bias_rows(atm_bias, HA), jnp.zeros((40, HA), F32)], axis=0
        )
        air_in[...] = columns.T.astype(BF16)

    @pl.when(is_ocean != 0)
    def _():
        bias = bias_rows(ocn_bias, 256)
        count = ocn_in.shape[2]
        for tap in range(3):
            whole = [ocn_in[3 * tap + side].astype(F32) for side in range(3)]
            whole = [jnp.pad(values, ((0, 0), (0, 256 - count))) for values in whole]
            rows = [values[:CH] for values in whole] + [values[CH:] for values in whole]
            rows.append(bias if tap == 0 else jnp.zeros((4, 256), F32))
            columns = jnp.concatenate(rows, axis=0).T
            first[:, tap * 256 : (tap + 1) * 256] = columns[:HIDK].astype(BF16)
        for tap in range(9):
            values = ocn_out[tap].astype(F32)
            at, column = tap // 3 * HIDP, tap % 3
            second[column * CH : (column + 1) * CH, at : at + HIDP] = jnp.pad(
                values, ((0, 0), (0, HIDP - count))
            ).astype(BF16)


def ends(flags):
    at_top, at_bottom, even = flags[1] != 0, flags[2] != 0, flags[3] == 0

    def up_and_down(one, two):
        above = jnp.where(even, two, one).astype(F32)
        below = jnp.where(even, one, two).astype(F32)
        return jnp.where(at_top, 0.0, above), jnp.where(at_bottom, 0.0, below)

    return up_and_down


def middle_kernel(d, opening, *refs):
    refs = list(refs)
    take = lambda count: [refs.pop(0) for _ in range(count)]
    flags, state, field_one, beside, field_two, from_one, from_two = take(7)
    if opening:
        planes, *far_weights = take(6)
    else:
        (plan_x,) = take(1)
    part_x, fields_x, rolled = take(3)
    if opening:
        plan_x, *made_weights = take(4)
    (coupled,) = take(1)
    if opening:
        *raw_weights, sems = take(6)
        copies = fetch(far_weights, raw_weights, sems)
    rows, tall = d.rows, d.tall
    is_ocean = flags[0]
    up_and_down = ends(flags)

    if opening:

        @pl.when(is_ocean != 0)
        def _():
            base = d.strip
            pair = up_and_down(from_one[base : base + 16, :], from_two[base : base + 16, :])
            plan_x[...] = jnp.zeros_like(plan_x)
            for step, strip in zip((0, rows + 2), pair):
                for index in range(2):
                    plan_x[pl.ds(step + index, 2 * NK, stride=tall), :] = strip[index * 8 : (index + 1) * 8]

        for plane in range(2 * NK):
            plan_x[plane * tall + 2 : plane * tall + 2 + rows, :] = planes[plane].astype(F32)

    for field in range(NS):
        pair = up_and_down(field_one[field], field_two[field])
        fields_x[field, 0:16, :] = pair[0][rows - 16 : rows]
        fields_x[field, 16 : 16 + rows, :] = beside[field].astype(F32)
        fields_x[field, 16 + rows : 32 + rows, :] = pair[1][0:16]

    unit = couple(fields_x, coupled, rows)

    @pl.when(is_ocean == 0)
    def _():
        regrid_inside(coupled, unit, plan_x, part_x, 2, rows // 8, tall)

    @pl.when(is_ocean != 0)
    def _():
        regrid_inside(coupled, unit, plan_x, part_x, 0, d.tiles, tall)
        upper, lower = up_and_down(from_one[0 : 2 * CH, :], from_two[0 : 2 * CH, :])
        roll_rows(state, upper.astype(BF16), lower.astype(BF16), rolled, d)

    if opening:
        for copy in copies:
            copy.wait()
        prepare(*raw_weights, *made_weights, is_ocean)


def step_kernel(d, opening, closing, *refs):
    refs = list(refs)
    take = lambda count: [refs.pop(0) for _ in range(count)]
    flags, state, wet, from_left, from_right = take(5)
    part_x, fields_x, rolled, edges, plan_x, air_in, first, second, atm_out = take(9)
    if not opening:
        (plan_e,) = take(1)
    if not closing:
        surface, places = take(2)
    (out,) = take(1)
    if not closing:
        fields, new_edges, one, two = take(4)
    if opening:
        (plan_e,) = take(1)
    window, forcing_x, forcing_y, stack, hidden, side, raw = take(7)
    if opening:
        (plan_y,) = take(1)
    rows, tall = d.rows, d.tall
    is_ocean, at_top, at_bottom = flags[0], flags[1], flags[2]
    up_and_down = ends(flags)

    if opening:

        @pl.when(is_ocean != 0)
        def _():
            plan_y[...] = jnp.zeros_like(plan_y)
            base = d.edge_rows
            parts = [
                (ref[base : base + 16, :], ref[base + 16 + rows : base + 32 + rows, :],
                 ref[base + 16 : base + 16 + rows, :])
                for ref in (from_left, from_right)
            ]
            for plane in range(2 * NK):
                first_end, second_end, own = [
                    unpack_columns(left, right, plane, 2 * NK, 2) for left, right in zip(*parts)
                ]
                above, below = up_and_down(first_end, second_end)
                at = plane * tall
                plan_y[at : at + 2, :] = above[14:16]
                plan_y[at + 2 : at + 2 + rows, :] = own
                plan_y[at + 2 + rows : at + 4 + rows, :] = below[0:2]

    base = d.edge_rows + (rows + 32 if opening else 0)
    parts = [
        (ref[base : base + 16, :], ref[base + 16 + rows : base + 32 + rows, :],
         ref[base + 16 : base + 16 + rows, :])
        for ref in (from_left, from_right)
    ]
    for field in range(NS):
        first_end, second_end, own = [
            unpack_columns(left, right, field, NS, REACH) for left, right in zip(*parts)
        ]
        above, below = up_and_down(first_end, second_end)
        for at, values in ((0, above), (16, own), (16 + rows, below)):
            count = values.shape[0]
            inside = roll(fields_x[field, at : at + count, :], 32)
            lane = lanes(values.shape)
            near = (lane >= 32 - REACH) & (lane < 32 + REACH)
            far = (lane < REACH) | (lane >= 128 - REACH)
            kept = jnp.where(near, inside, jnp.where(far, values, 0.0))
            window[field, at : at + count, :] = kept
    def finished():
        emission = None if closing else Emission(surface, flags, places, raw, d)

        def put(step, low, high):
            if closing:
                for row, values in ((step, low), (step + rows // 2, high)):
                    raw[row * CH : (row + 1) * CH, :] = values
                return
            out[step] = low.astype(BF16)
            out[step + rows // 2] = high.astype(BF16)

        def close():
            if not closing:
                emission.close(out, wet, fields, new_edges, one, two)

        return put, close

    @pl.when(is_ocean == 0)
    def _():
        if opening:
            plan_edges(plan_x, plan_y, plan_e, 2, rows // 8, tall, False)
        regrid_beside(
            window, plan_e, part_x, forcing_x, forcing_y, 2, rows // 8, tall, False
        )
        put, close = finished()
        air(state, put, forcing_x, air_in, atm_out, d)
        close()

    @pl.when(is_ocean != 0)
    def _():
        if opening:
            plan_edges(plan_x, plan_y, plan_e, 0, d.tiles, tall, True)
        regrid_beside(
            window, plan_e, part_x, forcing_x, forcing_y, 0, d.tiles, tall, True
        )
        put, close = finished()
        joined = [get_edges(ref, 0, d) for ref in (from_left, from_right)]
        sea(
            state, rolled, get_edges(edges, 0, d), *joined, put, forcing_x, forcing_y,
            first, second, wet, at_top, at_bottom, stack, hidden, side, d,
        )
        close()

    if closing:
        for channel in range(CH):
            out[channel] = raw[pl.ds(channel, rows, stride=CH), :].astype(BF16)


VMEM = pl.BlockSpec(memory_space=pltpu.VMEM)
HBM = pl.BlockSpec(memory_space=pltpu.HBM)
SMEM = pl.BlockSpec(memory_space=pltpu.SMEM)
PARAMS = pltpu.CompilerParams(vmem_limit_bytes=48 * 1024 * 1024)


def shape(*dims, dtype=BF16):
    return jax.ShapeDtypeStruct(dims, dtype)


def send(x, move):
    names = ("grp", "lat", "lon")
    sizes = [lax.axis_size(name) for name in names]
    pairs = []
    for group in range(sizes[0]):
        for lat in range(sizes[1]):
            for lon in range(sizes[2]):
                to = move(group, lat, lon)
                if to is None or not 0 <= to[1] < sizes[1]:
                    continue
                target = (to[0] * sizes[1] + to[1]) * sizes[2] + to[2] % sizes[2]
                pairs.append(((group * sizes[1] + lat) * sizes[2] + lon, target))
    return lax.ppermute(x, names, pairs)


def swap_rows(x, turn, across):
    count, columns = lax.axis_size("lat"), lax.axis_size("lon")

    def move(group, lat, lon):
        other = ((lat + turn) ^ 1) - turn
        if 0 <= other < count and (across or group == 1):
            return (1 - group if across else group), other, lon
        beside = lon ^ 1
        return group, lat, beside if beside < columns else lon

    return send(x, move)


def exchange(fields, own_edges, one, two, sides, d):
    rows = d.rows
    scale = jnp.where(lax.axis_index("grp") > 1, 0, 1).astype(BF16)
    later = fields * scale
    beside = send(fields, lambda g, i, j: (1 - g, i, j))
    from_one = swap_rows(one, 0, False)
    from_two = swap_rows(two, 1, False)
    field_one = swap_rows(later, 0, True)
    field_two = swap_rows(later, 1, True)
    beside, from_one = lax.optimization_barrier((beside, from_one))
    from_two, beside = lax.optimization_barrier((from_two, beside))
    field_one, from_two = lax.optimization_barrier((field_one, from_two))
    field_two, field_one = lax.optimization_barrier((field_two, field_one))
    lat, count = lax.axis_index("lat"), lax.axis_size("lat")
    odd = lat % 2 == 1
    edges = own_edges
    for turn, ref in ((0, from_one), (1, from_two)):
        other = ((lat + turn) ^ 1) - turn
        there = (other >= 0) & (other < count)
        edges = edges + jnp.where(there, ref[2 * CH : d.strip], 0)
    outer = [field_one[NS], field_two[NS]]
    if rows != 16:
        outer = [
            jnp.where(odd, outer[0][rows - 16 :], outer[0][:16]),
            jnp.where(odd, outer[1][:16], outer[1][rows - 16 :]),
        ]
    packed = [edges]
    if sides is not None:
        packed += [from_one[d.strip + 16 :], sides, from_two[d.strip + 16 :]]
    packed += [outer[0], beside[NS], outer[1]]
    packed = jnp.concatenate(packed, axis=0)
    from_left = send(packed, lambda g, i, j: (g, i, j + 1))
    from_right = send(packed, lambda g, i, j: (g, i, j - 1))
    return (field_one, beside, field_two, from_one, from_two), (from_left, from_right), edges


def local(
    coupled_state, land_mask, regrid_offsets, regrid_weights, surface_proj,
    atm_in, atm_bias, atm_out, ocn_in, ocn_bias, ocn_out,
):
    rows = coupled_state.shape[2]
    assert coupled_state.shape[3] == 128
    d = Dims(rows)
    group = lax.axis_index("grp")
    lat = lax.axis_index("lat")
    flags = jnp.stack(
        [group, lat == 0, lat == lax.axis_size("lat") - 1, lat % 2]
    ).astype(jnp.int32)
    raw_weights = (
        atm_in.T,
        atm_bias.reshape(HA // 128, 128),
        jnp.transpose(ocn_in, (1, 2, 0)),
        ocn_bias[None],
        jnp.transpose(ocn_out, (1, 0, 2)),
    )
    state_shape = shape(rows, CH, 128)
    emitted = [
        shape(NS + 1, rows, 128),
        shape(d.edge_rows, 128),
        shape(d.strip, 128),
        shape(d.strip, 128),
    ]
    raw = pltpu.VMEM((rows * 8, 128), F32)
    turned = pltpu.VMEM((CH * rows, 128), F32)

    def call(kernel, operands, outs, scratch, name, far=()):
        scratch = scratch + [pltpu.VMEM(x.shape, x.dtype) for x in far]
        if far:
            scratch.append(pltpu.SemaphoreType.DMA((len(far) + CH // 16,)))

        far = [pltpu.with_memory_space_constraint(x, pltpu.HBM) for x in far]
        return pl.pallas_call(
            kernel,
            out_shape=outs,
            in_specs=[SMEM] + [VMEM] * len(operands) + [HBM] * len(far),
            out_specs=[VMEM] * len(outs),
            scratch_shapes=scratch,
            compiler_params=PARAMS,
            name=name,
        )(flags, *operands, *far)

    state, planes, sides, places, fields, edges, one, two = call(
        functools.partial(start_kernel, d),
        (),
        [state_shape, shape(2 * NK, rows, 128), shape(rows, 128), shape(rows * 128, d.edge)]
        + emitted[:2]
        + [shape(d.strip + 32, 128)] * 2,
        [raw, pltpu.VMEM((2 * NK * rows, 128), F32), turned],
        "start",
        (coupled_state[0], surface_proj, land_mask, regrid_offsets[0], regrid_weights[0]),
    )

    plan = shape(2 * NK * d.tall, 128, dtype=F32)
    between = [
        shape(NS * d.tall, 128, dtype=F32),
        shape(NS, rows + 32, 128, dtype=F32),
        shape(rows + 4, 3 * CH, 128),
    ]
    made = [shape(HA, 128), shape(HIDK, 768), shape(3 * CH, 3 * HIDP)]
    coupled = pltpu.VMEM((NS // 2, rows + 32, 128), jnp.int32)
    scratch = [
        pltpu.VMEM((NS, rows + 32, 128), F32),
        pltpu.VMEM((d.tall * 8, 128), F32),
        pltpu.VMEM((d.tall * 8, 128), F32),
        pltpu.VMEM((rows + 4, 256, 128), BF16),
        pltpu.VMEM((rows + 2, HIDP, 128), BF16),
        pltpu.VMEM((768, d.edge), BF16),
    ]

    vertical, horizontal, edges = exchange(fields, edges, one, two, sides, d)
    *shared, plan_x, air_in, first, second = call(
        functools.partial(middle_kernel, d, True),
        (state, *vertical, planes),
        between + [plan] + made,
        [coupled],
        "first_middle",
        raw_weights,
    )
    weights = (air_in, first, second, atm_out)
    state, fields, edges, one, two, plan_e = call(
        functools.partial(step_kernel, d, True, False),
        (state, land_mask, *horizontal, *shared, edges, plan_x, *weights, surface_proj, places),
        [state_shape] + emitted + [shape(2 * d.tall, 128, dtype=F32)],
        scratch + [raw, pltpu.VMEM(plan.shape, F32)],
        "first_step",
    )

    vertical, horizontal, edges = exchange(fields, edges, one, two, None, d)
    shared = call(
        functools.partial(middle_kernel, d, False),
        (state, *vertical, plan_x),
        between,
        [coupled],
        "second_middle",
    )
    (state,) = call(
        functools.partial(step_kernel, d, False, True),
        (state, land_mask, *horizontal, *shared, edges, plan_x, *weights, plan_e),
        [shape(CH, rows, 128)],
        scratch + [turned],
        "second_step",
    )
    return state[None]


def solution(mesh):
    return jax.shard_map(
        local,
        mesh=mesh,
        in_specs=(
            P("grp", None, "lat", "lon"),
            P("lat", "lon"),
            P("grp", None, None, "lat", "lon"),
            P("grp", None, "lat", "lon"),
            P(),
            P(),
            P(),
            P(),
            P(),
            P(),
            P(),
        ),
        out_specs=P("grp", None, "lat", "lon"),
        check_vma=False,
    )
```
